32 devices in a mesh: lvl: 2 (over x), patch: 16 (over z, y, core).
Axes of the slice: x: 2, y: 2, z: 4, core: 2. Of those that a mesh axis runs over, the one named last changes fastest.
Arguments:
- coarse_input: float32 [16, 64, 192], P('patch', 'lvl'), may hold values from -6 to 6
- coarse_weight: float32 [192, 320], replicated, may hold values from -0.4375 to 0.4375
- fine_input: float32 [256, 256, 768], P(('lvl', 'patch')), may hold values from -6 to 6
- fine_target: float32 [256, 256, 768], P(('lvl', 'patch')), may hold values from -6 to 6
- crops: int32 [256, 4], P(('lvl', 'patch')), may hold values from 0 to 15, as said below
- in_weight: float32 [768, 320], replicated, may hold values from -0.21875 to 0.21875
- context_weight: float32 [320, 320], replicated, may hold values from -0.3125 to 0.3125
- out_weight: float32 [320, 768], replicated, may hold values from -0.3125 to 0.3125
Outputs:
- coarse_grad: float32 [16, 64, 192], P('patch', 'lvl')
- fine_grad: float32 [256, 256, 768], P(('lvl', 'patch'))
The draws below stay inside these ranges and needn't reach their ends.
Inputs may be any that keep to these rules, and one draw needn't show every extreme that they name: `crops`: Columns: frame 0 to 15, offsets y and x 0 to 8 - 2 s, scale s 1 or 2; frames are unevenly used. In one device's aligned block of 8 patches no frame is named twice, and at most min(8, 1) of them name frames of one index of patch (frames 1 i to 1 i + 1 - 1); this most is reached on every device.
All inputs are finite; a program needn't handle non-finite values.
Results may differ from the reference program's by a relative error of at most 0.0003.
Values sent between devices are 32-bit elements; how exact they have to be, the bound alone decides.
No kernel may reach another device: no remote copies, remote signals or barrier semaphores. Data moves between devices by JAX's collectives and lax.ppermute only.
A program may use at most 128 MiB of HBM per device.

```python
import jax
import jax.numpy as jnp
from jax import lax

C = 320
FV = 768
CV = 192
FR_DEV = 1
PD = 8
F = 16
NP = 256


def draw_crops(key, part):
    key = jax.random.fold_in(key, 7)
    keys = jax.random.split(key, 5)
    blocks = NP // PD
    owners = F // FR_DEV
    first = jax.random.randint(keys[0], (blocks,), 0, owners)
    second = jax.random.randint(keys[1], (blocks,), 0, owners)
    start = FR_DEV * jnp.maximum(first, second)
    frame = ((start[:, None] + jnp.arange(PD, dtype=jnp.int32)[None, :]) % F).reshape(NP)
    scale = jax.random.randint(keys[2], (NP,), 1, 3)
    limit = 9 - 2 * scale
    offset_y = jax.random.randint(keys[3], (NP,), 0, 1024) % limit
    offset_x = jax.random.randint(keys[4], (NP,), 0, 1024) % limit
    return jnp.stack([frame, offset_y, offset_x, scale], axis=1).astype(jnp.int32)


def levels(stream_key, dims, cuts, least, top_value):
    gain, own = 1.0, jax.random.fold_in(stream_key, 6)
    for axis_at, parts in cuts:
        steps = jnp.exp(jax.random.uniform(jax.random.fold_in(own, axis_at), (parts,), jnp.float32, least / len(cuts), top_value / len(cuts)))
        gain = gain * jnp.repeat(steps, dims[axis_at] // parts).reshape([-1 if axis == axis_at else 1 for axis in range(len(dims))])
    return gain


def gaussian(rng, dims, scale, most, cuts=(), kind=jnp.bfloat16):
    gain = levels(rng, dims, cuts, -0.22, 0.18) if cuts else 1.0
    array = jax.random.normal(rng, dims, jnp.float32) * scale * gain
    return jnp.minimum(jnp.maximum(array, -most), most).astype(kind)


def setup_inputs(seed: int = 0) -> dict:
    streams_of = jax.random.split(jax.random.key(seed), 9)
    coarse_input = gaussian(streams_of[0], (F, 64, CV), 1.0, 6.0, ((0, 16), (1, 2)), jnp.float32)
    coarse_weight = gaussian(streams_of[1], (CV, C), CV ** -0.5, 0.4375, (), jnp.float32)
    fine_input = gaussian(streams_of[2], (NP, 256, FV), 1.0, 6.0, ((0, 32),), jnp.float32)
    fine_target = gaussian(streams_of[3], (NP, 256, FV), 1.0, 6.0, ((0, 32),), jnp.float32)
    crops = draw_crops(jax.random.fold_in(streams_of[8], 71), 0)
    in_weight = gaussian(streams_of[5], (FV, C), FV ** -0.5, 0.21875, (), jnp.float32)
    context_weight = gaussian(streams_of[6], (C, C), C ** -0.5, 0.3125, (), jnp.float32)
    out_weight = gaussian(streams_of[7], (C, FV), C ** -0.5, 0.3125, (), jnp.float32)
    return dict(coarse_input=coarse_input, coarse_weight=coarse_weight, fine_input=fine_input, fine_target=fine_target, crops=crops, in_weight=in_weight, context_weight=context_weight, out_weight=out_weight)


def silu_grad(value):
    gate = jax.nn.sigmoid(value)
    return gate * (1.0 + value * (1.0 - gate))

def slot_tables(crops):
    frame = crops[:, 0]
    offset_y = crops[:, 1]
    offset_x = crops[:, 2]
    span = 2 * crops[:, 3][:, None]
    slots = jnp.arange(16, dtype=jnp.int32)
    row_a = slots // 4
    col_b = slots % 4
    valid = (row_a[None, :] < span) & (col_b[None, :] < span)
    token = (offset_y[:, None] + row_a[None, :]) * 8 + offset_x[:, None] + col_b[None, :]
    row_ids = jnp.where(valid, frame[:, None] * 64 + token, -1).astype(jnp.int32)
    fine_tok = jnp.arange(256, dtype=jnp.int32)
    slot_of = fine_tok[None, :] // 16 * span // 16 * 4 + fine_tok[None, :] % 16 * span // 16
    select = (slot_of[:, :, None] == slots[None, None, :]).astype(jnp.float32)
    return (row_ids, select)

def fine_block(fine_input, fine_target, select, context_slot, in_weight, context_weight, out_weight):
    high = lax.Precision.HIGHEST
    context = jnp.einsum('ptk,pkc->ptc', select, context_slot, precision=high)
    pre_fine = jnp.einsum('ptv,vc->ptc', fine_input, in_weight, precision=high)
    pre_fine = pre_fine + jnp.einsum('ptd,dc->ptc', context, context_weight, precision=high)
    hidden = jax.nn.silu(pre_fine)
    output = jnp.einsum('ptc,cv->ptv', hidden, out_weight, precision=high)
    residual = output - fine_target
    dhidden = jnp.einsum('ptv,cv->ptc', residual, out_weight, precision=high)
    dpre = dhidden * silu_grad(pre_fine)
    fine_grad = jnp.einsum('ptc,vc->ptv', dpre, in_weight, precision=high)
    dcontext = jnp.einsum('ptc,dc->ptd', dpre, context_weight, precision=high)
    dslot = jnp.einsum('ptk,ptd->pkd', select, dcontext, precision=high)
    return (fine_grad, dslot)

def reference(coarse_input, coarse_weight, fine_input, fine_target, crops, in_weight, context_weight, out_weight):
    high = lax.Precision.HIGHEST
    pre = jnp.einsum('ftv,vc->ftc', coarse_input, coarse_weight, precision=high)
    feat = jax.nn.silu(pre)
    width = feat.shape[2]
    rows = feat.reshape(F * 64, width)
    row_ids, select = slot_tables(crops)
    valid = row_ids >= 0
    context_slot = rows[jnp.maximum(row_ids, 0)] * valid[:, :, None].astype(jnp.float32)
    blocks = NP // PD

    def one(pieces):
        return fine_block(pieces[0], pieces[1], pieces[2], pieces[3], in_weight, context_weight, out_weight)
    fine_grad, dslot = lax.map(one, (fine_input.reshape(blocks, PD, 256, -1), fine_target.reshape(blocks, PD, 256, -1), select.reshape(blocks, PD, 256, 16), context_slot.reshape(blocks, PD, 16, width)))
    fine_grad = fine_grad.reshape(NP, 256, -1)
    dslot = dslot.reshape(NP * 16, width)
    targets = jnp.where(valid, row_ids, F * 64).reshape(-1)
    dfeat = jax.ops.segment_sum(dslot, targets, num_segments=F * 64 + 1)[:F * 64].reshape(F, 64, width)
    dpre = dfeat * silu_grad(pre)
    coarse_grad = jnp.einsum('ftc,vc->ftv', dpre, coarse_weight, precision=high)
    return (coarse_grad, fine_grad)
```

```python
import functools

import jax
import jax.numpy as jnp
from jax import lax
from jax.experimental import pallas as pl
from jax.experimental.pallas import tpu as pltpu
from jax.sharding import PartitionSpec as P

F32 = jnp.float32
BF16 = jnp.bfloat16
NN = (((1,), (0,)), ((), ()))
NT = (((1,), (1,)), ((), ()))
TN = (((0,), (0,)), ((), ()))
ROWS = 512
SIDE = 8
TALL = 12
LIMIT = 40 * 1024 * 1024


def split(value):
    high = value.astype(BF16)
    low = (value - high.astype(F32)).astype(BF16)
    return high, low


def dot(left, right, dims=NN):
    return lax.dot_general(left, right, dims, preferred_element_type=F32)


def dot3(left, right, dims=NN):
    return (
        dot(left[0], right[1], dims) + dot(left[1], right[0], dims) + dot(left[0], right[0], dims)
    )


def call(kernel, name, flops, out_shape, **kwargs):
    shapes = jax.tree.leaves(out_shape)
    moved = 2 * sum(s.size * 4 for s in shapes)
    return pl.pallas_call(
        kernel,
        out_shape=out_shape,
        name=name,
        cost_estimate=pl.CostEstimate(flops=flops, bytes_accessed=moved, transcendentals=0),
        compiler_params=pltpu.CompilerParams(vmem_limit_bytes=LIMIT),
        **kwargs,
    )


SMEM = pl.BlockSpec(memory_space=pltpu.SMEM)
VMEM = pl.BlockSpec(memory_space=pltpu.VMEM)


def find_crops(place_ref, table_ref, found_ref, peers, patches):
    for d in range(peers):
        found_ref[d] = -1

        def one(j, _):
            @pl.when(table_ref[d * patches + j, 0] == place_ref[0])
            def _():
                found_ref[d] = table_ref[d * patches + j, 1] * SIDE + table_ref[d * patches + j, 2]

            return 0

        lax.fori_loop(0, patches, one, 0, unroll=True)


def grid_row(row):
    return pl.ds(pl.multiple_of(row * SIDE, SIDE), SIDE)


def crop_kernel(peers, patches, place_ref, table_ref, mine_ref, other_ref, send_ref, found_ref, pad):
    half = place_ref[1]
    pad[8 * SIDE :, :] = jnp.zeros((4 * SIDE, pad.shape[1]), F32)
    for row in range(4):
        pad[grid_row(half * 4 + row), :] = mine_ref[0, row * SIDE : (row + 1) * SIDE, :]
        pad[grid_row((1 - half) * 4 + row), :] = other_ref[0, row * SIDE : (row + 1) * SIDE, :]
    find_crops(place_ref, table_ref, found_ref, peers, patches)
    for d in range(peers):
        base = jnp.maximum(found_ref[d], 0)
        top, left = base // SIDE, base % SIDE
        for a in range(4):
            line = pltpu.roll(pad[grid_row(top + a), :], SIDE - left, 0)
            send_ref[d * 16 + a * 4 : d * 16 + a * 4 + 4, :] = line[:4, :]


def scatter_kernel(peers, place_ref, found_ref, recv_ref, mine_ref, other_ref, pad):
    pad[...] = jnp.zeros_like(pad)
    blank = jnp.zeros((4, pad.shape[1]), F32)
    for d in range(peers):

        @pl.when(found_ref[d] >= 0)
        def _():
            top, left = found_ref[d] // SIDE, found_ref[d] % SIDE
            for a in range(4):
                part = recv_ref[d * 16 + a * 4 : d * 16 + a * 4 + 4, :]
                line = pltpu.roll(jnp.concatenate([part, blank], axis=0), left, 0)
                pad[grid_row(top + a), :] += line

    half = place_ref[1]
    for row in range(4):
        mine_ref[0, row * SIDE : (row + 1) * SIDE, :] = pad[grid_row(half * 4 + row), :]
        other_ref[0, row * SIDE : (row + 1) * SIDE, :] = pad[grid_row((1 - half) * 4 + row), :]


def first_kernel(x_ref, t_ref, win_ref, wo_ref, xw_ref, tw_ref, gram_ref, win_hi, win_lo, wo_hi, wo_lo):
    @pl.when(pl.program_id(0) == 0)
    def _():
        win_hi[...], win_lo[...] = split(win_ref[...])
        high, low = split(wo_ref[...])
        wo_hi[...], wo_lo[...] = high, low
        gram_ref[...] = dot3((high, low), (high, low), NT) + dot(low, low, NT)

    xw_ref[...] = dot3(split(x_ref[...]), (win_hi[...], win_lo[...]))
    tw_ref[...] = dot3(split(t_ref[...]), (wo_hi[...], wo_lo[...]), NT)


def row_scale(crops_ref, patches, shape, axis, each):
    index = lax.broadcasted_iota(jnp.int32, shape, axis) // each
    scale = jnp.zeros(shape, jnp.int32)
    for j in range(patches):
        scale = jnp.where(index == j, crops_ref[j, 3], scale)
    return scale


def chosen(crops_ref, patches, rows_first):
    shape = (patches * 64, patches * 16) if rows_first else (patches * 16, patches * 64)
    token_axis = 0 if rows_first else 1
    token = lax.broadcasted_iota(jnp.int32, shape, token_axis)
    slot = lax.broadcasted_iota(jnp.int32, shape, 1 - token_axis)
    scale = row_scale(crops_ref, patches, shape, token_axis, 64)
    group, column = (token // 16) % 4, token % 16
    wanted = token // 64 * 16 + (group * scale // 2) * 4 + column * scale // 8
    return jnp.where(slot == wanted, 1.0, 0.0).astype(BF16)


def middle_kernel(
    patches,
    peers,
    crops_ref,
    recv_ref,
    xw_ref,
    tw_ref,
    gram_ref,
    cwgt_ref,
    xwgt_ref,
    de_ref,
    send_ref,
    rows,
    slope,
    context,
    sums,
    gram_hi,
    gram_lo,
):
    step = pl.program_id(0)
    per_step = ROWS // 4

    @pl.when(step == 0)
    def _():
        for j in range(patches):
            start = pl.multiple_of(crops_ref[j, 0] * 16, 16)
            rows[j * 16 : j * 16 + 16, :] = recv_ref[pl.ds(start, 16), :]
        pre = dot3(split(rows[...]), split(cwgt_ref[...]))
        gate = jax.nn.sigmoid(pre)
        slope[...] = gate * (1.0 + pre * (1.0 - gate))
        projected = split(dot3(split(pre * gate), split(xwgt_ref[...])))
        pick = chosen(crops_ref, patches, True)
        context[...] = dot(pick, projected[1]) + dot(pick, projected[0])
        gram_hi[...], gram_lo[...] = split(gram_ref[...])

    width = xw_ref.shape[1]
    here = pl.ds(pl.multiple_of(step * per_step, per_step), per_step)
    groups = per_step // 16
    spread = context[here, :].reshape(groups, 1, 16, width)
    pre = xw_ref[...].reshape(groups, 4, 16, width) + spread
    pre = pre.reshape(ROWS, width)
    gate = jax.nn.sigmoid(pre)
    hidden = pre * gate
    dhidden = dot3(split(hidden), (gram_hi[...], gram_lo[...])) - tw_ref[...]
    de = dhidden * (gate * (1.0 + pre * (1.0 - gate)))
    de_ref[...] = de
    sums[here, :] = de.reshape(groups, 4, 16, width).sum(axis=1).reshape(per_step, width)

    @pl.when(step == pl.num_programs(0) - 1)
    def _():
        pick = chosen(crops_ref, patches, False)
        high, low = split(sums[...])
        dslot = dot(pick, low) + dot(pick, high)
        dcontext = dot3(split(dslot), split(xwgt_ref[...]), NT)
        grad = dot3(split(dcontext * slope[...]), split(cwgt_ref[...]), NT)
        send_ref[...] = jnp.zeros_like(send_ref)
        for j in range(patches):
            start = pl.multiple_of(crops_ref[j, 0] * 16, 16)
            send_ref[pl.ds(start, 16), :] = grad[j * 16 : j * 16 + 16, :]


def last_kernel(de_ref, win_ref, out_ref, win_hi, win_lo):
    @pl.when(pl.program_id(0) == 0)
    def _():
        win_hi[...], win_lo[...] = split(win_ref[...])

    out_ref[...] = dot3(split(de_ref[...]), (win_hi[...], win_lo[...]), NT)


def whole(shape):
    return pl.BlockSpec(shape, lambda i: (0,) * len(shape))


def by_rows(width):
    return pl.BlockSpec((ROWS, width), lambda i: (i, 0))


def body(coarse_input, coarse_weight, fine_input, fine_target, crops, in_weight, context_weight, out_weight):
    peers = lax.axis_size("patch")
    patches, tokens, values = fine_input.shape
    width = in_weight.shape[1]
    pixels = coarse_weight.shape[0]
    half = coarse_input.shape[1]
    count = patches * tokens
    steps = count // ROWS
    place = jnp.stack([lax.axis_index("patch"), lax.axis_index("lvl")]).astype(jnp.int32)
    swap = [(0, 1), (1, 0)]

    table = lax.all_to_all(
        jnp.broadcast_to(crops[None], (peers,) + crops.shape), "patch", 0, 0
    ).reshape(peers * patches, 4)
    other = lax.ppermute(coarse_input, "lvl", swap)

    send, found = call(
        functools.partial(crop_kernel, peers, patches),
        "crop",
        10000,
        (
            jax.ShapeDtypeStruct((peers * 16, pixels), F32),
            jax.ShapeDtypeStruct((peers,), jnp.int32),
        ),
        in_specs=[SMEM, SMEM, VMEM, VMEM],
        out_specs=(VMEM, SMEM),
        scratch_shapes=[pltpu.VMEM((TALL * SIDE, pixels), F32)],
    )(place, table, coarse_input, other)
    recv = lax.all_to_all(send, "patch", 0, 0, tiled=True)

    xw, tw, gram = call(
        first_kernel,
        "first",
        12 * count * values * width,
        (
            jax.ShapeDtypeStruct((count, width), F32),
            jax.ShapeDtypeStruct((count, width), F32),
            jax.ShapeDtypeStruct((width, width), F32),
        ),
        grid=(steps,),
        in_specs=[by_rows(values), by_rows(values), whole((values, width)), whole((width, values))],
        out_specs=(by_rows(width), by_rows(width), whole((width, width))),
        scratch_shapes=[pltpu.VMEM((values, width), BF16)] * 2 + [pltpu.VMEM((width, values), BF16)] * 2,
    )(fine_input.reshape(count, values), fine_target.reshape(count, values), in_weight, out_weight)

    de, back = call(
        functools.partial(middle_kernel, patches, peers),
        "middle",
        6 * count * width * width,
        (
            jax.ShapeDtypeStruct((count, width), F32),
            jax.ShapeDtypeStruct((peers * 16, pixels), F32),
        ),
        grid=(steps,),
        in_specs=[
            SMEM,
            whole((peers * 16, pixels)),
            by_rows(width),
            by_rows(width),
            whole((width, width)),
            whole((pixels, width)),
            whole((width, width)),
        ],
        out_specs=(by_rows(width), whole((peers * 16, pixels))),
        scratch_shapes=[
            pltpu.VMEM((patches * 16, pixels), F32),
            pltpu.VMEM((patches * 16, width), F32),
            pltpu.VMEM((patches * 64, width), F32),
            pltpu.VMEM((patches * 64, width), F32),
            pltpu.VMEM((width, width), BF16),
            pltpu.VMEM((width, width), BF16),
        ],
    )(crops, recv, xw, tw, gram, coarse_weight, context_weight)
    returned = lax.all_to_all(back, "patch", 0, 0, tiled=True)

    fine_grad = call(
        last_kernel,
        "last",
        6 * count * values * width,
        jax.ShapeDtypeStruct((count, values), F32),
        grid=(steps,),
        in_specs=[by_rows(width), whole((values, width))],
        out_specs=by_rows(values),
        scratch_shapes=[pltpu.VMEM((values, width), BF16)] * 2,
    )(de, in_weight)

    mine, theirs = call(
        functools.partial(scatter_kernel, peers),
        "scatter",
        10000,
        (
            jax.ShapeDtypeStruct((1, half, pixels), F32),
            jax.ShapeDtypeStruct((1, half, pixels), F32),
        ),
        in_specs=[SMEM, SMEM, VMEM],
        out_specs=(VMEM, VMEM),
        scratch_shapes=[pltpu.VMEM((TALL * SIDE, pixels), F32)],
    )(place, found, returned)
    coarse_grad = mine + lax.ppermute(theirs, "lvl", swap)
    return (coarse_grad, fine_grad.reshape(fine_input.shape))


def solution(mesh):
    in_specs = (
        P("patch", "lvl", None),
        P(),
        P(("lvl", "patch"), None, None),
        P(("lvl", "patch"), None, None),
        P(("lvl", "patch"), None),
        P(),
        P(),
        P(),
    )
    out_specs = (P("patch", "lvl", None), P(("lvl", "patch"), None, None))
    return jax.shard_map(body, mesh=mesh, in_specs=in_specs, out_specs=out_specs, check_vma=False)
```

```python
import functools

import jax
import jax.numpy as jnp
from jax import lax
from jax.experimental import pallas as pl
from jax.experimental.pallas import tpu as pltpu
from jax.sharding import PartitionSpec as P

F32 = jnp.float32
BF16 = jnp.bfloat16
NN = (((1,), (0,)), ((), ()))
NT = (((1,), (1,)), ((), ()))
TN = (((0,), (0,)), ((), ()))
ROWS = 512
SIDE = 8
MAIN = 256
LANES = 256
LIMIT = 60 * 1024 * 1024
SMEM = pl.BlockSpec(memory_space=pltpu.SMEM)
VMEM = pl.BlockSpec(memory_space=pltpu.VMEM)


def split(value):
    high = value.astype(BF16)
    low = (value - high.astype(F32)).astype(BF16)
    return high, low


def dot(left, right, dims=NN):
    return lax.dot_general(left, right, dims, preferred_element_type=F32)


def dot3(left, right, dims=NN):
    return (
        dot(left[0], right[1], dims) + dot(left[1], right[0], dims) + dot(left[0], right[0], dims)
    )


def sigmoid(value):
    return 0.5 * jnp.tanh(0.5 * value) + 0.5


def deep_left(value):
    high, low = split(value)
    tails = [high[:, MAIN:], low[:, MAIN:], high[:, MAIN:]]
    return jnp.concatenate([high[:, :MAIN], low[:, :MAIN], high[:, :MAIN]] + tails, axis=1)


def fill_deep_right(ref, value):
    high, low = split(value)
    tail = value.shape[0] - MAIN
    for part, rows in enumerate((low, high, high)):
        ref[part * MAIN : (part + 1) * MAIN, :] = rows[:MAIN]
        start = 3 * MAIN + part * tail
        ref[start : start + tail, :] = rows[MAIN:]


def call(kernel, name, flops, out_shape, **kwargs):
    shapes = jax.tree.leaves(out_shape)
    moved = 2 * sum(s.size * 4 for s in shapes)
    return pl.pallas_call(
        kernel,
        out_shape=out_shape,
        name=name,
        cost_estimate=pl.CostEstimate(flops=flops, bytes_accessed=moved, transcendentals=0),
        compiler_params=pltpu.CompilerParams(vmem_limit_bytes=LIMIT),
        **kwargs,
    )


def fill_wide(weight_ref, main, tail):
    values = weight_ref.shape[1]
    high, low = split(weight_ref[...])
    for part, block in enumerate((low, high, high)):
        main[:, part * values : (part + 1) * values] = block[:MAIN]
    rest = high.shape[0] - MAIN
    tail[:rest, :values] = high[MAIN:]
    tail[:rest, values:] = high[MAIN:]
    tail[rest:, :values] = low[MAIN:]
    tail[rest:, values:] = jnp.zeros((rest, values), BF16)
    return high, low


def wide_product(value, main, tail, out_ref):
    high, low = split(value)
    rest = tail.shape[0] // 2
    out_ref[:, :MAIN] = dot(jnp.concatenate([high, low, high], axis=1), main[...], NT)
    both = dot(jnp.concatenate([high, low], axis=1), tail[...], NT)
    out_ref[:, MAIN:] = both[:, :rest] + both[:, rest:]


def input_kernel(x_ref, weight_ref, out_ref, main, tail):
    @pl.when(pl.program_id(0) == 0)
    def _():
        fill_wide(weight_ref, main, tail)

    wide_product(x_ref[...], main, tail, out_ref)


def target_kernel(t_ref, weight_ref, out_ref, gram_ref, main, tail):
    @pl.when(pl.program_id(0) == 0)
    def _():
        high, low = fill_wide(weight_ref, main, tail)
        gram_ref[...] = dot3((high, low), (high, low), NT) + dot(low, low, NT)

    wide_product(t_ref[...], main, tail, out_ref)


def row_value(crops_ref, column, patches, shape, axis, each):
    index = lax.broadcasted_iota(jnp.int32, shape, axis) // each
    found = jnp.zeros(shape, jnp.int32)
    for j in range(patches):
        found = jnp.where(index == j, crops_ref[column, j], found)
    return found


def chosen(crops_ref, patches, rows_first):
    shape = (patches * 64, patches * 16) if rows_first else (patches * 16, patches * 64)
    token_axis = 0 if rows_first else 1
    token = lax.broadcasted_iota(jnp.int32, shape, token_axis)
    slot = lax.broadcasted_iota(jnp.int32, shape, 1 - token_axis)
    scale = row_value(crops_ref, 3, patches, shape, token_axis, 64)
    group, column = (token // 16) % 4, token % 16
    wanted = token // 64 * 16 + (group * scale // 2) * 4 + column * scale // 8
    return jnp.where(slot == wanted, 1.0, 0.0).astype(BF16)


def middle_kernel(
    patches,
    peers,
    place_ref,
    crops_ref,
    *refs,
):
    shard_refs, refs = refs[:8], refs[8:]
    xw_ref, tw_ref, gram_ref, cwgt_ref, xwgt_ref, de_ref = refs[:6]
    send_refs, refs = refs[6 : 6 + peers], refs[6 + peers :]
    shards, rows, slope, context, sums, gram, grads = refs
    step = pl.program_id(0)
    per_step = ROWS // 4
    far = peers // 4
    half = shard_refs[0].shape[1]
    pixels = cwgt_ref.shape[0]

    @pl.when(step == 0)
    def _():
        for code, ref in enumerate(shard_refs):
            for k in range(far):
                start = (code * far + k) * half
                shards[start : start + half, :] = ref[k]
        me, side = place_ref[0], place_ref[1]
        for j in range(patches):
            frame, top, left = crops_ref[0, j], crops_ref[1, j], crops_ref[2, j]
            near = lax.bitwise_xor(frame % 4, me % 4)
            k = (me // 4 - frame // 4 + far) % far
            for a in range(4):
                row = jnp.minimum(top + a, SIDE - 1)
                code = lax.bitwise_xor(row // 4, side) * 4 + near
                start = pl.multiple_of(((code * far + k) * 4 + row % 4) * SIDE, SIDE)
                line = pltpu.roll(shards[pl.ds(start, SIDE), :], SIDE - left, 0)
                rows[j * 16 + a * 4 : j * 16 + a * 4 + 4, :] = line[:4, :]
        pre = dot3(split(rows[...]), split(cwgt_ref[...]))
        gate = sigmoid(pre)
        slope[...] = gate * (1.0 + pre * (1.0 - gate))
        projected = split(dot3(split(pre * gate), split(xwgt_ref[...])))
        pick = chosen(crops_ref, patches, True)
        context[...] = dot(pick, projected[1]) + dot(pick, projected[0])
        fill_deep_right(gram, gram_ref[...])

    width = xw_ref.shape[1]
    here = pl.ds(pl.multiple_of(step * per_step, per_step), per_step)
    groups = per_step // 16
    spread = context[here, :].reshape(groups, 1, 16, width)
    pre = xw_ref[...].reshape(groups, 4, 16, width) + spread
    pre = pre.reshape(ROWS, width)
    gate = sigmoid(pre)
    hidden = pre * gate
    dhidden = dot(deep_left(hidden), gram[...]) - tw_ref[...]
    de = dhidden * (gate + hidden * (1.0 - gate))
    de_ref[...] = de
    sums[here, :] = de.reshape(groups, 4, 16, width).sum(axis=1).reshape(per_step, width)

    @pl.when(step == pl.num_programs(0) - 1)
    def _():
        pick = chosen(crops_ref, patches, False)
        high, low = split(sums[...])
        dslot = dot(pick, low) + dot(pick, high)
        dcontext = dot3(split(dslot), split(xwgt_ref[...]), NT)
        grads[:, :pixels] = dot3(split(dcontext * slope[...]), split(cwgt_ref[...]), NT)
        shape = (patches * 16, LANES - pixels)
        slot = lax.broadcasted_iota(jnp.int32, shape, 0) % 16
        top = row_value(crops_ref, 1, patches, shape, 0, 16)
        left = row_value(crops_ref, 2, patches, shape, 0, 16)
        grads[:, pixels:] = ((top + slot // 4) * SIDE + left + slot % 4).astype(F32)
        for k, ref in enumerate(send_refs):
            target = (place_ref[0] + k) % peers
            found = jnp.int32(-1)
            for j in range(patches):
                found = jnp.where(crops_ref[0, j] == target, j, found)
            start = pl.multiple_of(jnp.maximum(found, 0) * 16, 16)
            ref[...] = jnp.where(found >= 0, grads[pl.ds(start, 16), :], 0.0)


def scatter_kernel(peers, place_ref, *refs):
    message_refs, (mine_ref, other_ref, total) = refs[:peers], refs[peers:]
    pixels = mine_ref.shape[2]
    message = jnp.concatenate([ref[...] for ref in message_refs], axis=0)
    number = lax.broadcasted_iota(jnp.int32, (peers * 16, SIDE * SIDE), 1).astype(F32)
    pick = jnp.where(message[:, pixels : pixels + 1] == number, 1.0, 0.0).astype(BF16)
    high, low = split(message[:, :pixels])
    total[...] = dot(pick, low, TN) + dot(pick, high, TN)
    half = mine_ref.shape[1]
    side = place_ref[1]
    mine_ref[0] = total[pl.ds(pl.multiple_of(side * half, half), half), :]
    other_ref[0] = total[pl.ds(pl.multiple_of((1 - side) * half, half), half), :]


def last_kernel(de_ref, weight_ref, out_ref, deep):
    @pl.when(pl.program_id(0) == 0)
    def _():
        fill_deep_right(deep, weight_ref[...])

    out_ref[...] = dot(deep_left(de_ref[...]), deep[...])


def whole(shape):
    return pl.BlockSpec(shape, lambda i: (0,) * len(shape))


def by_rows(width):
    return pl.BlockSpec((ROWS, width), lambda i: (i, 0))


def body(coarse_input, coarse_weight, fine_input, fine_target, crops, in_weight, context_weight, out_weight):
    peers = lax.axis_size("patch")
    far = peers // 4
    patches, tokens, values = fine_input.shape
    width = in_weight.shape[1]
    pixels = coarse_weight.shape[0]
    half = coarse_input.shape[1]
    count = patches * tokens
    steps = count // ROWS
    depth = 3 * width
    place = jnp.stack([lax.axis_index("patch"), lax.axis_index("lvl")]).astype(jnp.int32)

    def to_peer(value, shift):
        return lax.ppermute(value, "patch", [(p, (p + shift) % peers) for p in range(peers)])

    def to_near(value, side, flip):
        both = [(s * peers + p, (s ^ side) * peers + (p ^ flip)) for s in range(2) for p in range(peers)]
        return lax.ppermute(value, ("lvl", "patch"), both)

    column = [coarse_input] + [to_peer(coarse_input, 4 * k) for k in range(1, far)]
    column = jnp.concatenate(column, axis=0)
    shards = {0: column}
    for code in (4, 2, 6, 1):
        shards[code] = to_near(column, code // 4, code % 4)
    for code in (2, 4, 6):
        shards[code + 1] = to_near(shards[code], 0, 1)
    shards = [shards[code] for code in range(8)]

    weight = in_weight.T
    scratch = [pltpu.VMEM((MAIN, 3 * values), BF16), pltpu.VMEM((2 * (width - MAIN), 2 * values), BF16)]
    xw = call(
        input_kernel,
        "input",
        6 * count * values * width,
        jax.ShapeDtypeStruct((count, width), F32),
        grid=(steps,),
        in_specs=[by_rows(values), whole((width, values))],
        out_specs=by_rows(width),
        scratch_shapes=scratch,
    )(fine_input.reshape(count, values), weight)
    tw, gram = call(
        target_kernel,
        "target",
        6 * count * values * width,
        (jax.ShapeDtypeStruct((count, width), F32), jax.ShapeDtypeStruct((width, width), F32)),
        grid=(steps,),
        in_specs=[by_rows(values), whole((width, values))],
        out_specs=(by_rows(width), whole((width, width))),
        scratch_shapes=scratch,
    )(fine_target.reshape(count, values), out_weight)

    message = (16, LANES)
    de, *sends = call(
        functools.partial(middle_kernel, patches, peers),
        "middle",
        6 * count * width * width,
        [jax.ShapeDtypeStruct((count, width), F32)] + [jax.ShapeDtypeStruct(message, F32)] * peers,
        grid=(steps,),
        in_specs=[SMEM, SMEM]
        + [whole((far, half, pixels))] * 8
        + [
            by_rows(width),
            by_rows(width),
            whole((width, width)),
            whole((pixels, width)),
            whole((width, width)),
        ],
        out_specs=[by_rows(width)] + [whole(message)] * peers,
        scratch_shapes=[
            pltpu.VMEM((8 * far * half, pixels), F32),
            pltpu.VMEM((patches * 16, pixels), F32),
            pltpu.VMEM((patches * 16, width), F32),
            pltpu.VMEM((patches * 64, width), F32),
            pltpu.VMEM((patches * 64, width), F32),
            pltpu.VMEM((depth, width), BF16),
            pltpu.VMEM((patches * 16, LANES), F32),
        ],
    )(place, crops.T, *shards, xw, tw, gram, coarse_weight, context_weight)
    returned = [sends[0]] + [to_peer(sends[k], k) for k in range(1, peers)]

    fine_grad = call(
        last_kernel,
        "last",
        6 * count * values * width,
        jax.ShapeDtypeStruct((count, values), F32),
        grid=(steps,),
        in_specs=[by_rows(width), whole((width, values))],
        out_specs=by_rows(values),
        scratch_shapes=[pltpu.VMEM((depth, values), BF16)],
    )(de, weight)

    part = jax.ShapeDtypeStruct((1, half, pixels), F32)
    mine, theirs = call(
        functools.partial(scatter_kernel, peers),
        "scatter",
        10000,
        (part, part),
        in_specs=[SMEM] + [VMEM] * peers,
        out_specs=(VMEM, VMEM),
        scratch_shapes=[pltpu.VMEM((SIDE * SIDE, pixels), F32)],
    )(place, *returned)
    coarse_grad = mine + to_near(theirs, 1, 0)
    return (coarse_grad, fine_grad.reshape(fine_input.shape))


def solution(mesh):
    in_specs = (
        P("patch", "lvl", None),
        P(),
        P(("lvl", "patch"), None, None),
        P(("lvl", "patch"), None, None),
        P(("lvl", "patch"), None),
        P(),
        P(),
        P(),
    )
    out_specs = (P("patch", "lvl", None), P(("lvl", "patch"), None, None))
    return jax.shard_map(body, mesh=mesh, in_specs=in_specs, out_specs=out_specs, check_vma=False)
```

```python
import functools

import jax
import jax.numpy as jnp
from jax import lax
from jax.experimental import pallas as pl
from jax.experimental.pallas import tpu as pltpu
from jax.sharding import PartitionSpec as P

F32 = jnp.float32
BF16 = jnp.bfloat16
NN = (((1,), (0,)), ((), ()))
NT = (((1,), (1,)), ((), ()))
TN = (((0,), (0,)), ((), ()))
ROWS = 512
SIDE = 8
MAIN = 256
LANES = 256
LIMIT = 60 * 1024 * 1024
SMEM = pl.BlockSpec(memory_space=pltpu.SMEM)
VMEM = pl.BlockSpec(memory_space=pltpu.VMEM)


def split(value):
    high = value.astype(BF16)
    low = (value - high.astype(F32)).astype(BF16)
    return high, low


def dot(left, right, dims=NN):
    return lax.dot_general(left, right, dims, preferred_element_type=F32)


def dot3(left, right, dims=NN):
    return (
        dot(left[0], right[1], dims) + dot(left[1], right[0], dims) + dot(left[0], right[0], dims)
    )


def sigmoid(value):
    return 0.5 * jnp.tanh(0.5 * value) + 0.5


def call(kernel, name, flops, out_shape, **kwargs):
    shapes = jax.tree.leaves(out_shape)
    moved = 2 * sum(s.size * 4 for s in shapes)
    return pl.pallas_call(
        kernel,
        out_shape=out_shape,
        name=name,
        cost_estimate=pl.CostEstimate(flops=flops, bytes_accessed=moved, transcendentals=0),
        compiler_params=pltpu.CompilerParams(vmem_limit_bytes=LIMIT),
        **kwargs,
    )


def row_value(crops_ref, column, patches, shape, axis, each):
    index = lax.broadcasted_iota(jnp.int32, shape, axis) // each
    found = jnp.zeros(shape, jnp.int32)
    for j in range(patches):
        found = jnp.where(index == j, crops_ref[column, j], found)
    return found


def chosen(crops_ref, patches, rows_first):
    shape = (patches * 64, patches * 16) if rows_first else (patches * 16, patches * 64)
    token_axis = 0 if rows_first else 1
    token = lax.broadcasted_iota(jnp.int32, shape, token_axis)
    slot = lax.broadcasted_iota(jnp.int32, shape, 1 - token_axis)
    scale = row_value(crops_ref, 3, patches, shape, token_axis, 64)
    group, column = (token // 16) % 4, token % 16
    wanted = token // 64 * 16 + (group * scale // 2) * 4 + column * scale // 8
    return jnp.where(slot == wanted, 1.0, 0.0).astype(BF16)


def middle_kernel(
    patches,
    peers,
    place_ref,
    crops_ref,
    own_ref,
    other_ref,
    xw_ref,
    tw_ref,
    gram_ref,
    cwgt_ref,
    xwgt_ref,
    de_ref,
    send_ref,
    rows,
    slope,
    context,
    sums,
    gram_hi,
    gram_lo,
):
    step = pl.program_id(0)
    per_step = ROWS // 4
    far = peers // 4
    pixels = cwgt_ref.shape[0]

    @pl.when(step == 0)
    def _():
        core = place_ref[0] % 2
        for j in range(patches):
            frame, top, left = crops_ref[0, j], crops_ref[1, j], crops_ref[2, j]
            here = frame % 2 == core
            for a in range(4):
                row = jnp.minimum(top + a, SIDE - 1)
                shard = (row // 4 * 2 + frame // 2 % 2) * far + frame // 4
                start = pl.ds(pl.multiple_of((shard * 4 + row % 4) * SIDE, SIDE), SIDE)
                line = jnp.where(here, own_ref[start, :], other_ref[start, :])
                rows[j * 16 + a * 4 : j * 16 + a * 4 + 4, :] = pltpu.roll(line, SIDE - left, 0)[:4, :]
        pre = dot3(split(rows[...]), split(cwgt_ref[...]))
        gate = sigmoid(pre)
        slope[...] = gate * (1.0 + pre * (1.0 - gate))
        projected = split(dot3(split(pre * gate), split(xwgt_ref[...])))
        pick = chosen(crops_ref, patches, True)
        context[...] = dot(pick, projected[1]) + dot(pick, projected[0])
        gram_hi[...], gram_lo[...] = split(gram_ref[...])

    width = xw_ref.shape[1]
    here = pl.ds(pl.multiple_of(step * per_step, per_step), per_step)
    groups = per_step // 16
    spread = context[here, :].reshape(groups, 1, 16, width)
    pre = xw_ref[...].reshape(groups, 4, 16, width) + spread
    pre = pre.reshape(ROWS, width)
    gate = sigmoid(pre)
    hidden = pre * gate
    dhidden = dot3(split(hidden), (gram_hi[...], gram_lo[...])) - tw_ref[...]
    de = dhidden * (gate + hidden * (1.0 - gate))
    de_ref[...] = de
    sums[here, :] = de.reshape(groups, 4, 16, width).sum(axis=1).reshape(per_step, width)

    @pl.when(step == pl.num_programs(0) - 1)
    def _():
        pick = chosen(crops_ref, patches, False)
        high, low = split(sums[...])
        dslot = dot(pick, low) + dot(pick, high)
        dcontext = dot3(split(dslot), split(xwgt_ref[...]), NT)
        grad = dot3(split(dcontext * slope[...]), split(cwgt_ref[...]), NT)
        shape = (patches * 16, LANES - pixels)
        slot = lax.broadcasted_iota(jnp.int32, shape, 0) % 16
        top = row_value(crops_ref, 1, patches, shape, 0, 16)
        left = row_value(crops_ref, 2, patches, shape, 0, 16)
        number = ((top + slot // 4) * SIDE + left + slot % 4).astype(F32)
        send_ref[...] = jnp.zeros_like(send_ref)
        for j in range(patches):
            start = pl.ds(pl.multiple_of(crops_ref[0, j] * 16, 16), 16)
            send_ref[start, :pixels] = grad[j * 16 : j * 16 + 16, :]
            send_ref[start, pixels:] = number[j * 16 : j * 16 + 16, :]


def scatter_kernel(place_ref, message_ref, done_ref, mine_ref, other_ref, total):
    del done_ref
    pixels = mine_ref.shape[2]
    message = message_ref[...]
    number = lax.broadcasted_iota(jnp.int32, (message.shape[0], SIDE * SIDE), 1).astype(F32)
    pick = jnp.where(message[:, pixels : pixels + 1] == number, 1.0, 0.0).astype(BF16)
    high, low = split(message[:, :pixels])
    total[...] = dot(pick, low, TN) + dot(pick, high, TN)
    half = mine_ref.shape[1]
    side = place_ref[1]
    mine_ref[0] = total[pl.ds(pl.multiple_of(side * half, half), half), :]
    other_ref[0] = total[pl.ds(pl.multiple_of((1 - side) * half, half), half), :]


def whole(shape):
    return pl.BlockSpec(shape, lambda i: (0,) * len(shape))


def by_rows(width):
    return pl.BlockSpec((ROWS, width), lambda i: (i, 0))


def body(coarse_input, coarse_weight, fine_input, fine_target, crops, in_weight, context_weight, out_weight):
    high = lax.Precision.HIGH
    patch = ("far", "y", "core")
    peers = lax.axis_size(patch)
    far = peers // 4
    patches, tokens, values = fine_input.shape
    width = in_weight.shape[1]
    pixels = coarse_weight.shape[0]
    half = coarse_input.shape[1]
    count = patches * tokens
    place = jnp.stack([lax.axis_index(patch), lax.axis_index("lvl")]).astype(jnp.int32)
    swap = [(0, 1), (1, 0)]

    def gather(value, axes):
        copies = jnp.broadcast_to(value[None], (lax.axis_size(axes),) + value.shape)
        return lax.all_to_all(copies, axes, 0, 0)

    column = gather(coarse_input[0], "far")
    own = gather(column, ("lvl", "y")).reshape(-1, pixels)
    other = lax.ppermute(own, "core", swap)

    xw = jnp.dot(fine_input.reshape(count, values), in_weight, precision=high)
    tw = jnp.dot(fine_target.reshape(count, values), out_weight.T, precision=high)
    gram = jnp.dot(out_weight, out_weight.T, precision=lax.Precision.HIGHEST)

    shape = (peers * 16, LANES)
    de, back = call(
        functools.partial(middle_kernel, patches, peers),
        "middle",
        6 * count * width * width,
        (jax.ShapeDtypeStruct((count, width), F32), jax.ShapeDtypeStruct(shape, F32)),
        grid=(count // ROWS,),
        in_specs=[
            SMEM,
            SMEM,
            whole(own.shape),
            whole(own.shape),
            by_rows(width),
            by_rows(width),
            whole((width, width)),
            whole((pixels, width)),
            whole((width, width)),
        ],
        out_specs=(by_rows(width), whole(shape)),
        scratch_shapes=[
            pltpu.VMEM((patches * 16, pixels), F32),
            pltpu.VMEM((patches * 16, width), F32),
            pltpu.VMEM((patches * 64, width), F32),
            pltpu.VMEM((patches * 64, width), F32),
            pltpu.VMEM((width, width), BF16),
            pltpu.VMEM((width, width), BF16),
        ],
    )(place, crops.T, own, other, xw, tw, gram, coarse_weight, context_weight)
    returned = lax.all_to_all(back, patch, 0, 0, tiled=True)
    fine_grad = jnp.dot(de, in_weight.T, precision=high)

    part = jax.ShapeDtypeStruct((1, half, pixels), F32)
    mine, theirs = call(
        scatter_kernel,
        "scatter",
        10000,
        (part, part),
        in_specs=[SMEM, VMEM, pl.BlockSpec(memory_space=pl.ANY)],
        out_specs=(VMEM, VMEM),
        scratch_shapes=[pltpu.VMEM((SIDE * SIDE, pixels), F32)],
    )(place, returned, fine_grad)
    coarse_grad = mine + lax.ppermute(theirs, "lvl", swap)
    return (coarse_grad, fine_grad.reshape(fine_input.shape))


def solution(mesh):
    sides, peers = mesh.shape["lvl"], mesh.shape["patch"]
    fine = jax.sharding.Mesh(mesh.devices.reshape(sides, peers // 4, 2, 2), ("lvl", "far", "y", "core"))
    patch = ("far", "y", "core")
    both = ("lvl",) + patch
    in_specs = (
        P(patch, "lvl", None),
        P(),
        P(both, None, None),
        P(both, None, None),
        P(both, None),
        P(),
        P(),
        P(),
    )
    out_specs = (P(patch, "lvl", None), P(both, None, None))
    return jax.shard_map(body, mesh=fine, in_specs=in_specs, out_specs=out_specs, check_vma=False)
```

```python
import functools
import math

import jax
import jax.numpy as jnp
from jax import lax
from jax.experimental import pallas as pl
from jax.experimental.pallas import tpu as pltpu
from jax.sharding import PartitionSpec as P

F32 = jnp.float32
BF16 = jnp.bfloat16
NN = (((1,), (0,)), ((), ()))
NT = (((1,), (1,)), ((), ()))
TN = (((0,), (0,)), ((), ()))
ROWS = 512
SIDE = 8
MAIN = 256
LANES = 256
LIMIT = 60 * 1024 * 1024
ROOM = 40 * 1024 * 1024
SMEM = pl.BlockSpec(memory_space=pltpu.SMEM)
VMEM = pl.BlockSpec(memory_space=pltpu.VMEM)
HBM = pl.BlockSpec(memory_space=pltpu.HBM)


def split(value):
    high = value.astype(BF16)
    low = (value - high.astype(F32)).astype(BF16)
    return high, low


def dot(left, right, dims=NN):
    return lax.dot_general(left, right, dims, preferred_element_type=F32)


def dot3(left, right, dims=NN):
    return (
        dot(left[0], right[1], dims) + dot(left[1], right[0], dims) + dot(left[0], right[0], dims)
    )


def sigmoid(value):
    return 0.5 * jnp.tanh(0.5 * value) + 0.5


def call(kernel, name, flops, out_shape, limit=LIMIT, **kwargs):
    moved = 8 * sum(math.prod(s.shape) for s in jax.tree.leaves(out_shape))
    return pl.pallas_call(
        kernel,
        out_shape=out_shape,
        name=name,
        cost_estimate=pl.CostEstimate(flops=flops, bytes_accessed=moved, transcendentals=0),
        compiler_params=pltpu.CompilerParams(vmem_limit_bytes=limit),
        **kwargs,
    )


def wide_product(value, main_hi, main_lo, tail, out_ref, dims):
    high, low = split(value)
    rest = out_ref.shape[1] - MAIN
    out_ref[:, :MAIN] = dot3((high, low), (main_hi[...], main_lo[...]), dims)
    both = dot(high, tail[...], dims)
    tail_hi = tail[:rest] if dims == NT else tail[:, :rest]
    out_ref[:, MAIN:] = both[:, :rest] + (both[:, rest:] + dot(low, tail_hi, dims))


def input_kernel(x_ref, weight_ref, out_ref, high_ref, low_ref, tail):
    @pl.when(pl.program_id(0) == 0)
    def _():
        high, low = split(weight_ref[...])
        high_ref[...], low_ref[...] = high, low
        rest = high.shape[0] - MAIN
        tail[:rest], tail[rest:] = high[MAIN:], low[MAIN:]

    wide_product(x_ref[...], high_ref.at[:MAIN], low_ref.at[:MAIN], tail, out_ref, NT)


def gram_kernel(weight_ref, before_ref, gram_ref):
    del before_ref
    high, low = split(weight_ref[...])
    gram_ref[...] = dot3((high, low), (high, low), NT) + dot(low, low, NT)


def stack_kernel(*refs):
    *block_refs, _, out_ref = refs
    size = block_refs[0].shape[0]
    for k, ref in enumerate(block_refs):
        out_ref[k * size : (k + 1) * size] = ref[...]


def target_kernel(t_ref, weight_ref, out_ref, main_hi, main_lo, tail):
    @pl.when(pl.program_id(0) == 0)
    def _():
        high, low = split(weight_ref[...].T)
        main_hi[...], main_lo[...] = high[:, :MAIN], low[:, :MAIN]
        tail[...] = jnp.concatenate([high[:, MAIN:], low[:, MAIN:]], axis=1)

    wide_product(t_ref[...], main_hi, main_lo, tail, out_ref, NN)


def row_value(crops_ref, column, patches, shape, axis, each):
    index = lax.broadcasted_iota(jnp.int32, shape, axis) // each
    found = jnp.zeros(shape, jnp.int32)
    for j in range(patches):
        found = jnp.where(index == j, crops_ref[column, j], found)
    return found


def chosen(crops_ref, patches, rows_first):
    shape = (patches * 64, patches * 16) if rows_first else (patches * 16, patches * 64)
    token_axis = 0 if rows_first else 1
    token = lax.broadcasted_iota(jnp.int32, shape, token_axis)
    slot = lax.broadcasted_iota(jnp.int32, shape, 1 - token_axis)
    scale = row_value(crops_ref, 3, patches, shape, token_axis, 64)
    group, column = (token // 16) % 4, token % 16
    wanted = token // 64 * 16 + (group * scale // 2) * 4 + column * scale // 8
    return jnp.where(slot == wanted, 1.0, 0.0).astype(BF16)


def middle_kernel(
    patches,
    peers,
    crops_ref,
    own_ref,
    other_ref,
    xw_hbm,
    tw_hbm,
    gram_hbm,
    cwgt_hbm,
    xwgt_hbm,
    de_hbm,
    send_ref,
    xw,
    tw,
    gram,
    cwgt,
    xwgt,
    rows,
    context,
    sums,
    small_sems,
    in_sems,
    out_sems,
):
    pixels = cwgt.shape[0]
    count, width = xw.shape
    far = peers // 4
    steps = count // ROWS
    small = [
        pltpu.make_async_copy(source, target, small_sems.at[i])
        for i, (source, target) in enumerate(((cwgt_hbm, cwgt), (xwgt_hbm, xwgt), (gram_hbm, gram)))
    ]
    large = []
    for i in range(steps):
        here = slice(i * ROWS, (i + 1) * ROWS)
        large.append(
            (
                pltpu.make_async_copy(xw_hbm.at[here], xw.at[here], in_sems.at[0, i]),
                pltpu.make_async_copy(tw_hbm.at[here], tw.at[here], in_sems.at[1, i]),
            )
        )
    for copy in small:
        copy.start()
    for pair in large:
        for copy in pair:
            copy.start()

    me, side = lax.axis_index(("far", "y", "core")), lax.axis_index("lvl")
    for j in range(patches):
        frame, top, left = crops_ref[0, j], crops_ref[1, j], crops_ref[2, j]
        near = lax.bitwise_xor(frame % 4, me % 4)
        k = (me // 4 - frame // 4 + far) % far
        for a in range(4):
            row = jnp.minimum(top + a, SIDE - 1)
            shard = (lax.bitwise_xor(row // 4, side) * 2 + near // 2) * far + k
            start = pl.ds(pl.multiple_of((shard * 4 + row % 4) * SIDE, SIDE), SIDE)
            line = jnp.where(near % 2 == 0, own_ref[start, :], other_ref[start, :])
            rows[j * 16 + a * 4 : j * 16 + a * 4 + 4, :] = pltpu.roll(line, SIDE - left, 0)[:4, :]
    small[0].wait()
    coarse = split(cwgt[...])
    pre = dot3(split(rows[...]), coarse)
    gate = sigmoid(pre)
    slope = gate * (1.0 + pre * (1.0 - gate))
    small[1].wait()
    project = split(xwgt[...])
    projected = split(dot3(split(pre * gate), project))
    pick = chosen(crops_ref, patches, True)
    context[...] = dot(pick, projected[1]) + dot(pick, projected[0])
    small[2].wait()
    grams = split(gram[...])

    groups, part = ROWS // 64, ROWS // 4
    stores = []
    for i in range(steps):
        here = slice(i * ROWS, (i + 1) * ROWS)
        for copy in large[i]:
            copy.wait()
        spread = context[i * part : (i + 1) * part, :].reshape(groups, 1, 16, width)
        pre = (xw[here, :].reshape(groups, 4, 16, width) + spread).reshape(ROWS, width)
        gate = sigmoid(pre)
        hidden = pre * gate
        dhidden = dot3(split(hidden), grams) - tw[here, :]
        de = dhidden * (gate + hidden * (1.0 - gate))
        xw[here, :] = de
        stores.append(pltpu.make_async_copy(xw.at[here], de_hbm.at[here], out_sems.at[i]))
        stores[i].start()
        sums[i * part : (i + 1) * part, :] = de.reshape(groups, 4, 16, width).sum(axis=1).reshape(part, width)

    pick = chosen(crops_ref, patches, False)
    high, low = split(sums[...])
    dslot = dot(pick, low) + dot(pick, high)
    dcontext = dot3(split(dslot), project, NT)
    grad = dot3(split(dcontext * slope), coarse, NT)
    shape = (patches * 16, LANES - pixels)
    slot = lax.broadcasted_iota(jnp.int32, shape, 0) % 16
    top = row_value(crops_ref, 1, patches, shape, 0, 16)
    left = row_value(crops_ref, 2, patches, shape, 0, 16)
    number = ((top + slot // 4) * SIDE + left + slot % 4).astype(F32)
    send_ref[...] = jnp.zeros_like(send_ref)
    for j in range(patches):
        start = pl.ds(pl.multiple_of(crops_ref[0, j] * 16, 16), 16)
        send_ref[start, :pixels] = grad[j * 16 : j * 16 + 16, :]
        send_ref[start, pixels:] = number[j * 16 : j * 16 + 16, :]
    for copy in stores:
        copy.wait()


def scatter_kernel(message_ref, done_ref, mine_ref, other_ref, total):
    del done_ref
    pixels = mine_ref.shape[2]
    message = message_ref[...]
    number = lax.broadcasted_iota(jnp.int32, (message.shape[0], SIDE * SIDE), 1).astype(F32)
    pick = jnp.where(message[:, pixels : pixels + 1] == number, 1.0, 0.0).astype(BF16)
    high, low = split(message[:, :pixels])
    total[...] = dot(pick, low, TN) + dot(pick, high, TN)
    half = mine_ref.shape[1]
    side = lax.axis_index("lvl")
    mine_ref[0] = total[pl.ds(pl.multiple_of(side * half, half), half), :]
    other_ref[0] = total[pl.ds(pl.multiple_of((1 - side) * half, half), half), :]


def last_kernel(de_ref, high_ref, low_ref, *refs):
    out_ref, tail = refs[-2:]
    depth = high_ref.shape[0]
    rest = depth - MAIN

    @pl.when(pl.program_id(0) == 0)
    def _():
        tail[:rest], tail[rest : 2 * rest], tail[2 * rest :] = low_ref[MAIN:], high_ref[MAIN:], high_ref[MAIN:]

    high, low = split(de_ref[...])
    tails = jnp.concatenate([high[:, MAIN:], low[:, MAIN:], high[:, MAIN:]], axis=1)
    main = dot3((high[:, :MAIN], low[:, :MAIN]), (high_ref[:MAIN], low_ref[:MAIN]))
    out_ref[...] = main + dot(tails, tail[...])


def fixed(*values):
    return [pltpu.with_memory_space_constraint(value, pltpu.HBM) for value in values]


def stack(blocks, before):
    shape = (len(blocks) * blocks[0].shape[0],) + blocks[0].shape[1:]
    return call(
        stack_kernel,
        "stack",
        1000,
        jax.ShapeDtypeStruct(shape, F32),
        limit=ROOM,
        in_specs=[VMEM] * len(blocks) + [HBM],
        out_specs=VMEM,
    )(*blocks, *fixed(before))


def whole(shape):
    return pl.BlockSpec(shape, lambda i: (0,) * len(shape))


def by_rows(width, first=0):
    return pl.BlockSpec((ROWS, width), lambda i: (i + first, 0))


def body(coarse_input, coarse_weight, fine_input, fine_target, crops, in_weight, context_weight, out_weight):
    patch = ("far", "y", "core")
    peers = lax.axis_size(patch)
    far = peers // 4
    patches, tokens, values = fine_input.shape
    width = in_weight.shape[1]
    pixels = coarse_weight.shape[0]
    half = coarse_input.shape[1]
    count = patches * tokens
    steps = count // ROWS
    rest = width - MAIN
    swap = [(0, 1), (1, 0)]

    column = [coarse_input]
    for k in range(1, far):
        column.append(lax.ppermute(coarse_input, "far", [(p, (p + k) % far) for p in range(far)]))
    weight = in_weight.T
    weight_shape = jax.ShapeDtypeStruct((width, values), BF16)
    xw, win_hi, win_lo = call(
        input_kernel,
        "input",
        6 * count * values * width,
        (jax.ShapeDtypeStruct((count, width), F32), weight_shape, weight_shape),
        grid=(steps,),
        in_specs=[by_rows(values), whole((width, values))],
        out_specs=(by_rows(width), whole((width, values)), whole((width, values))),
        scratch_shapes=[pltpu.VMEM((2 * rest, values), BF16)],
    )(fine_input.reshape(count, values), weight)
    column = stack(column, xw)
    own = [column]
    for flip in range(1, 4):
        own.append(lax.ppermute(column, ("lvl", "y"), [(p, p ^ flip) for p in range(4)]))
    tw = call(
        target_kernel,
        "target",
        6 * count * values * width,
        jax.ShapeDtypeStruct((count, width), F32),
        grid=(steps,),
        in_specs=[by_rows(values), whole((width, values))],
        out_specs=by_rows(width),
        scratch_shapes=[
            pltpu.VMEM((values, MAIN), BF16),
            pltpu.VMEM((values, MAIN), BF16),
            pltpu.VMEM((values, 2 * rest), BF16),
        ],
    )(fine_target.reshape(count, values), out_weight)
    own = stack(own, tw).reshape(-1, pixels)
    other = lax.ppermute(own, "core", swap)
    gram = call(
        gram_kernel,
        "gram",
        8 * values * width * width,
        pltpu.HBM((width, width), F32),
        limit=ROOM,
        in_specs=[VMEM, HBM],
        out_specs=VMEM,
    )(out_weight, own)

    shape = (peers * 16, LANES)
    de, back = call(
        functools.partial(middle_kernel, patches, peers),
        "middle",
        6 * count * width * width,
        (pltpu.HBM((count, width), F32), jax.ShapeDtypeStruct(shape, F32)),
        limit=ROOM,
        in_specs=[SMEM, VMEM, VMEM] + [HBM] * 5,
        out_specs=(HBM, VMEM),
        scratch_shapes=[
            pltpu.VMEM((count, width), F32),
            pltpu.VMEM((count, width), F32),
            pltpu.VMEM((width, width), F32),
            pltpu.VMEM((pixels, width), F32),
            pltpu.VMEM((width, width), F32),
            pltpu.VMEM((patches * 16, pixels), F32),
            pltpu.VMEM((patches * 64, width), F32),
            pltpu.VMEM((patches * 64, width), F32),
            pltpu.SemaphoreType.DMA((3,)),
            pltpu.SemaphoreType.DMA((2, steps)),
            pltpu.SemaphoreType.DMA((steps,)),
        ],
    )(crops.T, own, other, *fixed(xw, tw, gram, coarse_weight, context_weight))
    returned = lax.all_to_all(back, patch, 0, 0, tiled=True)

    def last(first, number, *extra):
        return call(
            last_kernel,
            "last",
            6 * number * ROWS * values * width,
            jax.ShapeDtypeStruct((count, values), F32),
            grid=(number,),
            in_specs=[by_rows(width, first), whole((width, values)), whole((width, values))]
            + [HBM] * len(extra),
            out_specs=by_rows(values, first),
            scratch_shapes=[pltpu.VMEM((3 * rest, values), BF16)],
            input_output_aliases={3: 0} if extra else {},
        )(de, win_hi, win_lo, *fixed(*extra))

    early = steps - 1
    fine_grad = last(0, early)
    part = (1, half, pixels)
    mine, theirs = call(
        scatter_kernel,
        "scatter",
        10000,
        (pltpu.HBM(part, F32), jax.ShapeDtypeStruct(part, F32)),
        limit=ROOM,
        in_specs=[VMEM, HBM],
        out_specs=(VMEM, VMEM),
        scratch_shapes=[pltpu.VMEM((SIDE * SIDE, pixels), F32)],
    )(returned, *fixed(fine_grad))
    fine_grad = last(early, steps - early, fine_grad, mine)
    coarse_grad = mine + lax.ppermute(theirs, "lvl", swap)
    return (coarse_grad, fine_grad.reshape(fine_input.shape))


def solution(mesh):
    sides, peers = mesh.shape["lvl"], mesh.shape["patch"]
    fine = jax.sharding.Mesh(mesh.devices.reshape(sides, peers // 4, 2, 2), ("lvl", "far", "y", "core"))
    patch = ("far", "y", "core")
    both = ("lvl",) + patch
    in_specs = (
        P(patch, "lvl", None),
        P(),
        P(both, None, None),
        P(both, None, None),
        P(both, None),
        P(),
        P(),
        P(),
    )
    out_specs = (P(patch, "lvl", None), P(both, None, None))
    return jax.shard_map(body, mesh=fine, in_specs=in_specs, out_specs=out_specs, check_vma=False)
```

```python
import functools
import math

import jax
import jax.numpy as jnp
from jax import lax
from jax.experimental import pallas as pl
from jax.experimental.pallas import tpu as pltpu
from jax.sharding import PartitionSpec as P

F32 = jnp.float32
BF16 = jnp.bfloat16
NN = (((1,), (0,)), ((), ()))
NT = (((1,), (1,)), ((), ()))
TN = (((0,), (0,)), ((), ()))
ROWS = 512
SIDE = 8
AHEAD = 2
LANES = 256
LIMIT = 60 * 1024 * 1024
ROOM = 40 * 1024 * 1024
SMEM = pl.BlockSpec(memory_space=pltpu.SMEM)
VMEM = pl.BlockSpec(memory_space=pltpu.VMEM)
HBM = pl.BlockSpec(memory_space=pltpu.HBM)


def split(value):
    high = value.astype(BF16)
    low = (value - high.astype(F32)).astype(BF16)
    return high, low


def dot(left, right, dims=NN):
    return lax.dot_general(left, right, dims, preferred_element_type=F32)


def dot3(left, right, dims=NN):
    return (
        dot(left[0], right[1], dims) + dot(left[1], right[0], dims) + dot(left[0], right[0], dims)
    )


def sigmoid(value):
    return 0.5 * jnp.tanh(0.5 * value) + 0.5


def call(kernel, name, flops, out_shape, limit=LIMIT, **kwargs):
    moved = 8 * sum(math.prod(s.shape) for s in jax.tree.leaves(out_shape))
    return pl.pallas_call(
        kernel,
        out_shape=out_shape,
        name=name,
        cost_estimate=pl.CostEstimate(flops=flops, bytes_accessed=moved, transcendentals=0),
        compiler_params=pltpu.CompilerParams(vmem_limit_bytes=limit),
        **kwargs,
    )


def stream(chunks, source, held, result, target, in_sems, out_sems, product, prepare=None):
    loads, stores = [], []
    for i, (start, size) in enumerate(chunks):
        here = pl.ds(start, size)
        loads.append(pltpu.make_async_copy(source.at[here], held.at[here], in_sems.at[i]))
        stores.append(pltpu.make_async_copy(result.at[here], target.at[here], out_sems.at[i]))
    for copy in loads[:AHEAD]:
        copy.start()
    if prepare is not None:
        prepare()
    for i, (start, size) in enumerate(chunks):
        loads[i].wait()
        if i + AHEAD < len(chunks):
            loads[i + AHEAD].start()
        result[start : start + size, :] = product(held[start : start + size, :])
        stores[i].start()
    for copy in stores:
        copy.wait()


def chunk_rows(first, last):
    cuts = [first] + list(range(first + ROWS // 2, last - ROWS // 2 + 1, ROWS)) + [last]
    return [(low, high - low) for low, high in zip(cuts, cuts[1:])]


def wide_kernel(chunks, x_hbm, weight_hbm, *refs):
    out_hbm, *split_hbm, x, out, weight, high_ref, low_ref, in_sems, out_sems, sems = refs
    fetch = pltpu.make_async_copy(weight_hbm, weight, sems.at[0])
    fetch.start()
    keep = []

    def prepare():
        fetch.wait()
        high_ref[...], low_ref[...] = split(weight[...])
        for i, (ref, hbm) in enumerate(zip((high_ref, low_ref), split_hbm)):
            keep.append(pltpu.make_async_copy(ref, hbm, sems.at[1 + i]))
            keep[i].start()

    def product(value):
        return dot3(split(value), (high_ref[...], low_ref[...]), NT)

    stream(chunks, x_hbm, x, out, out_hbm, in_sems, out_sems, product, prepare)
    for copy in keep:
        copy.wait()


def gram_kernel(weight_ref, before_ref, gram_ref):
    del before_ref
    high, low = split(weight_ref[...])
    gram_ref[...] = dot3((high, low), (high, low), NT) + dot(low, low, NT)


def stack_kernel(*refs):
    *block_refs, _, out_ref = refs
    size = block_refs[0].shape[0]
    for k, ref in enumerate(block_refs):
        out_ref[k * size : (k + 1) * size] = ref[...]


def row_value(crops_ref, column, patches, shape, axis, each):
    index = lax.broadcasted_iota(jnp.int32, shape, axis) // each
    found = jnp.zeros(shape, jnp.int32)
    for j in range(patches):
        found = jnp.where(index == j, crops_ref[column, j], found)
    return found


def chosen(crops_ref, patches, rows_first):
    shape = (patches * 64, patches * 16) if rows_first else (patches * 16, patches * 64)
    token_axis = 0 if rows_first else 1
    token = lax.broadcasted_iota(jnp.int32, shape, token_axis)
    slot = lax.broadcasted_iota(jnp.int32, shape, 1 - token_axis)
    scale = row_value(crops_ref, 3, patches, shape, token_axis, 64)
    group, column = (token // 16) % 4, token % 16
    wanted = token // 64 * 16 + (group * scale // 2) * 4 + column * scale // 8
    return jnp.where(slot == wanted, 1.0, 0.0).astype(BF16)


def middle_kernel(
    patches,
    peers,
    crops_ref,
    own_ref,
    other_ref,
    xw_hbm,
    tw_hbm,
    gram_hbm,
    cwgt_hbm,
    xwgt_hbm,
    de_hbm,
    send_ref,
    xw,
    tw,
    gram,
    cwgt,
    xwgt,
    rows,
    context,
    sums,
    small_sems,
    in_sems,
    out_sems,
):
    pixels = cwgt.shape[0]
    count, width = xw.shape
    far = peers // 4
    steps = count // ROWS
    small = [
        pltpu.make_async_copy(source, target, small_sems.at[i])
        for i, (source, target) in enumerate(((cwgt_hbm, cwgt), (xwgt_hbm, xwgt), (gram_hbm, gram)))
    ]
    large = []
    for i in range(steps):
        here = slice(i * ROWS, (i + 1) * ROWS)
        large.append(
            (
                pltpu.make_async_copy(xw_hbm.at[here], xw.at[here], in_sems.at[0, i]),
                pltpu.make_async_copy(tw_hbm.at[here], tw.at[here], in_sems.at[1, i]),
            )
        )
    for copy in small:
        copy.start()
    for pair in large:
        for copy in pair:
            copy.start()

    me, side = lax.axis_index(("far", "y", "core")), lax.axis_index("lvl")
    for j in range(patches):
        frame, top, left = crops_ref[0, j], crops_ref[1, j], crops_ref[2, j]
        near = lax.bitwise_xor(frame % 4, me % 4)
        k = (me // 4 - frame // 4 + far) % far
        for a in range(4):
            row = jnp.minimum(top + a, SIDE - 1)
            shard = (lax.bitwise_xor(row // 4, side) * 2 + near // 2) * far + k
            start = pl.ds(pl.multiple_of((shard * 4 + row % 4) * SIDE, SIDE), SIDE)
            line = jnp.where(near % 2 == 0, own_ref[start, :], other_ref[start, :])
            rows[j * 16 + a * 4 : j * 16 + a * 4 + 4, :] = pltpu.roll(line, SIDE - left, 0)[:4, :]
    small[0].wait()
    coarse = split(cwgt[...])
    pre = dot3(split(rows[...]), coarse)
    gate = sigmoid(pre)
    slope = gate * (1.0 + pre * (1.0 - gate))
    small[1].wait()
    project = split(xwgt[...])
    projected = split(dot3(split(pre * gate), project))
    pick = chosen(crops_ref, patches, True)
    context[...] = dot(pick, projected[1]) + dot(pick, projected[0])
    small[2].wait()
    grams = split(gram[...])

    groups, part = ROWS // 64, ROWS // 4
    stores = []
    for pair in large:
        for copy in pair:
            copy.wait()
    for i in range(steps):
        here = slice(i * ROWS, (i + 1) * ROWS)
        spread = context[i * part : (i + 1) * part, :].reshape(groups, 1, 16, width)
        pre = (xw[here, :].reshape(groups, 4, 16, width) + spread).reshape(ROWS, width)
        gate = sigmoid(pre)
        hidden = pre * gate
        dhidden = dot3(split(hidden), grams) - tw[here, :]
        de = dhidden * (gate + hidden * (1.0 - gate))
        xw[here, :] = de
        stores.append(pltpu.make_async_copy(xw.at[here], de_hbm.at[here], out_sems.at[i]))
        stores[i].start()
        sums[i * part : (i + 1) * part, :] = de.reshape(groups, 4, 16, width).sum(axis=1).reshape(part, width)

    pick = chosen(crops_ref, patches, False)
    high, low = split(sums[...])
    dslot = dot(pick, low) + dot(pick, high)
    dcontext = dot3(split(dslot), project, NT)
    grad = dot3(split(dcontext * slope), coarse, NT)
    shape = (patches * 16, LANES - pixels)
    slot = lax.broadcasted_iota(jnp.int32, shape, 0) % 16
    top = row_value(crops_ref, 1, patches, shape, 0, 16)
    left = row_value(crops_ref, 2, patches, shape, 0, 16)
    number = ((top + slot // 4) * SIDE + left + slot % 4).astype(F32)
    send_ref[...] = jnp.zeros_like(send_ref)
    for j in range(patches):
        start = pl.ds(pl.multiple_of(crops_ref[0, j] * 16, 16), 16)
        send_ref[start, :pixels] = grad[j * 16 : j * 16 + 16, :]
        send_ref[start, pixels:] = number[j * 16 : j * 16 + 16, :]
    for copy in stores:
        copy.wait()


def scatter_kernel(message_ref, done_ref, mine_ref, other_ref, total):
    del done_ref
    pixels = mine_ref.shape[2]
    message = message_ref[...]
    number = lax.broadcasted_iota(jnp.int32, (message.shape[0], SIDE * SIDE), 1).astype(F32)
    pick = jnp.where(message[:, pixels : pixels + 1] == number, 1.0, 0.0).astype(BF16)
    high, low = split(message[:, :pixels])
    total[...] = dot(pick, low, TN) + dot(pick, high, TN)
    half = mine_ref.shape[1]
    side = lax.axis_index("lvl")
    mine_ref[0] = total[pl.ds(pl.multiple_of(side * half, half), half), :]
    other_ref[0] = total[pl.ds(pl.multiple_of((1 - side) * half, half), half), :]


def last_kernel(chunks, de_hbm, high_hbm, low_hbm, *refs):
    out_hbm, de, out, high_ref, low_ref, in_sems, out_sems, sems = refs[-8:]
    fetches = [
        pltpu.make_async_copy(high_hbm, high_ref, sems.at[0]),
        pltpu.make_async_copy(low_hbm, low_ref, sems.at[1]),
    ]
    for copy in fetches:
        copy.start()

    def prepare():
        for copy in fetches:
            copy.wait()

    def product(value):
        return dot3(split(value), (high_ref[...], low_ref[...]))

    stream(chunks, de_hbm, de, out, out_hbm, in_sems, out_sems, product, prepare)


def fixed(*values):
    return [pltpu.with_memory_space_constraint(value, pltpu.HBM) for value in values]


def stack(blocks, before):
    shape = (len(blocks) * blocks[0].shape[0],) + blocks[0].shape[1:]
    return call(
        stack_kernel,
        "stack",
        1000,
        jax.ShapeDtypeStruct(shape, F32),
        limit=ROOM,
        in_specs=[VMEM] * len(blocks) + [HBM],
        out_specs=VMEM,
    )(*blocks, *fixed(before))


def body(coarse_input, coarse_weight, fine_input, fine_target, crops, in_weight, context_weight, out_weight):
    patch = ("far", "y", "core")
    peers = lax.axis_size(patch)
    far = peers // 4
    patches, tokens, values = fine_input.shape
    width = in_weight.shape[1]
    pixels = coarse_weight.shape[0]
    half = coarse_input.shape[1]
    count = patches * tokens
    steps = count // ROWS
    swap = [(0, 1), (1, 0)]

    column = [coarse_input]
    for k in range(1, far):
        column.append(lax.ppermute(coarse_input, "far", [(p, (p + k) % far) for p in range(far)]))
    chunks = chunk_rows(0, count)

    def wide(name, value, weight, keep):
        split_shape = (width, values)
        out_shape = [pltpu.HBM((count, width), F32)] + [pltpu.HBM(split_shape, BF16)] * (2 * keep)
        return call(
            functools.partial(wide_kernel, chunks),
            name,
            6 * count * values * width,
            out_shape,
            in_specs=[HBM, HBM],
            out_specs=[HBM] * len(out_shape),
            scratch_shapes=[
                pltpu.VMEM((count, values), F32),
                pltpu.VMEM((count, width), F32),
                pltpu.VMEM(split_shape, F32),
                pltpu.VMEM(split_shape, BF16),
                pltpu.VMEM(split_shape, BF16),
                pltpu.SemaphoreType.DMA((len(chunks),)),
                pltpu.SemaphoreType.DMA((len(chunks),)),
                pltpu.SemaphoreType.DMA((3,)),
            ],
        )(*fixed(value.reshape(count, values), weight))

    xw, win_hi, win_lo = wide("input", fine_input, in_weight.T, True)
    column = stack(column, xw)
    own = [column]
    for flip in range(1, 4):
        own.append(lax.ppermute(column, ("lvl", "y"), [(p, p ^ flip) for p in range(4)]))
    (tw,) = wide("target", fine_target, out_weight, False)
    own = stack(own, tw).reshape(-1, pixels)
    other = lax.ppermute(own, "core", swap)
    gram = call(
        gram_kernel,
        "gram",
        8 * values * width * width,
        pltpu.HBM((width, width), F32),
        limit=ROOM,
        in_specs=[VMEM, HBM],
        out_specs=VMEM,
    )(out_weight, own)

    shape = (peers * 16, LANES)
    de, back = call(
        functools.partial(middle_kernel, patches, peers),
        "middle",
        6 * count * width * width,
        (pltpu.HBM((count, width), F32), jax.ShapeDtypeStruct(shape, F32)),
        limit=ROOM,
        in_specs=[SMEM, VMEM, VMEM] + [HBM] * 5,
        out_specs=(HBM, VMEM),
        scratch_shapes=[
            pltpu.VMEM((count, width), F32),
            pltpu.VMEM((count, width), F32),
            pltpu.VMEM((width, width), F32),
            pltpu.VMEM((pixels, width), F32),
            pltpu.VMEM((width, width), F32),
            pltpu.VMEM((patches * 16, pixels), F32),
            pltpu.VMEM((patches * 64, width), F32),
            pltpu.VMEM((patches * 64, width), F32),
            pltpu.SemaphoreType.DMA((3,)),
            pltpu.SemaphoreType.DMA((2, steps)),
            pltpu.SemaphoreType.DMA((steps,)),
        ],
    )(crops.T, own, other, *fixed(xw, tw, gram, coarse_weight, context_weight))
    returned = lax.all_to_all(back, patch, 0, 0, tiled=True)

    def last(first, end, *extra):
        mine = chunk_rows(first, end)
        return call(
            functools.partial(last_kernel, mine),
            "last",
            6 * (end - first) * values * width,
            pltpu.HBM((count, values), F32),
            in_specs=[HBM] * (3 + len(extra)),
            out_specs=HBM,
            scratch_shapes=[
                pltpu.VMEM((count, width), F32),
                pltpu.VMEM((count, values), F32),
                pltpu.VMEM((width, values), BF16),
                pltpu.VMEM((width, values), BF16),
                pltpu.SemaphoreType.DMA((len(mine),)),
                pltpu.SemaphoreType.DMA((len(mine),)),
                pltpu.SemaphoreType.DMA((2,)),
            ],
            input_output_aliases={3: 0} if extra else {},
        )(*fixed(de, win_hi, win_lo, *extra))

    early = count - ROWS
    fine_grad = last(0, early)
    part = (1, half, pixels)
    mine, theirs = call(
        scatter_kernel,
        "scatter",
        10000,
        (pltpu.HBM(part, F32), jax.ShapeDtypeStruct(part, F32)),
        limit=ROOM,
        in_specs=[VMEM, HBM],
        out_specs=(VMEM, VMEM),
        scratch_shapes=[pltpu.VMEM((SIDE * SIDE, pixels), F32)],
    )(returned, *fixed(fine_grad))
    fine_grad = last(early, count, fine_grad, mine)
    coarse_grad = mine + lax.ppermute(theirs, "lvl", swap)
    return (coarse_grad, fine_grad.reshape(fine_input.shape))


def solution(mesh):
    sides, peers = mesh.shape["lvl"], mesh.shape["patch"]
    fine = jax.sharding.Mesh(mesh.devices.reshape(sides, peers // 4, 2, 2), ("lvl", "far", "y", "core"))
    patch = ("far", "y", "core")
    both = ("lvl",) + patch
    in_specs = (
        P(patch, "lvl", None),
        P(),
        P(both, None, None),
        P(both, None, None),
        P(both, None),
        P(),
        P(),
        P(),
    )
    out_specs = (P(patch, "lvl", None), P(both, None, None))
    return jax.shard_map(body, mesh=fine, in_specs=in_specs, out_specs=out_specs, check_vma=False)
```

```python
import functools
import math

import jax
import jax.numpy as jnp
from jax import lax
from jax.experimental import pallas as pl
from jax.experimental.pallas import tpu as pltpu
from jax.sharding import PartitionSpec as P

F32 = jnp.float32
BF16 = jnp.bfloat16
NN = (((1,), (0,)), ((), ()))
NT = (((1,), (1,)), ((), ()))
TN = (((0,), (0,)), ((), ()))
ROWS = 1024
SIDE = 8
AHEAD = 2
LANES = 256
LIMIT = 60 * 1024 * 1024
ROOM = 40 * 1024 * 1024
SMEM = pl.BlockSpec(memory_space=pltpu.SMEM)
VMEM = pl.BlockSpec(memory_space=pltpu.VMEM)
HBM = pl.BlockSpec(memory_space=pltpu.HBM)


def split(value):
    high = value.astype(BF16)
    low = (value - high.astype(F32)).astype(BF16)
    return high, low


def dot(left, right, dims=NN):
    return lax.dot_general(left, right, dims, preferred_element_type=F32)


def dot3(left, right, dims=NN):
    return (
        dot(left[0], right[1], dims) + dot(left[1], right[0], dims) + dot(left[0], right[0], dims)
    )


def sigmoid(value):
    return 0.5 * jnp.tanh(0.5 * value) + 0.5


def call(kernel, name, flops, out_shape, limit=LIMIT, **kwargs):
    moved = 8 * sum(math.prod(s.shape) for s in jax.tree.leaves(out_shape))
    return pl.pallas_call(
        kernel,
        out_shape=out_shape,
        name=name,
        cost_estimate=pl.CostEstimate(flops=flops, bytes_accessed=moved, transcendentals=0),
        compiler_params=pltpu.CompilerParams(vmem_limit_bytes=limit),
        **kwargs,
    )


def stream(chunks, source, held, result, target, in_sems, out_sems, product, prepare=None):
    loads, stores = [], []
    for i, (start, size) in enumerate(chunks):
        here = pl.ds(start, size)
        loads.append(pltpu.make_async_copy(source.at[here], held.at[here], in_sems.at[i]))
        stores.append(pltpu.make_async_copy(result.at[here], target.at[here], out_sems.at[i]))
    for copy in loads[:AHEAD]:
        copy.start()
    if prepare is not None:
        prepare()
    for i, (start, size) in enumerate(chunks):
        loads[i].wait()
        if i + AHEAD < len(chunks):
            loads[i + AHEAD].start()
        result[start : start + size, :] = product(held[start : start + size, :])
        stores[i].start()
    for copy in stores:
        copy.wait()


def chunk_rows(first, last, size):
    return [(start, size) for start in range(first, last, size)]


def wide_kernel(chunks, x_hbm, weight_hbm, *refs):
    out_hbm, *split_hbm, x, out, weight, high_ref, low_ref, in_sems, out_sems, sems = refs
    fetch = pltpu.make_async_copy(weight_hbm, weight, sems.at[0])
    fetch.start()
    keep = []

    def prepare():
        fetch.wait()
        high_ref[...], low_ref[...] = split(weight[...])
        for i, (ref, hbm) in enumerate(zip((high_ref, low_ref), split_hbm)):
            keep.append(pltpu.make_async_copy(ref, hbm, sems.at[1 + i]))
            keep[i].start()

    def product(value):
        return dot3(split(value), (high_ref[...], low_ref[...]), NT)

    stream(chunks, x_hbm, x, out, out_hbm, in_sems, out_sems, product, prepare)
    for copy in keep:
        copy.wait()


def gram_kernel(weight_ref, before_ref, gram_ref):
    del before_ref
    high, low = split(weight_ref[...])
    gram_ref[...] = dot3((high, low), (high, low), NT) + dot(low, low, NT)


def stack_kernel(*refs):
    *block_refs, _, out_ref = refs
    size = block_refs[0].shape[0]
    for k, ref in enumerate(block_refs):
        out_ref[k * size : (k + 1) * size] = ref[...]


def row_value(crops_ref, column, patches, shape, axis, each):
    index = lax.broadcasted_iota(jnp.int32, shape, axis) // each
    found = jnp.zeros(shape, jnp.int32)
    for j in range(patches):
        found = jnp.where(index == j, crops_ref[column, j], found)
    return found


def chosen(crops_ref, patches, rows_first):
    shape = (patches * 64, patches * 16) if rows_first else (patches * 16, patches * 64)
    token_axis = 0 if rows_first else 1
    token = lax.broadcasted_iota(jnp.int32, shape, token_axis)
    slot = lax.broadcasted_iota(jnp.int32, shape, 1 - token_axis)
    scale = row_value(crops_ref, 3, patches, shape, token_axis, 64)
    group, column = (token // 16) % 4, token % 16
    wanted = token // 64 * 16 + (group * scale // 2) * 4 + column * scale // 8
    return jnp.where(slot == wanted, 1.0, 0.0).astype(BF16)


def middle_kernel(
    patches,
    peers,
    crops_ref,
    own_ref,
    other_ref,
    xw_hbm,
    tw_hbm,
    gram_hbm,
    cwgt_hbm,
    xwgt_hbm,
    de_hbm,
    send_ref,
    xw,
    tw,
    gram,
    cwgt,
    xwgt,
    rows,
    context,
    sums,
    small_sems,
    in_sems,
    out_sems,
):
    pixels = cwgt.shape[0]
    count, width = xw.shape
    far = peers // 4
    steps = count // ROWS
    small = [
        pltpu.make_async_copy(source, target, small_sems.at[i])
        for i, (source, target) in enumerate(((cwgt_hbm, cwgt), (xwgt_hbm, xwgt), (gram_hbm, gram)))
    ]
    large = []
    for i in range(steps):
        here = slice(i * ROWS, (i + 1) * ROWS)
        large.append(
            (
                pltpu.make_async_copy(xw_hbm.at[here], xw.at[here], in_sems.at[0, i]),
                pltpu.make_async_copy(tw_hbm.at[here], tw.at[here], in_sems.at[1, i]),
            )
        )
    for copy in small:
        copy.start()
    for pair in large:
        for copy in pair:
            copy.start()

    me, side = lax.axis_index(("far", "y", "core")), lax.axis_index("lvl")
    for j in range(patches):
        frame, top, left = crops_ref[0, j], crops_ref[1, j], crops_ref[2, j]
        near = lax.bitwise_xor(frame % 4, me % 4)
        k = (me // 4 - frame // 4 + far) % far
        for a in range(4):
            row = jnp.minimum(top + a, SIDE - 1)
            shard = (lax.bitwise_xor(row // 4, side) * 2 + near // 2) * far + k
            start = pl.ds(pl.multiple_of((shard * 4 + row % 4) * SIDE, SIDE), SIDE)
            line = jnp.where(near % 2 == 0, own_ref[start, :], other_ref[start, :])
            rows[j * 16 + a * 4 : j * 16 + a * 4 + 4, :] = pltpu.roll(line, SIDE - left, 0)[:4, :]
    small[0].wait()
    coarse = split(cwgt[...])
    pre = dot3(split(rows[...]), coarse)
    gate = sigmoid(pre)
    slope = gate * (1.0 + pre * (1.0 - gate))
    small[1].wait()
    project = split(xwgt[...])
    projected = split(dot3(split(pre * gate), project))
    pick = chosen(crops_ref, patches, True)
    context[...] = dot(pick, projected[1]) + dot(pick, projected[0])
    small[2].wait()
    grams = split(gram[...])

    groups, part = ROWS // 64, ROWS // 4
    stores = []
    for pair in large:
        for copy in pair:
            copy.wait()
    for i in range(steps):
        here = slice(i * ROWS, (i + 1) * ROWS)
        spread = context[i * part : (i + 1) * part, :].reshape(groups, 1, 16, width)
        pre = (xw[here, :].reshape(groups, 4, 16, width) + spread).reshape(ROWS, width)
        gate = sigmoid(pre)
        hidden = pre * gate
        dhidden = dot3(split(hidden), grams) - tw[here, :]
        de = dhidden * (gate + hidden * (1.0 - gate))
        xw[here, :] = de
        stores.append(pltpu.make_async_copy(xw.at[here], de_hbm.at[here], out_sems.at[i]))
        stores[i].start()
        sums[i * part : (i + 1) * part, :] = de.reshape(groups, 4, 16, width).sum(axis=1).reshape(part, width)

    pick = chosen(crops_ref, patches, False)
    high, low = split(sums[...])
    dslot = dot(pick, low) + dot(pick, high)
    dcontext = dot3(split(dslot), project, NT)
    grad = dot3(split(dcontext * slope), coarse, NT)
    shape = (patches * 16, LANES - pixels)
    slot = lax.broadcasted_iota(jnp.int32, shape, 0) % 16
    top = row_value(crops_ref, 1, patches, shape, 0, 16)
    left = row_value(crops_ref, 2, patches, shape, 0, 16)
    number = ((top + slot // 4) * SIDE + left + slot % 4).astype(F32)
    send_ref[...] = jnp.zeros_like(send_ref)
    for j in range(patches):
        start = pl.ds(pl.multiple_of(crops_ref[0, j] * 16, 16), 16)
        send_ref[start, :pixels] = grad[j * 16 : j * 16 + 16, :]
        send_ref[start, pixels:] = number[j * 16 : j * 16 + 16, :]
    for copy in stores:
        copy.wait()


def scatter_kernel(message_ref, done_ref, mine_ref, other_ref, total):
    del done_ref
    pixels = mine_ref.shape[2]
    message = message_ref[...]
    number = lax.broadcasted_iota(jnp.int32, (message.shape[0], SIDE * SIDE), 1).astype(F32)
    pick = jnp.where(message[:, pixels : pixels + 1] == number, 1.0, 0.0).astype(BF16)
    high, low = split(message[:, :pixels])
    total[...] = dot(pick, low, TN) + dot(pick, high, TN)
    half = mine_ref.shape[1]
    side = lax.axis_index("lvl")
    mine_ref[0] = total[pl.ds(pl.multiple_of(side * half, half), half), :]
    other_ref[0] = total[pl.ds(pl.multiple_of((1 - side) * half, half), half), :]


def last_kernel(chunks, de_hbm, high_hbm, low_hbm, *refs):
    out_hbm, de, out, high_ref, low_ref, in_sems, out_sems, sems = refs[-8:]
    fetches = [
        pltpu.make_async_copy(high_hbm, high_ref, sems.at[0]),
        pltpu.make_async_copy(low_hbm, low_ref, sems.at[1]),
    ]
    for copy in fetches:
        copy.start()

    def prepare():
        for copy in fetches:
            copy.wait()

    def product(value):
        return dot3(split(value), (high_ref[...], low_ref[...]))

    stream(chunks, de_hbm, de, out, out_hbm, in_sems, out_sems, product, prepare)


def fixed(*values):
    return [pltpu.with_memory_space_constraint(value, pltpu.HBM) for value in values]


def stack(blocks, before):
    shape = (len(blocks) * blocks[0].shape[0],) + blocks[0].shape[1:]
    return call(
        stack_kernel,
        "stack",
        1000,
        jax.ShapeDtypeStruct(shape, F32),
        limit=ROOM,
        in_specs=[VMEM] * len(blocks) + [HBM],
        out_specs=VMEM,
    )(*blocks, *fixed(before))


def body(coarse_input, coarse_weight, fine_input, fine_target, crops, in_weight, context_weight, out_weight):
    patch = ("far", "y", "core")
    peers = lax.axis_size(patch)
    far = peers // 4
    patches, tokens, values = fine_input.shape
    width = in_weight.shape[1]
    pixels = coarse_weight.shape[0]
    half = coarse_input.shape[1]
    count = patches * tokens
    steps = count // ROWS
    swap = [(0, 1), (1, 0)]

    column = [coarse_input]
    for k in range(1, far):
        column.append(lax.ppermute(coarse_input, "far", [(p, (p + k) % far) for p in range(far)]))

    def wide(name, value, weight, keep, rows):
        chunks = chunk_rows(0, count, rows)
        split_shape = (width, values)
        out_shape = [pltpu.HBM((count, width), F32)] + [pltpu.HBM(split_shape, BF16)] * (2 * keep)
        return call(
            functools.partial(wide_kernel, chunks),
            name,
            6 * count * values * width,
            out_shape,
            in_specs=[HBM, HBM],
            out_specs=[HBM] * len(out_shape),
            scratch_shapes=[
                pltpu.VMEM((count, values), F32),
                pltpu.VMEM((count, width), F32),
                pltpu.VMEM(split_shape, F32),
                pltpu.VMEM(split_shape, BF16),
                pltpu.VMEM(split_shape, BF16),
                pltpu.SemaphoreType.DMA((len(chunks),)),
                pltpu.SemaphoreType.DMA((len(chunks),)),
                pltpu.SemaphoreType.DMA((3,)),
            ],
        )(*fixed(value.reshape(count, values), weight))

    xw, win_hi, win_lo = wide("input", fine_input, in_weight.T, True, count // 2)
    column = stack(column, xw)
    own = [column]
    for flip in range(1, 4):
        own.append(lax.ppermute(column, ("lvl", "y"), [(p, p ^ flip) for p in range(4)]))
    (tw,) = wide("target", fine_target, out_weight, False, count // 4)
    own = stack(own, tw).reshape(-1, pixels)
    other = lax.ppermute(own, "core", swap)
    gram = call(
        gram_kernel,
        "gram",
        8 * values * width * width,
        pltpu.HBM((width, width), F32),
        limit=ROOM,
        in_specs=[VMEM, HBM],
        out_specs=VMEM,
    )(out_weight, own)

    shape = (peers * 16, LANES)
    de, back = call(
        functools.partial(middle_kernel, patches, peers),
        "middle",
        6 * count * width * width,
        (pltpu.HBM((count, width), F32), jax.ShapeDtypeStruct(shape, F32)),
        limit=ROOM,
        in_specs=[SMEM, VMEM, VMEM] + [HBM] * 5,
        out_specs=(HBM, VMEM),
        scratch_shapes=[
            pltpu.VMEM((count, width), F32),
            pltpu.VMEM((count, width), F32),
            pltpu.VMEM((width, width), F32),
            pltpu.VMEM((pixels, width), F32),
            pltpu.VMEM((width, width), F32),
            pltpu.VMEM((patches * 16, pixels), F32),
            pltpu.VMEM((patches * 64, width), F32),
            pltpu.VMEM((patches * 64, width), F32),
            pltpu.SemaphoreType.DMA((3,)),
            pltpu.SemaphoreType.DMA((2, steps)),
            pltpu.SemaphoreType.DMA((steps,)),
        ],
    )(crops.T, own, other, *fixed(xw, tw, gram, coarse_weight, context_weight))
    returned = lax.all_to_all(back, patch, 0, 0, tiled=True)

    def last(first, end, rows, *extra):
        mine = chunk_rows(first, end, rows)
        return call(
            functools.partial(last_kernel, mine),
            "last",
            6 * (end - first) * values * width,
            pltpu.HBM((count, values), F32),
            in_specs=[HBM] * (3 + len(extra)),
            out_specs=HBM,
            scratch_shapes=[
                pltpu.VMEM((count, width), F32),
                pltpu.VMEM((count, values), F32),
                pltpu.VMEM((width, values), BF16),
                pltpu.VMEM((width, values), BF16),
                pltpu.SemaphoreType.DMA((len(mine),)),
                pltpu.SemaphoreType.DMA((len(mine),)),
                pltpu.SemaphoreType.DMA((2,)),
            ],
            input_output_aliases={3: 0} if extra else {},
        )(*fixed(de, win_hi, win_lo, *extra))

    early = count * 3 // 4
    fine_grad = last(0, early, early // 2)
    part = (1, half, pixels)
    mine, theirs = call(
        scatter_kernel,
        "scatter",
        10000,
        (pltpu.HBM(part, F32), jax.ShapeDtypeStruct(part, F32)),
        limit=ROOM,
        in_specs=[VMEM, HBM],
        out_specs=(VMEM, VMEM),
        scratch_shapes=[pltpu.VMEM((SIDE * SIDE, pixels), F32)],
    )(returned, *fixed(fine_grad))
    fine_grad = last(early, count, count - early, fine_grad, mine)
    coarse_grad = mine + lax.ppermute(theirs, "lvl", swap)
    return (coarse_grad, fine_grad.reshape(fine_input.shape))


def solution(mesh):
    sides, peers = mesh.shape["lvl"], mesh.shape["patch"]
    fine = jax.sharding.Mesh(mesh.devices.reshape(sides, peers // 4, 2, 2), ("lvl", "far", "y", "core"))
    patch = ("far", "y", "core")
    both = ("lvl",) + patch
    in_specs = (
        P(patch, "lvl", None),
        P(),
        P(both, None, None),
        P(both, None, None),
        P(both, None),
        P(),
        P(),
        P(),
    )
    out_specs = (P(patch, "lvl", None), P(both, None, None))
    return jax.shard_map(body, mesh=fine, in_specs=in_specs, out_specs=out_specs, check_vma=False)
```

```python
import functools
import math

import jax
import jax.numpy as jnp
from jax import lax
from jax.experimental import pallas as pl
from jax.experimental.pallas import tpu as pltpu
from jax.sharding import PartitionSpec as P

F32 = jnp.float32
BF16 = jnp.bfloat16
NN = (((1,), (0,)), ((), ()))
NT = (((1,), (1,)), ((), ()))
TN = (((0,), (0,)), ((), ()))
ROWS = 512
SIDE = 8
AHEAD = 2
LANES = 256
LIMIT = 60 * 1024 * 1024
ROOM = 40 * 1024 * 1024
SMEM = pl.BlockSpec(memory_space=pltpu.SMEM)
VMEM = pl.BlockSpec(memory_space=pltpu.VMEM)
HBM = pl.BlockSpec(memory_space=pltpu.HBM)


def split(value):
    high = value.astype(BF16)
    low = (value - high.astype(F32)).astype(BF16)
    return high, low


def dot(left, right, dims=NN):
    return lax.dot_general(left, right, dims, preferred_element_type=F32)


def dot3(left, right, dims=NN):
    return (
        dot(left[0], right[1], dims) + dot(left[1], right[0], dims) + dot(left[0], right[0], dims)
    )


def sigmoid(value):
    return 0.5 * jnp.tanh(0.5 * value) + 0.5


def call(kernel, name, flops, out_shape, limit=LIMIT, **kwargs):
    moved = 8 * sum(math.prod(s.shape) for s in jax.tree.leaves(out_shape))
    return pl.pallas_call(
        kernel,
        out_shape=out_shape,
        name=name,
        cost_estimate=pl.CostEstimate(flops=flops, bytes_accessed=moved, transcendentals=0),
        compiler_params=pltpu.CompilerParams(vmem_limit_bytes=limit),
        **kwargs,
    )


def stream(loads, stores, product):
    for copy in loads[:AHEAD]:
        copy.start()
    for i, (load, store) in enumerate(zip(loads, stores)):
        load.wait()
        if i + AHEAD < len(loads):
            loads[i + AHEAD].start()
        product(i)
        store.start()
    for copy in stores:
        copy.wait()


def wide_kernel(chunks, x_hbm, weight_hbm, *refs):
    out_hbm, *split_hbm, x, out, weight, pair, in_sems, out_sems, sems = refs
    width = weight.shape[0]
    fetch = pltpu.make_async_copy(weight_hbm, weight, sems.at[0])
    fetch.start()
    loads = [
        pltpu.make_async_copy(x_hbm.at[here], x.at[here], in_sems.at[i]) for i, here in enumerate(chunks)
    ]
    stores = [
        pltpu.make_async_copy(out.at[:, here], out_hbm.at[:, here], out_sems.at[i])
        for i, here in enumerate(chunks)
    ]
    keep = [pltpu.make_async_copy(pair, hbm, sems.at[1]) for hbm in split_hbm]

    def product(i):
        if i == 0:
            fetch.wait()
            pair[:width], pair[width:] = split(weight[...])
            for copy in keep:
                copy.start()
        high, low = split(x[chunks[i], :])
        both = dot(pair[...], high, NT)
        out[:, chunks[i]] = both[:width] + (both[width:] + dot(pair[:width], low, NT))

    stream(loads, stores, product)
    for copy in keep:
        copy.wait()


def gram_kernel(weight_ref, before_ref, gram_ref):
    del before_ref
    high, low = split(weight_ref[...])
    gram_ref[...] = dot3((high, low), (high, low), NT) + dot(low, low, NT)


def stack_kernel(*refs):
    *block_refs, _, out_ref = refs
    size = block_refs[0].shape[0]
    for k, ref in enumerate(block_refs):
        out_ref[k * size : (k + 1) * size] = ref[...]


def row_value(crops_ref, column, patches, shape, axis, each):
    index = lax.broadcasted_iota(jnp.int32, shape, axis) // each
    found = jnp.zeros(shape, jnp.int32)
    for j in range(patches):
        found = jnp.where(index == j, crops_ref[column, j], found)
    return found


def chosen(crops_ref, patches, tokens):
    scale = row_value(crops_ref, 3, patches, (1, patches * tokens), 1, tokens)
    token = lax.broadcasted_iota(jnp.int32, (1, patches * tokens), 1)
    row, column = (token % tokens) // 16, token % 16
    wanted = token // tokens * 16 + (row * scale // 8) * 4 + column * scale // 8
    slot = lax.broadcasted_iota(jnp.int32, (patches * 16, patches * tokens), 0)
    return jnp.where(slot == wanted, 1.0, 0.0).astype(BF16)


def middle_kernel(
    patches,
    peers,
    crops_ref,
    own_ref,
    other_ref,
    xw_hbm,
    tw_hbm,
    gram_hbm,
    cwgt_hbm,
    xwgt_hbm,
    de_hbm,
    send_ref,
    xw,
    tw,
    gram,
    cwgt,
    xwgt,
    rows,
    pick,
    small_sems,
    in_sems,
    out_sems,
):
    pixels = cwgt.shape[0]
    width, count = xw.shape
    slots = patches * 16
    far = peers // 4
    chunks = chunk_rows(0, count)
    small = [
        pltpu.make_async_copy(source, target, small_sems.at[i])
        for i, (source, target) in enumerate(((cwgt_hbm, cwgt), (xwgt_hbm, xwgt), (gram_hbm, gram)))
    ]
    large = [pltpu.make_async_copy(xw_hbm, xw, in_sems.at[0]), pltpu.make_async_copy(tw_hbm, tw, in_sems.at[1])]
    stores = [
        pltpu.make_async_copy(xw.at[:, here], de_hbm.at[:, here], out_sems.at[i])
        for i, here in enumerate(chunks)
    ]
    for copy in small + large:
        copy.start()
    pick[...] = chosen(crops_ref, patches, count // patches)

    me, side = lax.axis_index(("far", "y", "core")), lax.axis_index("lvl")
    for j in range(patches):
        frame, top, left = crops_ref[0, j], crops_ref[1, j], crops_ref[2, j]
        near = lax.bitwise_xor(frame % 4, me % 4)
        k = (me // 4 - frame // 4 + far) % far
        for a in range(4):
            row = jnp.minimum(top + a, SIDE - 1)
            shard = (lax.bitwise_xor(row // 4, side) * 2 + near // 2) * far + k
            start = pl.ds(pl.multiple_of((shard * 4 + row % 4) * SIDE, SIDE), SIDE)
            line = jnp.where(near % 2 == 0, own_ref[start, :], other_ref[start, :])
            rows[j * 16 + a * 4 : j * 16 + a * 4 + 4, :] = pltpu.roll(line, SIDE - left, 0)[:4, :]
    small[0].wait()
    coarse = split(cwgt[...])
    pre = dot3(split(rows[...]), coarse)
    gate = sigmoid(pre)
    slope = gate * (1.0 + pre * (1.0 - gate))
    small[1].wait()
    project = split(xwgt[...])
    high, low = split(dot3(split(pre * gate), project).T)
    projected = jnp.concatenate([high, low], axis=1)
    small[2].wait()
    high, low = split(gram[...])
    grams = jnp.concatenate([high, low, high], axis=1)
    for copy in large:
        copy.wait()

    dslot = jnp.zeros((2 * width, slots), F32)
    for i, here in enumerate(chunks):
        taken = pick[:, here]
        pre = xw[:, here] + dot(projected, jnp.concatenate([taken, taken], axis=0))
        gate = sigmoid(pre)
        hidden = pre * gate
        high, low = split(hidden)
        dhidden = dot(grams, jnp.concatenate([high, high, low], axis=0)) - tw[:, here]
        de = dhidden * (gate + hidden * (1.0 - gate))
        xw[:, here] = de
        stores[i].start()
        dslot = dslot + dot(jnp.concatenate(split(de), axis=0), taken, NT)

    dslot = (dslot[:width] + dslot[width:]).T
    dcontext = dot3(split(dslot), project, NT)
    grad = dot3(split(dcontext * slope), coarse, NT)
    shape = (patches * 16, LANES - pixels)
    slot = lax.broadcasted_iota(jnp.int32, shape, 0) % 16
    top = row_value(crops_ref, 1, patches, shape, 0, 16)
    left = row_value(crops_ref, 2, patches, shape, 0, 16)
    number = ((top + slot // 4) * SIDE + left + slot % 4).astype(F32)
    send_ref[...] = jnp.zeros_like(send_ref)
    for j in range(patches):
        start = pl.ds(pl.multiple_of(crops_ref[0, j] * 16, 16), 16)
        send_ref[start, :pixels] = grad[j * 16 : j * 16 + 16, :]
        send_ref[start, pixels:] = number[j * 16 : j * 16 + 16, :]
    for copy in stores:
        copy.wait()


def scatter_kernel(message_ref, done_ref, mine_ref, other_ref, total):
    del done_ref
    pixels = mine_ref.shape[2]
    message = message_ref[...]
    number = lax.broadcasted_iota(jnp.int32, (message.shape[0], SIDE * SIDE), 1).astype(F32)
    pick = jnp.where(message[:, pixels : pixels + 1] == number, 1.0, 0.0).astype(BF16)
    high, low = split(message[:, :pixels])
    total[...] = dot(pick, low, TN) + dot(pick, high, TN)
    half = mine_ref.shape[1]
    side = lax.axis_index("lvl")
    mine_ref[0] = total[pl.ds(pl.multiple_of(side * half, half), half), :]
    other_ref[0] = total[pl.ds(pl.multiple_of((1 - side) * half, half), half), :]


def last_kernel(chunks, de_hbm, pair_hbm, *refs):
    out_hbm, de, out, deep, in_sems, out_sems, sems = refs[-7:]
    width = de.shape[0]
    fetches = [
        pltpu.make_async_copy(pair_hbm, deep.at[: 2 * width], sems.at[0]),
        pltpu.make_async_copy(pair_hbm.at[:width], deep.at[2 * width :], sems.at[1]),
    ]
    for copy in fetches:
        copy.start()
    loads = [
        pltpu.make_async_copy(de_hbm.at[:, here], de.at[:, here], in_sems.at[i])
        for i, here in enumerate(chunks)
    ]
    stores = [
        pltpu.make_async_copy(out.at[here], out_hbm.at[here], out_sems.at[i])
        for i, here in enumerate(chunks)
    ]

    def product(i):
        if i == 0:
            for copy in fetches:
                copy.wait()
        high, low = split(de[:, chunks[i]])
        out[chunks[i], :] = dot(jnp.concatenate([high, high, low], axis=0), deep[...], TN)

    stream(loads, stores, product)


def chunk_rows(first, last):
    return [slice(start, start + ROWS) for start in range(first, last, ROWS)]


def fixed(*values):
    return [pltpu.with_memory_space_constraint(value, pltpu.HBM) for value in values]


def stack(blocks, before):
    shape = (len(blocks) * blocks[0].shape[0],) + blocks[0].shape[1:]
    return call(
        stack_kernel,
        "stack",
        1000,
        jax.ShapeDtypeStruct(shape, F32),
        limit=ROOM,
        in_specs=[VMEM] * len(blocks) + [HBM],
        out_specs=VMEM,
    )(*blocks, *fixed(before))


def body(coarse_input, coarse_weight, fine_input, fine_target, crops, in_weight, context_weight, out_weight):
    patch = ("far", "y", "core")
    peers = lax.axis_size(patch)
    far = peers // 4
    patches, tokens, values = fine_input.shape
    width = in_weight.shape[1]
    pixels = coarse_weight.shape[0]
    half = coarse_input.shape[1]
    count = patches * tokens
    swap = [(0, 1), (1, 0)]

    column = [coarse_input]
    for k in range(1, far):
        column.append(lax.ppermute(coarse_input, "far", [(p, (p + k) % far) for p in range(far)]))

    chunks = chunk_rows(0, count)
    pair_shape = (2 * width, values)

    def wide(name, value, weight, keep):
        out_shape = [pltpu.HBM((width, count), F32)] + [pltpu.HBM(pair_shape, BF16)] * keep
        return call(
            functools.partial(wide_kernel, chunks),
            name,
            6 * count * values * width,
            out_shape,
            in_specs=[HBM, HBM],
            out_specs=[HBM] * len(out_shape),
            scratch_shapes=[
                pltpu.VMEM((count, values), F32),
                pltpu.VMEM((width, count), F32),
                pltpu.VMEM((width, values), F32),
                pltpu.VMEM(pair_shape, BF16),
                pltpu.SemaphoreType.DMA((len(chunks),)),
                pltpu.SemaphoreType.DMA((len(chunks),)),
                pltpu.SemaphoreType.DMA((2,)),
            ],
        )(*fixed(value.reshape(count, values), weight))

    xw, pair = wide("input", fine_input, in_weight.T, True)
    column = stack(column, xw)
    own = [column]
    for flip in range(1, 4):
        own.append(lax.ppermute(column, ("lvl", "y"), [(p, p ^ flip) for p in range(4)]))
    (tw,) = wide("target", fine_target, out_weight, False)
    own = stack(own, tw).reshape(-1, pixels)
    other = lax.ppermute(own, "core", swap)
    gram = call(
        gram_kernel,
        "gram",
        8 * values * width * width,
        pltpu.HBM((width, width), F32),
        limit=ROOM,
        in_specs=[VMEM, HBM],
        out_specs=VMEM,
    )(out_weight, own)

    shape = (peers * 16, LANES)
    de, back = call(
        functools.partial(middle_kernel, patches, peers),
        "middle",
        6 * count * width * width,
        (pltpu.HBM((width, count), F32), jax.ShapeDtypeStruct(shape, F32)),
        limit=ROOM,
        in_specs=[SMEM, VMEM, VMEM] + [HBM] * 5,
        out_specs=(HBM, VMEM),
        scratch_shapes=[
            pltpu.VMEM((width, count), F32),
            pltpu.VMEM((width, count), F32),
            pltpu.VMEM((width, width), F32),
            pltpu.VMEM((pixels, width), F32),
            pltpu.VMEM((width, width), F32),
            pltpu.VMEM((patches * 16, pixels), F32),
            pltpu.VMEM((patches * 16, count), BF16),
            pltpu.SemaphoreType.DMA((3,)),
            pltpu.SemaphoreType.DMA((2,)),
            pltpu.SemaphoreType.DMA((len(chunks),)),
        ],
    )(crops.T, own, other, *fixed(xw, tw, gram, coarse_weight, context_weight))
    returned = lax.all_to_all(back, patch, 0, 0, tiled=True)

    def last(first, end, *extra):
        mine = chunk_rows(first, end)
        return call(
            functools.partial(last_kernel, mine),
            "last",
            6 * (end - first) * values * width,
            pltpu.HBM((count, values), F32),
            in_specs=[HBM] * (2 + len(extra)),
            out_specs=HBM,
            scratch_shapes=[
                pltpu.VMEM((width, count), F32),
                pltpu.VMEM((count, values), F32),
                pltpu.VMEM((3 * width, values), BF16),
                pltpu.SemaphoreType.DMA((len(mine),)),
                pltpu.SemaphoreType.DMA((len(mine),)),
                pltpu.SemaphoreType.DMA((2,)),
            ],
            input_output_aliases={2: 0} if extra else {},
        )(*fixed(de, pair, *extra))

    early = count - ROWS
    fine_grad = last(0, early)
    part = (1, half, pixels)
    mine, theirs = call(
        scatter_kernel,
        "scatter",
        10000,
        (pltpu.HBM(part, F32), jax.ShapeDtypeStruct(part, F32)),
        limit=ROOM,
        in_specs=[VMEM, HBM],
        out_specs=(VMEM, VMEM),
        scratch_shapes=[pltpu.VMEM((SIDE * SIDE, pixels), F32)],
    )(returned, *fixed(fine_grad))
    fine_grad = last(early, count, fine_grad, mine)
    coarse_grad = mine + lax.ppermute(theirs, "lvl", swap)
    return (coarse_grad, fine_grad.reshape(fine_input.shape))


def solution(mesh):
    sides, peers = mesh.shape["lvl"], mesh.shape["patch"]
    fine = jax.sharding.Mesh(mesh.devices.reshape(sides, peers // 4, 2, 2), ("lvl", "far", "y", "core"))
    patch = ("far", "y", "core")
    both = ("lvl",) + patch
    in_specs = (
        P(patch, "lvl", None),
        P(),
        P(both, None, None),
        P(both, None, None),
        P(both, None),
        P(),
        P(),
        P(),
    )
    out_specs = (P(patch, "lvl", None), P(both, None, None))
    return jax.shard_map(body, mesh=fine, in_specs=in_specs, out_specs=out_specs, check_vma=False)
```

```python
import functools
import math

import jax
import jax.numpy as jnp
from jax import lax
from jax.experimental import pallas as pl
from jax.experimental.pallas import tpu as pltpu
from jax.sharding import PartitionSpec as P

F32 = jnp.float32
BF16 = jnp.bfloat16
NN = (((1,), (0,)), ((), ()))
NT = (((1,), (1,)), ((), ()))
TN = (((0,), (0,)), ((), ()))
ROWS = 512
SIDE = 8
AHEAD = 2
LANES = 256
LIMIT = 60 * 1024 * 1024
ROOM = 40 * 1024 * 1024
SMEM = pl.BlockSpec(memory_space=pltpu.SMEM)
VMEM = pl.BlockSpec(memory_space=pltpu.VMEM)
HBM = pl.BlockSpec(memory_space=pltpu.HBM)


def split(value):
    high = value.astype(BF16)
    low = (value - high.astype(F32)).astype(BF16)
    return high, low


def dot(left, right, dims=NN):
    return lax.dot_general(left, right, dims, preferred_element_type=F32)


def dot3(left, right, dims=NN):
    return (
        dot(left[0], right[1], dims) + dot(left[1], right[0], dims) + dot(left[0], right[0], dims)
    )


def stacked(value):
    high, low = split(value)
    return jnp.concatenate([high, high, low], axis=0)


def side_by_side(value):
    high, low = split(value)
    return jnp.concatenate([high, low, high], axis=1)


def sigmoid(value):
    return 0.5 * jnp.tanh(0.5 * value) + 0.5


def call(kernel, name, flops, out_shape, limit=LIMIT, **kwargs):
    moved = 8 * sum(math.prod(s.shape) for s in jax.tree.leaves(out_shape))
    return pl.pallas_call(
        kernel,
        out_shape=out_shape,
        name=name,
        cost_estimate=pl.CostEstimate(flops=flops, bytes_accessed=moved, transcendentals=0),
        compiler_params=pltpu.CompilerParams(vmem_limit_bytes=limit),
        **kwargs,
    )


def stream(loads, stores, prepare, product):
    for copy in loads[:AHEAD]:
        copy.start()
    loads[0].wait()
    prepare(0)
    for i, store in enumerate(stores):
        if i + AHEAD < len(loads):
            loads[i + AHEAD].start()
        if i + 1 < len(loads):
            loads[i + 1].wait()
        product(i)
        if i + 1 < len(loads):
            prepare(i + 1)
        store.start()
    for copy in stores:
        copy.wait()


def wide_kernel(chunks, x_hbm, weight_hbm, *refs):
    out_hbm, *split_hbm, x, out, weight, pair, high, low, in_sems, out_sems, sems = refs
    width = weight.shape[0]
    fetch = pltpu.make_async_copy(weight_hbm, weight, sems.at[0])
    fetch.start()
    loads = [
        pltpu.make_async_copy(x_hbm.at[here], x.at[here], in_sems.at[i]) for i, here in enumerate(chunks)
    ]
    stores = [
        pltpu.make_async_copy(out.at[:, here], out_hbm.at[:, here], out_sems.at[i])
        for i, here in enumerate(chunks)
    ]
    keep = [pltpu.make_async_copy(pair, hbm, sems.at[1]) for hbm in split_hbm]

    def prepare(i):
        high[i % 2], low[i % 2] = split(x[chunks[i], :])
        if i == 0:
            fetch.wait()
            pair[:width], pair[width:] = split(weight[...])
            for copy in keep:
                copy.start()

    def product(i):
        both = dot(pair[...], high[i % 2], NT)
        out[:, chunks[i]] = both[:width] + (both[width:] + dot(pair[:width], low[i % 2], NT))

    stream(loads, stores, prepare, product)
    for copy in keep:
        copy.wait()


def gram_kernel(weight_ref, before_ref, gram_ref):
    del before_ref
    high, low = split(weight_ref[...])
    gram_ref[...] = dot3((high, low), (high, low), NT) + dot(low, low, NT)


def stack_kernel(*refs):
    *block_refs, _, out_ref = refs
    size = block_refs[0].shape[0]
    for k, ref in enumerate(block_refs):
        out_ref[k * size : (k + 1) * size] = ref[...]


def row_value(crops_ref, column, patches, shape, axis, each):
    index = lax.broadcasted_iota(jnp.int32, shape, axis) // each
    found = jnp.zeros(shape, jnp.int32)
    for j in range(patches):
        found = jnp.where(index == j, crops_ref[column, j], found)
    return found


def chosen(crops_ref, patches, tokens):
    scale = row_value(crops_ref, 3, patches, (1, patches * tokens), 1, tokens)
    token = lax.broadcasted_iota(jnp.int32, (1, patches * tokens), 1)
    row, column = (token % tokens) // 16, token % 16
    wanted = token // tokens * 16 + (row * scale // 8) * 4 + column * scale // 8
    slot = lax.broadcasted_iota(jnp.int32, (patches * 16, patches * tokens), 0)
    return jnp.where(slot == wanted, 1.0, 0.0).astype(BF16)


def middle_kernel(
    patches,
    peers,
    crops_ref,
    own_ref,
    other_ref,
    xw_hbm,
    tw_hbm,
    gram_hbm,
    cwgt_hbm,
    xwgt_hbm,
    de_hbm,
    send_ref,
    xw,
    tw,
    gram,
    cwgt,
    xwgt,
    rows,
    pick,
    small_sems,
    in_sems,
    out_sems,
):
    pixels = cwgt.shape[0]
    width, count = xw.shape
    slots = patches * 16
    far = peers // 4
    chunks = chunk_rows(0, count)
    small = [
        pltpu.make_async_copy(source, target, small_sems.at[i])
        for i, (source, target) in enumerate(((cwgt_hbm, cwgt), (xwgt_hbm, xwgt), (gram_hbm, gram)))
    ]
    large = [pltpu.make_async_copy(xw_hbm, xw, in_sems.at[0]), pltpu.make_async_copy(tw_hbm, tw, in_sems.at[1])]
    stores = [
        pltpu.make_async_copy(xw.at[:, here], de_hbm.at[:, here], out_sems.at[i])
        for i, here in enumerate(chunks)
    ]
    for copy in small + large:
        copy.start()
    pick[...] = chosen(crops_ref, patches, count // patches)

    me, side = lax.axis_index(("far", "y", "core")), lax.axis_index("lvl")
    for j in range(patches):
        frame, top, left = crops_ref[0, j], crops_ref[1, j], crops_ref[2, j]
        near = lax.bitwise_xor(frame % 4, me % 4)
        k = (me // 4 - frame // 4 + far) % far
        for a in range(4):
            row = jnp.minimum(top + a, SIDE - 1)
            shard = (lax.bitwise_xor(row // 4, side) * 2 + near // 2) * far + k
            start = pl.ds(pl.multiple_of((shard * 4 + row % 4) * SIDE, SIDE), SIDE)
            line = jnp.where(near % 2 == 0, own_ref[start, :], other_ref[start, :])
            rows[j * 16 + a * 4 : j * 16 + a * 4 + 4, :] = pltpu.roll(line, SIDE - left, 0)[:4, :]
    small[0].wait()
    coarse = split(cwgt[...])
    pre = dot3(split(rows[...]), coarse)
    gate = sigmoid(pre)
    slope = gate * (1.0 + pre * (1.0 - gate))
    small[1].wait()
    project = split(xwgt[...])
    high, low = split(dot3(split(pre * gate), project).T)
    projected = jnp.concatenate([high, low], axis=1)
    small[2].wait()
    grams, projects, coarses = side_by_side(gram[...]), side_by_side(xwgt[...]), side_by_side(cwgt[...])
    slope = slope.T
    for copy in large:
        copy.wait()

    def first(i):
        taken = pick[:, chunks[i]]
        pre = xw[:, chunks[i]] + dot(projected, jnp.concatenate([taken, taken], axis=0))
        gate = sigmoid(pre)
        hidden = pre * gate
        return gate + hidden * (1.0 - gate), stacked(hidden)

    dslot = jnp.zeros((2 * width, slots), F32)
    ready = first(0)
    for i, here in enumerate(chunks):
        factor, stack = ready
        product = dot(grams, stack)
        if i + 1 < len(chunks):
            ready = first(i + 1)
        de = (product - tw[:, here]) * factor
        xw[:, here] = de
        dslot = dslot + dot(jnp.concatenate(split(de), axis=0), pick[:, here], NT)
    for copy in stores:
        copy.start()

    dcontext = dot(projects, stacked(dslot[:width] + dslot[width:]))
    grad = dot(coarses, stacked(dcontext * slope)).T
    shape = (patches * 16, LANES - pixels)
    slot = lax.broadcasted_iota(jnp.int32, shape, 0) % 16
    top = row_value(crops_ref, 1, patches, shape, 0, 16)
    left = row_value(crops_ref, 2, patches, shape, 0, 16)
    number = ((top + slot // 4) * SIDE + left + slot % 4).astype(F32)
    send_ref[...] = jnp.zeros_like(send_ref)
    for j in range(patches):
        start = pl.ds(pl.multiple_of(crops_ref[0, j] * 16, 16), 16)
        send_ref[start, :pixels] = grad[j * 16 : j * 16 + 16, :]
        send_ref[start, pixels:] = number[j * 16 : j * 16 + 16, :]
    for copy in stores:
        copy.wait()


def scatter_kernel(message_ref, done_ref, mine_ref, other_ref, total):
    del done_ref
    pixels = mine_ref.shape[2]
    message = message_ref[...]
    number = lax.broadcasted_iota(jnp.int32, (message.shape[0], SIDE * SIDE), 1).astype(F32)
    pick = jnp.where(message[:, pixels : pixels + 1] == number, 1.0, 0.0).astype(BF16)
    high, low = split(message[:, :pixels])
    total[...] = dot(pick, low, TN) + dot(pick, high, TN)
    half = mine_ref.shape[1]
    side = lax.axis_index("lvl")
    mine_ref[0] = total[pl.ds(pl.multiple_of(side * half, half), half), :]
    other_ref[0] = total[pl.ds(pl.multiple_of((1 - side) * half, half), half), :]


def last_kernel(chunks, de_hbm, pair_hbm, *refs):
    out_hbm, de, out, deep, cat, in_sems, out_sems, sems = refs
    width = de.shape[0]
    fetches = [
        pltpu.make_async_copy(pair_hbm, deep.at[: 2 * width], sems.at[0]),
        pltpu.make_async_copy(pair_hbm.at[:width], deep.at[2 * width :], sems.at[1]),
    ]
    for copy in fetches:
        copy.start()
    loads = [
        pltpu.make_async_copy(de_hbm.at[:, here], de.at[:, here], in_sems.at[i])
        for i, here in enumerate(chunks)
    ]
    stores = [
        pltpu.make_async_copy(out.at[here], out_hbm.at[here], out_sems.at[i])
        for i, here in enumerate(chunks)
    ]

    def prepare(i):
        high, low = split(de[:, chunks[i]])
        cat[i % 2, :width], cat[i % 2, width : 2 * width], cat[i % 2, 2 * width :] = high, high, low
        if i == 0:
            for copy in fetches:
                copy.wait()

    def product(i):
        out[chunks[i], :] = dot(cat[i % 2], deep[...], TN)

    stream(loads, stores, prepare, product)


def chunk_rows(first, last):
    return [slice(start, start + ROWS) for start in range(first, last, ROWS)]


def fixed(*values):
    return [pltpu.with_memory_space_constraint(value, pltpu.HBM) for value in values]


def stack(blocks, before):
    shape = (len(blocks) * blocks[0].shape[0],) + blocks[0].shape[1:]
    return call(
        stack_kernel,
        "stack",
        1000,
        jax.ShapeDtypeStruct(shape, F32),
        limit=ROOM,
        in_specs=[VMEM] * len(blocks) + [HBM],
        out_specs=VMEM,
    )(*blocks, *fixed(before))


def body(coarse_input, coarse_weight, fine_input, fine_target, crops, in_weight, context_weight, out_weight):
    patch = ("far", "y", "core")
    peers = lax.axis_size(patch)
    far = peers // 4
    patches, tokens, values = fine_input.shape
    width = in_weight.shape[1]
    pixels = coarse_weight.shape[0]
    half = coarse_input.shape[1]
    count = patches * tokens
    swap = [(0, 1), (1, 0)]

    column = [coarse_input]
    for k in range(1, far):
        column.append(lax.ppermute(coarse_input, "far", [(p, (p + k) % far) for p in range(far)]))

    chunks = chunk_rows(0, count)
    pair_shape = (2 * width, values)

    def wide(name, value, weight, keep):
        out_shape = [pltpu.HBM((width, count), F32)] + [pltpu.HBM(pair_shape, BF16)] * keep
        return call(
            functools.partial(wide_kernel, chunks),
            name,
            6 * count * values * width,
            out_shape,
            in_specs=[HBM, HBM],
            out_specs=[HBM] * len(out_shape),
            scratch_shapes=[
                pltpu.VMEM((count, values), F32),
                pltpu.VMEM((width, count), F32),
                pltpu.VMEM((width, values), F32),
                pltpu.VMEM(pair_shape, BF16),
                pltpu.VMEM((2, ROWS, values), BF16),
                pltpu.VMEM((2, ROWS, values), BF16),
                pltpu.SemaphoreType.DMA((len(chunks),)),
                pltpu.SemaphoreType.DMA((len(chunks),)),
                pltpu.SemaphoreType.DMA((2,)),
            ],
        )(*fixed(value.reshape(count, values), weight))

    xw, pair = wide("input", fine_input, in_weight.T, True)
    column = stack(column, xw)
    own = [column]
    for flip in range(1, 4):
        own.append(lax.ppermute(column, ("lvl", "y"), [(p, p ^ flip) for p in range(4)]))
    (tw,) = wide("target", fine_target, out_weight, False)
    own = stack(own, tw).reshape(-1, pixels)
    other = lax.ppermute(own, "core", swap)
    gram = call(
        gram_kernel,
        "gram",
        8 * values * width * width,
        pltpu.HBM((width, width), F32),
        limit=ROOM,
        in_specs=[VMEM, HBM],
        out_specs=VMEM,
    )(out_weight, own)

    shape = (peers * 16, LANES)
    de, back = call(
        functools.partial(middle_kernel, patches, peers),
        "middle",
        6 * count * width * width,
        (pltpu.HBM((width, count), F32), jax.ShapeDtypeStruct(shape, F32)),
        limit=ROOM,
        in_specs=[SMEM, VMEM, VMEM] + [HBM] * 5,
        out_specs=(HBM, VMEM),
        scratch_shapes=[
            pltpu.VMEM((width, count), F32),
            pltpu.VMEM((width, count), F32),
            pltpu.VMEM((width, width), F32),
            pltpu.VMEM((pixels, width), F32),
            pltpu.VMEM((width, width), F32),
            pltpu.VMEM((patches * 16, pixels), F32),
            pltpu.VMEM((patches * 16, count), BF16),
            pltpu.SemaphoreType.DMA((3,)),
            pltpu.SemaphoreType.DMA((2,)),
            pltpu.SemaphoreType.DMA((len(chunks),)),
        ],
    )(crops.T, own, other, *fixed(xw, tw, gram, coarse_weight, context_weight))
    returned = lax.all_to_all(back, patch, 0, 0, tiled=True)

    fine_grad = call(
        functools.partial(last_kernel, chunks),
        "last",
        6 * count * values * width,
        pltpu.HBM((count, values), F32),
        in_specs=[HBM, HBM],
        out_specs=HBM,
        scratch_shapes=[
            pltpu.VMEM((width, count), F32),
            pltpu.VMEM((count, values), F32),
            pltpu.VMEM((3 * width, values), BF16),
            pltpu.VMEM((2, 3 * width, ROWS), BF16),
            pltpu.SemaphoreType.DMA((len(chunks),)),
            pltpu.SemaphoreType.DMA((len(chunks),)),
            pltpu.SemaphoreType.DMA((2,)),
        ],
    )(*fixed(de, pair))
    part = (1, half, pixels)
    mine, theirs = call(
        scatter_kernel,
        "scatter",
        10000,
        (pltpu.HBM(part, F32), jax.ShapeDtypeStruct(part, F32)),
        limit=ROOM,
        in_specs=[VMEM, HBM],
        out_specs=(VMEM, VMEM),
        scratch_shapes=[pltpu.VMEM((SIDE * SIDE, pixels), F32)],
    )(returned, *fixed(fine_grad))
    coarse_grad = mine + lax.ppermute(theirs, "lvl", swap)
    return (coarse_grad, fine_grad.reshape(fine_input.shape))


def solution(mesh):
    sides, peers = mesh.shape["lvl"], mesh.shape["patch"]
    fine = jax.sharding.Mesh(mesh.devices.reshape(sides, peers // 4, 2, 2), ("lvl", "far", "y", "core"))
    patch = ("far", "y", "core")
    both = ("lvl",) + patch
    in_specs = (
        P(patch, "lvl", None),
        P(),
        P(both, None, None),
        P(both, None, None),
        P(both, None),
        P(),
        P(),
        P(),
    )
    out_specs = (P(patch, "lvl", None), P(both, None, None))
    return jax.shard_map(body, mesh=fine, in_specs=in_specs, out_specs=out_specs, check_vma=False)
```

```python
import functools
import math

import jax
import jax.numpy as jnp
from jax import lax
from jax.experimental import pallas as pl
from jax.experimental.pallas import tpu as pltpu
from jax.sharding import PartitionSpec as P

F32 = jnp.float32
BF16 = jnp.bfloat16
NN = (((1,), (0,)), ((), ()))
NT = (((1,), (1,)), ((), ()))
TN = (((0,), (0,)), ((), ()))
ROWS = 512
SIDE = 8
AHEAD = 2
LANES = 256
LIMIT = 60 * 1024 * 1024
ROOM = 40 * 1024 * 1024
SMEM = pl.BlockSpec(memory_space=pltpu.SMEM)
VMEM = pl.BlockSpec(memory_space=pltpu.VMEM)
HBM = pl.BlockSpec(memory_space=pltpu.HBM)


def split(value):
    high = value.astype(BF16)
    low = (value - high.astype(F32)).astype(BF16)
    return high, low


def dot(left, right, dims=NN):
    return lax.dot_general(left, right, dims, preferred_element_type=F32)


def dot3(left, right, dims=NN):
    return (
        dot(left[0], right[1], dims) + dot(left[1], right[0], dims) + dot(left[0], right[0], dims)
    )


def stacked(value):
    high, low = split(value)
    return jnp.concatenate([high, high, low], axis=0)


def side_by_side(value):
    high, low = split(value)
    return jnp.concatenate([high, low, high], axis=1)


def sigmoid(value):
    return 0.5 * jnp.tanh(0.5 * value) + 0.5


def call(kernel, name, flops, out_shape, limit=LIMIT, **kwargs):
    moved = 8 * sum(math.prod(s.shape) for s in jax.tree.leaves(out_shape))
    return pl.pallas_call(
        kernel,
        out_shape=out_shape,
        name=name,
        cost_estimate=pl.CostEstimate(flops=flops, bytes_accessed=moved, transcendentals=0),
        compiler_params=pltpu.CompilerParams(vmem_limit_bytes=limit),
        **kwargs,
    )


def stream(loads, stores, product):
    for copy in loads[:AHEAD]:
        copy.start()
    for i, store in enumerate(stores):
        loads[i].wait()
        if i + AHEAD < len(loads):
            loads[i + AHEAD].start()
        product(i)
        store.start()
    for copy in stores:
        copy.wait()


def wide_product(pair, value):
    width = pair.shape[0] // 2
    high, low = split(value)
    both = dot(pair[...], high, NT)
    return both[:width] + (both[width:] + dot(pair[:width], low, NT))


def input_kernel(
    chunks,
    x_hbm,
    weight_hbm,
    t_hbm,
    next_weight_hbm,
    out_hbm,
    pair_hbm,
    next_rows,
    next_pair,
    x,
    out,
    weight,
    next_weight,
    pair,
    in_sems,
    out_sems,
    sems,
):
    width = weight.shape[0]
    fetch = pltpu.make_async_copy(weight_hbm, weight, sems.at[0])
    keep = pltpu.make_async_copy(pair, pair_hbm, sems.at[1])
    fetch_next = pltpu.make_async_copy(next_weight_hbm, next_weight, sems.at[2])
    fetch_rows = pltpu.make_async_copy(t_hbm.at[: next_rows.shape[0]], next_rows, sems.at[3])
    fetch.start()
    loads = [
        pltpu.make_async_copy(x_hbm.at[here], x.at[here], in_sems.at[i]) for i, here in enumerate(chunks)
    ]
    stores = [
        pltpu.make_async_copy(out.at[:, here], out_hbm.at[:, here], out_sems.at[i])
        for i, here in enumerate(chunks)
    ]

    def product(i):
        if i == 0:
            fetch.wait()
            pair[:width], pair[width:] = split(weight[...])
            keep.start()
            fetch_next.start()
        if i == 1:
            fetch_rows.start()
        if i == len(chunks) - 1:
            fetch_next.wait()
            next_pair[:width], next_pair[width:] = split(next_weight[...])
        out[:, chunks[i]] = wide_product(pair, x[chunks[i], :])

    stream(loads, stores, product)
    keep.wait()
    fetch_rows.wait()


def target_kernel(chunks, t_hbm, rows, pair, out_hbm, t, out, in_sems, out_sems):
    loads = [
        pltpu.make_async_copy(t_hbm.at[here], t.at[here], in_sems.at[i])
        for i, here in enumerate(chunks[1:])
    ]
    stores = [
        pltpu.make_async_copy(out.at[:, here], out_hbm.at[:, here], out_sems.at[i])
        for i, here in enumerate(chunks)
    ]
    for copy in loads[:AHEAD]:
        copy.start()
    out[:, chunks[0]] = wide_product(pair, rows[...])
    stores[0].start()
    for i, copy in enumerate(loads):
        copy.wait()
        if i + AHEAD < len(loads):
            loads[i + AHEAD].start()
        here = chunks[i + 1]
        out[:, here] = wide_product(pair, t[here, :])
        stores[i + 1].start()
    for copy in stores:
        copy.wait()


def prepare_kernel(patches, pair, cwgt, xwgt, crops_ref, before_ref, grams, projects, coarses, pick):
    del before_ref
    width = xwgt.shape[0]
    high, low = pair[:width], pair[width:]
    grams[...] = side_by_side(dot3((high, low), (high, low), NT) + dot(low, low, NT))
    projects[...] = side_by_side(xwgt[...])
    coarses[...] = side_by_side(cwgt[...])
    pick[...] = chosen(crops_ref, patches, pick.shape[1] // patches)


def stack_kernel(*refs):
    *block_refs, _, out_ref = refs
    size = block_refs[0].shape[0]
    for k, ref in enumerate(block_refs):
        out_ref[k * size : (k + 1) * size] = ref[...]


def row_value(crops_ref, column, patches, shape, axis, each):
    index = lax.broadcasted_iota(jnp.int32, shape, axis) // each
    found = jnp.zeros(shape, jnp.int32)
    for j in range(patches):
        found = jnp.where(index == j, crops_ref[column, j], found)
    return found


def chosen(crops_ref, patches, tokens):
    scale = row_value(crops_ref, 3, patches, (1, patches * tokens), 1, tokens)
    token = lax.broadcasted_iota(jnp.int32, (1, patches * tokens), 1)
    row, column = (token % tokens) // 16, token % 16
    wanted = token // tokens * 16 + (row * scale // 8) * 4 + column * scale // 8
    slot = lax.broadcasted_iota(jnp.int32, (patches * 16, patches * tokens), 0)
    return jnp.where(slot == wanted, 1.0, 0.0).astype(BF16)


def middle_kernel(
    patches,
    peers,
    crops_ref,
    own_ref,
    other_ref,
    grams,
    projects,
    coarses,
    pick,
    xw_hbm,
    tw_hbm,
    de_hbm,
    send_ref,
    xw,
    tw,
    rows,
    in_sems,
    out_sems,
):
    pixels = coarses.shape[0]
    width, count = xw.shape
    slots = patches * 16
    far = peers // 4
    chunks = chunk_rows(0, count)
    large = [pltpu.make_async_copy(xw_hbm, xw, in_sems.at[0]), pltpu.make_async_copy(tw_hbm, tw, in_sems.at[1])]
    stores = [
        pltpu.make_async_copy(xw.at[:, here], de_hbm.at[:, here], out_sems.at[i])
        for i, here in enumerate(chunks)
    ]
    for copy in large:
        copy.start()

    me, side = lax.axis_index(("far", "y", "core")), lax.axis_index("lvl")
    for j in range(patches):
        frame, top, left = crops_ref[0, j], crops_ref[1, j], crops_ref[2, j]
        near = lax.bitwise_xor(frame % 4, me % 4)
        k = (me // 4 - frame // 4 + far) % far
        for a in range(4):
            row = jnp.minimum(top + a, SIDE - 1)
            shard = (lax.bitwise_xor(row // 4, side) * 2 + near // 2) * far + k
            start = pl.ds(pl.multiple_of((shard * 4 + row % 4) * SIDE, SIDE), SIDE)
            line = jnp.where(near % 2 == 0, own_ref[start, :], other_ref[start, :])
            rows[j * 16 + a * 4 : j * 16 + a * 4 + 4, :] = pltpu.roll(line, SIDE - left, 0)[:4, :]
    pre = dot3(split(rows[...]), (coarses[:, :width], coarses[:, width : 2 * width]))
    gate = sigmoid(pre)
    slope = (gate * (1.0 + pre * (1.0 - gate))).T
    projected = dot3(split(pre * gate), (projects[:, :width], projects[:, width : 2 * width])).T
    projected = jnp.concatenate(split(projected), axis=1)
    for copy in large:
        copy.wait()

    def first(i):
        taken = pick[:, chunks[i]]
        pre = xw[:, chunks[i]] + dot(projected, jnp.concatenate([taken, taken], axis=0))
        gate = sigmoid(pre)
        hidden = pre * gate
        return gate + hidden * (1.0 - gate), stacked(hidden)

    dslot = jnp.zeros((2 * width, slots), F32)
    ready = first(0)
    for i, here in enumerate(chunks):
        factor, stack = ready
        product = dot(grams[...], stack)
        if i + 1 < len(chunks):
            ready = first(i + 1)
        de = (product - tw[:, here]) * factor
        xw[:, here] = de
        dslot = dslot + dot(jnp.concatenate(split(de), axis=0), pick[:, here], NT)
    for copy in stores:
        copy.start()

    dcontext = dot(projects[...], stacked(dslot[:width] + dslot[width:]))
    grad = dot(coarses[...], stacked(dcontext * slope)).T
    shape = (patches * 16, LANES - pixels)
    slot = lax.broadcasted_iota(jnp.int32, shape, 0) % 16
    top = row_value(crops_ref, 1, patches, shape, 0, 16)
    left = row_value(crops_ref, 2, patches, shape, 0, 16)
    number = ((top + slot // 4) * SIDE + left + slot % 4).astype(F32)
    send_ref[...] = jnp.zeros_like(send_ref)
    for j in range(patches):
        start = pl.ds(pl.multiple_of(crops_ref[0, j] * 16, 16), 16)
        send_ref[start, :pixels] = grad[j * 16 : j * 16 + 16, :]
        send_ref[start, pixels:] = number[j * 16 : j * 16 + 16, :]
    for copy in stores:
        copy.wait()


def scatter_kernel(message_ref, done_ref, mine_ref, other_ref, total):
    del done_ref
    pixels = mine_ref.shape[2]
    message = message_ref[...]
    number = lax.broadcasted_iota(jnp.int32, (message.shape[0], SIDE * SIDE), 1).astype(F32)
    pick = jnp.where(message[:, pixels : pixels + 1] == number, 1.0, 0.0).astype(BF16)
    high, low = split(message[:, :pixels])
    total[...] = dot(pick, low, TN) + dot(pick, high, TN)
    half = mine_ref.shape[1]
    side = lax.axis_index("lvl")
    mine_ref[0] = total[pl.ds(pl.multiple_of(side * half, half), half), :]
    other_ref[0] = total[pl.ds(pl.multiple_of((1 - side) * half, half), half), :]


def last_kernel(chunks, de_hbm, pair_hbm, *refs):
    out_hbm, de, out, deep, in_sems, out_sems, sems = refs
    width = de.shape[0]
    fetches = [
        pltpu.make_async_copy(pair_hbm, deep.at[: 2 * width], sems.at[0]),
        pltpu.make_async_copy(pair_hbm.at[:width], deep.at[2 * width :], sems.at[1]),
    ]
    for copy in fetches:
        copy.start()
    loads = [
        pltpu.make_async_copy(de_hbm.at[:, here], de.at[:, here], in_sems.at[i])
        for i, here in enumerate(chunks)
    ]
    stores = [
        pltpu.make_async_copy(out.at[here], out_hbm.at[here], out_sems.at[i])
        for i, here in enumerate(chunks)
    ]

    def product(i):
        if i == 0:
            for copy in fetches:
                copy.wait()
        out[chunks[i], :] = dot(stacked(de[:, chunks[i]]), deep[...], TN)

    stream(loads, stores, product)


def chunk_rows(first, last, edge=ROWS):
    cuts = [first] + list(range(first + edge, last, ROWS))
    if cuts[-1] != last - edge:
        cuts.append(last - edge)
    return [slice(low, high) for low, high in zip(cuts, cuts[1:] + [last])]


def fixed(*values):
    return [pltpu.with_memory_space_constraint(value, pltpu.HBM) for value in values]


def near(*values):
    return [pltpu.with_memory_space_constraint(value, pltpu.VMEM) for value in values]


def stack(blocks, before):
    shape = (len(blocks) * blocks[0].shape[0],) + blocks[0].shape[1:]
    return call(
        stack_kernel,
        "stack",
        1000,
        jax.ShapeDtypeStruct(shape, F32),
        limit=ROOM,
        in_specs=[VMEM] * len(blocks) + [HBM],
        out_specs=VMEM,
    )(*blocks, *fixed(before))


def body(coarse_input, coarse_weight, fine_input, fine_target, crops, in_weight, context_weight, out_weight):
    patch = ("far", "y", "core")
    peers = lax.axis_size(patch)
    far = peers // 4
    patches, tokens, values = fine_input.shape
    width = in_weight.shape[1]
    pixels = coarse_weight.shape[0]
    half = coarse_input.shape[1]
    count = patches * tokens
    swap = [(0, 1), (1, 0)]

    column = [coarse_input]
    for k in range(1, far):
        column.append(lax.ppermute(coarse_input, "far", [(p, (p + k) % far) for p in range(far)]))

    chunks = chunk_rows(0, count)
    edges = chunk_rows(0, count, ROWS // 2)
    pair_shape = (2 * width, values)
    x, t = fine_input.reshape(count, values), fine_target.reshape(count, values)
    xw, pair, rows, next_pair = call(
        functools.partial(input_kernel, edges),
        "input",
        6 * count * values * width,
        (
            pltpu.HBM((width, count), F32),
            pltpu.HBM(pair_shape, BF16),
            pltpu.VMEM((ROWS // 2, values), F32),
            pltpu.VMEM(pair_shape, BF16),
        ),
        in_specs=[HBM] * 4,
        out_specs=(HBM, HBM, VMEM, VMEM),
        scratch_shapes=[
            pltpu.VMEM((count, values), F32),
            pltpu.VMEM((width, count), F32),
            pltpu.VMEM((width, values), F32),
            pltpu.VMEM((width, values), F32),
            pltpu.VMEM(pair_shape, BF16),
            pltpu.SemaphoreType.DMA((len(edges),)),
            pltpu.SemaphoreType.DMA((len(edges),)),
            pltpu.SemaphoreType.DMA((4,)),
        ],
    )(*fixed(x, in_weight.T, t, out_weight))
    column = stack(column, xw)
    own = [column]
    for flip in range(1, 4):
        own.append(lax.ppermute(column, ("lvl", "y"), [(p, p ^ flip) for p in range(4)]))
    tw = call(
        functools.partial(target_kernel, edges),
        "target",
        6 * count * values * width,
        pltpu.HBM((width, count), F32),
        limit=ROOM,
        in_specs=[HBM, VMEM, VMEM],
        out_specs=HBM,
        scratch_shapes=[
            pltpu.VMEM((count, values), F32),
            pltpu.VMEM((width, count), F32),
            pltpu.SemaphoreType.DMA((len(edges),)),
            pltpu.SemaphoreType.DMA((len(edges),)),
        ],
    )(*fixed(t), *near(rows, next_pair))
    own = stack(own, tw).reshape(-1, pixels)
    other = lax.ppermute(own, "core", swap)
    crops = crops.T
    prepared = call(
        functools.partial(prepare_kernel, patches),
        "prepare",
        8 * values * width * width,
        (
            pltpu.VMEM((width, 3 * width), BF16),
            pltpu.VMEM((width, 3 * width), BF16),
            pltpu.VMEM((pixels, 3 * width), BF16),
            pltpu.VMEM((patches * 16, count), BF16),
        ),
        limit=ROOM,
        in_specs=[VMEM, VMEM, VMEM, SMEM, HBM],
        out_specs=(VMEM,) * 4,
    )(*near(next_pair), coarse_weight, context_weight, crops, own)

    shape = (peers * 16, LANES)
    de, back = call(
        functools.partial(middle_kernel, patches, peers),
        "middle",
        6 * count * width * width,
        (pltpu.HBM((width, count), F32), jax.ShapeDtypeStruct(shape, F32)),
        limit=ROOM,
        in_specs=[SMEM] + [VMEM] * 6 + [HBM] * 2,
        out_specs=(HBM, VMEM),
        scratch_shapes=[
            pltpu.VMEM((width, count), F32),
            pltpu.VMEM((width, count), F32),
            pltpu.VMEM((patches * 16, pixels), F32),
            pltpu.SemaphoreType.DMA((2,)),
            pltpu.SemaphoreType.DMA((len(chunks),)),
        ],
    )(crops, own, other, *near(*prepared), *fixed(xw, tw))
    returned = lax.all_to_all(back, patch, 0, 0, tiled=True)

    fine_grad = call(
        functools.partial(last_kernel, chunks),
        "last",
        6 * count * values * width,
        pltpu.HBM((count, values), F32),
        in_specs=[HBM, HBM],
        out_specs=HBM,
        scratch_shapes=[
            pltpu.VMEM((width, count), F32),
            pltpu.VMEM((count, values), F32),
            pltpu.VMEM((3 * width, values), BF16),
            pltpu.SemaphoreType.DMA((len(chunks),)),
            pltpu.SemaphoreType.DMA((len(chunks),)),
            pltpu.SemaphoreType.DMA((2,)),
        ],
    )(*fixed(de, pair))
    part = (1, half, pixels)
    mine, theirs = call(
        scatter_kernel,
        "scatter",
        10000,
        (jax.ShapeDtypeStruct(part, F32), jax.ShapeDtypeStruct(part, F32)),
        limit=ROOM,
        in_specs=[VMEM, HBM],
        out_specs=(VMEM, VMEM),
        scratch_shapes=[pltpu.VMEM((SIDE * SIDE, pixels), F32)],
    )(returned, *fixed(fine_grad))
    coarse_grad = mine + lax.ppermute(theirs, "lvl", swap)
    return (coarse_grad, fine_grad.reshape(fine_input.shape))


def solution(mesh):
    sides, peers = mesh.shape["lvl"], mesh.shape["patch"]
    fine = jax.sharding.Mesh(mesh.devices.reshape(sides, peers // 4, 2, 2), ("lvl", "far", "y", "core"))
    patch = ("far", "y", "core")
    both = ("lvl",) + patch
    in_specs = (
        P(patch, "lvl", None),
        P(),
        P(both, None, None),
        P(both, None, None),
        P(both, None),
        P(),
        P(),
        P(),
    )
    out_specs = (P(patch, "lvl", None), P(both, None, None))
    return jax.shard_map(body, mesh=fine, in_specs=in_specs, out_specs=out_specs, check_vma=False)
```

```python
import functools
import math

import jax
import jax.numpy as jnp
from jax import lax
from jax.experimental import pallas as pl
from jax.experimental.pallas import tpu as pltpu
from jax.sharding import PartitionSpec as P

F32 = jnp.float32
BF16 = jnp.bfloat16
NN = (((1,), (0,)), ((), ()))
NT = (((1,), (1,)), ((), ()))
TN = (((0,), (0,)), ((), ()))
ROWS = 512
SIDE = 8
AHEAD = 2
LANES = 256
LIMIT = 60 * 1024 * 1024
ROOM = 40 * 1024 * 1024
SMEM = pl.BlockSpec(memory_space=pltpu.SMEM)
VMEM = pl.BlockSpec(memory_space=pltpu.VMEM)
HBM = pl.BlockSpec(memory_space=pltpu.HBM)


def split(value):
    high = value.astype(BF16)
    low = (value - high.astype(F32)).astype(BF16)
    return high, low


def dot(left, right, dims=NN):
    return lax.dot_general(left, right, dims, preferred_element_type=F32)


def dot3(left, right, dims=NN):
    return (
        dot(left[0], right[1], dims) + dot(left[1], right[0], dims) + dot(left[0], right[0], dims)
    )


def stacked(value):
    high, low = split(value)
    return jnp.concatenate([high, high, low], axis=0)


def side_by_side(value):
    high, low = split(value)
    return jnp.concatenate([high, low, high], axis=1)


def sigmoid(value):
    return 0.5 * jnp.tanh(0.5 * value) + 0.5


def call(kernel, name, flops, out_shape, limit=LIMIT, **kwargs):
    moved = 8 * sum(math.prod(s.shape) for s in jax.tree.leaves(out_shape))
    return pl.pallas_call(
        kernel,
        out_shape=out_shape,
        name=name,
        cost_estimate=pl.CostEstimate(flops=flops, bytes_accessed=moved, transcendentals=0),
        compiler_params=pltpu.CompilerParams(vmem_limit_bytes=limit),
        **kwargs,
    )


def stream(loads, stores, product):
    for copy in loads[:AHEAD]:
        copy.start()
    for i, store in enumerate(stores):
        loads[i].wait()
        if i + AHEAD < len(loads):
            loads[i + AHEAD].start()
        product(i)
        store.start()
    for copy in stores:
        copy.wait()


def pair_product(pair, value, dims):
    rows = pair.shape[0] // 2
    high, low = split(value)
    both = dot(pair[...], high, dims)
    return both[:rows] + (both[rows:] + dot(pair[:rows], low, dims))


def input_kernel(
    chunks,
    x_hbm,
    weight_hbm,
    t_hbm,
    next_weight_hbm,
    out_hbm,
    pair_hbm,
    next_rows,
    next_pair,
    x,
    out,
    weight,
    next_weight,
    pair,
    in_sems,
    out_sems,
    sems,
):
    width = weight.shape[0]
    fetch = pltpu.make_async_copy(weight_hbm, weight, sems.at[0])
    keep = pltpu.make_async_copy(pair, pair_hbm, sems.at[1])
    fetch_next = pltpu.make_async_copy(next_weight_hbm, next_weight, sems.at[2])
    fetch_rows = pltpu.make_async_copy(t_hbm.at[: next_rows.shape[0]], next_rows, sems.at[3])
    fetch.start()
    loads = [
        pltpu.make_async_copy(x_hbm.at[here], x.at[here], in_sems.at[i]) for i, here in enumerate(chunks)
    ]
    stores = [
        pltpu.make_async_copy(out.at[:, here], out_hbm.at[:, here], out_sems.at[i])
        for i, here in enumerate(chunks)
    ]

    def product(i):
        if i == 0:
            fetch.wait()
            pair[:width], pair[width:] = split(weight[...])
            keep.start()
            fetch_next.start()
        if i == 1:
            fetch_rows.start()
        if i == len(chunks) - 1:
            fetch_next.wait()
            next_pair[:width], next_pair[width:] = split(next_weight[...])
        out[:, chunks[i]] = pair_product(pair, x[chunks[i], :], NT)

    stream(loads, stores, product)
    keep.wait()
    fetch_rows.wait()


def target_kernel(chunks, t_hbm, rows, pair, out_hbm, t, out, in_sems, out_sems):
    loads = [
        pltpu.make_async_copy(t_hbm.at[here], t.at[here], in_sems.at[i])
        for i, here in enumerate(chunks[1:])
    ]
    stores = [
        pltpu.make_async_copy(out.at[:, here], out_hbm.at[:, here], out_sems.at[i])
        for i, here in enumerate(chunks)
    ]
    for copy in loads[:AHEAD]:
        copy.start()
    out[:, chunks[0]] = pair_product(pair, rows[...], NT)
    stores[0].start()
    for i, copy in enumerate(loads):
        copy.wait()
        if i + AHEAD < len(loads):
            loads[i + AHEAD].start()
        here = chunks[i + 1]
        out[:, here] = pair_product(pair, t[here, :], NT)
        stores[i + 1].start()
    for copy in stores:
        copy.wait()


def prepare_kernel(patches, pair, cwgt, xwgt, crops_ref, before_ref, grams, projects, coarses, pick):
    del before_ref
    width = xwgt.shape[0]
    high, low = pair[:width], pair[width:]
    grams[...] = side_by_side(dot3((high, low), (high, low), NT) + dot(low, low, NT))
    projects[...] = jnp.concatenate(split(xwgt[...]), axis=0)
    coarses[...] = jnp.concatenate(split(cwgt[...]), axis=0)
    pick[...] = chosen(crops_ref, patches, pick.shape[1] // patches)


def stack_kernel(*refs):
    *block_refs, _, out_ref = refs
    size = block_refs[0].shape[0]
    for k, ref in enumerate(block_refs):
        out_ref[k * size : (k + 1) * size] = ref[...]


def row_value(crops_ref, column, patches, shape, axis, each):
    index = lax.broadcasted_iota(jnp.int32, shape, axis) // each
    found = jnp.zeros(shape, jnp.int32)
    for j in range(patches):
        found = jnp.where(index == j, crops_ref[column, j], found)
    return found


def chosen(crops_ref, patches, tokens):
    scale = row_value(crops_ref, 3, patches, (1, patches * tokens), 1, tokens)
    token = lax.broadcasted_iota(jnp.int32, (1, patches * tokens), 1)
    row, column = (token % tokens) // 16, token % 16
    wanted = token // tokens * 16 + (row * scale // 8) * 4 + column * scale // 8
    slot = lax.broadcasted_iota(jnp.int32, (patches * 16, patches * tokens), 0)
    return jnp.where(slot == wanted, 1.0, 0.0).astype(BF16)


def middle_kernel(
    patches,
    peers,
    crops_ref,
    own_ref,
    other_ref,
    grams,
    projects,
    coarses,
    pick,
    xw_hbm,
    tw_hbm,
    de_hbm,
    send_ref,
    xw,
    tw,
    rows,
    in_sems,
    out_sems,
):
    pixels = coarses.shape[0] // 2
    width, count = xw.shape
    slots = patches * 16
    far = peers // 4
    chunks = chunk_rows(0, count)
    large = [pltpu.make_async_copy(xw_hbm, xw, in_sems.at[0]), pltpu.make_async_copy(tw_hbm, tw, in_sems.at[1])]
    stores = [
        pltpu.make_async_copy(xw.at[:, here], de_hbm.at[:, here], out_sems.at[i])
        for i, here in enumerate(chunks)
    ]
    for copy in large:
        copy.start()

    me, side = lax.axis_index(("far", "y", "core")), lax.axis_index("lvl")
    for j in range(patches):
        frame, top, left = crops_ref[0, j], crops_ref[1, j], crops_ref[2, j]
        near = lax.bitwise_xor(frame % 4, me % 4)
        k = (me // 4 - frame // 4 + far) % far
        for a in range(4):
            row = jnp.minimum(top + a, SIDE - 1)
            shard = (lax.bitwise_xor(row // 4, side) * 2 + near // 2) * far + k
            start = pl.ds(pl.multiple_of((shard * 4 + row % 4) * SIDE, SIDE), SIDE)
            line = jnp.where(near % 2 == 0, own_ref[start, :], other_ref[start, :])
            rows[j * 16 + a * 4 : j * 16 + a * 4 + 4, :] = pltpu.roll(line, SIDE - left, 0)[:4, :]
    pre = dot3(split(rows[...]), (coarses[:pixels], coarses[pixels:]))
    gate = sigmoid(pre)
    slope = (gate * (1.0 + pre * (1.0 - gate))).T
    projected = dot3(split(pre * gate), (projects[:width], projects[width:])).T
    projected = jnp.concatenate(split(projected), axis=1)
    for copy in large:
        copy.wait()

    def first(i):
        taken = pick[:, chunks[i]]
        pre = xw[:, chunks[i]] + dot(projected, jnp.concatenate([taken, taken], axis=0))
        gate = sigmoid(pre)
        hidden = pre * gate
        return gate + hidden * (1.0 - gate), stacked(hidden)

    dslot = jnp.zeros((2 * width, slots), F32)
    ready = first(0)
    for i, here in enumerate(chunks):
        factor, stack = ready
        product = dot(grams[...], stack)
        if i + 1 < len(chunks):
            ready = first(i + 1)
        de = (product - tw[:, here]) * factor
        xw[:, here] = de
        dslot = dslot + dot(jnp.concatenate(split(de), axis=0), pick[:, here], NT)
    for copy in stores:
        copy.start()

    dcontext = pair_product(projects, dslot[:width] + dslot[width:], NN)
    grad = pair_product(coarses, dcontext * slope, NN).T
    shape = (patches * 16, LANES - pixels)
    slot = lax.broadcasted_iota(jnp.int32, shape, 0) % 16
    top = row_value(crops_ref, 1, patches, shape, 0, 16)
    left = row_value(crops_ref, 2, patches, shape, 0, 16)
    number = ((top + slot // 4) * SIDE + left + slot % 4).astype(F32)
    send_ref[...] = jnp.zeros_like(send_ref)
    for j in range(patches):
        start = pl.ds(pl.multiple_of(crops_ref[0, j] * 16, 16), 16)
        send_ref[start, :pixels] = grad[j * 16 : j * 16 + 16, :]
        send_ref[start, pixels:] = number[j * 16 : j * 16 + 16, :]
    for copy in stores:
        copy.wait()


def scatter_kernel(message_ref, done_ref, mine_ref, other_ref, total):
    del done_ref
    pixels = mine_ref.shape[2]
    message = message_ref[...]
    number = lax.broadcasted_iota(jnp.int32, (message.shape[0], SIDE * SIDE), 1).astype(F32)
    pick = jnp.where(message[:, pixels : pixels + 1] == number, 1.0, 0.0).astype(BF16)
    high, low = split(message[:, :pixels])
    total[...] = dot(pick, low, TN) + dot(pick, high, TN)
    half = mine_ref.shape[1]
    side = lax.axis_index("lvl")
    mine_ref[0] = total[pl.ds(pl.multiple_of(side * half, half), half), :]
    other_ref[0] = total[pl.ds(pl.multiple_of((1 - side) * half, half), half), :]


def last_kernel(chunks, de_hbm, pair_hbm, *refs):
    out_hbm, de, out, deep, cat, in_sems, out_sems, sems = refs
    width = de.shape[0]
    fetches = [
        pltpu.make_async_copy(pair_hbm, deep.at[: 2 * width], sems.at[0]),
        pltpu.make_async_copy(pair_hbm.at[:width], deep.at[2 * width :], sems.at[1]),
    ]
    for copy in fetches:
        copy.start()
    loads = [
        pltpu.make_async_copy(de_hbm.at[:, here], de.at[:, here], in_sems.at[i])
        for i, here in enumerate(chunks)
    ]
    stores = [
        pltpu.make_async_copy(out.at[here], out_hbm.at[here], out_sems.at[i])
        for i, here in enumerate(chunks)
    ]

    def prepare(i):
        loads[i].wait()
        cat[i % 2] = stacked(de[:, chunks[i]])

    for copy in loads:
        copy.start()
    prepare(0)
    for copy in fetches:
        copy.wait()
    for i, here in enumerate(chunks):
        out[here, :] = dot(cat[i % 2], deep[...], TN)
        if i + 1 < len(chunks):
            prepare(i + 1)
        stores[i].start()
    for copy in stores:
        copy.wait()


def chunk_rows(first, last):
    return [slice(start, start + ROWS) for start in range(first, last, ROWS)]


def fixed(*values):
    return [pltpu.with_memory_space_constraint(value, pltpu.HBM) for value in values]


def near(*values):
    return [pltpu.with_memory_space_constraint(value, pltpu.VMEM) for value in values]


def stack(blocks, before):
    shape = (len(blocks) * blocks[0].shape[0],) + blocks[0].shape[1:]
    return call(
        stack_kernel,
        "stack",
        1000,
        jax.ShapeDtypeStruct(shape, F32),
        limit=ROOM,
        in_specs=[VMEM] * len(blocks) + [HBM],
        out_specs=VMEM,
    )(*blocks, *fixed(before))


def body(coarse_input, coarse_weight, fine_input, fine_target, crops, in_weight, context_weight, out_weight):
    patch = ("far", "y", "core")
    peers = lax.axis_size(patch)
    far = peers // 4
    patches, tokens, values = fine_input.shape
    width = in_weight.shape[1]
    pixels = coarse_weight.shape[0]
    half = coarse_input.shape[1]
    count = patches * tokens
    swap = [(0, 1), (1, 0)]

    column = [coarse_input]
    for k in range(1, far):
        column.append(lax.ppermute(coarse_input, "far", [(p, (p + k) % far) for p in range(far)]))

    chunks = chunk_rows(0, count)
    pair_shape = (2 * width, values)
    x, t = fine_input.reshape(count, values), fine_target.reshape(count, values)
    xw, pair, rows, next_pair = call(
        functools.partial(input_kernel, chunks),
        "input",
        6 * count * values * width,
        (
            pltpu.HBM((width, count), F32),
            pltpu.HBM(pair_shape, BF16),
            pltpu.VMEM((ROWS, values), F32),
            pltpu.VMEM(pair_shape, BF16),
        ),
        in_specs=[HBM] * 4,
        out_specs=(HBM, HBM, VMEM, VMEM),
        scratch_shapes=[
            pltpu.VMEM((count, values), F32),
            pltpu.VMEM((width, count), F32),
            pltpu.VMEM((width, values), F32),
            pltpu.VMEM((width, values), F32),
            pltpu.VMEM(pair_shape, BF16),
            pltpu.SemaphoreType.DMA((len(chunks),)),
            pltpu.SemaphoreType.DMA((len(chunks),)),
            pltpu.SemaphoreType.DMA((4,)),
        ],
    )(*fixed(x, in_weight.T, t, out_weight))
    column = stack(column, xw)
    own = [column]
    for flip in range(1, 4):
        own.append(lax.ppermute(column, ("lvl", "y"), [(p, p ^ flip) for p in range(4)]))
    tw = call(
        functools.partial(target_kernel, chunks),
        "target",
        6 * count * values * width,
        pltpu.HBM((width, count), F32),
        limit=ROOM,
        in_specs=[HBM, VMEM, VMEM],
        out_specs=HBM,
        scratch_shapes=[
            pltpu.VMEM((count, values), F32),
            pltpu.VMEM((width, count), F32),
            pltpu.SemaphoreType.DMA((len(chunks),)),
            pltpu.SemaphoreType.DMA((len(chunks),)),
        ],
    )(*fixed(t), *near(rows, next_pair))
    own = stack(own, tw).reshape(-1, pixels)
    other = lax.ppermute(own, "core", swap)
    crops = crops.T
    prepared = call(
        functools.partial(prepare_kernel, patches),
        "prepare",
        8 * values * width * width,
        (
            pltpu.VMEM((width, 3 * width), BF16),
            pltpu.VMEM((2 * width, width), BF16),
            pltpu.VMEM((2 * pixels, width), BF16),
            pltpu.VMEM((patches * 16, count), BF16),
        ),
        limit=ROOM,
        in_specs=[VMEM, VMEM, VMEM, SMEM, HBM],
        out_specs=(VMEM,) * 4,
    )(*near(next_pair), coarse_weight, context_weight, crops, own)

    shape = (peers * 16, LANES)
    de, back = call(
        functools.partial(middle_kernel, patches, peers),
        "middle",
        6 * count * width * width,
        (pltpu.HBM((width, count), F32), jax.ShapeDtypeStruct(shape, F32)),
        limit=ROOM,
        in_specs=[SMEM] + [VMEM] * 6 + [HBM] * 2,
        out_specs=(HBM, VMEM),
        scratch_shapes=[
            pltpu.VMEM((width, count), F32),
            pltpu.VMEM((width, count), F32),
            pltpu.VMEM((patches * 16, pixels), F32),
            pltpu.SemaphoreType.DMA((2,)),
            pltpu.SemaphoreType.DMA((len(chunks),)),
        ],
    )(crops, own, other, *near(*prepared), *fixed(xw, tw))
    returned = lax.all_to_all(back, patch, 0, 0, tiled=True)

    fine_grad = call(
        functools.partial(last_kernel, chunks),
        "last",
        6 * count * values * width,
        pltpu.HBM((count, values), F32),
        in_specs=[HBM, HBM],
        out_specs=HBM,
        scratch_shapes=[
            pltpu.VMEM((width, count), F32),
            pltpu.VMEM((count, values), F32),
            pltpu.VMEM((3 * width, values), BF16),
            pltpu.VMEM((2, 3 * width, ROWS), BF16),
            pltpu.SemaphoreType.DMA((len(chunks),)),
            pltpu.SemaphoreType.DMA((len(chunks),)),
            pltpu.SemaphoreType.DMA((2,)),
        ],
    )(*fixed(de, pair))
    part = (1, half, pixels)
    mine, theirs = call(
        scatter_kernel,
        "scatter",
        10000,
        (jax.ShapeDtypeStruct(part, F32), jax.ShapeDtypeStruct(part, F32)),
        limit=ROOM,
        in_specs=[VMEM, HBM],
        out_specs=(VMEM, VMEM),
        scratch_shapes=[pltpu.VMEM((SIDE * SIDE, pixels), F32)],
    )(returned, *fixed(fine_grad))
    coarse_grad = mine + lax.ppermute(theirs, "lvl", swap)
    return (coarse_grad, fine_grad.reshape(fine_input.shape))


def solution(mesh):
    sides, peers = mesh.shape["lvl"], mesh.shape["patch"]
    fine = jax.sharding.Mesh(mesh.devices.reshape(sides, peers // 4, 2, 2), ("lvl", "far", "y", "core"))
    patch = ("far", "y", "core")
    both = ("lvl",) + patch
    in_specs = (
        P(patch, "lvl", None),
        P(),
        P(both, None, None),
        P(both, None, None),
        P(both, None),
        P(),
        P(),
        P(),
    )
    out_specs = (P(patch, "lvl", None), P(both, None, None))
    return jax.shard_map(body, mesh=fine, in_specs=in_specs, out_specs=out_specs, check_vma=False)
```

```python
import functools
import math

import jax
import jax.numpy as jnp
from jax import lax
from jax.experimental import pallas as pl
from jax.experimental.pallas import tpu as pltpu
from jax.sharding import PartitionSpec as P

F32 = jnp.float32
BF16 = jnp.bfloat16
NN = (((1,), (0,)), ((), ()))
NT = (((1,), (1,)), ((), ()))
TN = (((0,), (0,)), ((), ()))
ROWS = 512
SIDE = 8
AHEAD = 2
LANES = 256
LIMIT = 60 * 1024 * 1024
ROOM = 40 * 1024 * 1024
SMEM = pl.BlockSpec(memory_space=pltpu.SMEM)
VMEM = pl.BlockSpec(memory_space=pltpu.VMEM)
HBM = pl.BlockSpec(memory_space=pltpu.HBM)


def split(value):
    high = value.astype(BF16)
    low = (value - high.astype(F32)).astype(BF16)
    return high, low


def dot(left, right, dims=NN):
    return lax.dot_general(left, right, dims, preferred_element_type=F32)


def dot3(left, right, dims=NN):
    return (
        dot(left[0], right[1], dims) + dot(left[1], right[0], dims) + dot(left[0], right[0], dims)
    )


def side_by_side(value):
    high, low = split(value)
    return jnp.concatenate([high, low, high], axis=1)


def sigmoid(value):
    return 0.5 * jnp.tanh(0.5 * value) + 0.5


def call(kernel, name, flops, out_shape, limit=LIMIT, **kwargs):
    moved = 8 * sum(math.prod(s.shape) for s in jax.tree.leaves(out_shape))
    return pl.pallas_call(
        kernel,
        out_shape=out_shape,
        name=name,
        cost_estimate=pl.CostEstimate(flops=flops, bytes_accessed=moved, transcendentals=0),
        compiler_params=pltpu.CompilerParams(vmem_limit_bytes=limit),
        **kwargs,
    )


def stream(loads, stores, product):
    for copy in loads[:AHEAD]:
        copy.start()
    for i, store in enumerate(stores):
        loads[i].wait()
        if i + AHEAD < len(loads):
            loads[i + AHEAD].start()
        product(i)
        store.start()
    for copy in stores:
        copy.wait()


def blocks(rows, size):
    return [slice(start, start + size) for start in range(0, rows, size)]


def shift(here, by):
    return slice(here.start + by, here.stop + by)


def pair_product(pair, value, dims):
    rows = pair.shape[0] // 2
    high, low = split(value)
    both = dot(pair[...], high, dims)
    return both[:rows] + (both[rows:] + dot(pair[:rows], low, dims))


def wide_product(pair, value, high, low, out, tokens):
    width = pair.shape[0] // 2
    for here in blocks(high.shape[0], 16):
        high[here], low[here] = split(value[here])
    both = dot(pair[...], high[...], NT)
    rest = dot(pair[:width], low[...], NT)
    for here in blocks(width, 32):
        out[here, tokens] = both[here] + (both[shift(here, width)] + rest[here])


def input_kernel(
    chunks,
    x_hbm,
    weight_hbm,
    t_hbm,
    next_weight_hbm,
    out_hbm,
    pair_hbm,
    next_rows,
    next_pair,
    x,
    out,
    weight,
    next_weight,
    pair,
    high,
    low,
    in_sems,
    out_sems,
    sems,
):
    width = weight.shape[0]
    fetch = pltpu.make_async_copy(weight_hbm, weight, sems.at[0])
    keep = pltpu.make_async_copy(pair, pair_hbm, sems.at[1])
    fetch_next = pltpu.make_async_copy(next_weight_hbm, next_weight, sems.at[2])
    fetch_rows = pltpu.make_async_copy(t_hbm.at[: next_rows.shape[0]], next_rows, sems.at[3])
    fetch.start()
    loads = [
        pltpu.make_async_copy(x_hbm.at[here], x.at[here], in_sems.at[i]) for i, here in enumerate(chunks)
    ]
    stores = [
        pltpu.make_async_copy(out.at[:, here], out_hbm.at[:, here], out_sems.at[i])
        for i, here in enumerate(chunks)
    ]

    def product(i):
        if i == 0:
            fetch.wait()
            pair[:width], pair[width:] = split(weight[...])
            keep.start()
            fetch_next.start()
        if i == 1:
            fetch_rows.start()
        if i == len(chunks) - 1:
            fetch_next.wait()
            next_pair[:width], next_pair[width:] = split(next_weight[...])
        wide_product(pair, x.at[chunks[i]], high, low, out, chunks[i])

    stream(loads, stores, product)
    keep.wait()
    fetch_rows.wait()


def target_kernel(chunks, t_hbm, rows, pair, out_hbm, t, out, high, low, in_sems, out_sems):
    loads = [
        pltpu.make_async_copy(t_hbm.at[here], t.at[here], in_sems.at[i])
        for i, here in enumerate(chunks[1:])
    ]
    stores = [
        pltpu.make_async_copy(out.at[:, here], out_hbm.at[:, here], out_sems.at[i])
        for i, here in enumerate(chunks)
    ]
    for copy in loads[:AHEAD]:
        copy.start()
    wide_product(pair, rows, high, low, out, chunks[0])
    stores[0].start()
    for i, copy in enumerate(loads):
        copy.wait()
        if i + AHEAD < len(loads):
            loads[i + AHEAD].start()
        here = chunks[i + 1]
        wide_product(pair, t.at[here], high, low, out, here)
        stores[i + 1].start()
    for copy in stores:
        copy.wait()


def prepare_kernel(patches, pair, cwgt, xwgt, crops_ref, before_ref, grams, projects, coarses, pick):
    del before_ref
    width = xwgt.shape[0]
    high, low = pair[:width], pair[width:]
    grams[...] = side_by_side(dot3((high, low), (high, low), NT) + dot(low, low, NT))
    projects[...] = jnp.concatenate(split(xwgt[...]), axis=0)
    coarses[...] = jnp.concatenate(split(cwgt[...]), axis=0)
    pick[...] = chosen(crops_ref, patches, pick.shape[1] // patches)


def stack_kernel(*refs):
    *block_refs, _, out_ref = refs
    size = block_refs[0].shape[0]
    for k, ref in enumerate(block_refs):
        out_ref[k * size : (k + 1) * size] = ref[...]


def row_value(crops_ref, column, patches, shape, axis, each):
    index = lax.broadcasted_iota(jnp.int32, shape, axis) // each
    found = jnp.zeros(shape, jnp.int32)
    for j in range(patches):
        found = jnp.where(index == j, crops_ref[column, j], found)
    return found


def chosen(crops_ref, patches, tokens):
    scale = row_value(crops_ref, 3, patches, (1, patches * tokens), 1, tokens)
    token = lax.broadcasted_iota(jnp.int32, (1, patches * tokens), 1)
    row, column = (token % tokens) // 16, token % 16
    wanted = token // tokens * 16 + (row * scale // 8) * 4 + column * scale // 8
    slot = lax.broadcasted_iota(jnp.int32, (patches * 16, patches * tokens), 0)
    return jnp.where(slot == wanted, 1.0, 0.0).astype(BF16)


def middle_kernel(
    patches,
    peers,
    crops_ref,
    own_ref,
    other_ref,
    grams,
    projects,
    coarses,
    pick,
    xw_hbm,
    tw_hbm,
    de_hbm,
    send_ref,
    xw,
    tw,
    rows,
    taken,
    factor,
    deep,
    parts,
    in_sems,
    out_sems,
):
    pixels = coarses.shape[0] // 2
    width, count = xw.shape
    slots = patches * 16
    far = peers // 4
    chunks = chunk_rows(0, count)
    large = [pltpu.make_async_copy(xw_hbm, xw, in_sems.at[0]), pltpu.make_async_copy(tw_hbm, tw, in_sems.at[1])]
    stores = [
        pltpu.make_async_copy(xw.at[:, here], de_hbm.at[:, here], out_sems.at[i])
        for i, here in enumerate(chunks)
    ]
    for copy in large:
        copy.start()

    me, side = lax.axis_index(("far", "y", "core")), lax.axis_index("lvl")
    for j in range(patches):
        frame, top, left = crops_ref[0, j], crops_ref[1, j], crops_ref[2, j]
        near = lax.bitwise_xor(frame % 4, me % 4)
        k = (me // 4 - frame // 4 + far) % far
        for a in range(4):
            row = jnp.minimum(top + a, SIDE - 1)
            shard = (lax.bitwise_xor(row // 4, side) * 2 + near // 2) * far + k
            start = pl.ds(pl.multiple_of((shard * 4 + row % 4) * SIDE, SIDE), SIDE)
            line = jnp.where(near % 2 == 0, own_ref[start, :], other_ref[start, :])
            rows[j * 16 + a * 4 : j * 16 + a * 4 + 4, :] = pltpu.roll(line, SIDE - left, 0)[:4, :]
    pre = dot3(split(rows[...]), (coarses[:pixels], coarses[pixels:]))
    gate = sigmoid(pre)
    slope = (gate * (1.0 + pre * (1.0 - gate))).T
    projected = dot3(split(pre * gate), (projects[:width], projects[width:])).T
    projected = jnp.concatenate(split(projected), axis=1)
    for copy in large:
        copy.wait()

    dslot = jnp.zeros((2 * width, slots), F32)
    for tokens in chunks:
        taken[:slots], taken[slots:] = pick[:, tokens], pick[:, tokens]
        spread = dot(projected, taken[...])
        for here in blocks(width, 32):
            pre = xw[here, tokens] + spread[here]
            gate = sigmoid(pre)
            hidden = pre * gate
            factor[here] = gate + hidden * (1.0 - gate)
            high, low = split(hidden)
            deep[here], deep[shift(here, width)], deep[shift(here, 2 * width)] = high, high, low
        product = dot(grams[...], deep[...])
        for here in blocks(width, 32):
            de = (product[here] - tw[here, tokens]) * factor[here]
            xw[here, tokens] = de
            parts[here], parts[shift(here, width)] = split(de)
        dslot = dslot + dot(parts[...], pick[:, tokens], NT)
    for copy in stores:
        copy.start()

    dcontext = pair_product(projects, dslot[:width] + dslot[width:], NN)
    grad = pair_product(coarses, dcontext * slope, NN).T
    shape = (patches * 16, LANES - pixels)
    slot = lax.broadcasted_iota(jnp.int32, shape, 0) % 16
    top = row_value(crops_ref, 1, patches, shape, 0, 16)
    left = row_value(crops_ref, 2, patches, shape, 0, 16)
    number = ((top + slot // 4) * SIDE + left + slot % 4).astype(F32)
    send_ref[...] = jnp.zeros_like(send_ref)
    for j in range(patches):
        start = pl.ds(pl.multiple_of(crops_ref[0, j] * 16, 16), 16)
        send_ref[start, :pixels] = grad[j * 16 : j * 16 + 16, :]
        send_ref[start, pixels:] = number[j * 16 : j * 16 + 16, :]
    for copy in stores:
        copy.wait()


def scatter_kernel(message_ref, done_ref, mine_ref, other_ref, total):
    del done_ref
    pixels = mine_ref.shape[2]
    message = message_ref[...]
    number = lax.broadcasted_iota(jnp.int32, (message.shape[0], SIDE * SIDE), 1).astype(F32)
    pick = jnp.where(message[:, pixels : pixels + 1] == number, 1.0, 0.0).astype(BF16)
    high, low = split(message[:, :pixels])
    total[...] = dot(pick, low, TN) + dot(pick, high, TN)
    half = mine_ref.shape[1]
    side = lax.axis_index("lvl")
    mine_ref[0] = total[pl.ds(pl.multiple_of(side * half, half), half), :]
    other_ref[0] = total[pl.ds(pl.multiple_of((1 - side) * half, half), half), :]


def last_kernel(chunks, de_hbm, pair_hbm, *refs):
    out_hbm, de, out, deep, cat, in_sems, out_sems, sems = refs
    width = de.shape[0]
    fetches = [
        pltpu.make_async_copy(pair_hbm, deep.at[: 2 * width], sems.at[0]),
        pltpu.make_async_copy(pair_hbm.at[:width], deep.at[2 * width :], sems.at[1]),
    ]
    for copy in fetches:
        copy.start()
    loads = [
        pltpu.make_async_copy(de_hbm.at[:, here], de.at[:, here], in_sems.at[i])
        for i, here in enumerate(chunks)
    ]
    stores = [
        pltpu.make_async_copy(out.at[here], out_hbm.at[here], out_sems.at[i])
        for i, here in enumerate(chunks)
    ]

    def prepare(i):
        loads[i].wait()
        for here in blocks(width, 32):
            high, low = split(de[here, chunks[i]])
            cat[i % 2, here], cat[i % 2, shift(here, width)], cat[i % 2, shift(here, 2 * width)] = high, high, low

    for copy in loads:
        copy.start()
    prepare(0)
    for copy in fetches:
        copy.wait()
    for i, here in enumerate(chunks):
        out[here, :] = dot(cat[i % 2], deep[...], TN)
        if i + 1 < len(chunks):
            prepare(i + 1)
        stores[i].start()
    for copy in stores:
        copy.wait()


def chunk_rows(first, last):
    return [slice(start, start + ROWS) for start in range(first, last, ROWS)]


def fixed(*values):
    return [pltpu.with_memory_space_constraint(value, pltpu.HBM) for value in values]


def near(*values):
    return [pltpu.with_memory_space_constraint(value, pltpu.VMEM) for value in values]


def stack(blocks, before):
    shape = (len(blocks) * blocks[0].shape[0],) + blocks[0].shape[1:]
    return call(
        stack_kernel,
        "stack",
        1000,
        jax.ShapeDtypeStruct(shape, F32),
        limit=ROOM,
        in_specs=[VMEM] * len(blocks) + [HBM],
        out_specs=VMEM,
    )(*blocks, *fixed(before))


def body(coarse_input, coarse_weight, fine_input, fine_target, crops, in_weight, context_weight, out_weight):
    patch = ("far", "y", "core")
    peers = lax.axis_size(patch)
    far = peers // 4
    patches, tokens, values = fine_input.shape
    width = in_weight.shape[1]
    pixels = coarse_weight.shape[0]
    half = coarse_input.shape[1]
    count = patches * tokens
    swap = [(0, 1), (1, 0)]

    column = [coarse_input]
    for k in range(1, far):
        column.append(lax.ppermute(coarse_input, "far", [(p, (p + k) % far) for p in range(far)]))

    chunks = chunk_rows(0, count)
    pair_shape = (2 * width, values)
    x, t = fine_input.reshape(count, values), fine_target.reshape(count, values)
    xw, pair, rows, next_pair = call(
        functools.partial(input_kernel, chunks),
        "input",
        6 * count * values * width,
        (
            pltpu.HBM((width, count), F32),
            pltpu.HBM(pair_shape, BF16),
            pltpu.VMEM((ROWS, values), F32),
            pltpu.VMEM(pair_shape, BF16),
        ),
        in_specs=[HBM] * 4,
        out_specs=(HBM, HBM, VMEM, VMEM),
        scratch_shapes=[
            pltpu.VMEM((count, values), F32),
            pltpu.VMEM((width, count), F32),
            pltpu.VMEM((width, values), F32),
            pltpu.VMEM((width, values), F32),
            pltpu.VMEM(pair_shape, BF16),
            pltpu.VMEM((ROWS, values), BF16),
            pltpu.VMEM((ROWS, values), BF16),
            pltpu.SemaphoreType.DMA((len(chunks),)),
            pltpu.SemaphoreType.DMA((len(chunks),)),
            pltpu.SemaphoreType.DMA((4,)),
        ],
    )(*fixed(x, in_weight.T, t, out_weight))
    column = stack(column, xw)
    own = [column]
    for flip in range(1, 4):
        own.append(lax.ppermute(column, ("lvl", "y"), [(p, p ^ flip) for p in range(4)]))
    tw = call(
        functools.partial(target_kernel, chunks),
        "target",
        6 * count * values * width,
        pltpu.HBM((width, count), F32),
        limit=ROOM,
        in_specs=[HBM, VMEM, VMEM],
        out_specs=HBM,
        scratch_shapes=[
            pltpu.VMEM((count, values), F32),
            pltpu.VMEM((width, count), F32),
            pltpu.VMEM((ROWS, values), BF16),
            pltpu.VMEM((ROWS, values), BF16),
            pltpu.SemaphoreType.DMA((len(chunks),)),
            pltpu.SemaphoreType.DMA((len(chunks),)),
        ],
    )(*fixed(t), *near(rows, next_pair))
    own = stack(own, tw).reshape(-1, pixels)
    other = lax.ppermute(own, "core", swap)
    crops = crops.T
    prepared = call(
        functools.partial(prepare_kernel, patches),
        "prepare",
        8 * values * width * width,
        (
            pltpu.VMEM((width, 3 * width), BF16),
            pltpu.VMEM((2 * width, width), BF16),
            pltpu.VMEM((2 * pixels, width), BF16),
            pltpu.VMEM((patches * 16, count), BF16),
        ),
        limit=ROOM,
        in_specs=[VMEM, VMEM, VMEM, SMEM, HBM],
        out_specs=(VMEM,) * 4,
    )(*near(next_pair), coarse_weight, context_weight, crops, own)

    shape = (peers * 16, LANES)
    de, back = call(
        functools.partial(middle_kernel, patches, peers),
        "middle",
        6 * count * width * width,
        (pltpu.HBM((width, count), F32), jax.ShapeDtypeStruct(shape, F32)),
        limit=ROOM,
        in_specs=[SMEM] + [VMEM] * 6 + [HBM] * 2,
        out_specs=(HBM, VMEM),
        scratch_shapes=[
            pltpu.VMEM((width, count), F32),
            pltpu.VMEM((width, count), F32),
            pltpu.VMEM((patches * 16, pixels), F32),
            pltpu.VMEM((2 * patches * 16, ROWS), BF16),
            pltpu.VMEM((width, ROWS), F32),
            pltpu.VMEM((3 * width, ROWS), BF16),
            pltpu.VMEM((2 * width, ROWS), BF16),
            pltpu.SemaphoreType.DMA((2,)),
            pltpu.SemaphoreType.DMA((len(chunks),)),
        ],
    )(crops, own, other, *near(*prepared), *fixed(xw, tw))
    returned = lax.all_to_all(back, patch, 0, 0, tiled=True)

    fine_grad = call(
        functools.partial(last_kernel, chunks),
        "last",
        6 * count * values * width,
        pltpu.HBM((count, values), F32),
        in_specs=[HBM, HBM],
        out_specs=HBM,
        scratch_shapes=[
            pltpu.VMEM((width, count), F32),
            pltpu.VMEM((count, values), F32),
            pltpu.VMEM((3 * width, values), BF16),
            pltpu.VMEM((2, 3 * width, ROWS), BF16),
            pltpu.SemaphoreType.DMA((len(chunks),)),
            pltpu.SemaphoreType.DMA((len(chunks),)),
            pltpu.SemaphoreType.DMA((2,)),
        ],
    )(*fixed(de, pair))
    part = (1, half, pixels)
    mine, theirs = call(
        scatter_kernel,
        "scatter",
        10000,
        (jax.ShapeDtypeStruct(part, F32), jax.ShapeDtypeStruct(part, F32)),
        limit=ROOM,
        in_specs=[VMEM, HBM],
        out_specs=(VMEM, VMEM),
        scratch_shapes=[pltpu.VMEM((SIDE * SIDE, pixels), F32)],
    )(returned, *fixed(fine_grad))
    coarse_grad = mine + lax.ppermute(theirs, "lvl", swap)
    return (coarse_grad, fine_grad.reshape(fine_input.shape))


def solution(mesh):
    sides, peers = mesh.shape["lvl"], mesh.shape["patch"]
    fine = jax.sharding.Mesh(mesh.devices.reshape(sides, peers // 4, 2, 2), ("lvl", "far", "y", "core"))
    patch = ("far", "y", "core")
    both = ("lvl",) + patch
    in_specs = (
        P(patch, "lvl", None),
        P(),
        P(both, None, None),
        P(both, None, None),
        P(both, None),
        P(),
        P(),
        P(),
    )
    out_specs = (P(patch, "lvl", None), P(both, None, None))
    return jax.shard_map(body, mesh=fine, in_specs=in_specs, out_specs=out_specs, check_vma=False)
```

```python
import functools
import math

import jax
import jax.numpy as jnp
from jax import lax
from jax.experimental import pallas as pl
from jax.experimental.pallas import tpu as pltpu
from jax.sharding import PartitionSpec as P

F32 = jnp.float32
BF16 = jnp.bfloat16
NN = (((1,), (0,)), ((), ()))
NT = (((1,), (1,)), ((), ()))
TN = (((0,), (0,)), ((), ()))
ROWS = 512
SIDE = 8
AHEAD = 2
LANES = 256
LIMIT = 60 * 1024 * 1024
ROOM = 40 * 1024 * 1024
SMEM = pl.BlockSpec(memory_space=pltpu.SMEM)
VMEM = pl.BlockSpec(memory_space=pltpu.VMEM)
HBM = pl.BlockSpec(memory_space=pltpu.HBM)


def split(value):
    high = value.astype(BF16)
    low = (value - high.astype(F32)).astype(BF16)
    return high, low


def dot(left, right, dims=NN):
    return lax.dot_general(left, right, dims, preferred_element_type=F32)


def dot3(left, right, dims=NN):
    return (
        dot(left[0], right[1], dims) + dot(left[1], right[0], dims) + dot(left[0], right[0], dims)
    )


def side_by_side(value):
    high, low = split(value)
    return jnp.concatenate([high, low, high], axis=1)


def sigmoid(value):
    return 0.5 * jnp.tanh(0.5 * value) + 0.5


def call(kernel, name, flops, out_shape, limit=LIMIT, **kwargs):
    moved = 8 * sum(math.prod(s.shape) for s in jax.tree.leaves(out_shape))
    return pl.pallas_call(
        kernel,
        out_shape=out_shape,
        name=name,
        cost_estimate=pl.CostEstimate(flops=flops, bytes_accessed=moved, transcendentals=0),
        compiler_params=pltpu.CompilerParams(vmem_limit_bytes=limit),
        **kwargs,
    )


def stream(loads, stores, product):
    for copy in loads[:AHEAD]:
        copy.start()
    for i, store in enumerate(stores):
        loads[i].wait()
        if i + AHEAD < len(loads):
            loads[i + AHEAD].start()
        product(i)
        store.start()
    for copy in stores:
        copy.wait()


def blocks(rows, size):
    return [slice(start, start + size) for start in range(0, rows, size)]


def shift(here, by):
    return slice(here.start + by, here.stop + by)


def pair_product(pair, value, dims):
    rows = pair.shape[0] // 2
    high, low = split(value)
    both = dot(pair[...], high, dims)
    return both[:rows] + (both[rows:] + dot(pair[:rows], low, dims))


def wide_product(pair, value, high, low, out, tokens):
    width = pair.shape[0] // 2
    for here in blocks(high.shape[0], 16):
        high[here], low[here] = split(value[here])
    both = dot(pair[...], high[...], NT)
    rest = dot(pair[:width], low[...], NT)
    for here in blocks(width, 32):
        out[here, tokens] = both[here] + (both[shift(here, width)] + rest[here])


def input_kernel(
    chunks,
    x_hbm,
    weight_hbm,
    t_hbm,
    next_weight_hbm,
    crops_hbm,
    out_hbm,
    pair_hbm,
    next_rows,
    next_pair,
    crops,
    x,
    out,
    weight,
    next_weight,
    pair,
    high,
    low,
    in_sems,
    out_sems,
    sems,
):
    width = weight.shape[0]
    fetch = pltpu.make_async_copy(weight_hbm, weight, sems.at[0])
    keep = pltpu.make_async_copy(pair, pair_hbm, sems.at[1])
    fetch_next = pltpu.make_async_copy(next_weight_hbm, next_weight, sems.at[2])
    fetch_rows = pltpu.make_async_copy(t_hbm.at[: next_rows.shape[0]], next_rows, sems.at[3])
    fetch_crops = pltpu.make_async_copy(crops_hbm, crops, sems.at[4])
    fetch.start()
    loads = [
        pltpu.make_async_copy(x_hbm.at[here], x.at[here], in_sems.at[i]) for i, here in enumerate(chunks)
    ]
    stores = [
        pltpu.make_async_copy(out.at[:, here], out_hbm.at[:, here], out_sems.at[i])
        for i, here in enumerate(chunks)
    ]

    def product(i):
        if i == 0:
            fetch.wait()
            pair[:width], pair[width:] = split(weight[...])
            keep.start()
            fetch_next.start()
        if i == 1:
            fetch_rows.start()
            fetch_crops.start()
        if i == len(chunks) - 1:
            fetch_next.wait()
            next_pair[:width], next_pair[width:] = split(next_weight[...])
        wide_product(pair, x.at[chunks[i]], high, low, out, chunks[i])

    stream(loads, stores, product)
    keep.wait()
    fetch_rows.wait()
    fetch_crops.wait()


def target_kernel(
    chunks,
    t_hbm,
    cwgt_hbm,
    xwgt_hbm,
    rows,
    pair,
    out_hbm,
    coarses,
    projects,
    t,
    out,
    high,
    low,
    cwgt,
    xwgt,
    in_sems,
    out_sems,
    sems,
):
    fetches = [
        pltpu.make_async_copy(cwgt_hbm, cwgt, sems.at[0]),
        pltpu.make_async_copy(xwgt_hbm, xwgt, sems.at[1]),
    ]
    loads = [
        pltpu.make_async_copy(t_hbm.at[here], t.at[here], in_sems.at[i])
        for i, here in enumerate(chunks[1:])
    ]
    stores = [
        pltpu.make_async_copy(out.at[:, here], out_hbm.at[:, here], out_sems.at[i])
        for i, here in enumerate(chunks)
    ]
    for copy in loads[:AHEAD] + fetches:
        copy.start()
    wide_product(pair, rows, high, low, out, chunks[0])
    stores[0].start()
    for i, copy in enumerate(loads):
        copy.wait()
        if i + AHEAD < len(loads):
            loads[i + AHEAD].start()
        if i == 0:
            for fetch in fetches:
                fetch.wait()
            coarses[...] = jnp.concatenate(split(cwgt[...]), axis=0)
            projects[...] = jnp.concatenate(split(xwgt[...]), axis=0)
        here = chunks[i + 1]
        wide_product(pair, t.at[here], high, low, out, here)
        stores[i + 1].start()
    for copy in stores:
        copy.wait()


def prepare_kernel(patches, pair, crops_ref, before_ref, grams, pick):
    del before_ref
    width = grams.shape[0]
    high, low = pair[:width], pair[width:]
    grams[...] = side_by_side(dot3((high, low), (high, low), NT) + dot(low, low, NT))
    pick[...] = chosen(crops_ref, patches, pick.shape[1] // patches)


def stack_kernel(*refs):
    *block_refs, _, out_ref = refs
    size = block_refs[0].shape[0]
    for k, ref in enumerate(block_refs):
        out_ref[k * size : (k + 1) * size] = ref[...]


def row_value(crops_ref, column, patches, shape, axis, each):
    index = lax.broadcasted_iota(jnp.int32, shape, axis) // each
    found = jnp.zeros(shape, jnp.int32)
    for j in range(patches):
        found = jnp.where(index == j, crops_ref[column, j], found)
    return found


def chosen(crops_ref, patches, tokens):
    scale = row_value(crops_ref, 3, patches, (1, patches * tokens), 1, tokens)
    token = lax.broadcasted_iota(jnp.int32, (1, patches * tokens), 1)
    row, column = (token % tokens) // 16, token % 16
    wanted = token // tokens * 16 + (row * scale // 8) * 4 + column * scale // 8
    slot = lax.broadcasted_iota(jnp.int32, (patches * 16, patches * tokens), 0)
    return jnp.where(slot == wanted, 1.0, 0.0).astype(BF16)


def context_kernel(
    patches,
    peers,
    crops_ref,
    own_ref,
    other_ref,
    coarses,
    projects,
    xw_hbm,
    projected_ref,
    slope_ref,
    first_ref,
    rows,
    sem,
):
    fetch = pltpu.make_async_copy(xw_hbm.at[:, : first_ref.shape[1]], first_ref, sem)
    fetch.start()
    pixels = coarses.shape[0] // 2
    width = projects.shape[1]
    far = peers // 4
    me, side = lax.axis_index(("far", "y", "core")), lax.axis_index("lvl")
    for j in range(patches):
        frame, top, left = crops_ref[0, j], crops_ref[1, j], crops_ref[2, j]
        near = lax.bitwise_xor(frame % 4, me % 4)
        k = (me // 4 - frame // 4 + far) % far
        for a in range(4):
            row = jnp.minimum(top + a, SIDE - 1)
            shard = (lax.bitwise_xor(row // 4, side) * 2 + near // 2) * far + k
            start = pl.ds(pl.multiple_of((shard * 4 + row % 4) * SIDE, SIDE), SIDE)
            line = jnp.where(near % 2 == 0, own_ref[start, :], other_ref[start, :])
            rows[j * 16 + a * 4 : j * 16 + a * 4 + 4, :] = pltpu.roll(line, SIDE - left, 0)[:4, :]
    pre = dot3(split(rows[...]), (coarses[:pixels], coarses[pixels:]))
    gate = sigmoid(pre)
    slope_ref[...] = gate * (1.0 + pre * (1.0 - gate))
    projected = dot3(split(pre * gate), (projects[:width], projects[width:])).T
    projected_ref[...] = jnp.concatenate(split(projected), axis=1)
    fetch.wait()


def middle_kernel(
    chunks,
    projected,
    grams,
    pick,
    first,
    xw_hbm,
    tw_hbm,
    pair_hbm,
    de_hbm,
    de_ref,
    deep_ref,
    dslot_ref,
    xw,
    tw,
    taken,
    factor,
    deep,
    parts,
    xw_sems,
    tw_sems,
    out_sems,
    sems,
):
    width = grams.shape[0]
    slots = pick.shape[0]
    each = slots // len(chunks)
    tw_loads = [
        pltpu.make_async_copy(tw_hbm.at[:, here], tw.at[:, here], tw_sems.at[i]) for i, here in enumerate(chunks)
    ]
    xw_loads = [
        pltpu.make_async_copy(xw_hbm.at[:, here], xw.at[:, here], xw_sems.at[i])
        for i, here in enumerate(chunks[1:])
    ]
    stores = [
        pltpu.make_async_copy(xw.at[:, here], de_hbm.at[:, here], out_sems.at[i])
        for i, here in enumerate(chunks[:-1])
    ]
    fetches = [
        pltpu.make_async_copy(pair_hbm, deep_ref.at[: 2 * width], sems.at[0]),
        pltpu.make_async_copy(pair_hbm.at[:width], deep_ref.at[2 * width :], sems.at[1]),
    ]
    tw_loads[0].start()
    for pair in zip(xw_loads, tw_loads[1:]):
        for copy in pair:
            copy.start()
    for copy in fetches:
        copy.start()
    for i, tokens in enumerate(chunks):
        if i > 0:
            xw_loads[i - 1].wait()
            tw_loads[i].wait()
        source = first if i == 0 else xw.at[:, tokens]
        target = de_ref if i == len(chunks) - 1 else xw.at[:, tokens]
        taken[:slots], taken[slots:] = pick[:, tokens], pick[:, tokens]
        spread = dot(projected[...], taken[...])
        for here in blocks(width, 32):
            pre = source[here] + spread[here]
            gate = sigmoid(pre)
            hidden = pre * gate
            factor[here] = gate + hidden * (1.0 - gate)
            high, low = split(hidden)
            deep[here], deep[shift(here, width)], deep[shift(here, 2 * width)] = high, high, low
        product = dot(grams[...], deep[...])
        if i == 0:
            tw_loads[0].wait()
        for here in blocks(width, 32):
            de = (product[here] - tw[here, tokens]) * factor[here]
            target[here] = de
            parts[here], parts[shift(here, width)] = split(de)
        mine = slice(i * each, (i + 1) * each)
        dslot_ref[mine] = dot(pick[mine, tokens], parts[...], NT)
        if i < len(stores):
            stores[i].start()
    for copy in stores + fetches:
        copy.wait()


def closing_kernel(patches, crops_ref, dslot_ref, slope_ref, coarses, projects, send_ref):
    pixels = coarses.shape[0] // 2
    width = projects.shape[1]
    dslot = dslot_ref[:, :width] + dslot_ref[:, width:]
    dcontext = dot3(split(dslot), (projects[:width], projects[width:]), NT)
    grad = dot3(split(dcontext * slope_ref[...]), (coarses[:pixels], coarses[pixels:]), NT)
    shape = (patches * 16, LANES - pixels)
    slot = lax.broadcasted_iota(jnp.int32, shape, 0) % 16
    top = row_value(crops_ref, 1, patches, shape, 0, 16)
    left = row_value(crops_ref, 2, patches, shape, 0, 16)
    number = ((top + slot // 4) * SIDE + left + slot % 4).astype(F32)
    send_ref[...] = jnp.zeros_like(send_ref)
    for j in range(patches):
        start = pl.ds(pl.multiple_of(crops_ref[0, j] * 16, 16), 16)
        send_ref[start, :pixels] = grad[j * 16 : j * 16 + 16, :]
        send_ref[start, pixels:] = number[j * 16 : j * 16 + 16, :]


def scatter_kernel(message_ref, done_ref, mine_ref, other_ref, total):
    del done_ref
    pixels = mine_ref.shape[2]
    message = message_ref[...]
    number = lax.broadcasted_iota(jnp.int32, (message.shape[0], SIDE * SIDE), 1).astype(F32)
    pick = jnp.where(message[:, pixels : pixels + 1] == number, 1.0, 0.0).astype(BF16)
    high, low = split(message[:, :pixels])
    total[...] = dot(pick, low, TN) + dot(pick, high, TN)
    half = mine_ref.shape[1]
    side = lax.axis_index("lvl")
    mine_ref[0] = total[pl.ds(pl.multiple_of(side * half, half), half), :]
    other_ref[0] = total[pl.ds(pl.multiple_of((1 - side) * half, half), half), :]


def last_kernel(chunks, de_hbm, first, deep, out_hbm, de, out, cat, in_sems, out_sems):
    width = de.shape[0]
    order = chunks[-1:] + chunks[:-1]
    loads = [
        pltpu.make_async_copy(de_hbm.at[:, here], de.at[:, here], in_sems.at[i])
        for i, here in enumerate(order[1:])
    ]
    stores = [
        pltpu.make_async_copy(out.at[here], out_hbm.at[here], out_sems.at[i]) for i, here in enumerate(order)
    ]

    def prepare(i, source):
        for here in blocks(width, 32):
            high, low = split(source[here])
            cat[i % 2, here], cat[i % 2, shift(here, width)], cat[i % 2, shift(here, 2 * width)] = high, high, low

    for copy in loads:
        copy.start()
    prepare(0, first)
    for i, here in enumerate(order):
        if i < len(loads):
            loads[i].wait()
        out[here, :] = dot(cat[i % 2], deep[...], TN)
        if i < len(loads):
            prepare(i + 1, de.at[:, order[i + 1]])
        stores[i].start()
    for copy in stores:
        copy.wait()


def chunk_rows(first, last):
    return [slice(start, start + ROWS) for start in range(first, last, ROWS)]


def fixed(*values):
    return [pltpu.with_memory_space_constraint(value, pltpu.HBM) for value in values]


def near(*values):
    return [pltpu.with_memory_space_constraint(value, pltpu.VMEM) for value in values]


def stack(blocks, before):
    shape = (len(blocks) * blocks[0].shape[0],) + blocks[0].shape[1:]
    return call(
        stack_kernel,
        "stack",
        1000,
        jax.ShapeDtypeStruct(shape, F32),
        limit=ROOM,
        in_specs=[VMEM] * len(blocks) + [HBM],
        out_specs=VMEM,
    )(*blocks, *fixed(before))


def body(coarse_input, coarse_weight, fine_input, fine_target, crops, in_weight, context_weight, out_weight):
    patch = ("far", "y", "core")
    peers = lax.axis_size(patch)
    far = peers // 4
    patches, tokens, values = fine_input.shape
    width = in_weight.shape[1]
    pixels = coarse_weight.shape[0]
    half = coarse_input.shape[1]
    count = patches * tokens
    swap = [(0, 1), (1, 0)]

    column = [coarse_input]
    for k in range(1, far):
        column.append(lax.ppermute(coarse_input, "far", [(p, (p + k) % far) for p in range(far)]))

    chunks = chunk_rows(0, count)
    pair_shape = (2 * width, values)
    x, t = fine_input.reshape(count, values), fine_target.reshape(count, values)
    xw, pair, rows, next_pair, crops = call(
        functools.partial(input_kernel, chunks),
        "input",
        6 * count * values * width,
        (
            pltpu.HBM((width, count), F32),
            pltpu.HBM(pair_shape, BF16),
            pltpu.VMEM((ROWS, values), F32),
            pltpu.VMEM(pair_shape, BF16),
            pltpu.VMEM((4, patches), jnp.int32),
        ),
        in_specs=[HBM] * 5,
        out_specs=(HBM, HBM, VMEM, VMEM, VMEM),
        scratch_shapes=[
            pltpu.VMEM((count, values), F32),
            pltpu.VMEM((width, count), F32),
            pltpu.VMEM((width, values), F32),
            pltpu.VMEM((width, values), F32),
            pltpu.VMEM(pair_shape, BF16),
            pltpu.VMEM((ROWS, values), BF16),
            pltpu.VMEM((ROWS, values), BF16),
            pltpu.SemaphoreType.DMA((len(chunks),)),
            pltpu.SemaphoreType.DMA((len(chunks),)),
            pltpu.SemaphoreType.DMA((5,)),
        ],
    )(*fixed(x, in_weight.T, t, out_weight, crops.T))
    column = stack(column, xw)
    own = [column]
    for flip in range(1, 4):
        own.append(lax.ppermute(column, ("lvl", "y"), [(p, p ^ flip) for p in range(4)]))
    tw, coarses, projects = call(
        functools.partial(target_kernel, chunks),
        "target",
        6 * count * values * width,
        (
            pltpu.HBM((width, count), F32),
            pltpu.VMEM((2 * pixels, width), BF16),
            pltpu.VMEM((2 * width, width), BF16),
        ),
        limit=ROOM,
        in_specs=[HBM] * 3 + [VMEM] * 2,
        out_specs=(HBM, VMEM, VMEM),
        scratch_shapes=[
            pltpu.VMEM((count, values), F32),
            pltpu.VMEM((width, count), F32),
            pltpu.VMEM((ROWS, values), BF16),
            pltpu.VMEM((ROWS, values), BF16),
            pltpu.VMEM((pixels, width), F32),
            pltpu.VMEM((width, width), F32),
            pltpu.SemaphoreType.DMA((len(chunks),)),
            pltpu.SemaphoreType.DMA((len(chunks),)),
            pltpu.SemaphoreType.DMA((2,)),
        ],
    )(*fixed(t, coarse_weight, context_weight), *near(rows, next_pair))
    own = stack(own, tw).reshape(-1, pixels)
    other = lax.ppermute(own, "core", swap)
    (crops,) = near(crops)
    grams, pick = call(
        functools.partial(prepare_kernel, patches),
        "prepare",
        8 * values * width * width,
        (pltpu.VMEM((width, 3 * width), BF16), pltpu.VMEM((patches * 16, count), BF16)),
        limit=ROOM,
        in_specs=[VMEM, SMEM, HBM],
        out_specs=(VMEM, VMEM),
    )(*near(next_pair), crops, own)

    projected, slope, first = call(
        functools.partial(context_kernel, patches, peers),
        "context",
        6 * patches * 16 * width * width,
        (
            pltpu.VMEM((width, 2 * patches * 16), BF16),
            pltpu.VMEM((patches * 16, width), F32),
            pltpu.VMEM((width, ROWS), F32),
        ),
        limit=ROOM,
        in_specs=[SMEM] + [VMEM] * 4 + [HBM],
        out_specs=(VMEM,) * 3,
        scratch_shapes=[pltpu.VMEM((patches * 16, pixels), F32), pltpu.SemaphoreType.DMA],
    )(crops, own, other, *near(coarses, projects), *fixed(xw))
    de, last_de, deep, dslot = call(
        functools.partial(middle_kernel, chunks),
        "middle",
        6 * count * width * width,
        (
            pltpu.HBM((width, count), F32),
            pltpu.VMEM((width, ROWS), F32),
            pltpu.VMEM((3 * width, values), BF16),
            pltpu.VMEM((patches * 16, 2 * width), F32),
        ),
        limit=ROOM,
        in_specs=[VMEM] * 4 + [HBM] * 3,
        out_specs=(HBM,) + (VMEM,) * 3,
        scratch_shapes=[
            pltpu.VMEM((width, count), F32),
            pltpu.VMEM((width, count), F32),
            pltpu.VMEM((2 * patches * 16, ROWS), BF16),
            pltpu.VMEM((width, ROWS), F32),
            pltpu.VMEM((3 * width, ROWS), BF16),
            pltpu.VMEM((2 * width, ROWS), BF16),
            pltpu.SemaphoreType.DMA((len(chunks),)),
            pltpu.SemaphoreType.DMA((len(chunks),)),
            pltpu.SemaphoreType.DMA((len(chunks),)),
            pltpu.SemaphoreType.DMA((2,)),
        ],
    )(*near(projected, grams, pick, first), *fixed(xw, tw, pair))
    back = call(
        functools.partial(closing_kernel, patches),
        "closing",
        6 * patches * 16 * width * width,
        jax.ShapeDtypeStruct((peers * 16, LANES), F32),
        limit=ROOM,
        in_specs=[SMEM] + [VMEM] * 4,
        out_specs=VMEM,
    )(crops, *near(dslot, slope, coarses, projects))
    returned = lax.all_to_all(back, patch, 0, 0, tiled=True)

    fine_grad = call(
        functools.partial(last_kernel, chunks),
        "last",
        6 * count * values * width,
        pltpu.HBM((count, values), F32),
        limit=ROOM,
        in_specs=[HBM, VMEM, VMEM],
        out_specs=HBM,
        scratch_shapes=[
            pltpu.VMEM((width, count), F32),
            pltpu.VMEM((count, values), F32),
            pltpu.VMEM((2, 3 * width, ROWS), BF16),
            pltpu.SemaphoreType.DMA((len(chunks),)),
            pltpu.SemaphoreType.DMA((len(chunks),)),
        ],
    )(*fixed(de), *near(last_de, deep))
    part = (1, half, pixels)
    mine, theirs = call(
        scatter_kernel,
        "scatter",
        10000,
        (jax.ShapeDtypeStruct(part, F32), jax.ShapeDtypeStruct(part, F32)),
        limit=ROOM,
        in_specs=[VMEM, HBM],
        out_specs=(VMEM, VMEM),
        scratch_shapes=[pltpu.VMEM((SIDE * SIDE, pixels), F32)],
    )(returned, *fixed(fine_grad))
    coarse_grad = mine + lax.ppermute(theirs, "lvl", swap)
    return (coarse_grad, fine_grad.reshape(fine_input.shape))


def solution(mesh):
    sides, peers = mesh.shape["lvl"], mesh.shape["patch"]
    fine = jax.sharding.Mesh(mesh.devices.reshape(sides, peers // 4, 2, 2), ("lvl", "far", "y", "core"))
    patch = ("far", "y", "core")
    both = ("lvl",) + patch
    in_specs = (
        P(patch, "lvl", None),
        P(),
        P(both, None, None),
        P(both, None, None),
        P(both, None),
        P(),
        P(),
        P(),
    )
    out_specs = (P(patch, "lvl", None), P(both, None, None))
    return jax.shard_map(body, mesh=fine, in_specs=in_specs, out_specs=out_specs, check_vma=False)
```

```python
import functools
import math

import jax
import jax.numpy as jnp
from jax import lax
from jax.experimental import pallas as pl
from jax.experimental.pallas import tpu as pltpu
from jax.sharding import PartitionSpec as P

F32 = jnp.float32
BF16 = jnp.bfloat16
NN = (((1,), (0,)), ((), ()))
NT = (((1,), (1,)), ((), ()))
TN = (((0,), (0,)), ((), ()))
ROWS = 512
SIDE = 8
AHEAD = 2
LANES = 256
LIMIT = 60 * 1024 * 1024
ROOM = 40 * 1024 * 1024
SMEM = pl.BlockSpec(memory_space=pltpu.SMEM)
VMEM = pl.BlockSpec(memory_space=pltpu.VMEM)
HBM = pl.BlockSpec(memory_space=pltpu.HBM)


def split(value):
    high = value.astype(BF16)
    low = (value - high.astype(F32)).astype(BF16)
    return high, low


def dot(left, right, dims=NN):
    return lax.dot_general(left, right, dims, preferred_element_type=F32)


def dot3(left, right, dims=NN):
    return (
        dot(left[0], right[1], dims) + dot(left[1], right[0], dims) + dot(left[0], right[0], dims)
    )


def side_by_side(value):
    high, low = split(value)
    return jnp.concatenate([high, low, high], axis=1)


def sigmoid(value):
    return 0.5 * jnp.tanh(0.5 * value) + 0.5


def call(kernel, name, flops, out_shape, limit=LIMIT, **kwargs):
    moved = 8 * sum(math.prod(s.shape) for s in jax.tree.leaves(out_shape))
    return pl.pallas_call(
        kernel,
        out_shape=out_shape,
        name=name,
        cost_estimate=pl.CostEstimate(flops=flops, bytes_accessed=moved, transcendentals=0),
        compiler_params=pltpu.CompilerParams(vmem_limit_bytes=limit),
        **kwargs,
    )


def stream(loads, stores, product):
    for copy in loads[:AHEAD]:
        copy.start()
    for i, store in enumerate(stores):
        loads[i].wait()
        if i + AHEAD < len(loads):
            loads[i + AHEAD].start()
        product(i)
        store.start()
    for copy in stores:
        copy.wait()


def blocks(rows, size):
    return [slice(start, start + size) for start in range(0, rows, size)]


def shift(here, by):
    return slice(here.start + by, here.stop + by)


def pair_product(pair, value, dims):
    rows = pair.shape[0] // 2
    high, low = split(value)
    both = dot(pair[...], high, dims)
    return both[:rows] + (both[rows:] + dot(pair[:rows], low, dims))


def wide_product(pair, value, high, low, out, tokens):
    width = pair.shape[0] // 2
    for here in blocks(high.shape[0], 16):
        high[here], low[here] = split(value[here])
    both = dot(pair[...], high[...], NT)
    rest = dot(pair[:width], low[...], NT)
    for here in blocks(width, 32):
        out[here, tokens] = both[here] + (both[shift(here, width)] + rest[here])


def input_kernel(
    chunks,
    x_hbm,
    weight_hbm,
    t_hbm,
    next_weight_hbm,
    crops_hbm,
    out_hbm,
    pair_hbm,
    next_rows,
    next_pair,
    crops,
    x,
    out,
    weight,
    next_weight,
    pair,
    high,
    low,
    in_sems,
    out_sems,
    sems,
):
    width = weight.shape[0]
    fetch = pltpu.make_async_copy(weight_hbm, weight, sems.at[0])
    keep = pltpu.make_async_copy(pair, pair_hbm, sems.at[1])
    fetch_next = pltpu.make_async_copy(next_weight_hbm, next_weight, sems.at[2])
    fetch_rows = pltpu.make_async_copy(t_hbm.at[: next_rows.shape[0]], next_rows, sems.at[3])
    fetch_crops = pltpu.make_async_copy(crops_hbm, crops, sems.at[4])
    fetch.start()
    loads = [
        pltpu.make_async_copy(x_hbm.at[here], x.at[here], in_sems.at[i]) for i, here in enumerate(chunks)
    ]
    stores = [
        pltpu.make_async_copy(out.at[:, here], out_hbm.at[:, here], out_sems.at[i])
        for i, here in enumerate(chunks)
    ]

    def product(i):
        if i == 0:
            fetch.wait()
            pair[:width], pair[width:] = split(weight[...])
            keep.start()
            fetch_next.start()
        if i == 1:
            fetch_rows.start()
            fetch_crops.start()
        if i == len(chunks) - 1:
            fetch_next.wait()
            next_pair[:width], next_pair[width:] = split(next_weight[...])
        wide_product(pair, x.at[chunks[i]], high, low, out, chunks[i])

    stream(loads, stores, product)
    keep.wait()
    fetch_rows.wait()
    fetch_crops.wait()


def target_kernel(
    chunks,
    t_hbm,
    cwgt_hbm,
    xwgt_hbm,
    rows,
    pair,
    out_hbm,
    coarses,
    projects,
    t,
    out,
    high,
    low,
    cwgt,
    xwgt,
    in_sems,
    out_sems,
    sems,
):
    fetches = [
        pltpu.make_async_copy(cwgt_hbm, cwgt, sems.at[0]),
        pltpu.make_async_copy(xwgt_hbm, xwgt, sems.at[1]),
    ]
    loads = [
        pltpu.make_async_copy(t_hbm.at[here], t.at[here], in_sems.at[i])
        for i, here in enumerate(chunks[1:])
    ]
    stores = [
        pltpu.make_async_copy(out.at[:, here], out_hbm.at[:, here], out_sems.at[i])
        for i, here in enumerate(chunks)
    ]
    for copy in loads[:AHEAD] + fetches:
        copy.start()
    wide_product(pair, rows, high, low, out, chunks[0])
    stores[0].start()
    for i, copy in enumerate(loads):
        copy.wait()
        if i + AHEAD < len(loads):
            loads[i + AHEAD].start()
        if i == len(loads) - 1:
            for fetch in fetches:
                fetch.wait()
            coarses[...] = jnp.concatenate(split(cwgt[...]), axis=0)
            projects[...] = jnp.concatenate(split(xwgt[...]), axis=0)
        here = chunks[i + 1]
        wide_product(pair, t.at[here], high, low, out, here)
        stores[i + 1].start()
    for copy in stores:
        copy.wait()


def prepare_kernel(patches, pair, crops_ref, before_ref, grams, pick, lay, number):
    del before_ref
    width = grams.shape[0]
    both = dot(pair[...], pair[:width], NT)
    grams[...] = side_by_side(both[:width] + (both[width:] + both[width:].T))
    pick[...] = chosen(crops_ref, patches, pick.shape[1] // patches)
    frame = row_value(crops_ref, 0, patches, (1, patches * 16), 1, 16)
    slot = lax.broadcasted_iota(jnp.int32, (1, patches * 16), 1) % 16
    line = lax.broadcasted_iota(jnp.int32, lay.shape, 0)
    lay[...] = jnp.where(line == frame * 16 + slot, 1.0, 0.0).astype(BF16)
    slot = lax.broadcasted_iota(jnp.int32, number.shape, 0) % 16
    top = row_value(crops_ref, 1, patches, number.shape, 0, 16)
    left = row_value(crops_ref, 2, patches, number.shape, 0, 16)
    number[...] = ((top + slot // 4) * SIDE + left + slot % 4).astype(F32)


def stack_kernel(*refs):
    *block_refs, _, out_ref = refs
    size = block_refs[0].shape[0]
    for k, ref in enumerate(block_refs):
        out_ref[k * size : (k + 1) * size] = ref[...]


def row_value(crops_ref, column, patches, shape, axis, each):
    index = lax.broadcasted_iota(jnp.int32, shape, axis) // each
    found = jnp.zeros(shape, jnp.int32)
    for j in range(patches):
        found = jnp.where(index == j, crops_ref[column, j], found)
    return found


def chosen(crops_ref, patches, tokens):
    scale = row_value(crops_ref, 3, patches, (1, patches * tokens), 1, tokens)
    token = lax.broadcasted_iota(jnp.int32, (1, patches * tokens), 1)
    row, column = (token % tokens) // 16, token % 16
    wanted = token // tokens * 16 + (row * scale // 8) * 4 + column * scale // 8
    slot = lax.broadcasted_iota(jnp.int32, (patches * 16, patches * tokens), 0)
    return jnp.where(slot == wanted, 1.0, 0.0).astype(BF16)


def context_kernel(
    patches,
    peers,
    crops_ref,
    own_ref,
    other_ref,
    coarses,
    projects,
    xw_hbm,
    projected_ref,
    slope_ref,
    first_ref,
    rows,
    sem,
):
    fetch = pltpu.make_async_copy(xw_hbm.at[:, : first_ref.shape[1]], first_ref, sem)
    fetch.start()
    pixels = coarses.shape[0] // 2
    width = projects.shape[1]
    far = peers // 4
    me, side = lax.axis_index(("far", "y", "core")), lax.axis_index("lvl")
    for j in range(patches):
        frame, top, left = crops_ref[0, j], crops_ref[1, j], crops_ref[2, j]
        near = lax.bitwise_xor(frame % 4, me % 4)
        k = (me // 4 - frame // 4 + far) % far
        for a in range(4):
            row = jnp.minimum(top + a, SIDE - 1)
            shard = (lax.bitwise_xor(row // 4, side) * 2 + near // 2) * far + k
            start = pl.ds(pl.multiple_of((shard * 4 + row % 4) * SIDE, SIDE), SIDE)
            line = jnp.where(near % 2 == 0, own_ref[start, :], other_ref[start, :])
            rows[j * 16 + a * 4 : j * 16 + a * 4 + 4, :] = pltpu.roll(line, SIDE - left, 0)[:4, :]
    pre = dot3(split(rows[...]), (coarses[:pixels], coarses[pixels:]))
    gate = sigmoid(pre)
    slope_ref[...] = gate * (1.0 + pre * (1.0 - gate))
    projected = dot3(split(pre * gate), (projects[:width], projects[width:])).T
    projected_ref[...] = jnp.concatenate(split(projected), axis=1)
    fetch.wait()


def middle_kernel(
    chunks,
    projected,
    grams,
    pick,
    first,
    xw_hbm,
    tw_hbm,
    pair_hbm,
    de_hbm,
    de_ref,
    deep_ref,
    dslot_ref,
    xw,
    tw,
    taken,
    factor,
    deep,
    parts,
    xw_sems,
    tw_sems,
    out_sems,
    sems,
):
    width = grams.shape[0]
    slots = pick.shape[0]
    each = slots // len(chunks)
    tw_loads = [
        pltpu.make_async_copy(tw_hbm.at[:, here], tw.at[:, here], tw_sems.at[i]) for i, here in enumerate(chunks)
    ]
    xw_loads = [
        pltpu.make_async_copy(xw_hbm.at[:, here], xw.at[:, here], xw_sems.at[i])
        for i, here in enumerate(chunks[1:])
    ]
    stores = [
        pltpu.make_async_copy(xw.at[:, here], de_hbm.at[:, here], out_sems.at[i])
        for i, here in enumerate(chunks[:-1])
    ]
    fetches = [
        pltpu.make_async_copy(pair_hbm, deep_ref.at[: 2 * width], sems.at[0]),
        pltpu.make_async_copy(pair_hbm.at[:width], deep_ref.at[2 * width :], sems.at[1]),
    ]
    tw_loads[0].start()
    for pair in zip(xw_loads, tw_loads[1:]):
        for copy in pair:
            copy.start()
    for copy in fetches:
        copy.start()

    def begin(i):
        tokens = chunks[i]
        source = first if i == 0 else xw.at[:, tokens]
        taken[:slots], taken[slots:] = pick[:, tokens], pick[:, tokens]
        spread = dot(projected[...], taken[...])
        for here in blocks(width, 32):
            pre = source[here] + spread[here]
            gate = sigmoid(pre)
            hidden = pre * gate
            factor[i % 2, here] = gate + hidden * (1.0 - gate)
            high, low = split(hidden)
            for part, value in enumerate((high, high, low)):
                deep[i % 2, shift(here, part * width)] = value

    begin(0)
    for i, tokens in enumerate(chunks):
        tw_loads[i].wait()
        if i + 1 < len(chunks):
            xw_loads[i].wait()
        target = de_ref if i == len(chunks) - 1 else xw.at[:, tokens]
        product = dot(grams[...], deep[i % 2])
        if i + 1 < len(chunks):
            begin(i + 1)
        for here in blocks(width, 32):
            de = (product[here] - tw[here, tokens]) * factor[i % 2, here]
            target[here] = de
            parts[here], parts[shift(here, width)] = split(de)
        mine = slice(i * each, (i + 1) * each)
        both = dot(pick[mine, tokens], parts[...], NT)
        dslot_ref[mine] = both[:, :width] + both[:, width:]
        if i < len(stores):
            stores[i].start()
    for copy in stores + fetches:
        copy.wait()


def through(value, pair):
    count, rows = value.shape[0], pair.shape[0] // 2
    high, low = split(value)
    both = dot(jnp.concatenate([high, low], axis=0), pair[:rows], NT)
    return both[:count] + (both[count:] + dot(high, pair[rows:], NT))


def closing_kernel(dslot_ref, slope_ref, coarses, projects, lay, number, send_ref):
    grad = through(through(dslot_ref[...], projects) * slope_ref[...], coarses)
    high, low = split(jnp.concatenate([grad, number[...]], axis=1))
    send_ref[...] = dot(lay[...], high) + dot(lay[...], low)


def scatter_kernel(message_ref, done_ref, mine_ref, other_ref, total):
    del done_ref
    pixels = mine_ref.shape[2]
    message = message_ref[...]
    number = lax.broadcasted_iota(jnp.int32, (message.shape[0], SIDE * SIDE), 1).astype(F32)
    pick = jnp.where(message[:, pixels : pixels + 1] == number, 1.0, 0.0).astype(BF16)
    high, low = split(message[:, :pixels])
    total[...] = dot(pick, low, TN) + dot(pick, high, TN)
    half = mine_ref.shape[1]
    side = lax.axis_index("lvl")
    mine_ref[0] = total[pl.ds(pl.multiple_of(side * half, half), half), :]
    other_ref[0] = total[pl.ds(pl.multiple_of((1 - side) * half, half), half), :]


def last_kernel(chunks, de_hbm, first, deep, out_hbm, de, out, cat, in_sems, out_sems):
    width = de.shape[0]
    order = chunks[-1:] + chunks[:-1]
    loads = [
        pltpu.make_async_copy(de_hbm.at[:, here], de.at[:, here], in_sems.at[i])
        for i, here in enumerate(order[1:])
    ]
    stores = [
        pltpu.make_async_copy(out.at[here], out_hbm.at[here], out_sems.at[i]) for i, here in enumerate(order)
    ]

    def prepare(i, source):
        for here in blocks(width, 32):
            high, low = split(source[here])
            cat[i % 2, here], cat[i % 2, shift(here, width)], cat[i % 2, shift(here, 2 * width)] = high, high, low

    for copy in loads:
        copy.start()
    prepare(0, first)
    for i, here in enumerate(order):
        if i < len(loads):
            loads[i].wait()
        out[here, :] = dot(cat[i % 2], deep[...], TN)
        if i < len(loads):
            prepare(i + 1, de.at[:, order[i + 1]])
        stores[i].start()
    for copy in stores:
        copy.wait()


def chunk_rows(first, last):
    return [slice(start, start + ROWS) for start in range(first, last, ROWS)]


def fixed(*values):
    return [pltpu.with_memory_space_constraint(value, pltpu.HBM) for value in values]


def near(*values):
    return [pltpu.with_memory_space_constraint(value, pltpu.VMEM) for value in values]


def stack(blocks, before):
    shape = (len(blocks) * blocks[0].shape[0],) + blocks[0].shape[1:]
    return call(
        stack_kernel,
        "stack",
        1000,
        jax.ShapeDtypeStruct(shape, F32),
        limit=ROOM,
        in_specs=[VMEM] * len(blocks) + [HBM],
        out_specs=VMEM,
    )(*blocks, *fixed(before))


def body(coarse_input, coarse_weight, fine_input, fine_target, crops, in_weight, context_weight, out_weight):
    patch = ("far", "y", "core")
    peers = lax.axis_size(patch)
    far = peers // 4
    patches, tokens, values = fine_input.shape
    width = in_weight.shape[1]
    pixels = coarse_weight.shape[0]
    half = coarse_input.shape[1]
    count = patches * tokens
    swap = [(0, 1), (1, 0)]

    column = [coarse_input]
    for k in range(1, far):
        column.append(lax.ppermute(coarse_input, "far", [(p, (p + k) % far) for p in range(far)]))

    chunks = chunk_rows(0, count)
    pair_shape = (2 * width, values)
    x, t = fine_input.reshape(count, values), fine_target.reshape(count, values)
    xw, pair, rows, next_pair, crops = call(
        functools.partial(input_kernel, chunks),
        "input",
        6 * count * values * width,
        (
            pltpu.HBM((width, count), F32),
            pltpu.HBM(pair_shape, BF16),
            pltpu.VMEM((ROWS, values), F32),
            pltpu.VMEM(pair_shape, BF16),
            pltpu.VMEM((4, patches), jnp.int32),
        ),
        in_specs=[HBM] * 5,
        out_specs=(HBM, HBM, VMEM, VMEM, VMEM),
        scratch_shapes=[
            pltpu.VMEM((count, values), F32),
            pltpu.VMEM((width, count), F32),
            pltpu.VMEM((width, values), F32),
            pltpu.VMEM((width, values), F32),
            pltpu.VMEM(pair_shape, BF16),
            pltpu.VMEM((ROWS, values), BF16),
            pltpu.VMEM((ROWS, values), BF16),
            pltpu.SemaphoreType.DMA((len(chunks),)),
            pltpu.SemaphoreType.DMA((len(chunks),)),
            pltpu.SemaphoreType.DMA((5,)),
        ],
    )(*fixed(x, in_weight.T, t, out_weight, crops.T))
    column = stack(column, xw)
    own = [column]
    for flip in range(1, 4):
        own.append(lax.ppermute(column, ("lvl", "y"), [(p, p ^ flip) for p in range(4)]))
    tw, coarses, projects = call(
        functools.partial(target_kernel, chunks),
        "target",
        6 * count * values * width,
        (
            pltpu.HBM((width, count), F32),
            pltpu.VMEM((2 * pixels, width), BF16),
            pltpu.VMEM((2 * width, width), BF16),
        ),
        limit=ROOM,
        in_specs=[HBM] * 3 + [VMEM] * 2,
        out_specs=(HBM, VMEM, VMEM),
        scratch_shapes=[
            pltpu.VMEM((count, values), F32),
            pltpu.VMEM((width, count), F32),
            pltpu.VMEM((ROWS, values), BF16),
            pltpu.VMEM((ROWS, values), BF16),
            pltpu.VMEM((pixels, width), F32),
            pltpu.VMEM((width, width), F32),
            pltpu.SemaphoreType.DMA((len(chunks),)),
            pltpu.SemaphoreType.DMA((len(chunks),)),
            pltpu.SemaphoreType.DMA((2,)),
        ],
    )(*fixed(t, coarse_weight, context_weight), *near(rows, next_pair))
    own = stack(own, tw).reshape(-1, pixels)
    other = lax.ppermute(own, "core", swap)
    (crops,) = near(crops)
    grams, pick, lay, number = call(
        functools.partial(prepare_kernel, patches),
        "prepare",
        8 * values * width * width,
        (
            pltpu.VMEM((width, 3 * width), BF16),
            pltpu.VMEM((patches * 16, count), BF16),
            pltpu.VMEM((peers * 16, patches * 16), BF16),
            pltpu.VMEM((patches * 16, LANES - pixels), F32),
        ),
        limit=ROOM,
        in_specs=[VMEM, SMEM, HBM],
        out_specs=(VMEM,) * 4,
    )(*near(next_pair), crops, own)

    projected, slope, first = call(
        functools.partial(context_kernel, patches, peers),
        "context",
        6 * patches * 16 * width * width,
        (
            pltpu.VMEM((width, 2 * patches * 16), BF16),
            pltpu.VMEM((patches * 16, width), F32),
            pltpu.VMEM((width, ROWS), F32),
        ),
        limit=ROOM,
        in_specs=[SMEM] + [VMEM] * 4 + [HBM],
        out_specs=(VMEM,) * 3,
        scratch_shapes=[pltpu.VMEM((patches * 16, pixels), F32), pltpu.SemaphoreType.DMA],
    )(crops, own, other, *near(coarses, projects), *fixed(xw))
    de, last_de, deep, dslot = call(
        functools.partial(middle_kernel, chunks),
        "middle",
        6 * count * width * width,
        (
            pltpu.HBM((width, count), F32),
            pltpu.VMEM((width, ROWS), F32),
            pltpu.VMEM((3 * width, values), BF16),
            pltpu.VMEM((patches * 16, width), F32),
        ),
        limit=ROOM,
        in_specs=[VMEM] * 4 + [HBM] * 3,
        out_specs=(HBM,) + (VMEM,) * 3,
        scratch_shapes=[
            pltpu.VMEM((width, count), F32),
            pltpu.VMEM((width, count), F32),
            pltpu.VMEM((2 * patches * 16, ROWS), BF16),
            pltpu.VMEM((2, width, ROWS), F32),
            pltpu.VMEM((2, 3 * width, ROWS), BF16),
            pltpu.VMEM((2 * width, ROWS), BF16),
            pltpu.SemaphoreType.DMA((len(chunks),)),
            pltpu.SemaphoreType.DMA((len(chunks),)),
            pltpu.SemaphoreType.DMA((len(chunks),)),
            pltpu.SemaphoreType.DMA((2,)),
        ],
    )(*near(projected, grams, pick, first), *fixed(xw, tw, pair))
    back = call(
        closing_kernel,
        "closing",
        6 * patches * 16 * width * width,
        jax.ShapeDtypeStruct((peers * 16, LANES), F32),
        limit=ROOM,
        in_specs=[VMEM] * 6,
        out_specs=VMEM,
    )(*near(dslot, slope, coarses, projects, lay, number))
    returned = lax.all_to_all(back, patch, 0, 0, tiled=True)

    fine_grad = call(
        functools.partial(last_kernel, chunks),
        "last",
        6 * count * values * width,
        pltpu.HBM((count, values), F32),
        limit=ROOM,
        in_specs=[HBM, VMEM, VMEM],
        out_specs=HBM,
        scratch_shapes=[
            pltpu.VMEM((width, count), F32),
            pltpu.VMEM((count, values), F32),
            pltpu.VMEM((2, 3 * width, ROWS), BF16),
            pltpu.SemaphoreType.DMA((len(chunks),)),
            pltpu.SemaphoreType.DMA((len(chunks),)),
        ],
    )(*fixed(de), *near(last_de, deep))
    part = (1, half, pixels)
    mine, theirs = call(
        scatter_kernel,
        "scatter",
        10000,
        (jax.ShapeDtypeStruct(part, F32), jax.ShapeDtypeStruct(part, F32)),
        limit=ROOM,
        in_specs=[VMEM, HBM],
        out_specs=(VMEM, VMEM),
        scratch_shapes=[pltpu.VMEM((SIDE * SIDE, pixels), F32)],
    )(returned, *fixed(fine_grad))
    coarse_grad = mine + lax.ppermute(theirs, "lvl", swap)
    return (coarse_grad, fine_grad.reshape(fine_input.shape))


def solution(mesh):
    sides, peers = mesh.shape["lvl"], mesh.shape["patch"]
    fine = jax.sharding.Mesh(mesh.devices.reshape(sides, peers // 4, 2, 2), ("lvl", "far", "y", "core"))
    patch = ("far", "y", "core")
    both = ("lvl",) + patch
    in_specs = (
        P(patch, "lvl", None),
        P(),
        P(both, None, None),
        P(both, None, None),
        P(both, None),
        P(),
        P(),
        P(),
    )
    out_specs = (P(patch, "lvl", None), P(both, None, None))
    return jax.shard_map(body, mesh=fine, in_specs=in_specs, out_specs=out_specs, check_vma=False)
```

```python
import functools
import math

import jax
import jax.numpy as jnp
from jax import lax
from jax.experimental import pallas as pl
from jax.experimental.pallas import tpu as pltpu
from jax.sharding import PartitionSpec as P

F32 = jnp.float32
BF16 = jnp.bfloat16
NN = (((1,), (0,)), ((), ()))
NT = (((1,), (1,)), ((), ()))
TN = (((0,), (0,)), ((), ()))
ROWS = 512
SIDE = 8
LANES = 256
LIMIT = 60 * 1024 * 1024
ROOM = 40 * 1024 * 1024
SMEM = pl.BlockSpec(memory_space=pltpu.SMEM)
VMEM = pl.BlockSpec(memory_space=pltpu.VMEM)
HBM = pl.BlockSpec(memory_space=pltpu.HBM)


def split(value):
    high = value.astype(BF16)
    low = (value - high.astype(F32)).astype(BF16)
    return high, low


def dot(left, right, dims=NN):
    return lax.dot_general(left, right, dims, preferred_element_type=F32)


def dot3(left, right, dims=NN):
    return (
        dot(left[0], right[1], dims) + dot(left[1], right[0], dims) + dot(left[0], right[0], dims)
    )


def side_by_side(value):
    high, low = split(value)
    return jnp.concatenate([high, low, high], axis=1)


def sigmoid(value):
    return 0.5 * jnp.tanh(0.5 * value) + 0.5


def call(kernel, name, flops, out_shape, limit=LIMIT, **kwargs):
    moved = 8 * sum(math.prod(s.shape) for s in jax.tree.leaves(out_shape))
    return pl.pallas_call(
        kernel,
        out_shape=out_shape,
        name=name,
        cost_estimate=pl.CostEstimate(flops=flops, bytes_accessed=moved, transcendentals=0),
        compiler_params=pltpu.CompilerParams(vmem_limit_bytes=limit),
        **kwargs,
    )


def blocks(rows, size):
    return [slice(start, start + size) for start in range(0, rows, size)]


def shift(here, by):
    return slice(here.start + by, here.stop + by)


def pair_product(pair, value, dims):
    rows = pair.shape[0] // 2
    high, low = split(value)
    both = dot(pair[...], high, dims)
    return both[:rows] + (both[rows:] + dot(pair[:rows], low, dims))


def chunk(i):
    return pl.ds(pl.multiple_of(i * ROWS, ROWS), ROWS)


def split_rows(source, high, low):
    for here in blocks(high.shape[0], 16):
        high[here], low[here] = split(source[here])


def wide_chunk(pair, high, low, out, tokens):
    width = pair.shape[0] // 2
    both = dot(pair[...], high[...], NT)
    rest = dot(pair[:width], low[...], NT)
    for here in blocks(width, 32):
        out[here, tokens] = both[here] + (both[shift(here, width)] + rest[here])


def input_kernel(
    x_hbm,
    weight_hbm,
    t_hbm,
    next_weight_hbm,
    crops_hbm,
    out_hbm,
    pair_hbm,
    next_rows,
    next_pair,
    crops,
    x,
    out,
    weight,
    next_weight,
    pair,
    high,
    low,
    in_sems,
    out_sems,
    sems,
):
    width = weight.shape[0]
    steps = x.shape[0] // ROWS
    fetch = pltpu.make_async_copy(weight_hbm, weight, sems.at[0])
    keep = pltpu.make_async_copy(pair, pair_hbm, sems.at[1])
    fetch_next = pltpu.make_async_copy(next_weight_hbm, next_weight, sems.at[2])
    fetch_rows = pltpu.make_async_copy(t_hbm.at[: next_rows.shape[0]], next_rows, sems.at[3])
    fetch_crops = pltpu.make_async_copy(crops_hbm, crops, sems.at[4])

    def load(i):
        return pltpu.make_async_copy(x_hbm.at[chunk(i)], x.at[chunk(i)], in_sems.at[i])

    def store(i):
        return pltpu.make_async_copy(out.at[:, chunk(i)], out_hbm.at[:, chunk(i)], out_sems.at[i])

    fetch.start()
    load(0).start()
    fetch.wait()
    for i in range(1, steps):
        load(i).start()
    for copy in (fetch_next, fetch_crops, fetch_rows):
        copy.start()
    pair[:width], pair[width:] = split(weight[...])
    keep.start()
    load(0).wait()
    split_rows(x.at[chunk(0)], high, low)

    def step(i, _):
        wide_chunk(pair, high, low, out, chunk(i))
        store(i).start()

        @pl.when(i + 1 < steps)
        def _():
            load(i + 1).wait()
            split_rows(x.at[chunk(i + 1)], high, low)

        return 0

    lax.fori_loop(0, steps, step, 0)
    fetch_next.wait()
    next_pair[:width], next_pair[width:] = split(next_weight[...])
    for copy in (keep, fetch_rows, fetch_crops):
        copy.wait()
    for i in range(steps):
        store(i).wait()


def target_kernel(
    t_hbm,
    cwgt_hbm,
    xwgt_hbm,
    rows,
    pair,
    out_hbm,
    out,
    coarses,
    projects,
    t,
    high,
    low,
    cwgt,
    xwgt,
    in_sems,
    out_sems,
    sems,
):
    steps = t.shape[0] // ROWS
    fetches = [
        pltpu.make_async_copy(cwgt_hbm, cwgt, sems.at[0]),
        pltpu.make_async_copy(xwgt_hbm, xwgt, sems.at[1]),
    ]

    def load(i):
        return pltpu.make_async_copy(t_hbm.at[chunk(i)], t.at[chunk(i)], in_sems.at[i])

    def store(i):
        return pltpu.make_async_copy(out, out_hbm.at[:, chunk(i)], out_sems.at[i])

    for i in range(1, steps):
        load(i).start()
    for copy in fetches:
        copy.start()
    split_rows(rows, high, low)

    def step(i, _):
        @pl.when(i > 0)
        def _():
            store(i - 1).wait()

        wide_chunk(pair, high, low, out, slice(None))

        @pl.when(i + 1 < steps)
        def _():
            store(i).start()
            load(i + 1).wait()
            split_rows(t.at[chunk(i + 1)], high, low)

        return 0

    lax.fori_loop(0, steps, step, 0)
    for copy in fetches:
        copy.wait()
    coarses[...] = jnp.concatenate(split(cwgt[...]), axis=0)
    projects[...] = jnp.concatenate(split(xwgt[...]), axis=0)


def prepare_kernel(patches, pair, crops_ref, before_ref, grams, wanted, lay, number):
    del before_ref
    width = grams.shape[0]
    both = dot(pair[...], pair[:width], NT)
    grams[...] = side_by_side(both[:width] + (both[width:] + both[width:].T))
    wanted[...] = slot_row(crops_ref, patches, wanted.shape[1] // patches)
    frame = row_value(crops_ref, 0, patches, (1, patches * 16), 1, 16)
    slot = lax.broadcasted_iota(jnp.int32, (1, patches * 16), 1) % 16
    line = lax.broadcasted_iota(jnp.int32, lay.shape, 0)
    lay[...] = jnp.where(line == frame * 16 + slot, 1.0, 0.0).astype(BF16)
    slot = lax.broadcasted_iota(jnp.int32, number.shape, 0) % 16
    top = row_value(crops_ref, 1, patches, number.shape, 0, 16)
    left = row_value(crops_ref, 2, patches, number.shape, 0, 16)
    number[...] = ((top + slot // 4) * SIDE + left + slot % 4).astype(F32)


def stack_kernel(*refs):
    *block_refs, _, out_ref = refs
    size = block_refs[0].shape[0]
    for k, ref in enumerate(block_refs):
        out_ref[k * size : (k + 1) * size] = ref[...]


def row_value(crops_ref, column, patches, shape, axis, each):
    index = lax.broadcasted_iota(jnp.int32, shape, axis) // each
    found = jnp.zeros(shape, jnp.int32)
    for j in range(patches):
        found = jnp.where(index == j, crops_ref[column, j], found)
    return found


def slot_row(crops_ref, patches, tokens):
    scale = row_value(crops_ref, 3, patches, (1, patches * tokens), 1, tokens)
    token = lax.broadcasted_iota(jnp.int32, (1, patches * tokens), 1)
    row, column = (token % tokens) // 16, token % 16
    return token // tokens * 16 + (row * scale // 8) * 4 + column * scale // 8


def taking(wanted, slots, first):
    slot = lax.broadcasted_iota(jnp.int32, (slots, wanted.shape[1]), 0) + first
    return jnp.where(slot == wanted, 1.0, 0.0).astype(BF16)


def context_kernel(
    patches,
    peers,
    crops_ref,
    own_ref,
    other_ref,
    coarses,
    projects,
    xw_hbm,
    projected_ref,
    slope_ref,
    first_ref,
    rows,
    sem,
):
    fetch = pltpu.make_async_copy(xw_hbm.at[:, : first_ref.shape[1]], first_ref, sem)
    fetch.start()
    pixels = coarses.shape[0] // 2
    width = projects.shape[1]
    far = peers // 4
    me, side = lax.axis_index(("far", "y", "core")), lax.axis_index("lvl")
    for j in range(patches):
        frame, top, left = crops_ref[0, j], crops_ref[1, j], crops_ref[2, j]
        near = lax.bitwise_xor(frame % 4, me % 4)
        k = (me // 4 - frame // 4 + far) % far
        for a in range(4):
            row = jnp.minimum(top + a, SIDE - 1)
            shard = (lax.bitwise_xor(row // 4, side) * 2 + near // 2) * far + k
            start = pl.ds(pl.multiple_of((shard * 4 + row % 4) * SIDE, SIDE), SIDE)
            line = jnp.where(near % 2 == 0, own_ref[start, :], other_ref[start, :])
            rows[j * 16 + a * 4 : j * 16 + a * 4 + 4, :] = pltpu.roll(line, SIDE - left, 0)[:4, :]
    pre = dot3(split(rows[...]), (coarses[:pixels], coarses[pixels:]))
    gate = sigmoid(pre)
    slope_ref[...] = gate * (1.0 + pre * (1.0 - gate))
    projected = dot3(split(pre * gate), (projects[:width], projects[width:])).T
    projected_ref[...] = jnp.concatenate(split(projected), axis=1)
    fetch.wait()


def middle_kernel(
    projected,
    grams,
    wanted,
    first,
    tw_last,
    xw_hbm,
    tw_hbm,
    pair_hbm,
    de_hbm,
    de_ref,
    deep_ref,
    dslot_ref,
    xw,
    tw,
    taken,
    factor,
    deep,
    parts,
    xw_sems,
    tw_sems,
    out_sems,
    sems,
):
    width, count = xw.shape
    slots = dslot_ref.shape[0]
    steps = count // ROWS
    each = slots // steps

    def load_xw(i):
        return pltpu.make_async_copy(xw_hbm.at[:, chunk(i)], xw.at[:, chunk(i)], xw_sems.at[i])

    def load_tw(i):
        return pltpu.make_async_copy(tw_hbm.at[:, chunk(i)], tw.at[:, chunk(i)], tw_sems.at[i])

    def store(i):
        return pltpu.make_async_copy(de_ref, de_hbm.at[:, chunk(i)], out_sems.at[i])

    fetches = [
        pltpu.make_async_copy(pair_hbm, deep_ref.at[: 2 * width], sems.at[0]),
        pltpu.make_async_copy(pair_hbm.at[:width], deep_ref.at[2 * width :], sems.at[1]),
    ]
    for i in range(steps):
        if i < steps - 1:
            load_tw(i).start()
            load_xw(i + 1).start()
    for copy in fetches:
        copy.start()
    tw[:, (steps - 1) * ROWS :] = tw_last[...]

    def begin(i, source):
        here = taking(wanted[:, chunk(i)], slots, 0)
        taken[:slots], taken[slots:] = here, here
        spread = dot(projected[...], taken[...])
        for here in blocks(width, 32):
            pre = source[here] + spread[here]
            gate = sigmoid(pre)
            hidden = pre * gate
            factor[here] = gate + hidden * (1.0 - gate)
            high, low = split(hidden)
            deep[here], deep[shift(here, width)], deep[shift(here, 2 * width)] = high, high, low

    begin(0, first)

    def step(i, _):
        product = dot(grams[...], deep[...])

        @pl.when(i + 1 < steps)
        def _():
            load_tw(i).wait()

        @pl.when(i > 0)
        def _():
            store(i - 1).wait()

        tokens = chunk(i)
        for here in blocks(width, 32):
            de = (product[here] - tw[here, tokens]) * factor[here]
            de_ref[here] = de
            parts[here], parts[shift(here, width)] = split(de)
        mine = taking(wanted[:, tokens], each, i * each)
        both = dot(mine, parts[...], NT)
        dslot_ref[pl.ds(pl.multiple_of(i * each, each), each)] = both[:, :width] + both[:, width:]

        @pl.when(i + 1 < steps)
        def _():
            store(i).start()
            load_xw(i + 1).wait()
            begin(i + 1, xw.at[:, chunk(i + 1)])

        return 0

    lax.fori_loop(0, steps, step, 0)
    for copy in fetches:
        copy.wait()


def through(value, pair):
    count, rows = value.shape[0], pair.shape[0] // 2
    high, low = split(value)
    both = dot(jnp.concatenate([high, low], axis=0), pair[:rows], NT)
    return both[:count] + (both[count:] + dot(high, pair[rows:], NT))


def closing_kernel(dslot_ref, slope_ref, coarses, projects, lay, number, send_ref):
    grad = through(through(dslot_ref[...], projects) * slope_ref[...], coarses)
    high, low = split(jnp.concatenate([grad, number[...]], axis=1))
    send_ref[...] = dot(lay[...], high) + dot(lay[...], low)


def scatter_kernel(message_ref, done_ref, mine_ref, other_ref, total):
    del done_ref
    pixels = mine_ref.shape[2]
    message = message_ref[...]
    number = lax.broadcasted_iota(jnp.int32, (message.shape[0], SIDE * SIDE), 1).astype(F32)
    pick = jnp.where(message[:, pixels : pixels + 1] == number, 1.0, 0.0).astype(BF16)
    high, low = split(message[:, :pixels])
    total[...] = dot(pick, low, TN) + dot(pick, high, TN)
    half = mine_ref.shape[1]
    side = lax.axis_index("lvl")
    mine_ref[0] = total[pl.ds(pl.multiple_of(side * half, half), half), :]
    other_ref[0] = total[pl.ds(pl.multiple_of((1 - side) * half, half), half), :]


def last_kernel(de_hbm, first, deep, out_hbm, de, out, cat, in_sems, out_sems):
    width = de.shape[0]
    steps = de.shape[1] // ROWS

    def load(i):
        return pltpu.make_async_copy(de_hbm.at[:, chunk(i)], de.at[:, chunk(i)], in_sems.at[i])

    def store(i):
        return pltpu.make_async_copy(out.at[chunk(i)], out_hbm.at[chunk(i)], out_sems.at[i])

    def prepare(source):
        for here in blocks(width, 32):
            high, low = split(source[here])
            cat[here], cat[shift(here, width)], cat[shift(here, 2 * width)] = high, high, low

    for i in range(steps - 1):
        load(i).start()
    prepare(first)

    def step(i, _):
        mine = lax.rem(i + steps - 1, steps)
        out[chunk(mine), :] = dot(cat[...], deep[...], TN)
        store(mine).start()

        @pl.when(i + 1 < steps)
        def _():
            load(i).wait()
            prepare(de.at[:, chunk(i)])

        return 0

    lax.fori_loop(0, steps, step, 0)
    for i in range(steps):
        store(i).wait()


def fixed(*values):
    return [pltpu.with_memory_space_constraint(value, pltpu.HBM) for value in values]


def near(*values):
    return [pltpu.with_memory_space_constraint(value, pltpu.VMEM) for value in values]


def stack(blocks, before):
    shape = (len(blocks) * blocks[0].shape[0],) + blocks[0].shape[1:]
    return call(
        stack_kernel,
        "stack",
        1000,
        jax.ShapeDtypeStruct(shape, F32),
        limit=ROOM,
        in_specs=[VMEM] * len(blocks) + [HBM],
        out_specs=VMEM,
    )(*blocks, *fixed(before))


def body(coarse_input, coarse_weight, fine_input, fine_target, crops, in_weight, context_weight, out_weight):
    patch = ("far", "y", "core")
    peers = lax.axis_size(patch)
    far = peers // 4
    patches, tokens, values = fine_input.shape
    width = in_weight.shape[1]
    pixels = coarse_weight.shape[0]
    half = coarse_input.shape[1]
    count = patches * tokens
    swap = [(0, 1), (1, 0)]

    column = [coarse_input]
    for k in range(1, far):
        column.append(lax.ppermute(coarse_input, "far", [(p, (p + k) % far) for p in range(far)]))

    steps = count // ROWS
    pair_shape = (2 * width, values)
    x, t = fine_input.reshape(count, values), fine_target.reshape(count, values)
    xw, pair, rows, next_pair, crops = call(
        input_kernel,
        "input",
        6 * count * values * width,
        (
            pltpu.HBM((width, count), F32),
            pltpu.HBM(pair_shape, BF16),
            pltpu.VMEM((ROWS, values), F32),
            pltpu.VMEM(pair_shape, BF16),
            pltpu.VMEM((4, patches), jnp.int32),
        ),
        in_specs=[HBM] * 5,
        out_specs=(HBM, HBM, VMEM, VMEM, VMEM),
        scratch_shapes=[
            pltpu.VMEM((count, values), F32),
            pltpu.VMEM((width, count), F32),
            pltpu.VMEM((width, values), F32),
            pltpu.VMEM((width, values), F32),
            pltpu.VMEM(pair_shape, BF16),
            pltpu.VMEM((ROWS, values), BF16),
            pltpu.VMEM((ROWS, values), BF16),
            pltpu.SemaphoreType.DMA((steps,)),
            pltpu.SemaphoreType.DMA((steps,)),
            pltpu.SemaphoreType.DMA((5,)),
        ],
    )(*fixed(x, in_weight.T, t, out_weight, crops.T))
    column = stack(column, xw)
    own = [column]
    for flip in range(1, 4):
        own.append(lax.ppermute(column, ("lvl", "y"), [(p, p ^ flip) for p in range(4)]))
    tw, tw_last, coarses, projects = call(
        target_kernel,
        "target",
        6 * count * values * width,
        (
            pltpu.HBM((width, count), F32),
            pltpu.VMEM((width, ROWS), F32),
            pltpu.VMEM((2 * pixels, width), BF16),
            pltpu.VMEM((2 * width, width), BF16),
        ),
        limit=ROOM,
        in_specs=[HBM] * 3 + [VMEM] * 2,
        out_specs=(HBM, VMEM, VMEM, VMEM),
        scratch_shapes=[
            pltpu.VMEM((count, values), F32),
            pltpu.VMEM((ROWS, values), BF16),
            pltpu.VMEM((ROWS, values), BF16),
            pltpu.VMEM((pixels, width), F32),
            pltpu.VMEM((width, width), F32),
            pltpu.SemaphoreType.DMA((steps,)),
            pltpu.SemaphoreType.DMA((steps,)),
            pltpu.SemaphoreType.DMA((2,)),
        ],
    )(*fixed(t, coarse_weight, context_weight), *near(rows, next_pair))
    own = stack(own, tw).reshape(-1, pixels)
    other = lax.ppermute(own, "core", swap)
    (crops,) = near(crops)
    grams, wanted, lay, number = call(
        functools.partial(prepare_kernel, patches),
        "prepare",
        8 * values * width * width,
        (
            pltpu.VMEM((width, 3 * width), BF16),
            pltpu.VMEM((1, count), jnp.int32),
            pltpu.VMEM((peers * 16, patches * 16), BF16),
            pltpu.VMEM((patches * 16, LANES - pixels), F32),
        ),
        limit=ROOM,
        in_specs=[VMEM, SMEM, HBM],
        out_specs=(VMEM,) * 4,
    )(*near(next_pair), crops, own)

    projected, slope, first = call(
        functools.partial(context_kernel, patches, peers),
        "context",
        6 * patches * 16 * width * width,
        (
            pltpu.VMEM((width, 2 * patches * 16), BF16),
            pltpu.VMEM((patches * 16, width), F32),
            pltpu.VMEM((width, ROWS), F32),
        ),
        limit=ROOM,
        in_specs=[SMEM] + [VMEM] * 4 + [HBM],
        out_specs=(VMEM,) * 3,
        scratch_shapes=[pltpu.VMEM((patches * 16, pixels), F32), pltpu.SemaphoreType.DMA],
    )(crops, own, other, *near(coarses, projects), *fixed(xw))
    de, last_de, deep, dslot = call(
        middle_kernel,
        "middle",
        6 * count * width * width,
        (
            pltpu.HBM((width, count), F32),
            pltpu.VMEM((width, ROWS), F32),
            pltpu.VMEM((3 * width, values), BF16),
            pltpu.VMEM((patches * 16, width), F32),
        ),
        limit=ROOM,
        in_specs=[VMEM] * 5 + [HBM] * 3,
        out_specs=(HBM,) + (VMEM,) * 3,
        scratch_shapes=[
            pltpu.VMEM((width, count), F32),
            pltpu.VMEM((width, count), F32),
            pltpu.VMEM((2 * patches * 16, ROWS), BF16),
            pltpu.VMEM((width, ROWS), F32),
            pltpu.VMEM((3 * width, ROWS), BF16),
            pltpu.VMEM((2 * width, ROWS), BF16),
            pltpu.SemaphoreType.DMA((steps,)),
            pltpu.SemaphoreType.DMA((steps,)),
            pltpu.SemaphoreType.DMA((steps,)),
            pltpu.SemaphoreType.DMA((2,)),
        ],
    )(*near(projected, grams, wanted, first, tw_last), *fixed(xw, tw, pair))
    back = call(
        closing_kernel,
        "closing",
        6 * patches * 16 * width * width,
        jax.ShapeDtypeStruct((peers * 16, LANES), F32),
        limit=ROOM,
        in_specs=[VMEM] * 6,
        out_specs=VMEM,
    )(*near(dslot, slope, coarses, projects, lay, number))
    returned = lax.all_to_all(back, patch, 0, 0, tiled=True)

    fine_grad = call(
        last_kernel,
        "last",
        6 * count * values * width,
        pltpu.HBM((count, values), F32),
        limit=ROOM,
        in_specs=[HBM, VMEM, VMEM],
        out_specs=HBM,
        scratch_shapes=[
            pltpu.VMEM((width, count), F32),
            pltpu.VMEM((count, values), F32),
            pltpu.VMEM((3 * width, ROWS), BF16),
            pltpu.SemaphoreType.DMA((steps,)),
            pltpu.SemaphoreType.DMA((steps,)),
        ],
    )(*fixed(de), *near(last_de, deep))
    part = (1, half, pixels)
    mine, theirs = call(
        scatter_kernel,
        "scatter",
        10000,
        (jax.ShapeDtypeStruct(part, F32), jax.ShapeDtypeStruct(part, F32)),
        limit=ROOM,
        in_specs=[VMEM, HBM],
        out_specs=(VMEM, VMEM),
        scratch_shapes=[pltpu.VMEM((SIDE * SIDE, pixels), F32)],
    )(returned, *fixed(fine_grad))
    coarse_grad = mine + lax.ppermute(theirs, "lvl", swap)
    return (coarse_grad, fine_grad.reshape(fine_input.shape))


def solution(mesh):
    sides, peers = mesh.shape["lvl"], mesh.shape["patch"]
    fine = jax.sharding.Mesh(mesh.devices.reshape(sides, peers // 4, 2, 2), ("lvl", "far", "y", "core"))
    patch = ("far", "y", "core")
    both = ("lvl",) + patch
    in_specs = (
        P(patch, "lvl", None),
        P(),
        P(both, None, None),
        P(both, None, None),
        P(both, None),
        P(),
        P(),
        P(),
    )
    out_specs = (P(patch, "lvl", None), P(both, None, None))
    return jax.shard_map(body, mesh=fine, in_specs=in_specs, out_specs=out_specs, check_vma=False)
```

```python
import functools
import math

import jax
import jax.numpy as jnp
from jax import lax
from jax.experimental import pallas as pl
from jax.experimental.pallas import tpu as pltpu
from jax.sharding import PartitionSpec as P

F32 = jnp.float32
BF16 = jnp.bfloat16
NN = (((1,), (0,)), ((), ()))
NT = (((1,), (1,)), ((), ()))
TN = (((0,), (0,)), ((), ()))
ROWS = 512
SIDE = 8
LANES = 256
LIMIT = 60 * 1024 * 1024
ROOM = 40 * 1024 * 1024
SMEM = pl.BlockSpec(memory_space=pltpu.SMEM)
VMEM = pl.BlockSpec(memory_space=pltpu.VMEM)
HBM = pl.BlockSpec(memory_space=pltpu.HBM)


def split(value):
    high = value.astype(BF16)
    low = (value - high.astype(F32)).astype(BF16)
    return high, low


def dot(left, right, dims=NN):
    return lax.dot_general(left, right, dims, preferred_element_type=F32)


def dot3(left, right, dims=NN):
    return (
        dot(left[0], right[1], dims) + dot(left[1], right[0], dims) + dot(left[0], right[0], dims)
    )


def side_by_side(value):
    high, low = split(value)
    return jnp.concatenate([high, low, high], axis=1)


def sigmoid(value):
    return 0.5 * jnp.tanh(0.5 * value) + 0.5


def call(kernel, name, flops, out_shape, limit=LIMIT, **kwargs):
    moved = 8 * sum(math.prod(s.shape) for s in jax.tree.leaves(out_shape))
    return pl.pallas_call(
        kernel,
        out_shape=out_shape,
        name=name,
        cost_estimate=pl.CostEstimate(flops=flops, bytes_accessed=moved, transcendentals=0),
        compiler_params=pltpu.CompilerParams(vmem_limit_bytes=limit),
        **kwargs,
    )


def blocks(rows, size):
    return [slice(start, start + size) for start in range(0, rows, size)]


def shift(here, by):
    return slice(here.start + by, here.stop + by)


def pair_product(pair, value, dims):
    rows = pair.shape[0] // 2
    high, low = split(value)
    both = dot(pair[...], high, dims)
    return both[:rows] + (both[rows:] + dot(pair[:rows], low, dims))


def chunk(i):
    return pl.ds(pl.multiple_of(i * ROWS, ROWS), ROWS)


def split_rows(source, high, low):
    for here in blocks(high.shape[0], 16):
        high[here], low[here] = split(source[here])


def wide_product(pair, value, high, low, out):
    width = pair.shape[0] // 2
    split_rows(value, high, low)
    both = dot(pair[...], high[...], NT)
    rest = dot(pair[:width], low[...], NT)
    for here in blocks(width, 32):
        out[here] = both[here] + (both[shift(here, width)] + rest[here])


def deep_product(wide, value, deep, out):
    values = value.shape[1]
    for here in blocks(deep.shape[0], 16):
        high, low = split(value[here])
        deep[here, :values], deep[here, values : 2 * values], deep[here, 2 * values :] = high, high, low
    out[...] = dot(wide[...], deep[...], NT)


def input_kernel(
    x_hbm,
    weight_hbm,
    t_hbm,
    next_weight_hbm,
    crops_hbm,
    out_hbm,
    pair_hbm,
    next_rows,
    next_wide,
    crops,
    x,
    out,
    weight,
    next_weight,
    pair,
    high,
    low,
    in_sems,
    out_sems,
    sems,
):
    width, values = weight.shape
    chunks = chunk_rows(x.shape[0])
    fetch = pltpu.make_async_copy(weight_hbm, weight, sems.at[0])
    keep = pltpu.make_async_copy(pair, pair_hbm, sems.at[1])
    fetch_next = pltpu.make_async_copy(next_weight_hbm, next_weight, sems.at[2])
    fetch_rows = pltpu.make_async_copy(t_hbm.at[: next_rows.shape[0]], next_rows, sems.at[3])
    fetch_crops = pltpu.make_async_copy(crops_hbm, crops, sems.at[4])
    loads = [
        pltpu.make_async_copy(x_hbm.at[here], x.at[here], in_sems.at[i]) for i, here in enumerate(chunks)
    ]
    stores = [
        pltpu.make_async_copy(out.at[:, here], out_hbm.at[:, here], out_sems.at[i])
        for i, here in enumerate(chunks)
    ]
    fetch.start()
    loads[0].start()
    fetch.wait()
    for copy in loads[1:] + [fetch_next, fetch_crops, fetch_rows]:
        copy.start()
    pair[:width], pair[width:] = split(weight[...])
    keep.start()
    for i, here in enumerate(chunks):
        loads[i].wait()
        wide_product(pair, x.at[here], high, low, out.at[:, here])
        stores[i].start()
    fetch_next.wait()
    high_part, low_part = split(next_weight[...])
    next_wide[:, :values], next_wide[:, values : 2 * values], next_wide[:, 2 * values :] = high_part, low_part, high_part
    for copy in [keep, fetch_rows, fetch_crops] + stores:
        copy.wait()


def target_kernel(
    t_hbm,
    cwgt_hbm,
    xwgt_hbm,
    rows,
    wide,
    out_hbm,
    out_last,
    coarses,
    projects,
    t,
    out,
    deep,
    cwgt,
    xwgt,
    in_sems,
    out_sems,
    sems,
):
    chunks = chunk_rows(t.shape[0])
    fetches = [
        pltpu.make_async_copy(cwgt_hbm, cwgt, sems.at[0]),
        pltpu.make_async_copy(xwgt_hbm, xwgt, sems.at[1]),
    ]
    loads = [
        pltpu.make_async_copy(t_hbm.at[here], t.at[here], in_sems.at[i])
        for i, here in enumerate(chunks[1:])
    ]
    stores = [
        pltpu.make_async_copy(out.at[:, here], out_hbm.at[:, here], out_sems.at[i])
        for i, here in enumerate(chunks[:-1])
    ]
    for copy in loads + fetches:
        copy.start()
    for i, here in enumerate(chunks):
        if i > 0:
            loads[i - 1].wait()
        source = rows if i == 0 else t.at[here]
        if i < len(stores):
            deep_product(wide, source, deep, out.at[:, here])
            stores[i].start()
        else:
            deep_product(wide, source, deep, out_last)
    for copy in fetches:
        copy.wait()
    coarses[...] = jnp.concatenate(split(cwgt[...]), axis=0)
    projects[...] = jnp.concatenate(split(xwgt[...]), axis=0)
    for copy in stores:
        copy.wait()


def chunk_rows(count):
    return [slice(start, start + ROWS) for start in range(0, count, ROWS)]


def prepare_kernel(patches, wide, crops_ref, before_ref, grams, wanted, lay, number):
    del before_ref
    width = grams.shape[0]
    values = wide.shape[1] // 3
    high = wide[:, :values]
    mixed = dot(wide[:, values : 2 * values], high, NT)
    grams[...] = side_by_side(dot(high, high, NT) + (mixed + mixed.T))
    wanted[...] = slot_row(crops_ref, patches, wanted.shape[1] // patches)
    frame = row_value(crops_ref, 0, patches, (1, patches * 16), 1, 16)
    slot = lax.broadcasted_iota(jnp.int32, (1, patches * 16), 1) % 16
    line = lax.broadcasted_iota(jnp.int32, lay.shape, 0)
    lay[...] = jnp.where(line == frame * 16 + slot, 1.0, 0.0).astype(BF16)
    slot = lax.broadcasted_iota(jnp.int32, number.shape, 0) % 16
    top = row_value(crops_ref, 1, patches, number.shape, 0, 16)
    left = row_value(crops_ref, 2, patches, number.shape, 0, 16)
    number[...] = ((top + slot // 4) * SIDE + left + slot % 4).astype(F32)


def stack_kernel(*refs):
    *block_refs, _, out_ref = refs
    size = block_refs[0].shape[0]
    for k, ref in enumerate(block_refs):
        out_ref[k * size : (k + 1) * size] = ref[...]


def row_value(crops_ref, column, patches, shape, axis, each):
    index = lax.broadcasted_iota(jnp.int32, shape, axis) // each
    found = jnp.zeros(shape, jnp.int32)
    for j in range(patches):
        found = jnp.where(index == j, crops_ref[column, j], found)
    return found


def slot_row(crops_ref, patches, tokens):
    scale = row_value(crops_ref, 3, patches, (1, patches * tokens), 1, tokens)
    token = lax.broadcasted_iota(jnp.int32, (1, patches * tokens), 1)
    row, column = (token % tokens) // 16, token % 16
    return token // tokens * 16 + (row * scale // 8) * 4 + column * scale // 8


def taking(wanted, slots, first):
    slot = lax.broadcasted_iota(jnp.int32, (slots, wanted.shape[1]), 0) + first
    return jnp.where(slot == wanted, 1.0, 0.0).astype(BF16)


def context_kernel(
    patches,
    peers,
    crops_ref,
    own_ref,
    other_ref,
    coarses,
    projects,
    xw_hbm,
    projected_ref,
    slope_ref,
    first_ref,
    rows,
    sem,
):
    fetch = pltpu.make_async_copy(xw_hbm.at[:, : first_ref.shape[1]], first_ref, sem)
    fetch.start()
    pixels = coarses.shape[0] // 2
    width = projects.shape[1]
    far = peers // 4
    me, side = lax.axis_index(("far", "y", "core")), lax.axis_index("lvl")
    for j in range(patches):
        frame, top, left = crops_ref[0, j], crops_ref[1, j], crops_ref[2, j]
        near = lax.bitwise_xor(frame % 4, me % 4)
        k = (me // 4 - frame // 4 + far) % far
        for a in range(4):
            row = jnp.minimum(top + a, SIDE - 1)
            shard = (lax.bitwise_xor(row // 4, side) * 2 + near // 2) * far + k
            start = pl.ds(pl.multiple_of((shard * 4 + row % 4) * SIDE, SIDE), SIDE)
            line = jnp.where(near % 2 == 0, own_ref[start, :], other_ref[start, :])
            rows[j * 16 + a * 4 : j * 16 + a * 4 + 4, :] = pltpu.roll(line, SIDE - left, 0)[:4, :]
    pre = dot3(split(rows[...]), (coarses[:pixels], coarses[pixels:]))
    gate = sigmoid(pre)
    slope_ref[...] = gate * (1.0 + pre * (1.0 - gate))
    projected = dot3(split(pre * gate), (projects[:width], projects[width:])).T
    projected_ref[...] = jnp.concatenate(split(projected), axis=1)
    fetch.wait()


def middle_kernel(
    projected,
    grams,
    wanted,
    first,
    tw_last,
    xw_hbm,
    tw_hbm,
    pair_hbm,
    de_hbm,
    de_ref,
    deep_ref,
    dslot_ref,
    xw,
    tw,
    taken,
    factor,
    deep,
    parts,
    xw_sems,
    tw_sems,
    out_sems,
    sems,
):
    width, count = xw.shape
    slots = dslot_ref.shape[0]
    chunks = chunk_rows(count)
    each = slots // len(chunks)
    tw_loads = [
        pltpu.make_async_copy(tw_hbm.at[:, here], tw.at[:, here], tw_sems.at[i])
        for i, here in enumerate(chunks[:-1])
    ]
    xw_loads = [
        pltpu.make_async_copy(xw_hbm.at[:, here], xw.at[:, here], xw_sems.at[i])
        for i, here in enumerate(chunks[1:])
    ]
    stores = [
        pltpu.make_async_copy(xw.at[:, here], de_hbm.at[:, here], out_sems.at[i])
        for i, here in enumerate(chunks[:-1])
    ]
    fetches = [
        pltpu.make_async_copy(pair_hbm, deep_ref.at[: 2 * width], sems.at[0]),
        pltpu.make_async_copy(pair_hbm.at[:width], deep_ref.at[2 * width :], sems.at[1]),
    ]
    for pair in zip(tw_loads, xw_loads):
        for copy in pair:
            copy.start()
    for copy in fetches:
        copy.start()

    def begin(i):
        tokens = chunks[i]
        source = first if i == 0 else xw.at[:, tokens]
        here = taking(wanted[:, tokens], slots, 0)
        taken[:slots], taken[slots:] = here, here
        spread = dot(projected[...], taken[...])
        for here in blocks(width, 32):
            pre = source[here] + spread[here]
            gate = sigmoid(pre)
            hidden = pre * gate
            factor[i % 2, here] = gate + hidden * (1.0 - gate)
            high, low = split(hidden)
            for part, value in enumerate((high, high, low)):
                deep[i % 2, shift(here, part * width)] = value

    begin(0)
    for i, tokens in enumerate(chunks):
        if i + 1 < len(chunks):
            tw_loads[i].wait()
            xw_loads[i].wait()
        minus = tw_last if i == len(chunks) - 1 else tw.at[:, tokens]
        target = de_ref if i == len(chunks) - 1 else xw.at[:, tokens]
        product = dot(grams[...], deep[i % 2])
        if i + 1 < len(chunks):
            begin(i + 1)
        for here in blocks(width, 32):
            de = (product[here] - minus[here]) * factor[i % 2, here]
            target[here] = de
            parts[here], parts[shift(here, width)] = split(de)
        mine = slice(i * each, (i + 1) * each)
        both = dot(taking(wanted[:, tokens], each, i * each), parts[...], NT)
        dslot_ref[mine] = both[:, :width] + both[:, width:]
        if i < len(stores):
            stores[i].start()
    for copy in stores + fetches:
        copy.wait()


def through(value, pair):
    count, rows = value.shape[0], pair.shape[0] // 2
    high, low = split(value)
    both = dot(jnp.concatenate([high, low], axis=0), pair[:rows], NT)
    return both[:count] + (both[count:] + dot(high, pair[rows:], NT))


def closing_kernel(dslot_ref, slope_ref, coarses, projects, lay, number, send_ref):
    grad = through(through(dslot_ref[...], projects) * slope_ref[...], coarses)
    high, low = split(jnp.concatenate([grad, number[...]], axis=1))
    send_ref[...] = dot(lay[...], high) + dot(lay[...], low)


def scatter_kernel(message_ref, done_ref, mine_ref, other_ref, total):
    del done_ref
    pixels = mine_ref.shape[2]
    message = message_ref[...]
    number = lax.broadcasted_iota(jnp.int32, (message.shape[0], SIDE * SIDE), 1).astype(F32)
    pick = jnp.where(message[:, pixels : pixels + 1] == number, 1.0, 0.0).astype(BF16)
    high, low = split(message[:, :pixels])
    total[...] = dot(pick, low, TN) + dot(pick, high, TN)
    half = mine_ref.shape[1]
    side = lax.axis_index("lvl")
    mine_ref[0] = total[pl.ds(pl.multiple_of(side * half, half), half), :]
    other_ref[0] = total[pl.ds(pl.multiple_of((1 - side) * half, half), half), :]


def last_kernel(de_hbm, first, deep, out_hbm, de, out, cat, in_sems, out_sems):
    width = de.shape[0]
    steps = de.shape[1] // ROWS

    def load(i):
        return pltpu.make_async_copy(de_hbm.at[:, chunk(i)], de.at[:, chunk(i)], in_sems.at[i])

    def store(i):
        return pltpu.make_async_copy(out.at[chunk(i)], out_hbm.at[chunk(i)], out_sems.at[i])

    def prepare(source):
        for here in blocks(width, 32):
            high, low = split(source[here])
            cat[here], cat[shift(here, width)], cat[shift(here, 2 * width)] = high, high, low

    for i in range(steps - 1):
        load(i).start()
    prepare(first)

    def step(i, _):
        mine = lax.rem(i + steps - 1, steps)
        out[chunk(mine), :] = dot(cat[...], deep[...], TN)
        store(mine).start()

        @pl.when(i + 1 < steps)
        def _():
            load(i).wait()
            prepare(de.at[:, chunk(i)])

        return 0

    lax.fori_loop(0, steps, step, 0)
    for i in range(steps):
        store(i).wait()


def fixed(*values):
    return [pltpu.with_memory_space_constraint(value, pltpu.HBM) for value in values]


def near(*values):
    return [pltpu.with_memory_space_constraint(value, pltpu.VMEM) for value in values]


def stack(blocks, before):
    shape = (len(blocks) * blocks[0].shape[0],) + blocks[0].shape[1:]
    return call(
        stack_kernel,
        "stack",
        1000,
        jax.ShapeDtypeStruct(shape, F32),
        limit=ROOM,
        in_specs=[VMEM] * len(blocks) + [HBM],
        out_specs=VMEM,
    )(*blocks, *fixed(before))


def body(coarse_input, coarse_weight, fine_input, fine_target, crops, in_weight, context_weight, out_weight):
    patch = ("far", "y", "core")
    peers = lax.axis_size(patch)
    far = peers // 4
    patches, tokens, values = fine_input.shape
    width = in_weight.shape[1]
    pixels = coarse_weight.shape[0]
    half = coarse_input.shape[1]
    count = patches * tokens
    swap = [(0, 1), (1, 0)]

    column = [coarse_input]
    for k in range(1, far):
        column.append(lax.ppermute(coarse_input, "far", [(p, (p + k) % far) for p in range(far)]))

    steps = count // ROWS
    pair_shape = (2 * width, values)
    x, t = fine_input.reshape(count, values), fine_target.reshape(count, values)
    xw, pair, rows, next_wide, crops = call(
        input_kernel,
        "input",
        6 * count * values * width,
        (
            pltpu.HBM((width, count), F32),
            pltpu.HBM(pair_shape, BF16),
            pltpu.VMEM((ROWS, values), F32),
            pltpu.VMEM((width, 3 * values), BF16),
            pltpu.VMEM((4, patches), jnp.int32),
        ),
        in_specs=[HBM] * 5,
        out_specs=(HBM, HBM, VMEM, VMEM, VMEM),
        scratch_shapes=[
            pltpu.VMEM((count, values), F32),
            pltpu.VMEM((width, count), F32),
            pltpu.VMEM((width, values), F32),
            pltpu.VMEM((width, values), F32),
            pltpu.VMEM(pair_shape, BF16),
            pltpu.VMEM((ROWS, values), BF16),
            pltpu.VMEM((ROWS, values), BF16),
            pltpu.SemaphoreType.DMA((steps,)),
            pltpu.SemaphoreType.DMA((steps,)),
            pltpu.SemaphoreType.DMA((5,)),
        ],
    )(*fixed(x, in_weight.T, t, out_weight, crops.T))
    column = stack(column, xw)
    own = [column]
    for flip in range(1, 4):
        own.append(lax.ppermute(column, ("lvl", "y"), [(p, p ^ flip) for p in range(4)]))
    tw, tw_last, coarses, projects = call(
        target_kernel,
        "target",
        6 * count * values * width,
        (
            pltpu.HBM((width, count), F32),
            pltpu.VMEM((width, ROWS), F32),
            pltpu.VMEM((2 * pixels, width), BF16),
            pltpu.VMEM((2 * width, width), BF16),
        ),
        limit=ROOM,
        in_specs=[HBM] * 3 + [VMEM] * 2,
        out_specs=(HBM, VMEM, VMEM, VMEM),
        scratch_shapes=[
            pltpu.VMEM((count, values), F32),
            pltpu.VMEM((width, count), F32),
            pltpu.VMEM((ROWS, 3 * values), BF16),
            pltpu.VMEM((pixels, width), F32),
            pltpu.VMEM((width, width), F32),
            pltpu.SemaphoreType.DMA((steps,)),
            pltpu.SemaphoreType.DMA((steps,)),
            pltpu.SemaphoreType.DMA((2,)),
        ],
    )(*fixed(t, coarse_weight, context_weight), *near(rows, next_wide))
    own = stack(own, tw).reshape(-1, pixels)
    other = lax.ppermute(own, "core", swap)
    (crops,) = near(crops)
    grams, wanted, lay, number = call(
        functools.partial(prepare_kernel, patches),
        "prepare",
        8 * values * width * width,
        (
            pltpu.VMEM((width, 3 * width), BF16),
            pltpu.VMEM((1, count), jnp.int32),
            pltpu.VMEM((peers * 16, patches * 16), BF16),
            pltpu.VMEM((patches * 16, LANES - pixels), F32),
        ),
        limit=ROOM,
        in_specs=[VMEM, SMEM, HBM],
        out_specs=(VMEM,) * 4,
    )(*near(next_wide), crops, own)

    projected, slope, first = call(
        functools.partial(context_kernel, patches, peers),
        "context",
        6 * patches * 16 * width * width,
        (
            pltpu.VMEM((width, 2 * patches * 16), BF16),
            pltpu.VMEM((patches * 16, width), F32),
            pltpu.VMEM((width, ROWS), F32),
        ),
        limit=ROOM,
        in_specs=[SMEM] + [VMEM] * 4 + [HBM],
        out_specs=(VMEM,) * 3,
        scratch_shapes=[pltpu.VMEM((patches * 16, pixels), F32), pltpu.SemaphoreType.DMA],
    )(crops, own, other, *near(coarses, projects), *fixed(xw))
    de, last_de, deep, dslot = call(
        middle_kernel,
        "middle",
        6 * count * width * width,
        (
            pltpu.HBM((width, count), F32),
            pltpu.VMEM((width, ROWS), F32),
            pltpu.VMEM((3 * width, values), BF16),
            pltpu.VMEM((patches * 16, width), F32),
        ),
        limit=ROOM,
        in_specs=[VMEM] * 5 + [HBM] * 3,
        out_specs=(HBM,) + (VMEM,) * 3,
        scratch_shapes=[
            pltpu.VMEM((width, count), F32),
            pltpu.VMEM((width, count), F32),
            pltpu.VMEM((2 * patches * 16, ROWS), BF16),
            pltpu.VMEM((2, width, ROWS), F32),
            pltpu.VMEM((2, 3 * width, ROWS), BF16),
            pltpu.VMEM((2 * width, ROWS), BF16),
            pltpu.SemaphoreType.DMA((steps,)),
            pltpu.SemaphoreType.DMA((steps,)),
            pltpu.SemaphoreType.DMA((steps,)),
            pltpu.SemaphoreType.DMA((2,)),
        ],
    )(*near(projected, grams, wanted, first, tw_last), *fixed(xw, tw, pair))
    back = call(
        closing_kernel,
        "closing",
        6 * patches * 16 * width * width,
        jax.ShapeDtypeStruct((peers * 16, LANES), F32),
        limit=ROOM,
        in_specs=[VMEM] * 6,
        out_specs=VMEM,
    )(*near(dslot, slope, coarses, projects, lay, number))
    returned = lax.all_to_all(back, patch, 0, 0, tiled=True)

    fine_grad = call(
        last_kernel,
        "last",
        6 * count * values * width,
        pltpu.HBM((count, values), F32),
        limit=ROOM,
        in_specs=[HBM, VMEM, VMEM],
        out_specs=HBM,
        scratch_shapes=[
            pltpu.VMEM((width, count), F32),
            pltpu.VMEM((count, values), F32),
            pltpu.VMEM((3 * width, ROWS), BF16),
            pltpu.SemaphoreType.DMA((steps,)),
            pltpu.SemaphoreType.DMA((steps,)),
        ],
    )(*fixed(de), *near(last_de, deep))
    part = (1, half, pixels)
    mine, theirs = call(
        scatter_kernel,
        "scatter",
        10000,
        (jax.ShapeDtypeStruct(part, F32), jax.ShapeDtypeStruct(part, F32)),
        limit=ROOM,
        in_specs=[VMEM, HBM],
        out_specs=(VMEM, VMEM),
        scratch_shapes=[pltpu.VMEM((SIDE * SIDE, pixels), F32)],
    )(returned, *fixed(fine_grad))
    coarse_grad = mine + lax.ppermute(theirs, "lvl", swap)
    return (coarse_grad, fine_grad.reshape(fine_input.shape))


def solution(mesh):
    sides, peers = mesh.shape["lvl"], mesh.shape["patch"]
    fine = jax.sharding.Mesh(mesh.devices.reshape(sides, peers // 4, 2, 2), ("lvl", "far", "y", "core"))
    patch = ("far", "y", "core")
    both = ("lvl",) + patch
    in_specs = (
        P(patch, "lvl", None),
        P(),
        P(both, None, None),
        P(both, None, None),
        P(both, None),
        P(),
        P(),
        P(),
    )
    out_specs = (P(patch, "lvl", None), P(both, None, None))
    return jax.shard_map(body, mesh=fine, in_specs=in_specs, out_specs=out_specs, check_vma=False)
```

```python
import functools
import math

import jax
import jax.numpy as jnp
from jax import lax
from jax.experimental import pallas as pl
from jax.experimental.pallas import tpu as pltpu
from jax.sharding import PartitionSpec as P

F32 = jnp.float32
BF16 = jnp.bfloat16
NN = (((1,), (0,)), ((), ()))
NT = (((1,), (1,)), ((), ()))
TN = (((0,), (0,)), ((), ()))
ROWS = 512
SIDE = 8
LANES = 256
LIMIT = 60 * 1024 * 1024
ROOM = 40 * 1024 * 1024
SMEM = pl.BlockSpec(memory_space=pltpu.SMEM)
VMEM = pl.BlockSpec(memory_space=pltpu.VMEM)
HBM = pl.BlockSpec(memory_space=pltpu.HBM)


def split(value):
    high = value.astype(BF16)
    low = (value - high.astype(F32)).astype(BF16)
    return high, low


def dot(left, right, dims=NN):
    return lax.dot_general(left, right, dims, preferred_element_type=F32)


def dot3(left, right, dims=NN):
    return (
        dot(left[0], right[1], dims) + dot(left[1], right[0], dims) + dot(left[0], right[0], dims)
    )


def side_by_side(value):
    high, low = split(value)
    return jnp.concatenate([high, low, high], axis=1)


def sigmoid(value):
    return 0.5 * jnp.tanh(0.5 * value) + 0.5


def call(kernel, name, flops, out_shape, limit=LIMIT, **kwargs):
    moved = 8 * sum(math.prod(s.shape) for s in jax.tree.leaves(out_shape))
    return pl.pallas_call(
        kernel,
        out_shape=out_shape,
        name=name,
        cost_estimate=pl.CostEstimate(flops=flops, bytes_accessed=moved, transcendentals=0),
        compiler_params=pltpu.CompilerParams(vmem_limit_bytes=limit),
        **kwargs,
    )


def blocks(rows, size):
    return [slice(start, start + size) for start in range(0, rows, size)]


def shift(here, by):
    return slice(here.start + by, here.stop + by)


def pair_product(pair, value, dims):
    rows = pair.shape[0] // 2
    high, low = split(value)
    both = dot(pair[...], high, dims)
    return both[:rows] + (both[rows:] + dot(pair[:rows], low, dims))


def chunk(i):
    return pl.ds(pl.multiple_of(i * ROWS, ROWS), ROWS)


def fill_wide(ref, high, low):
    values = high.shape[1]
    ref[:, :values], ref[:, values : 2 * values], ref[:, 2 * values :] = high, low, high


def deep_product(wide, value, deep, out):
    values = value.shape[1]
    for here in blocks(deep.shape[0], 16):
        high, low = split(value[here])
        deep[here, :values], deep[here, values : 2 * values], deep[here, 2 * values :] = high, high, low
    out[...] = dot(wide[...], deep[...], NT)


def input_kernel(
    x_hbm,
    weight_hbm,
    t_hbm,
    next_weight_hbm,
    crops_hbm,
    out_hbm,
    pair_hbm,
    next_rows,
    next_wide,
    crops,
    x,
    out,
    weight,
    next_weight,
    pair,
    wide,
    deep,
    in_sems,
    out_sems,
    sems,
):
    width = weight.shape[0]
    chunks = chunk_rows(x.shape[0])
    fetch = pltpu.make_async_copy(weight_hbm, weight, sems.at[0])
    keep = pltpu.make_async_copy(pair, pair_hbm, sems.at[1])
    fetch_next = pltpu.make_async_copy(next_weight_hbm, next_weight, sems.at[2])
    fetch_rows = pltpu.make_async_copy(t_hbm.at[: next_rows.shape[0]], next_rows, sems.at[3])
    fetch_crops = pltpu.make_async_copy(crops_hbm, crops, sems.at[4])
    loads = [
        pltpu.make_async_copy(x_hbm.at[here], x.at[here], in_sems.at[i]) for i, here in enumerate(chunks)
    ]
    stores = [
        pltpu.make_async_copy(out.at[:, here], out_hbm.at[:, here], out_sems.at[i])
        for i, here in enumerate(chunks)
    ]
    fetch.start()
    loads[0].start()
    fetch.wait()
    for copy in loads[1:] + [fetch_next, fetch_crops, fetch_rows]:
        copy.start()
    high, low = split(weight[...])
    fill_wide(wide, high, low)
    pair[:width], pair[width:] = high, low
    keep.start()
    for i, here in enumerate(chunks):
        loads[i].wait()
        if i == len(chunks) - 1:
            fetch_next.wait()
            fill_wide(next_wide, *split(next_weight[...]))
        deep_product(wide, x.at[here], deep, out.at[:, here])
        stores[i].start()
    for copy in [keep, fetch_rows, fetch_crops] + stores:
        copy.wait()


def target_kernel(
    t_hbm,
    cwgt_hbm,
    xwgt_hbm,
    rows,
    wide,
    out_hbm,
    out_last,
    coarses,
    projects,
    t,
    out,
    deep,
    cwgt,
    xwgt,
    in_sems,
    out_sems,
    sems,
):
    chunks = chunk_rows(t.shape[0])
    fetches = [
        pltpu.make_async_copy(cwgt_hbm, cwgt, sems.at[0]),
        pltpu.make_async_copy(xwgt_hbm, xwgt, sems.at[1]),
    ]
    loads = [
        pltpu.make_async_copy(t_hbm.at[here], t.at[here], in_sems.at[i])
        for i, here in enumerate(chunks[1:])
    ]
    stores = [
        pltpu.make_async_copy(out.at[:, here], out_hbm.at[:, here], out_sems.at[i])
        for i, here in enumerate(chunks[:-1])
    ]
    for copy in loads + fetches:
        copy.start()
    for i, here in enumerate(chunks):
        if i > 0:
            loads[i - 1].wait()
        source = rows if i == 0 else t.at[here]
        if i < len(stores):
            deep_product(wide, source, deep, out.at[:, here])
            stores[i].start()
        else:
            deep_product(wide, source, deep, out_last)
    for copy in fetches:
        copy.wait()
    coarses[...] = jnp.concatenate(split(cwgt[...]), axis=0)
    projects[...] = jnp.concatenate(split(xwgt[...]), axis=0)
    for copy in stores:
        copy.wait()


def chunk_rows(count):
    return [slice(start, start + ROWS) for start in range(0, count, ROWS)]


def prepare_kernel(patches, wide, crops_ref, before_ref, grams, wanted, lay, number):
    del before_ref
    width = grams.shape[0]
    values = wide.shape[1] // 3
    high = wide[:, :values]
    mixed = dot(wide[:, values : 2 * values], high, NT)
    grams[...] = side_by_side(dot(high, high, NT) + (mixed + mixed.T))
    wanted[...] = slot_row(crops_ref, patches, wanted.shape[1] // patches)
    frame = row_value(crops_ref, 0, patches, (1, patches * 16), 1, 16)
    slot = lax.broadcasted_iota(jnp.int32, (1, patches * 16), 1) % 16
    line = lax.broadcasted_iota(jnp.int32, lay.shape, 0)
    lay[...] = jnp.where(line == frame * 16 + slot, 1.0, 0.0).astype(BF16)
    slot = lax.broadcasted_iota(jnp.int32, number.shape, 0) % 16
    top = row_value(crops_ref, 1, patches, number.shape, 0, 16)
    left = row_value(crops_ref, 2, patches, number.shape, 0, 16)
    number[...] = ((top + slot // 4) * SIDE + left + slot % 4).astype(F32)


def stack_kernel(*refs):
    *block_refs, _, out_ref = refs
    size = block_refs[0].shape[0]
    for k, ref in enumerate(block_refs):
        out_ref[k * size : (k + 1) * size] = ref[...]


def pack_kernel(*refs):
    *block_refs, _, out_ref = refs
    tokens = block_refs[0].shape[1]
    size = tokens * 3 // 2
    for k, ref in enumerate(block_refs):
        out_ref[k * size : k * size + tokens] = ref[0, :, :128]
        tails = [ref[0, : tokens // 2, 128:], ref[0, tokens // 2 :, 128:]]
        out_ref[k * size + tokens : (k + 1) * size] = jnp.concatenate(tails, axis=1)


def row_value(crops_ref, column, patches, shape, axis, each):
    index = lax.broadcasted_iota(jnp.int32, shape, axis) // each
    found = jnp.zeros(shape, jnp.int32)
    for j in range(patches):
        found = jnp.where(index == j, crops_ref[column, j], found)
    return found


def slot_row(crops_ref, patches, tokens):
    scale = row_value(crops_ref, 3, patches, (1, patches * tokens), 1, tokens)
    token = lax.broadcasted_iota(jnp.int32, (1, patches * tokens), 1)
    row, column = (token % tokens) // 16, token % 16
    return token // tokens * 16 + (row * scale // 8) * 4 + column * scale // 8


def taking(wanted, slots, first):
    slot = lax.broadcasted_iota(jnp.int32, (slots, wanted.shape[1]), 0) + first
    return jnp.where(slot == wanted, 1.0, 0.0).astype(BF16)


def context_kernel(
    patches,
    peers,
    crops_ref,
    own_ref,
    other_ref,
    coarses,
    projects,
    xw_hbm,
    projected_ref,
    slope_ref,
    first_ref,
    rows,
    sem,
):
    fetch = pltpu.make_async_copy(xw_hbm.at[:, : first_ref.shape[1]], first_ref, sem)
    fetch.start()
    pixels = coarses.shape[0] // 2
    width = projects.shape[1]
    far = peers // 4
    me, side = lax.axis_index(("far", "y", "core")), lax.axis_index("lvl")
    for j in range(patches):
        frame, top, left = crops_ref[0, j], crops_ref[1, j], crops_ref[2, j]
        near_by = lax.bitwise_xor(frame % 4, me % 4)
        k = (me // 4 - frame // 4 + far) % far
        here = near_by % 2 == 0
        for a in range(4):
            row = jnp.minimum(top + a, SIDE - 1)
            shard = (lax.bitwise_xor(row // 4, side) * 2 + near_by // 2) * far + k
            row = row % 4
            start = shard * (6 * SIDE)
            wide = pl.ds(pl.multiple_of(start + row * SIDE, SIDE), SIDE)
            tail = pl.ds(pl.multiple_of(start + (4 + row % 2) * SIDE, SIDE), SIDE)
            into = slice(j * 16 + a * 4, j * 16 + a * 4 + 4)
            line = jnp.where(here, own_ref[wide, :], other_ref[wide, :])
            rows[into, :128] = pltpu.roll(line, SIDE - left, 0)[:4, :]
            line = pltpu.roll(jnp.where(here, own_ref[tail, :], other_ref[tail, :]), SIDE - left, 0)[:4, :]
            rows[into, 128:] = jnp.where(row >= 2, line[:, 64:], line[:, :64])
    pre = through(rows[...], coarses, NN)
    gate = sigmoid(pre)
    slope_ref[...] = gate * (1.0 + pre * (1.0 - gate))
    projected = through(pre * gate, projects, NN).T
    projected_ref[...] = jnp.concatenate(split(projected), axis=1)
    fetch.wait()


def middle_kernel(
    projected,
    grams,
    wanted,
    first,
    tw_last,
    xw_hbm,
    tw_hbm,
    pair_hbm,
    de_hbm,
    de_ref,
    deep_ref,
    dslot_ref,
    xw,
    tw,
    taken,
    factor,
    deep,
    parts,
    xw_sems,
    tw_sems,
    out_sems,
    sems,
):
    width, count = xw.shape
    slots = dslot_ref.shape[0]
    chunks = chunk_rows(count)
    each = slots // len(chunks)
    tw_loads = [
        pltpu.make_async_copy(tw_hbm.at[:, here], tw.at[:, here], tw_sems.at[i])
        for i, here in enumerate(chunks[:-1])
    ]
    xw_loads = [
        pltpu.make_async_copy(xw_hbm.at[:, here], xw.at[:, here], xw_sems.at[i])
        for i, here in enumerate(chunks[1:])
    ]
    stores = [
        pltpu.make_async_copy(xw.at[:, here], de_hbm.at[:, here], out_sems.at[i])
        for i, here in enumerate(chunks[:-1])
    ]
    fetches = [
        pltpu.make_async_copy(pair_hbm, deep_ref.at[: 2 * width], sems.at[0]),
        pltpu.make_async_copy(pair_hbm.at[:width], deep_ref.at[2 * width :], sems.at[1]),
    ]
    for pair in zip(tw_loads, xw_loads):
        for copy in pair:
            copy.start()
    for copy in fetches:
        copy.start()

    def begin(i):
        tokens = chunks[i]
        source = first if i == 0 else xw.at[:, tokens]
        here = taking(wanted[:, tokens], slots, 0)
        taken[:slots], taken[slots:] = here, here
        spread = dot(projected[...], taken[...])
        for here in blocks(width, 32):
            pre = source[here] + spread[here]
            gate = sigmoid(pre)
            hidden = pre * gate
            factor[i % 2, here] = gate + hidden * (1.0 - gate)
            high, low = split(hidden)
            for part, value in enumerate((high, high, low)):
                deep[i % 2, shift(here, part * width)] = value

    begin(0)
    for i, tokens in enumerate(chunks):
        if i + 1 < len(chunks):
            tw_loads[i].wait()
            xw_loads[i].wait()
        minus = tw_last if i == len(chunks) - 1 else tw.at[:, tokens]
        target = de_ref if i == len(chunks) - 1 else xw.at[:, tokens]
        product = dot(grams[...], deep[i % 2])
        if i + 1 < len(chunks):
            begin(i + 1)
        for here in blocks(width, 32):
            de = (product[here] - minus[here]) * factor[i % 2, here]
            target[here] = de
            parts[here], parts[shift(here, width)] = split(de)
        mine = slice(i * each, (i + 1) * each)
        both = dot(taking(wanted[:, tokens], each, i * each), parts[...], NT)
        dslot_ref[mine] = both[:, :width] + both[:, width:]
        if i < len(stores):
            stores[i].start()
    for copy in stores + fetches:
        copy.wait()


def through(value, pair, dims):
    count, rows = value.shape[0], pair.shape[0] // 2
    high, low = split(value)
    both = dot(jnp.concatenate([high, low], axis=0), pair[:rows], dims)
    return both[:count] + (both[count:] + dot(high, pair[rows:], dims))


def closing_kernel(dslot_ref, slope_ref, coarses, projects, lay, number, send_ref):
    grad = through(through(dslot_ref[...], projects, NT) * slope_ref[...], coarses, NT)
    high, low = split(jnp.concatenate([grad, number[...]], axis=1))
    send_ref[...] = dot(lay[...], high) + dot(lay[...], low)


def scatter_kernel(message_ref, done_ref, mine_ref, other_ref, total):
    del done_ref
    pixels = mine_ref.shape[2]
    message = message_ref[...]
    number = lax.broadcasted_iota(jnp.int32, (message.shape[0], SIDE * SIDE), 1).astype(F32)
    pick = jnp.where(message[:, pixels : pixels + 1] == number, 1.0, 0.0).astype(BF16)
    high, low = split(message[:, :pixels])
    total[...] = dot(pick, low, TN) + dot(pick, high, TN)
    half = mine_ref.shape[1]
    side = lax.axis_index("lvl")
    mine_ref[0] = total[pl.ds(pl.multiple_of(side * half, half), half), :]
    other_ref[0] = total[pl.ds(pl.multiple_of((1 - side) * half, half), half), :]


def last_kernel(de_hbm, first, deep, out_hbm, de, out, cat, in_sems, out_sems):
    width = de.shape[0]
    steps = de.shape[1] // ROWS

    def load(i):
        return pltpu.make_async_copy(de_hbm.at[:, chunk(i)], de.at[:, chunk(i)], in_sems.at[i])

    def store(i):
        return pltpu.make_async_copy(out.at[chunk(i)], out_hbm.at[chunk(i)], out_sems.at[i])

    def prepare(source):
        for here in blocks(width, 32):
            high, low = split(source[here])
            cat[here], cat[shift(here, width)], cat[shift(here, 2 * width)] = high, high, low

    for i in range(steps - 1):
        load(i).start()
    prepare(first)

    def step(i, _):
        mine = lax.rem(i + steps - 1, steps)
        out[chunk(mine), :] = dot(cat[...], deep[...], TN)
        store(mine).start()

        @pl.when(i + 1 < steps)
        def _():
            load(i).wait()
            prepare(de.at[:, chunk(i)])

        return 0

    lax.fori_loop(0, steps, step, 0)
    for i in range(steps):
        store(i).wait()


def fixed(*values):
    return [pltpu.with_memory_space_constraint(value, pltpu.HBM) for value in values]


def near(*values):
    return [pltpu.with_memory_space_constraint(value, pltpu.VMEM) for value in values]


def stack(kernel, blocks, before, rows):
    shape = (len(blocks) * rows, 128)
    return call(
        kernel,
        "stack",
        1000,
        jax.ShapeDtypeStruct(shape, F32),
        limit=ROOM,
        in_specs=[VMEM] * len(blocks) + [HBM],
        out_specs=VMEM,
    )(*blocks, *fixed(before))


def body(coarse_input, coarse_weight, fine_input, fine_target, crops, in_weight, context_weight, out_weight):
    patch = ("far", "y", "core")
    peers = lax.axis_size(patch)
    far = peers // 4
    patches, tokens, values = fine_input.shape
    width = in_weight.shape[1]
    pixels = coarse_weight.shape[0]
    half = coarse_input.shape[1]
    count = patches * tokens
    swap = [(0, 1), (1, 0)]

    column = [coarse_input]
    for k in range(1, far):
        column.append(lax.ppermute(coarse_input, "far", [(p, (p + k) % far) for p in range(far)]))

    steps = count // ROWS
    pair_shape = (2 * width, values)
    x, t = fine_input.reshape(count, values), fine_target.reshape(count, values)
    xw, pair, rows, next_wide, crops = call(
        input_kernel,
        "input",
        6 * count * values * width,
        (
            pltpu.HBM((width, count), F32),
            pltpu.HBM(pair_shape, BF16),
            pltpu.VMEM((ROWS, values), F32),
            pltpu.VMEM((width, 3 * values), BF16),
            pltpu.VMEM((4, patches), jnp.int32),
        ),
        in_specs=[HBM] * 5,
        out_specs=(HBM, HBM, VMEM, VMEM, VMEM),
        scratch_shapes=[
            pltpu.VMEM((count, values), F32),
            pltpu.VMEM((width, count), F32),
            pltpu.VMEM((width, values), F32),
            pltpu.VMEM((width, values), F32),
            pltpu.VMEM(pair_shape, BF16),
            pltpu.VMEM((width, 3 * values), BF16),
            pltpu.VMEM((ROWS, 3 * values), BF16),
            pltpu.SemaphoreType.DMA((steps,)),
            pltpu.SemaphoreType.DMA((steps,)),
            pltpu.SemaphoreType.DMA((5,)),
        ],
    )(*fixed(x, in_weight.T, t, out_weight, crops.T))
    column = stack(pack_kernel, column, xw, half * 3 // 2)
    own = [column]
    for flip in range(1, 4):
        own.append(lax.ppermute(column, ("lvl", "y"), [(p, p ^ flip) for p in range(4)]))
    tw, tw_last, coarses, projects = call(
        target_kernel,
        "target",
        6 * count * values * width,
        (
            pltpu.HBM((width, count), F32),
            pltpu.VMEM((width, ROWS), F32),
            pltpu.VMEM((2 * pixels, width), BF16),
            pltpu.VMEM((2 * width, width), BF16),
        ),
        limit=ROOM,
        in_specs=[HBM] * 3 + [VMEM] * 2,
        out_specs=(HBM, VMEM, VMEM, VMEM),
        scratch_shapes=[
            pltpu.VMEM((count, values), F32),
            pltpu.VMEM((width, count), F32),
            pltpu.VMEM((ROWS, 3 * values), BF16),
            pltpu.VMEM((pixels, width), F32),
            pltpu.VMEM((width, width), F32),
            pltpu.SemaphoreType.DMA((steps,)),
            pltpu.SemaphoreType.DMA((steps,)),
            pltpu.SemaphoreType.DMA((2,)),
        ],
    )(*fixed(t, coarse_weight, context_weight), *near(rows, next_wide))
    own = stack(stack_kernel, own, tw, column.shape[0])
    other = lax.ppermute(own, "core", swap)
    (crops,) = near(crops)
    grams, wanted, lay, number = call(
        functools.partial(prepare_kernel, patches),
        "prepare",
        8 * values * width * width,
        (
            pltpu.VMEM((width, 3 * width), BF16),
            pltpu.VMEM((1, count), jnp.int32),
            pltpu.VMEM((peers * 16, patches * 16), BF16),
            pltpu.VMEM((patches * 16, LANES - pixels), F32),
        ),
        limit=ROOM,
        in_specs=[VMEM, SMEM, HBM],
        out_specs=(VMEM,) * 4,
    )(*near(next_wide), crops, own)

    projected, slope, first = call(
        functools.partial(context_kernel, patches, peers),
        "context",
        6 * patches * 16 * width * width,
        (
            pltpu.VMEM((width, 2 * patches * 16), BF16),
            pltpu.VMEM((patches * 16, width), F32),
            pltpu.VMEM((width, ROWS), F32),
        ),
        limit=ROOM,
        in_specs=[SMEM] + [VMEM] * 4 + [HBM],
        out_specs=(VMEM,) * 3,
        scratch_shapes=[pltpu.VMEM((patches * 16, pixels), F32), pltpu.SemaphoreType.DMA],
    )(crops, own, other, *near(coarses, projects), *fixed(xw))
    de, last_de, deep, dslot = call(
        middle_kernel,
        "middle",
        6 * count * width * width,
        (
            pltpu.HBM((width, count), F32),
            pltpu.VMEM((width, ROWS), F32),
            pltpu.VMEM((3 * width, values), BF16),
            pltpu.VMEM((patches * 16, width), F32),
        ),
        limit=ROOM,
        in_specs=[VMEM] * 5 + [HBM] * 3,
        out_specs=(HBM,) + (VMEM,) * 3,
        scratch_shapes=[
            pltpu.VMEM((width, count), F32),
            pltpu.VMEM((width, count), F32),
            pltpu.VMEM((2 * patches * 16, ROWS), BF16),
            pltpu.VMEM((2, width, ROWS), F32),
            pltpu.VMEM((2, 3 * width, ROWS), BF16),
            pltpu.VMEM((2 * width, ROWS), BF16),
            pltpu.SemaphoreType.DMA((steps,)),
            pltpu.SemaphoreType.DMA((steps,)),
            pltpu.SemaphoreType.DMA((steps,)),
            pltpu.SemaphoreType.DMA((2,)),
        ],
    )(*near(projected, grams, wanted, first, tw_last), *fixed(xw, tw, pair))
    back = call(
        closing_kernel,
        "closing",
        6 * patches * 16 * width * width,
        jax.ShapeDtypeStruct((peers * 16, LANES), F32),
        limit=ROOM,
        in_specs=[VMEM] * 6,
        out_specs=VMEM,
    )(*near(dslot, slope, coarses, projects, lay, number))
    returned = lax.all_to_all(back, patch, 0, 0, tiled=True)

    fine_grad = call(
        last_kernel,
        "last",
        6 * count * values * width,
        pltpu.HBM((count, values), F32),
        limit=ROOM,
        in_specs=[HBM, VMEM, VMEM],
        out_specs=HBM,
        scratch_shapes=[
            pltpu.VMEM((width, count), F32),
            pltpu.VMEM((count, values), F32),
            pltpu.VMEM((3 * width, ROWS), BF16),
            pltpu.SemaphoreType.DMA((steps,)),
            pltpu.SemaphoreType.DMA((steps,)),
        ],
    )(*fixed(de), *near(last_de, deep))
    part = (1, half, pixels)
    mine, theirs = call(
        scatter_kernel,
        "scatter",
        10000,
        (jax.ShapeDtypeStruct(part, F32), jax.ShapeDtypeStruct(part, F32)),
        limit=ROOM,
        in_specs=[VMEM, HBM],
        out_specs=(VMEM, VMEM),
        scratch_shapes=[pltpu.VMEM((SIDE * SIDE, pixels), F32)],
    )(returned, *fixed(fine_grad))
    coarse_grad = mine + lax.ppermute(theirs, "lvl", swap)
    return (coarse_grad, fine_grad.reshape(fine_input.shape))


def solution(mesh):
    sides, peers = mesh.shape["lvl"], mesh.shape["patch"]
    fine = jax.sharding.Mesh(mesh.devices.reshape(sides, peers // 4, 2, 2), ("lvl", "far", "y", "core"))
    patch = ("far", "y", "core")
    both = ("lvl",) + patch
    in_specs = (
        P(patch, "lvl", None),
        P(),
        P(both, None, None),
        P(both, None, None),
        P(both, None),
        P(),
        P(),
        P(),
    )
    out_specs = (P(patch, "lvl", None), P(both, None, None))
    return jax.shard_map(body, mesh=fine, in_specs=in_specs, out_specs=out_specs, check_vma=False)
```

```python
import functools
import math

import jax
import jax.numpy as jnp
from jax import lax
from jax.experimental import pallas as pl
from jax.experimental.pallas import tpu as pltpu
from jax.sharding import PartitionSpec as P

F32 = jnp.float32
BF16 = jnp.bfloat16
NN = (((1,), (0,)), ((), ()))
NT = (((1,), (1,)), ((), ()))
TN = (((0,), (0,)), ((), ()))
ROWS = 512
SIDE = 8
LANES = 256
LIMIT = 60 * 1024 * 1024
ROOM = 40 * 1024 * 1024
SMEM = pl.BlockSpec(memory_space=pltpu.SMEM)
VMEM = pl.BlockSpec(memory_space=pltpu.VMEM)
HBM = pl.BlockSpec(memory_space=pltpu.HBM)


def split(value):
    high = value.astype(BF16)
    low = (value - high.astype(F32)).astype(BF16)
    return high, low


def dot(left, right, dims=NN):
    return lax.dot_general(left, right, dims, preferred_element_type=F32)


def dot3(left, right, dims=NN):
    return (
        dot(left[0], right[1], dims) + dot(left[1], right[0], dims) + dot(left[0], right[0], dims)
    )


def side_by_side(value):
    high, low = split(value)
    return jnp.concatenate([high, low, high], axis=1)


def sigmoid(value):
    return 0.5 * jnp.tanh(0.5 * value) + 0.5


def call(kernel, name, flops, out_shape, limit=LIMIT, **kwargs):
    moved = 8 * sum(math.prod(s.shape) for s in jax.tree.leaves(out_shape))
    return pl.pallas_call(
        kernel,
        out_shape=out_shape,
        name=name,
        cost_estimate=pl.CostEstimate(flops=flops, bytes_accessed=moved, transcendentals=0),
        compiler_params=pltpu.CompilerParams(vmem_limit_bytes=limit),
        **kwargs,
    )


def blocks(rows, size):
    return [slice(start, start + size) for start in range(0, rows, size)]


def shift(here, by):
    return slice(here.start + by, here.stop + by)


def pair_product(pair, value, dims):
    rows = pair.shape[0] // 2
    high, low = split(value)
    both = dot(pair[...], high, dims)
    return both[:rows] + (both[rows:] + dot(pair[:rows], low, dims))


def chunk(i):
    return pl.ds(pl.multiple_of(i * ROWS, ROWS), ROWS)


def fill_wide(ref, high, low):
    values = high.shape[1]
    ref[:, :values], ref[:, values : 2 * values], ref[:, 2 * values :] = high, low, high


def deep_product(wide, value, deep, out, following=()):
    values = value.shape[1]
    for here in blocks(deep.shape[0], 16):
        high, low = split(value[here])
        deep[here, :values], deep[here, values : 2 * values], deep[here, 2 * values :] = high, high, low
    for copy in following:
        copy.start()
    out[...] = dot(wide[...], deep[...], NT)


def input_kernel(
    x_hbm,
    weight_hbm,
    t_hbm,
    next_weight_hbm,
    crops_hbm,
    out_hbm,
    pair_hbm,
    next_rows,
    next_wide,
    crops,
    x,
    out,
    weight,
    next_weight,
    pair,
    wide,
    deep,
    in_sems,
    out_sems,
    sems,
):
    width = weight.shape[0]
    chunks = chunk_rows(x.shape[0])
    fetch = pltpu.make_async_copy(weight_hbm, weight, sems.at[0])
    keep = pltpu.make_async_copy(pair, pair_hbm, sems.at[1])
    fetch_next = pltpu.make_async_copy(next_weight_hbm, next_weight, sems.at[2])
    fetch_rows = pltpu.make_async_copy(t_hbm.at[: next_rows.shape[0]], next_rows, sems.at[3])
    fetch_crops = pltpu.make_async_copy(crops_hbm, crops, sems.at[4])
    loads = [
        pltpu.make_async_copy(x_hbm.at[here], x.at[here], in_sems.at[i]) for i, here in enumerate(chunks)
    ]
    stores = [
        pltpu.make_async_copy(out.at[:, here], out_hbm.at[:, here], out_sems.at[i])
        for i, here in enumerate(chunks)
    ]
    fetch.start()
    loads[0].start()
    fetch.wait()
    loads[1].start()
    later = [[load] for load in loads[2:]] + [[fetch_rows, fetch_crops], []]
    later[0].append(fetch_next)
    high, low = split(weight[...])
    fill_wide(wide, high, low)
    pair[:width], pair[width:] = high, low
    keep.start()
    for i, here in enumerate(chunks):
        loads[i].wait()
        if i == len(chunks) - 1:
            fetch_next.wait()
            fill_wide(next_wide, *split(next_weight[...]))
        deep_product(wide, x.at[here], deep, out.at[:, here], later[i])
        stores[i].start()
    for copy in [keep, fetch_rows, fetch_crops] + stores:
        copy.wait()


def target_kernel(
    t_hbm,
    cwgt_hbm,
    xwgt_hbm,
    rows,
    wide,
    out_hbm,
    out_last,
    coarses,
    projects,
    t,
    out,
    deep,
    cwgt,
    xwgt,
    in_sems,
    out_sems,
    sems,
):
    chunks = chunk_rows(t.shape[0])
    fetches = [
        pltpu.make_async_copy(cwgt_hbm, cwgt, sems.at[0]),
        pltpu.make_async_copy(xwgt_hbm, xwgt, sems.at[1]),
    ]
    loads = [
        pltpu.make_async_copy(t_hbm.at[here], t.at[here], in_sems.at[i])
        for i, here in enumerate(chunks[1:])
    ]
    stores = [
        pltpu.make_async_copy(out.at[:, here], out_hbm.at[:, here], out_sems.at[i])
        for i, here in enumerate(chunks[:-1])
    ]
    loads[0].start()
    later = [[load] for load in loads[1:]] + [fetches, []]
    for i, here in enumerate(chunks):
        if i > 0:
            loads[i - 1].wait()
        source = rows if i == 0 else t.at[here]
        if i < len(stores):
            deep_product(wide, source, deep, out.at[:, here], later[i])
            stores[i].start()
        else:
            deep_product(wide, source, deep, out_last)
    for copy in fetches:
        copy.wait()
    coarses[...] = jnp.concatenate(split(cwgt[...]), axis=0)
    projects[...] = jnp.concatenate(split(xwgt[...]), axis=0)
    for copy in stores:
        copy.wait()


def chunk_rows(count):
    return [slice(start, start + ROWS) for start in range(0, count, ROWS)]


def prepare_kernel(patches, wide, crops_ref, before_ref, grams, wanted, lay, number):
    del before_ref
    width = grams.shape[0]
    values = wide.shape[1] // 3
    high = wide[:, :values]
    mixed = dot(wide[:, values : 2 * values], high, NT)
    grams[...] = side_by_side(dot(high, high, NT) + (mixed + mixed.T))
    wanted[...] = slot_row(crops_ref, patches, wanted.shape[1] // patches)
    frame = row_value(crops_ref, 0, patches, (1, patches * 16), 1, 16)
    slot = lax.broadcasted_iota(jnp.int32, (1, patches * 16), 1) % 16
    line = lax.broadcasted_iota(jnp.int32, lay.shape, 0)
    lay[...] = jnp.where(line == frame * 16 + slot, 1.0, 0.0).astype(BF16)
    slot = lax.broadcasted_iota(jnp.int32, number.shape, 0) % 16
    top = row_value(crops_ref, 1, patches, number.shape, 0, 16)
    left = row_value(crops_ref, 2, patches, number.shape, 0, 16)
    number[...] = ((top + slot // 4) * SIDE + left + slot % 4).astype(F32)


def stack_kernel(*refs):
    *block_refs, _, out_ref = refs
    size = block_refs[0].shape[0]
    for k, ref in enumerate(block_refs):
        out_ref[k * size : (k + 1) * size] = ref[...]


def pack_kernel(*refs):
    *block_refs, _, out_ref = refs
    tokens = block_refs[0].shape[1]
    size = tokens * 3 // 2
    for k, ref in enumerate(block_refs):
        out_ref[k * size : k * size + tokens] = ref[0, :, :128]
        tails = [ref[0, : tokens // 2, 128:], ref[0, tokens // 2 :, 128:]]
        out_ref[k * size + tokens : (k + 1) * size] = jnp.concatenate(tails, axis=1)


def row_value(crops_ref, column, patches, shape, axis, each):
    index = lax.broadcasted_iota(jnp.int32, shape, axis) // each
    found = jnp.zeros(shape, jnp.int32)
    for j in range(patches):
        found = jnp.where(index == j, crops_ref[column, j], found)
    return found


def slot_row(crops_ref, patches, tokens):
    scale = row_value(crops_ref, 3, patches, (1, patches * tokens), 1, tokens)
    token = lax.broadcasted_iota(jnp.int32, (1, patches * tokens), 1)
    row, column = (token % tokens) // 16, token % 16
    return token // tokens * 16 + (row * scale // 8) * 4 + column * scale // 8


def taking(wanted, slots, first):
    slot = lax.broadcasted_iota(jnp.int32, (slots, wanted.shape[1]), 0) + first
    return jnp.where(slot == wanted, 1.0, 0.0).astype(BF16)


def context_kernel(
    patches,
    peers,
    crops_ref,
    own_ref,
    other_ref,
    coarses,
    projects,
    xw_hbm,
    tw_hbm,
    projected_ref,
    slope_ref,
    xw,
    tw,
    rows,
    sems,
):
    fetches = [
        pltpu.make_async_copy(xw_hbm, xw, sems.at[0]),
        pltpu.make_async_copy(tw_hbm.at[:, : tw.shape[1]], tw, sems.at[1]),
    ]
    for copy in fetches:
        copy.start()
    pixels = coarses.shape[0] // 2
    width = projects.shape[1]
    far = peers // 4
    me, side = lax.axis_index(("far", "y", "core")), lax.axis_index("lvl")
    for j in range(patches):
        frame, top, left = crops_ref[0, j], crops_ref[1, j], crops_ref[2, j]
        near_by = lax.bitwise_xor(frame % 4, me % 4)
        k = lax.bitwise_xor(frame // 4, me // 4)
        here = near_by % 2 == 0
        for a in range(4):
            row = jnp.minimum(top + a, SIDE - 1)
            shard = (lax.bitwise_xor(row // 4, side) * 2 + near_by // 2) * far + k
            row = row % 4
            start = shard * (6 * SIDE)
            wide = pl.ds(pl.multiple_of(start + row * SIDE, SIDE), SIDE)
            tail = pl.ds(pl.multiple_of(start + (4 + row % 2) * SIDE, SIDE), SIDE)
            into = slice(j * 16 + a * 4, j * 16 + a * 4 + 4)
            line = jnp.where(here, own_ref[wide, :], other_ref[wide, :])
            rows[into, :128] = pltpu.roll(line, SIDE - left, 0)[:4, :]
            line = pltpu.roll(jnp.where(here, own_ref[tail, :], other_ref[tail, :]), SIDE - left, 0)[:4, :]
            rows[into, 128:] = jnp.where(row >= 2, line[:, 64:], line[:, :64])
    pre = through(rows[...], coarses, NN)
    gate = sigmoid(pre)
    slope_ref[...] = gate * (1.0 + pre * (1.0 - gate))
    projected = through(pre * gate, projects, NN).T
    projected_ref[...] = jnp.concatenate(split(projected), axis=1)
    for copy in fetches:
        copy.wait()


def middle_kernel(
    projected,
    grams,
    wanted,
    xw,
    tw,
    tw_last,
    pair_hbm,
    de_hbm,
    de_ref,
    deep_ref,
    dslot_ref,
    des,
    taken,
    factor,
    deep,
    parts,
    out_sems,
    sems,
):
    width, count = xw.shape
    slots = dslot_ref.shape[0]
    chunks = chunk_rows(count)
    each = slots // len(chunks)
    stores = [
        pltpu.make_async_copy(des.at[:, here], de_hbm.at[:, here], out_sems.at[i])
        for i, here in enumerate(chunks[:-1])
    ]
    fetches = [
        pltpu.make_async_copy(pair_hbm, deep_ref.at[: 2 * width], sems.at[0]),
        pltpu.make_async_copy(pair_hbm.at[:width], deep_ref.at[2 * width :], sems.at[1]),
    ]
    for copy in fetches:
        copy.start()

    def begin(i):
        tokens = chunks[i]
        here = taking(wanted[:, tokens], slots, 0)
        taken[:slots], taken[slots:] = here, here
        spread = dot(projected[...], taken[...])
        for here in blocks(width, 32):
            pre = xw[here, tokens] + spread[here]
            gate = sigmoid(pre)
            hidden = pre * gate
            factor[i % 2, here] = gate + hidden * (1.0 - gate)
            high, low = split(hidden)
            for part, value in enumerate((high, high, low)):
                deep[i % 2, shift(here, part * width)] = value

    begin(0)
    for i, tokens in enumerate(chunks):
        minus = tw_last if i == len(chunks) - 1 else tw.at[:, tokens]
        target = de_ref if i == len(chunks) - 1 else des.at[:, tokens]
        product = dot(grams[...], deep[i % 2])
        if i + 1 < len(chunks):
            begin(i + 1)
        for here in blocks(width, 32):
            de = (product[here] - minus[here]) * factor[i % 2, here]
            target[here] = de
            parts[here], parts[shift(here, width)] = split(de)
        mine = slice(i * each, (i + 1) * each)
        both = dot(taking(wanted[:, tokens], each, i * each), parts[...], NT)
        dslot_ref[mine] = both[:, :width] + both[:, width:]
        if i < len(stores):
            stores[i].start()
    for copy in stores + fetches:
        copy.wait()


def through(value, pair, dims):
    count, rows = value.shape[0], pair.shape[0] // 2
    high, low = split(value)
    both = dot(jnp.concatenate([high, low], axis=0), pair[:rows], dims)
    return both[:count] + (both[count:] + dot(high, pair[rows:], dims))


def closing_kernel(dslot_ref, slope_ref, coarses, projects, lay, number, send_ref):
    grad = through(through(dslot_ref[...], projects, NT) * slope_ref[...], coarses, NT)
    high, low = split(jnp.concatenate([grad, number[...]], axis=1))
    send_ref[...] = dot(lay[...], high) + dot(lay[...], low)


def scatter_kernel(message_ref, done_ref, mine_ref, other_ref, total):
    del done_ref
    pixels = mine_ref.shape[2]
    message = message_ref[...]
    number = lax.broadcasted_iota(jnp.int32, (message.shape[0], SIDE * SIDE), 1).astype(F32)
    pick = jnp.where(message[:, pixels : pixels + 1] == number, 1.0, 0.0).astype(BF16)
    high, low = split(message[:, :pixels])
    total[...] = dot(pick, low, TN) + dot(pick, high, TN)
    half = mine_ref.shape[1]
    side = lax.axis_index("lvl")
    mine_ref[0] = total[pl.ds(pl.multiple_of(side * half, half), half), :]
    other_ref[0] = total[pl.ds(pl.multiple_of((1 - side) * half, half), half), :]


def last_kernel(de_hbm, first, deep, out_hbm, de, out, cat, in_sems, out_sems):
    width = de.shape[0]
    steps = de.shape[1] // ROWS

    def load(i):
        return pltpu.make_async_copy(de_hbm.at[:, chunk(i)], de.at[:, chunk(i)], in_sems.at[i])

    def store(i):
        return pltpu.make_async_copy(out.at[chunk(i)], out_hbm.at[chunk(i)], out_sems.at[i])

    def prepare(source):
        for here in blocks(width, 32):
            high, low = split(source[here])
            cat[here], cat[shift(here, width)], cat[shift(here, 2 * width)] = high, high, low

    for i in range(steps - 1):
        load(i).start()
    prepare(first)

    def step(i, _):
        mine = lax.rem(i + steps - 1, steps)
        out[chunk(mine), :] = dot(cat[...], deep[...], TN)
        store(mine).start()

        @pl.when(i + 1 < steps)
        def _():
            load(i).wait()
            prepare(de.at[:, chunk(i)])

        return 0

    lax.fori_loop(0, steps, step, 0)
    for i in range(steps):
        store(i).wait()


def fixed(*values):
    return [pltpu.with_memory_space_constraint(value, pltpu.HBM) for value in values]


def near(*values):
    return [pltpu.with_memory_space_constraint(value, pltpu.VMEM) for value in values]


def stack(kernel, blocks, before, rows):
    shape = (len(blocks) * rows, 128)
    return call(
        kernel,
        "stack",
        1000,
        jax.ShapeDtypeStruct(shape, F32),
        limit=ROOM,
        in_specs=[VMEM] * len(blocks) + [HBM],
        out_specs=VMEM,
    )(*blocks, *fixed(before))


def body(coarse_input, coarse_weight, fine_input, fine_target, crops, in_weight, context_weight, out_weight):
    patch = ("far", "y", "core")
    peers = lax.axis_size(patch)
    far = peers // 4
    patches, tokens, values = fine_input.shape
    width = in_weight.shape[1]
    pixels = coarse_weight.shape[0]
    half = coarse_input.shape[1]
    count = patches * tokens
    swap = [(0, 1), (1, 0)]

    column = [coarse_input]
    for k in range(1, far):
        column.append(lax.ppermute(coarse_input, "far", [(p, p ^ k) for p in range(far)]))

    steps = count // ROWS
    pair_shape = (2 * width, values)
    x, t = fine_input.reshape(count, values), fine_target.reshape(count, values)
    xw, pair, rows, next_wide, crops = call(
        input_kernel,
        "input",
        6 * count * values * width,
        (
            pltpu.HBM((width, count), F32),
            pltpu.HBM(pair_shape, BF16),
            pltpu.VMEM((ROWS, values), F32),
            pltpu.VMEM((width, 3 * values), BF16),
            pltpu.VMEM((4, patches), jnp.int32),
        ),
        in_specs=[HBM] * 5,
        out_specs=(HBM, HBM, VMEM, VMEM, VMEM),
        scratch_shapes=[
            pltpu.VMEM((count, values), F32),
            pltpu.VMEM((width, count), F32),
            pltpu.VMEM((width, values), F32),
            pltpu.VMEM((width, values), F32),
            pltpu.VMEM(pair_shape, BF16),
            pltpu.VMEM((width, 3 * values), BF16),
            pltpu.VMEM((ROWS, 3 * values), BF16),
            pltpu.SemaphoreType.DMA((steps,)),
            pltpu.SemaphoreType.DMA((steps,)),
            pltpu.SemaphoreType.DMA((5,)),
        ],
    )(*fixed(x, in_weight.T, t, out_weight, crops.T))
    column = stack(pack_kernel, column, xw, half * 3 // 2)
    own = [column]
    for flip in range(1, 4):
        own.append(lax.ppermute(column, ("lvl", "y"), [(p, p ^ flip) for p in range(4)]))
    tw, tw_last, coarses, projects = call(
        target_kernel,
        "target",
        6 * count * values * width,
        (
            pltpu.HBM((width, count), F32),
            pltpu.VMEM((width, ROWS), F32),
            pltpu.VMEM((2 * pixels, width), BF16),
            pltpu.VMEM((2 * width, width), BF16),
        ),
        limit=ROOM,
        in_specs=[HBM] * 3 + [VMEM] * 2,
        out_specs=(HBM, VMEM, VMEM, VMEM),
        scratch_shapes=[
            pltpu.VMEM((count, values), F32),
            pltpu.VMEM((width, count), F32),
            pltpu.VMEM((ROWS, 3 * values), BF16),
            pltpu.VMEM((pixels, width), F32),
            pltpu.VMEM((width, width), F32),
            pltpu.SemaphoreType.DMA((steps,)),
            pltpu.SemaphoreType.DMA((steps,)),
            pltpu.SemaphoreType.DMA((2,)),
        ],
    )(*fixed(t, coarse_weight, context_weight), *near(rows, next_wide))
    own = stack(stack_kernel, own, tw, column.shape[0])
    other = lax.ppermute(own, "core", swap)
    (crops,) = near(crops)
    grams, wanted, lay, number = call(
        functools.partial(prepare_kernel, patches),
        "prepare",
        8 * values * width * width,
        (
            pltpu.VMEM((width, 3 * width), BF16),
            pltpu.VMEM((1, count), jnp.int32),
            pltpu.VMEM((peers * 16, patches * 16), BF16),
            pltpu.VMEM((patches * 16, LANES - pixels), F32),
        ),
        limit=ROOM,
        in_specs=[VMEM, SMEM, HBM],
        out_specs=(VMEM,) * 4,
    )(*near(next_wide), crops, own)

    projected, slope, xw, tw = call(
        functools.partial(context_kernel, patches, peers),
        "context",
        6 * patches * 16 * width * width,
        (
            pltpu.VMEM((width, 2 * patches * 16), BF16),
            pltpu.VMEM((patches * 16, width), F32),
            pltpu.VMEM((width, count), F32),
            pltpu.VMEM((width, count - ROWS), F32),
        ),
        limit=ROOM,
        in_specs=[SMEM] + [VMEM] * 4 + [HBM] * 2,
        out_specs=(VMEM,) * 4,
        scratch_shapes=[pltpu.VMEM((patches * 16, pixels), F32), pltpu.SemaphoreType.DMA((2,))],
    )(crops, own, other, *near(coarses, projects), *fixed(xw, tw))
    de, last_de, deep, dslot = call(
        middle_kernel,
        "middle",
        6 * count * width * width,
        (
            pltpu.HBM((width, count), F32),
            pltpu.VMEM((width, ROWS), F32),
            pltpu.VMEM((3 * width, values), BF16),
            pltpu.VMEM((patches * 16, width), F32),
        ),
        limit=ROOM,
        in_specs=[VMEM] * 6 + [HBM],
        out_specs=(HBM,) + (VMEM,) * 3,
        scratch_shapes=[
            pltpu.VMEM((width, count), F32),
            pltpu.VMEM((2 * patches * 16, ROWS), BF16),
            pltpu.VMEM((2, width, ROWS), F32),
            pltpu.VMEM((2, 3 * width, ROWS), BF16),
            pltpu.VMEM((2 * width, ROWS), BF16),
            pltpu.SemaphoreType.DMA((steps,)),
            pltpu.SemaphoreType.DMA((2,)),
        ],
    )(*near(projected, grams, wanted, xw, tw, tw_last), *fixed(pair))
    back = call(
        closing_kernel,
        "closing",
        6 * patches * 16 * width * width,
        jax.ShapeDtypeStruct((peers * 16, LANES), F32),
        limit=ROOM,
        in_specs=[VMEM] * 6,
        out_specs=VMEM,
    )(*near(dslot, slope, coarses, projects, lay, number))
    returned = lax.all_to_all(back, patch, 0, 0, tiled=True)

    fine_grad = call(
        last_kernel,
        "last",
        6 * count * values * width,
        pltpu.HBM((count, values), F32),
        limit=ROOM,
        in_specs=[HBM, VMEM, VMEM],
        out_specs=HBM,
        scratch_shapes=[
            pltpu.VMEM((width, count), F32),
            pltpu.VMEM((count, values), F32),
            pltpu.VMEM((3 * width, ROWS), BF16),
            pltpu.SemaphoreType.DMA((steps,)),
            pltpu.SemaphoreType.DMA((steps,)),
        ],
    )(*fixed(de), *near(last_de, deep))
    part = (1, half, pixels)
    mine, theirs = call(
        scatter_kernel,
        "scatter",
        10000,
        (jax.ShapeDtypeStruct(part, F32), jax.ShapeDtypeStruct(part, F32)),
        limit=ROOM,
        in_specs=[VMEM, HBM],
        out_specs=(VMEM, VMEM),
        scratch_shapes=[pltpu.VMEM((SIDE * SIDE, pixels), F32)],
    )(returned, *fixed(fine_grad))
    coarse_grad = mine + lax.ppermute(theirs, "lvl", swap)
    return (coarse_grad, fine_grad.reshape(fine_input.shape))


def solution(mesh):
    sides, peers = mesh.shape["lvl"], mesh.shape["patch"]
    fine = jax.sharding.Mesh(mesh.devices.reshape(sides, peers // 4, 2, 2), ("lvl", "far", "y", "core"))
    patch = ("far", "y", "core")
    both = ("lvl",) + patch
    in_specs = (
        P(patch, "lvl", None),
        P(),
        P(both, None, None),
        P(both, None, None),
        P(both, None),
        P(),
        P(),
        P(),
    )
    out_specs = (P(patch, "lvl", None), P(both, None, None))
    return jax.shard_map(body, mesh=fine, in_specs=in_specs, out_specs=out_specs, check_vma=False)
```

```python
import functools
import math

import jax
import jax.numpy as jnp
from jax import lax
from jax.experimental import pallas as pl
from jax.experimental.pallas import tpu as pltpu
from jax.sharding import PartitionSpec as P

F32 = jnp.float32
BF16 = jnp.bfloat16
NN = (((1,), (0,)), ((), ()))
NT = (((1,), (1,)), ((), ()))
TN = (((0,), (0,)), ((), ()))
ROWS = 512
SIDE = 8
LANES = 256
LIMIT = 60 * 1024 * 1024
ROOM = 40 * 1024 * 1024
SMEM = pl.BlockSpec(memory_space=pltpu.SMEM)
VMEM = pl.BlockSpec(memory_space=pltpu.VMEM)
HBM = pl.BlockSpec(memory_space=pltpu.HBM)


def split(value):
    high = value.astype(BF16)
    low = (value - high.astype(F32)).astype(BF16)
    return high, low


def dot(left, right, dims=NN):
    return lax.dot_general(left, right, dims, preferred_element_type=F32)


def dot3(left, right, dims=NN):
    return (
        dot(left[0], right[1], dims) + dot(left[1], right[0], dims) + dot(left[0], right[0], dims)
    )


def side_by_side(value):
    high, low = split(value)
    return jnp.concatenate([high, low, high], axis=1)


def sigmoid(value):
    return 0.5 * jnp.tanh(0.5 * value) + 0.5


def call(kernel, name, flops, out_shape, limit=LIMIT, **kwargs):
    moved = 8 * sum(math.prod(s.shape) for s in jax.tree.leaves(out_shape))
    return pl.pallas_call(
        kernel,
        out_shape=out_shape,
        name=name,
        cost_estimate=pl.CostEstimate(flops=flops, bytes_accessed=moved, transcendentals=0),
        compiler_params=pltpu.CompilerParams(vmem_limit_bytes=limit),
        **kwargs,
    )


def blocks(rows, size):
    return [slice(start, start + size) for start in range(0, rows, size)]


def shift(here, by):
    return slice(here.start + by, here.stop + by)


def pair_product(pair, value, dims):
    rows = pair.shape[0] // 2
    high, low = split(value)
    both = dot(pair[...], high, dims)
    return both[:rows] + (both[rows:] + dot(pair[:rows], low, dims))


def chunk(i):
    return pl.ds(pl.multiple_of(i * ROWS, ROWS), ROWS)


def wide_product(pair, value, high, low, out):
    width = pair.shape[0] // 2
    for here in blocks(high.shape[0], 16):
        high[here], low[here] = split(value[here])
    both = dot(pair[...], high[...], NT)
    rest = dot(pair[:width], low[...], NT)
    for here in blocks(width, 32):
        out[here] = both[here] + (both[shift(here, width)] + rest[here])


def input_kernel(
    x_hbm,
    weight_hbm,
    t_hbm,
    next_weight_hbm,
    crops_hbm,
    out_hbm,
    pair_hbm,
    next_rows,
    next_pair,
    crops,
    x,
    out,
    weight,
    next_weight,
    pair,
    high,
    low,
    in_sems,
    out_sems,
    sems,
):
    width = weight.shape[0]
    chunks = chunk_rows(x.shape[0])
    fetch = pltpu.make_async_copy(weight_hbm, weight, sems.at[0])
    keep = pltpu.make_async_copy(pair, pair_hbm, sems.at[1])
    fetch_next = pltpu.make_async_copy(next_weight_hbm, next_weight, sems.at[2])
    fetch_rows = pltpu.make_async_copy(t_hbm.at[: next_rows.shape[0]], next_rows, sems.at[3])
    fetch_crops = pltpu.make_async_copy(crops_hbm, crops, sems.at[4])
    loads = [
        pltpu.make_async_copy(x_hbm.at[here], x.at[here], in_sems.at[i]) for i, here in enumerate(chunks)
    ]
    stores = [
        pltpu.make_async_copy(out.at[:, here], out_hbm.at[:, here], out_sems.at[i])
        for i, here in enumerate(chunks)
    ]
    for copy in [fetch] + loads[:2]:
        copy.start()
    for i, here in enumerate(chunks):
        loads[i].wait()
        if i + 2 < len(chunks):
            loads[i + 2].start()
        if i == 0:
            fetch.wait()
            pair[:width], pair[width:] = split(weight[...])
            keep.start()
            fetch_next.start()
        if i == 1:
            fetch_rows.start()
            fetch_crops.start()
        if i == len(chunks) - 1:
            fetch_next.wait()
            next_pair[:width], next_pair[width:] = split(next_weight[...])
        wide_product(pair, x.at[here], high, low, out.at[:, here])
        stores[i].start()
    for copy in [keep, fetch_rows, fetch_crops] + stores:
        copy.wait()


def target_kernel(
    t_hbm,
    cwgt_hbm,
    xwgt_hbm,
    rows,
    pair,
    out_hbm,
    out_last,
    coarses,
    projects,
    t,
    out,
    high,
    low,
    cwgt,
    xwgt,
    in_sems,
    out_sems,
    sems,
):
    chunks = chunk_rows(t.shape[0])
    fetches = [
        pltpu.make_async_copy(cwgt_hbm, cwgt, sems.at[0]),
        pltpu.make_async_copy(xwgt_hbm, xwgt, sems.at[1]),
    ]
    loads = [
        pltpu.make_async_copy(t_hbm.at[here], t.at[here], in_sems.at[i])
        for i, here in enumerate(chunks[1:])
    ]
    stores = [
        pltpu.make_async_copy(out.at[:, here], out_hbm.at[:, here], out_sems.at[i])
        for i, here in enumerate(chunks[:-1])
    ]
    for copy in loads + fetches:
        copy.start()
    for i, here in enumerate(chunks):
        if i > 0:
            loads[i - 1].wait()
        source = rows if i == 0 else t.at[here]
        if i < len(stores):
            wide_product(pair, source, high, low, out.at[:, here])
            stores[i].start()
        else:
            wide_product(pair, source, high, low, out_last)
    for copy in fetches:
        copy.wait()
    coarses[...] = jnp.concatenate(split(cwgt[...]), axis=0)
    projects[...] = jnp.concatenate(split(xwgt[...]), axis=0)
    for copy in stores:
        copy.wait()


def chunk_rows(count):
    return [slice(start, start + ROWS) for start in range(0, count, ROWS)]


def prepare_kernel(patches, pair, crops_ref, before_ref, grams, wanted, lay, number):
    del before_ref
    width = grams.shape[0]
    both = dot(pair[...], pair[:width], NT)
    grams[...] = side_by_side(both[:width] + (both[width:] + both[width:].T))
    wanted[...] = slot_row(crops_ref, patches, wanted.shape[1] // patches)
    frame = row_value(crops_ref, 0, patches, (1, patches * 16), 1, 16)
    slot = lax.broadcasted_iota(jnp.int32, (1, patches * 16), 1) % 16
    line = lax.broadcasted_iota(jnp.int32, lay.shape, 0)
    lay[...] = jnp.where(line == frame * 16 + slot, 1.0, 0.0).astype(BF16)
    slot = lax.broadcasted_iota(jnp.int32, number.shape, 0) % 16
    top = row_value(crops_ref, 1, patches, number.shape, 0, 16)
    left = row_value(crops_ref, 2, patches, number.shape, 0, 16)
    number[...] = ((top + slot // 4) * SIDE + left + slot % 4).astype(F32)


def stack_kernel(*refs):
    *block_refs, _, out_ref = refs
    size = block_refs[0].shape[0]
    for k, ref in enumerate(block_refs):
        out_ref[k * size : (k + 1) * size] = ref[...]


def pack_kernel(*refs):
    *block_refs, _, out_ref = refs
    tokens = block_refs[0].shape[1]
    size = tokens * 3 // 2
    for k, ref in enumerate(block_refs):
        out_ref[k * size : k * size + tokens] = ref[0, :, :128]
        tails = [ref[0, : tokens // 2, 128:], ref[0, tokens // 2 :, 128:]]
        out_ref[k * size + tokens : (k + 1) * size] = jnp.concatenate(tails, axis=1)


def row_value(crops_ref, column, patches, shape, axis, each):
    index = lax.broadcasted_iota(jnp.int32, shape, axis) // each
    found = jnp.zeros(shape, jnp.int32)
    for j in range(patches):
        found = jnp.where(index == j, crops_ref[column, j], found)
    return found


def slot_row(crops_ref, patches, tokens):
    scale = row_value(crops_ref, 3, patches, (1, patches * tokens), 1, tokens)
    token = lax.broadcasted_iota(jnp.int32, (1, patches * tokens), 1)
    row, column = (token % tokens) // 16, token % 16
    return token // tokens * 16 + (row * scale // 8) * 4 + column * scale // 8


def taking(wanted, slots, first):
    slot = lax.broadcasted_iota(jnp.int32, (slots, wanted.shape[1]), 0) + first
    return jnp.where(slot == wanted, 1.0, 0.0).astype(BF16)


def context_kernel(
    patches,
    peers,
    crops_ref,
    own_ref,
    other_ref,
    coarses,
    projects,
    xw_hbm,
    tw_hbm,
    projected_ref,
    slope_ref,
    xw_first,
    tw_first,
    rows,
    sems,
):
    fetches = [
        pltpu.make_async_copy(xw_hbm.at[:, : xw_first.shape[1]], xw_first, sems.at[0]),
        pltpu.make_async_copy(tw_hbm.at[:, : tw_first.shape[1]], tw_first, sems.at[1]),
    ]
    for copy in fetches:
        copy.start()
    pixels = coarses.shape[0] // 2
    width = projects.shape[1]
    far = peers // 4
    me, side = lax.axis_index(("far", "y", "core")), lax.axis_index("lvl")
    for j in range(patches):
        frame, top, left = crops_ref[0, j], crops_ref[1, j], crops_ref[2, j]
        near_by = lax.bitwise_xor(frame % 4, me % 4)
        k = (me // 4 - frame // 4 + far) % far
        here = near_by % 2 == 0
        for a in range(4):
            row = jnp.minimum(top + a, SIDE - 1)
            shard = (lax.bitwise_xor(row // 4, side) * 2 + near_by // 2) * far + k
            row = row % 4
            start = shard * (6 * SIDE)
            wide = pl.ds(pl.multiple_of(start + row * SIDE, SIDE), SIDE)
            tail = pl.ds(pl.multiple_of(start + (4 + row % 2) * SIDE, SIDE), SIDE)
            into = slice(j * 16 + a * 4, j * 16 + a * 4 + 4)
            line = jnp.where(here, own_ref[wide, :], other_ref[wide, :])
            rows[into, :128] = pltpu.roll(line, SIDE - left, 0)[:4, :]
            line = pltpu.roll(jnp.where(here, own_ref[tail, :], other_ref[tail, :]), SIDE - left, 0)[:4, :]
            rows[into, 128:] = jnp.where(row >= 2, line[:, 64:], line[:, :64])
    pre = through(rows[...], coarses, NN)
    gate = sigmoid(pre)
    slope_ref[...] = gate * (1.0 + pre * (1.0 - gate))
    projected = through(pre * gate, projects, NN).T
    projected_ref[...] = jnp.concatenate(split(projected), axis=1)
    for copy in fetches:
        copy.wait()


def middle_kernel(
    projected,
    grams,
    wanted,
    xw_first,
    tw_first,
    tw_last,
    xw_hbm,
    tw_hbm,
    pair_hbm,
    de_hbm,
    de_ref,
    deep_ref,
    dslot_ref,
    xw,
    tw,
    taken,
    factor,
    deep,
    parts,
    xw_sems,
    tw_sems,
    out_sems,
    sems,
):
    width, count = xw.shape
    slots = dslot_ref.shape[0]
    chunks = chunk_rows(count)
    each = slots // len(chunks)
    tw_loads = [
        pltpu.make_async_copy(tw_hbm.at[:, here], tw.at[:, here], tw_sems.at[i])
        for i, here in enumerate(chunks[1:-1])
    ]
    xw_loads = [
        pltpu.make_async_copy(xw_hbm.at[:, here], xw.at[:, here], xw_sems.at[i])
        for i, here in enumerate(chunks[2:])
    ]
    stores = [
        pltpu.make_async_copy(xw.at[:, here], de_hbm.at[:, here], out_sems.at[i])
        for i, here in enumerate(chunks[:-1])
    ]
    fetches = [
        pltpu.make_async_copy(pair_hbm, deep_ref.at[: 2 * width], sems.at[0]),
        pltpu.make_async_copy(pair_hbm.at[:width], deep_ref.at[2 * width :], sems.at[1]),
    ]
    for pair in zip(tw_loads, xw_loads):
        for copy in pair:
            copy.start()
    for copy in fetches:
        copy.start()

    def begin(i):
        tokens = chunks[i]
        source = xw_first.at[:, tokens] if i < 2 else xw.at[:, tokens]
        here = taking(wanted[:, tokens], slots, 0)
        taken[:slots], taken[slots:] = here, here
        spread = dot(projected[...], taken[...])
        for here in blocks(width, 32):
            pre = source[here] + spread[here]
            gate = sigmoid(pre)
            hidden = pre * gate
            factor[i % 2, here] = gate + hidden * (1.0 - gate)
            high, low = split(hidden)
            for part, value in enumerate((high, high, low)):
                deep[i % 2, shift(here, part * width)] = value

    begin(0)
    for i, tokens in enumerate(chunks):
        if 0 < i < len(chunks) - 1:
            tw_loads[i - 1].wait()
            xw_loads[i - 1].wait()
        minus = tw_first if i == 0 else tw_last if i == len(chunks) - 1 else tw.at[:, tokens]
        target = de_ref if i == len(chunks) - 1 else xw.at[:, tokens]
        product = dot(grams[...], deep[i % 2])
        if i + 1 < len(chunks):
            begin(i + 1)
        for here in blocks(width, 32):
            de = (product[here] - minus[here]) * factor[i % 2, here]
            target[here] = de
            parts[here], parts[shift(here, width)] = split(de)
        mine = slice(i * each, (i + 1) * each)
        both = dot(taking(wanted[:, tokens], each, i * each), parts[...], NT)
        dslot_ref[mine] = both[:, :width] + both[:, width:]
        if i < len(stores):
            stores[i].start()
    for copy in stores + fetches:
        copy.wait()


def through(value, pair, dims):
    count, rows = value.shape[0], pair.shape[0] // 2
    high, low = split(value)
    both = dot(jnp.concatenate([high, low], axis=0), pair[:rows], dims)
    return both[:count] + (both[count:] + dot(high, pair[rows:], dims))


def closing_kernel(dslot_ref, slope_ref, coarses, projects, lay, number, send_ref):
    grad = through(through(dslot_ref[...], projects, NT) * slope_ref[...], coarses, NT)
    high, low = split(jnp.concatenate([grad, number[...]], axis=1))
    send_ref[...] = dot(lay[...], high) + dot(lay[...], low)


def scatter_kernel(message_ref, done_ref, mine_ref, other_ref, total):
    del done_ref
    pixels = mine_ref.shape[2]
    message = message_ref[...]
    number = lax.broadcasted_iota(jnp.int32, (message.shape[0], SIDE * SIDE), 1).astype(F32)
    pick = jnp.where(message[:, pixels : pixels + 1] == number, 1.0, 0.0).astype(BF16)
    high, low = split(message[:, :pixels])
    total[...] = dot(pick, low, TN) + dot(pick, high, TN)
    half = mine_ref.shape[1]
    side = lax.axis_index("lvl")
    mine_ref[0] = total[pl.ds(pl.multiple_of(side * half, half), half), :]
    other_ref[0] = total[pl.ds(pl.multiple_of((1 - side) * half, half), half), :]


def last_kernel(de_hbm, first, deep, out_hbm, de, out, cat, in_sems, out_sems):
    width = de.shape[0]
    steps = de.shape[1] // ROWS

    def load(i):
        return pltpu.make_async_copy(de_hbm.at[:, chunk(i)], de.at[:, chunk(i)], in_sems.at[i])

    def store(i):
        return pltpu.make_async_copy(out.at[chunk(i)], out_hbm.at[chunk(i)], out_sems.at[i])

    def prepare(source):
        for here in blocks(width, 32):
            high, low = split(source[here])
            cat[here], cat[shift(here, width)], cat[shift(here, 2 * width)] = high, high, low

    for i in range(steps - 1):
        load(i).start()
    prepare(first)

    def step(i, _):
        mine = lax.rem(i + steps - 1, steps)
        out[chunk(mine), :] = dot(cat[...], deep[...], TN)
        store(mine).start()

        @pl.when(i + 1 < steps)
        def _():
            load(i).wait()
            prepare(de.at[:, chunk(i)])

        return 0

    lax.fori_loop(0, steps, step, 0)
    for i in range(steps):
        store(i).wait()


def fixed(*values):
    return [pltpu.with_memory_space_constraint(value, pltpu.HBM) for value in values]


def near(*values):
    return [pltpu.with_memory_space_constraint(value, pltpu.VMEM) for value in values]


def stack(kernel, blocks, before, rows):
    shape = (len(blocks) * rows, 128)
    return call(
        kernel,
        "stack",
        1000,
        jax.ShapeDtypeStruct(shape, F32),
        limit=ROOM,
        in_specs=[VMEM] * len(blocks) + [HBM],
        out_specs=VMEM,
    )(*blocks, *fixed(before))


def body(coarse_input, coarse_weight, fine_input, fine_target, crops, in_weight, context_weight, out_weight):
    patch = ("far", "y", "core")
    peers = lax.axis_size(patch)
    far = peers // 4
    patches, tokens, values = fine_input.shape
    width = in_weight.shape[1]
    pixels = coarse_weight.shape[0]
    half = coarse_input.shape[1]
    count = patches * tokens
    swap = [(0, 1), (1, 0)]

    column = [coarse_input]
    for k in range(1, far):
        column.append(lax.ppermute(coarse_input, "far", [(p, (p + k) % far) for p in range(far)]))

    steps = count // ROWS
    pair_shape = (2 * width, values)
    x, t = fine_input.reshape(count, values), fine_target.reshape(count, values)
    xw, pair, rows, next_pair, crops = call(
        input_kernel,
        "input",
        6 * count * values * width,
        (
            pltpu.HBM((width, count), F32),
            pltpu.HBM(pair_shape, BF16),
            pltpu.VMEM((ROWS, values), F32),
            pltpu.VMEM(pair_shape, BF16),
            pltpu.VMEM((4, patches), jnp.int32),
        ),
        in_specs=[HBM] * 5,
        out_specs=(HBM, HBM, VMEM, VMEM, VMEM),
        scratch_shapes=[
            pltpu.VMEM((count, values), F32),
            pltpu.VMEM((width, count), F32),
            pltpu.VMEM((width, values), F32),
            pltpu.VMEM((width, values), F32),
            pltpu.VMEM(pair_shape, BF16),
            pltpu.VMEM((ROWS, values), BF16),
            pltpu.VMEM((ROWS, values), BF16),
            pltpu.SemaphoreType.DMA((steps,)),
            pltpu.SemaphoreType.DMA((steps,)),
            pltpu.SemaphoreType.DMA((5,)),
        ],
    )(*fixed(x, in_weight.T, t, out_weight, crops.T))
    column = stack(pack_kernel, column, xw, half * 3 // 2)
    own = [column]
    for flip in range(1, 4):
        own.append(lax.ppermute(column, ("lvl", "y"), [(p, p ^ flip) for p in range(4)]))
    tw, tw_last, coarses, projects = call(
        target_kernel,
        "target",
        6 * count * values * width,
        (
            pltpu.HBM((width, count), F32),
            pltpu.VMEM((width, ROWS), F32),
            pltpu.VMEM((2 * pixels, width), BF16),
            pltpu.VMEM((2 * width, width), BF16),
        ),
        limit=ROOM,
        in_specs=[HBM] * 3 + [VMEM] * 2,
        out_specs=(HBM, VMEM, VMEM, VMEM),
        scratch_shapes=[
            pltpu.VMEM((count, values), F32),
            pltpu.VMEM((width, count), F32),
            pltpu.VMEM((ROWS, values), BF16),
            pltpu.VMEM((ROWS, values), BF16),
            pltpu.VMEM((pixels, width), F32),
            pltpu.VMEM((width, width), F32),
            pltpu.SemaphoreType.DMA((steps,)),
            pltpu.SemaphoreType.DMA((steps,)),
            pltpu.SemaphoreType.DMA((2,)),
        ],
    )(*fixed(t, coarse_weight, context_weight), *near(rows, next_pair))
    own = stack(stack_kernel, own, tw, column.shape[0])
    other = lax.ppermute(own, "core", swap)
    (crops,) = near(crops)
    grams, wanted, lay, number = call(
        functools.partial(prepare_kernel, patches),
        "prepare",
        8 * values * width * width,
        (
            pltpu.VMEM((width, 3 * width), BF16),
            pltpu.VMEM((1, count), jnp.int32),
            pltpu.VMEM((peers * 16, patches * 16), BF16),
            pltpu.VMEM((patches * 16, LANES - pixels), F32),
        ),
        limit=ROOM,
        in_specs=[VMEM, SMEM, HBM],
        out_specs=(VMEM,) * 4,
    )(*near(next_pair), crops, own)

    projected, slope, xw_first, tw_first = call(
        functools.partial(context_kernel, patches, peers),
        "context",
        6 * patches * 16 * width * width,
        (
            pltpu.VMEM((width, 2 * patches * 16), BF16),
            pltpu.VMEM((patches * 16, width), F32),
            pltpu.VMEM((width, 2 * ROWS), F32),
            pltpu.VMEM((width, ROWS), F32),
        ),
        limit=ROOM,
        in_specs=[SMEM] + [VMEM] * 4 + [HBM] * 2,
        out_specs=(VMEM,) * 4,
        scratch_shapes=[pltpu.VMEM((patches * 16, pixels), F32), pltpu.SemaphoreType.DMA((2,))],
    )(crops, own, other, *near(coarses, projects), *fixed(xw, tw))
    de, last_de, deep, dslot = call(
        middle_kernel,
        "middle",
        6 * count * width * width,
        (
            pltpu.HBM((width, count), F32),
            pltpu.VMEM((width, ROWS), F32),
            pltpu.VMEM((3 * width, values), BF16),
            pltpu.VMEM((patches * 16, width), F32),
        ),
        limit=ROOM,
        in_specs=[VMEM] * 6 + [HBM] * 3,
        out_specs=(HBM,) + (VMEM,) * 3,
        scratch_shapes=[
            pltpu.VMEM((width, count), F32),
            pltpu.VMEM((width, count), F32),
            pltpu.VMEM((2 * patches * 16, ROWS), BF16),
            pltpu.VMEM((2, width, ROWS), F32),
            pltpu.VMEM((2, 3 * width, ROWS), BF16),
            pltpu.VMEM((2 * width, ROWS), BF16),
            pltpu.SemaphoreType.DMA((steps,)),
            pltpu.SemaphoreType.DMA((steps,)),
            pltpu.SemaphoreType.DMA((steps,)),
            pltpu.SemaphoreType.DMA((2,)),
        ],
    )(*near(projected, grams, wanted, xw_first, tw_first, tw_last), *fixed(xw, tw, pair))
    back = call(
        closing_kernel,
        "closing",
        6 * patches * 16 * width * width,
        jax.ShapeDtypeStruct((peers * 16, LANES), F32),
        limit=ROOM,
        in_specs=[VMEM] * 6,
        out_specs=VMEM,
    )(*near(dslot, slope, coarses, projects, lay, number))
    returned = lax.all_to_all(back, patch, 0, 0, tiled=True)

    fine_grad = call(
        last_kernel,
        "last",
        6 * count * values * width,
        pltpu.HBM((count, values), F32),
        limit=ROOM,
        in_specs=[HBM, VMEM, VMEM],
        out_specs=HBM,
        scratch_shapes=[
            pltpu.VMEM((width, count), F32),
            pltpu.VMEM((count, values), F32),
            pltpu.VMEM((3 * width, ROWS), BF16),
            pltpu.SemaphoreType.DMA((steps,)),
            pltpu.SemaphoreType.DMA((steps,)),
        ],
    )(*fixed(de), *near(last_de, deep))
    part = (1, half, pixels)
    mine, theirs = call(
        scatter_kernel,
        "scatter",
        10000,
        (jax.ShapeDtypeStruct(part, F32), jax.ShapeDtypeStruct(part, F32)),
        limit=ROOM,
        in_specs=[VMEM, HBM],
        out_specs=(VMEM, VMEM),
        scratch_shapes=[pltpu.VMEM((SIDE * SIDE, pixels), F32)],
    )(returned, *fixed(fine_grad))
    coarse_grad = mine + lax.ppermute(theirs, "lvl", swap)
    return (coarse_grad, fine_grad.reshape(fine_input.shape))


def solution(mesh):
    sides, peers = mesh.shape["lvl"], mesh.shape["patch"]
    fine = jax.sharding.Mesh(mesh.devices.reshape(sides, peers // 4, 2, 2), ("lvl", "far", "y", "core"))
    patch = ("far", "y", "core")
    both = ("lvl",) + patch
    in_specs = (
        P(patch, "lvl", None),
        P(),
        P(both, None, None),
        P(both, None, None),
        P(both, None),
        P(),
        P(),
        P(),
    )
    out_specs = (P(patch, "lvl", None), P(both, None, None))
    return jax.shard_map(body, mesh=fine, in_specs=in_specs, out_specs=out_specs, check_vma=False)
```

```python
import functools
import math

import jax
import jax.numpy as jnp
from jax import lax
from jax.experimental import pallas as pl
from jax.experimental.pallas import tpu as pltpu
from jax.sharding import PartitionSpec as P

F32 = jnp.float32
BF16 = jnp.bfloat16
NN = (((1,), (0,)), ((), ()))
NT = (((1,), (1,)), ((), ()))
TN = (((0,), (0,)), ((), ()))
ROWS = 512
SIDE = 8
LANES = 256
LIMIT = 60 * 1024 * 1024
ROOM = 40 * 1024 * 1024
SMEM = pl.BlockSpec(memory_space=pltpu.SMEM)
VMEM = pl.BlockSpec(memory_space=pltpu.VMEM)
HBM = pl.BlockSpec(memory_space=pltpu.HBM)


def split(value):
    high = value.astype(BF16)
    low = (value - high.astype(F32)).astype(BF16)
    return high, low


def dot(left, right, dims=NN):
    return lax.dot_general(left, right, dims, preferred_element_type=F32)


def dot3(left, right, dims=NN):
    return (
        dot(left[0], right[1], dims) + dot(left[1], right[0], dims) + dot(left[0], right[0], dims)
    )


def side_by_side(value):
    high, low = split(value)
    return jnp.concatenate([high, low, high], axis=1)


def sigmoid(value):
    return 0.5 * jnp.tanh(0.5 * value) + 0.5


def call(kernel, name, flops, out_shape, limit=LIMIT, **kwargs):
    moved = 8 * sum(math.prod(s.shape) for s in jax.tree.leaves(out_shape))
    return pl.pallas_call(
        kernel,
        out_shape=out_shape,
        name=name,
        cost_estimate=pl.CostEstimate(flops=flops, bytes_accessed=moved, transcendentals=0),
        compiler_params=pltpu.CompilerParams(vmem_limit_bytes=limit),
        **kwargs,
    )


def blocks(rows, size):
    return [slice(start, start + size) for start in range(0, rows, size)]


def shift(here, by):
    return slice(here.start + by, here.stop + by)


def pair_product(pair, value, dims):
    rows = pair.shape[0] // 2
    high, low = split(value)
    both = dot(pair[...], high, dims)
    return both[:rows] + (both[rows:] + dot(pair[:rows], low, dims))


def chunk(i):
    return pl.ds(pl.multiple_of(i * ROWS, ROWS), ROWS)


def wide_product(pair, value, high, low, out):
    width = pair.shape[0] // 2
    for here in blocks(high.shape[0], 16):
        high[here], low[here] = split(value[here])
    both = dot(pair[...], high[...], NT)
    rest = dot(pair[:width], low[...], NT)
    for here in blocks(width, 32):
        out[here] = both[here] + (both[shift(here, width)] + rest[here])


def input_kernel(
    x_hbm,
    weight_hbm,
    t_hbm,
    next_weight_hbm,
    crops_hbm,
    out_hbm,
    out_last,
    pair_hbm,
    next_rows,
    next_pair,
    crops,
    x,
    out,
    weight,
    next_weight,
    pair,
    high,
    low,
    in_sems,
    out_sems,
    sems,
):
    width = weight.shape[0]
    chunks = chunk_rows(x.shape[0])
    fetch = pltpu.make_async_copy(weight_hbm, weight, sems.at[0])
    keep = pltpu.make_async_copy(pair, pair_hbm, sems.at[1])
    fetch_next = pltpu.make_async_copy(next_weight_hbm, next_weight, sems.at[2])
    fetch_rows = pltpu.make_async_copy(t_hbm.at[: next_rows.shape[0]], next_rows, sems.at[3])
    fetch_crops = pltpu.make_async_copy(crops_hbm, crops, sems.at[4])
    loads = [
        pltpu.make_async_copy(x_hbm.at[here], x.at[here], in_sems.at[i]) for i, here in enumerate(chunks)
    ]
    stores = [
        pltpu.make_async_copy(out.at[:, here], out_hbm.at[:, here], out_sems.at[i])
        for i, here in enumerate(chunks[:-1])
    ]
    for copy in [fetch] + loads[:2]:
        copy.start()
    for i, here in enumerate(chunks):
        loads[i].wait()
        if i + 2 < len(chunks):
            loads[i + 2].start()
        if i == 0:
            fetch.wait()
            pair[:width], pair[width:] = split(weight[...])
            keep.start()
            fetch_next.start()
        if i == 1:
            fetch_rows.start()
            fetch_crops.start()
        if i == len(chunks) - 1:
            fetch_next.wait()
            next_pair[:width], next_pair[width:] = split(next_weight[...])
        target = out.at[:, here] if i < len(stores) else out_last
        wide_product(pair, x.at[here], high, low, target)
        if i < len(stores):
            stores[i].start()
    for copy in [keep, fetch_rows, fetch_crops] + stores:
        copy.wait()


def target_kernel(
    t_hbm,
    cwgt_hbm,
    xwgt_hbm,
    rows,
    pair,
    before_last,
    out_hbm,
    before_hbm,
    out_last,
    coarses,
    projects,
    t,
    out,
    high,
    low,
    cwgt,
    xwgt,
    in_sems,
    out_sems,
    sems,
):
    chunks = chunk_rows(t.shape[0])
    fetches = [
        pltpu.make_async_copy(cwgt_hbm, cwgt, sems.at[0]),
        pltpu.make_async_copy(xwgt_hbm, xwgt, sems.at[1]),
    ]
    loads = [
        pltpu.make_async_copy(t_hbm.at[here], t.at[here], in_sems.at[i])
        for i, here in enumerate(chunks[1:])
    ]
    stores = [
        pltpu.make_async_copy(out.at[:, here], out_hbm.at[:, here], out_sems.at[i])
        for i, here in enumerate(chunks[:-1])
    ]
    keep = pltpu.make_async_copy(before_last, before_hbm, sems.at[2])
    for copy in loads + fetches + [keep]:
        copy.start()
    for i, here in enumerate(chunks):
        if i > 0:
            loads[i - 1].wait()
        source = rows if i == 0 else t.at[here]
        if i < len(stores):
            wide_product(pair, source, high, low, out.at[:, here])
            stores[i].start()
        else:
            wide_product(pair, source, high, low, out_last)
    for copy in fetches:
        copy.wait()
    coarses[...] = jnp.concatenate(split(cwgt[...]), axis=0)
    projects[...] = jnp.concatenate(split(xwgt[...]), axis=0)
    for copy in stores + [keep]:
        copy.wait()


def chunk_rows(count):
    return [slice(start, start + ROWS) for start in range(0, count, ROWS)]


def prepare_kernel(patches, pair, crops_ref, before_ref, grams, wanted, lay, number):
    del before_ref
    width = grams.shape[0]
    both = dot(pair[...], pair[:width], NT)
    grams[...] = side_by_side(both[:width] + (both[width:] + both[width:].T))
    wanted[...] = slot_row(crops_ref, patches, wanted.shape[1] // patches)
    frame = row_value(crops_ref, 0, patches, (1, patches * 16), 1, 16)
    slot = lax.broadcasted_iota(jnp.int32, (1, patches * 16), 1) % 16
    line = lax.broadcasted_iota(jnp.int32, lay.shape, 0)
    lay[...] = jnp.where(line == frame * 16 + slot, 1.0, 0.0).astype(BF16)
    slot = lax.broadcasted_iota(jnp.int32, number.shape, 0) % 16
    top = row_value(crops_ref, 1, patches, number.shape, 0, 16)
    left = row_value(crops_ref, 2, patches, number.shape, 0, 16)
    number[...] = ((top + slot // 4) * SIDE + left + slot % 4).astype(F32)


def stack_kernel(*refs):
    *block_refs, _, out_ref = refs
    size = block_refs[0].shape[0]
    for k, ref in enumerate(block_refs):
        out_ref[k * size : (k + 1) * size] = ref[...]


def pack_kernel(*refs):
    *block_refs, _, out_ref = refs
    tokens = block_refs[0].shape[1]
    size = tokens * 3 // 2
    for k, ref in enumerate(block_refs):
        out_ref[k * size : k * size + tokens] = ref[0, :, :128]
        tails = [ref[0, : tokens // 2, 128:], ref[0, tokens // 2 :, 128:]]
        out_ref[k * size + tokens : (k + 1) * size] = jnp.concatenate(tails, axis=1)


def row_value(crops_ref, column, patches, shape, axis, each):
    index = lax.broadcasted_iota(jnp.int32, shape, axis) // each
    found = jnp.zeros(shape, jnp.int32)
    for j in range(patches):
        found = jnp.where(index == j, crops_ref[column, j], found)
    return found


def slot_row(crops_ref, patches, tokens):
    scale = row_value(crops_ref, 3, patches, (1, patches * tokens), 1, tokens)
    token = lax.broadcasted_iota(jnp.int32, (1, patches * tokens), 1)
    row, column = (token % tokens) // 16, token % 16
    return token // tokens * 16 + (row * scale // 8) * 4 + column * scale // 8


def taking(wanted, slots, first):
    slot = lax.broadcasted_iota(jnp.int32, (slots, wanted.shape[1]), 0) + first
    return jnp.where(slot == wanted, 1.0, 0.0).astype(BF16)


def context_kernel(
    patches,
    peers,
    crops_ref,
    own_ref,
    other_ref,
    coarses,
    projects,
    xw_hbm,
    tw_hbm,
    projected_ref,
    slope_ref,
    xw_first,
    tw_first,
    rows,
    sems,
):
    fetches = [
        pltpu.make_async_copy(xw_hbm.at[:, : xw_first.shape[1]], xw_first, sems.at[0]),
        pltpu.make_async_copy(tw_hbm.at[:, : tw_first.shape[1]], tw_first, sems.at[1]),
    ]
    for copy in fetches:
        copy.start()
    pixels = coarses.shape[0] // 2
    width = projects.shape[1]
    far = peers // 4
    me, side = lax.axis_index(("far", "y", "core")), lax.axis_index("lvl")
    for j in range(patches):
        frame, top, left = crops_ref[0, j], crops_ref[1, j], crops_ref[2, j]
        near_by = lax.bitwise_xor(frame % 4, me % 4)
        k = (me // 4 - frame // 4 + far) % far
        here = near_by % 2 == 0
        for a in range(4):
            row = jnp.minimum(top + a, SIDE - 1)
            shard = (lax.bitwise_xor(row // 4, side) * 2 + near_by // 2) * far + k
            row = row % 4
            start = shard * (6 * SIDE)
            wide = pl.ds(pl.multiple_of(start + row * SIDE, SIDE), SIDE)
            tail = pl.ds(pl.multiple_of(start + (4 + row % 2) * SIDE, SIDE), SIDE)
            into = slice(j * 16 + a * 4, j * 16 + a * 4 + 4)
            line = jnp.where(here, own_ref[wide, :], other_ref[wide, :])
            rows[into, :128] = pltpu.roll(line, SIDE - left, 0)[:4, :]
            line = pltpu.roll(jnp.where(here, own_ref[tail, :], other_ref[tail, :]), SIDE - left, 0)[:4, :]
            rows[into, 128:] = jnp.where(row >= 2, line[:, 64:], line[:, :64])
    pre = through(rows[...], coarses, NN)
    gate = sigmoid(pre)
    slope_ref[...] = gate * (1.0 + pre * (1.0 - gate))
    projected = through(pre * gate, projects, NN).T
    projected_ref[...] = jnp.concatenate(split(projected), axis=1)
    for copy in fetches:
        copy.wait()


def middle_kernel(
    projected,
    grams,
    wanted,
    xw_first,
    tw_first,
    tw_last,
    xw_hbm,
    xw_last,
    tw_hbm,
    pair_hbm,
    de_hbm,
    de_ref,
    deep_ref,
    dslot_ref,
    xw,
    tw,
    taken,
    factor,
    deep,
    parts,
    xw_sems,
    tw_sems,
    out_sems,
    sems,
):
    width, count = xw.shape
    slots = dslot_ref.shape[0]
    chunks = chunk_rows(count)
    each = slots // len(chunks)
    tw_loads = [
        pltpu.make_async_copy(tw_hbm.at[:, here], tw.at[:, here], tw_sems.at[i])
        for i, here in enumerate(chunks[1:-1])
    ]
    xw_loads = [
        pltpu.make_async_copy(xw_hbm.at[:, here], xw.at[:, here], xw_sems.at[i])
        for i, here in enumerate(chunks[1:-1])
    ]
    xw_loads.append(pltpu.make_async_copy(xw_last, xw.at[:, chunks[-1]], xw_sems.at[len(xw_loads)]))
    stores = [
        pltpu.make_async_copy(xw.at[:, here], de_hbm.at[:, here], out_sems.at[i])
        for i, here in enumerate(chunks[:-1])
    ]
    fetches = [
        pltpu.make_async_copy(pair_hbm, deep_ref.at[: 2 * width], sems.at[0]),
        pltpu.make_async_copy(pair_hbm.at[:width], deep_ref.at[2 * width :], sems.at[1]),
    ]
    xw_loads[0].start()

    def begin(i):
        tokens = chunks[i]
        source = xw_first if i == 0 else xw.at[:, tokens]
        here = taking(wanted[:, tokens], slots, 0)
        taken[:slots], taken[slots:] = here, here
        spread = dot(projected[...], taken[...])
        for here in blocks(width, 32):
            pre = source[here] + spread[here]
            gate = sigmoid(pre)
            hidden = pre * gate
            factor[i % 2, here] = gate + hidden * (1.0 - gate)
            high, low = split(hidden)
            for part, value in enumerate((high, high, low)):
                deep[i % 2, shift(here, part * width)] = value

    begin(0)
    for pair in zip(tw_loads, xw_loads[1:]):
        for copy in pair:
            copy.start()
    for i, tokens in enumerate(chunks):
        if i < len(xw_loads):
            xw_loads[i].wait()
        if 0 < i < len(chunks) - 1:
            tw_loads[i - 1].wait()
        if i == 1:
            for copy in fetches:
                copy.start()
        minus = tw_first if i == 0 else tw_last if i == len(chunks) - 1 else tw.at[:, tokens]
        target = de_ref if i == len(chunks) - 1 else xw.at[:, tokens]
        product = dot(grams[...], deep[i % 2])
        if i + 1 < len(chunks):
            begin(i + 1)
        for here in blocks(width, 32):
            de = (product[here] - minus[here]) * factor[i % 2, here]
            target[here] = de
            parts[here], parts[shift(here, width)] = split(de)
        mine = slice(i * each, (i + 1) * each)
        both = dot(taking(wanted[:, tokens], each, i * each), parts[...], NT)
        dslot_ref[mine] = both[:, :width] + both[:, width:]
        if i < len(stores):
            stores[i].start()
    for copy in stores + fetches:
        copy.wait()


def through(value, pair, dims):
    count, rows = value.shape[0], pair.shape[0] // 2
    high, low = split(value)
    both = dot(jnp.concatenate([high, low], axis=0), pair[:rows], dims)
    return both[:count] + (both[count:] + dot(high, pair[rows:], dims))


def closing_kernel(dslot_ref, slope_ref, coarses, projects, lay, number, send_ref):
    grad = through(through(dslot_ref[...], projects, NT) * slope_ref[...], coarses, NT)
    high, low = split(jnp.concatenate([grad, number[...]], axis=1))
    send_ref[...] = dot(lay[...], high) + dot(lay[...], low)


def scatter_kernel(message_ref, done_ref, mine_ref, other_ref, total):
    del done_ref
    pixels = mine_ref.shape[2]
    message = message_ref[...]
    number = lax.broadcasted_iota(jnp.int32, (message.shape[0], SIDE * SIDE), 1).astype(F32)
    pick = jnp.where(message[:, pixels : pixels + 1] == number, 1.0, 0.0).astype(BF16)
    high, low = split(message[:, :pixels])
    total[...] = dot(pick, low, TN) + dot(pick, high, TN)
    half = mine_ref.shape[1]
    side = lax.axis_index("lvl")
    mine_ref[0] = total[pl.ds(pl.multiple_of(side * half, half), half), :]
    other_ref[0] = total[pl.ds(pl.multiple_of((1 - side) * half, half), half), :]


def last_kernel(de_hbm, first, deep, out_hbm, de, out, cat, in_sems, out_sems):
    width = de.shape[0]
    steps = de.shape[1] // ROWS

    def load(i):
        return pltpu.make_async_copy(de_hbm.at[:, chunk(i)], de.at[:, chunk(i)], in_sems.at[i])

    def store(i):
        return pltpu.make_async_copy(out.at[chunk(i)], out_hbm.at[chunk(i)], out_sems.at[i])

    def prepare(source):
        for here in blocks(width, 32):
            high, low = split(source[here])
            cat[here], cat[shift(here, width)], cat[shift(here, 2 * width)] = high, high, low

    for i in range(steps - 1):
        load(i).start()
    prepare(first)

    def step(i, _):
        mine = lax.rem(i + steps - 1, steps)
        out[chunk(mine), :] = dot(cat[...], deep[...], TN)
        store(mine).start()

        @pl.when(i + 1 < steps)
        def _():
            load(i).wait()
            prepare(de.at[:, chunk(i)])

        return 0

    lax.fori_loop(0, steps, step, 0)
    for i in range(steps):
        store(i).wait()


def fixed(*values):
    return [pltpu.with_memory_space_constraint(value, pltpu.HBM) for value in values]


def near(*values):
    return [pltpu.with_memory_space_constraint(value, pltpu.VMEM) for value in values]


def stack(kernel, blocks, before, rows):
    shape = (len(blocks) * rows, 128)
    return call(
        kernel,
        "stack",
        1000,
        jax.ShapeDtypeStruct(shape, F32),
        limit=ROOM,
        in_specs=[VMEM] * len(blocks) + [HBM],
        out_specs=VMEM,
    )(*blocks, *fixed(before))


def body(coarse_input, coarse_weight, fine_input, fine_target, crops, in_weight, context_weight, out_weight):
    patch = ("far", "y", "core")
    peers = lax.axis_size(patch)
    far = peers // 4
    patches, tokens, values = fine_input.shape
    width = in_weight.shape[1]
    pixels = coarse_weight.shape[0]
    half = coarse_input.shape[1]
    count = patches * tokens
    swap = [(0, 1), (1, 0)]

    column = [coarse_input]
    for k in range(1, far):
        column.append(lax.ppermute(coarse_input, "far", [(p, (p + k) % far) for p in range(far)]))

    steps = count // ROWS
    pair_shape = (2 * width, values)
    x, t = fine_input.reshape(count, values), fine_target.reshape(count, values)
    xw, xw_last, pair, rows, next_pair, crops = call(
        input_kernel,
        "input",
        6 * count * values * width,
        (
            pltpu.HBM((width, count - ROWS), F32),
            pltpu.VMEM((width, ROWS), F32),
            pltpu.HBM(pair_shape, BF16),
            pltpu.VMEM((ROWS, values), F32),
            pltpu.VMEM(pair_shape, BF16),
            pltpu.VMEM((4, patches), jnp.int32),
        ),
        in_specs=[HBM] * 5,
        out_specs=(HBM, VMEM, HBM, VMEM, VMEM, VMEM),
        scratch_shapes=[
            pltpu.VMEM((count, values), F32),
            pltpu.VMEM((width, count), F32),
            pltpu.VMEM((width, values), F32),
            pltpu.VMEM((width, values), F32),
            pltpu.VMEM(pair_shape, BF16),
            pltpu.VMEM((ROWS, values), BF16),
            pltpu.VMEM((ROWS, values), BF16),
            pltpu.SemaphoreType.DMA((steps,)),
            pltpu.SemaphoreType.DMA((steps,)),
            pltpu.SemaphoreType.DMA((5,)),
        ],
    )(*fixed(x, in_weight.T, t, out_weight, crops.T))
    column = stack(pack_kernel, column, xw, half * 3 // 2)
    own = [column]
    for flip in range(1, 4):
        own.append(lax.ppermute(column, ("lvl", "y"), [(p, p ^ flip) for p in range(4)]))
    tw, xw_last, tw_last, coarses, projects = call(
        target_kernel,
        "target",
        6 * count * values * width,
        (
            pltpu.HBM((width, count - ROWS), F32),
            pltpu.HBM((width, ROWS), F32),
            pltpu.VMEM((width, ROWS), F32),
            pltpu.VMEM((2 * pixels, width), BF16),
            pltpu.VMEM((2 * width, width), BF16),
        ),
        limit=ROOM,
        in_specs=[HBM] * 3 + [VMEM] * 3,
        out_specs=(HBM, HBM, VMEM, VMEM, VMEM),
        scratch_shapes=[
            pltpu.VMEM((count, values), F32),
            pltpu.VMEM((width, count), F32),
            pltpu.VMEM((ROWS, values), BF16),
            pltpu.VMEM((ROWS, values), BF16),
            pltpu.VMEM((pixels, width), F32),
            pltpu.VMEM((width, width), F32),
            pltpu.SemaphoreType.DMA((steps,)),
            pltpu.SemaphoreType.DMA((steps,)),
            pltpu.SemaphoreType.DMA((3,)),
        ],
    )(*fixed(t, coarse_weight, context_weight), *near(rows, next_pair, xw_last))
    own = stack(stack_kernel, own, tw, column.shape[0])
    other = lax.ppermute(own, "core", swap)
    (crops,) = near(crops)
    grams, wanted, lay, number = call(
        functools.partial(prepare_kernel, patches),
        "prepare",
        8 * values * width * width,
        (
            pltpu.VMEM((width, 3 * width), BF16),
            pltpu.VMEM((1, count), jnp.int32),
            pltpu.VMEM((peers * 16, patches * 16), BF16),
            pltpu.VMEM((patches * 16, LANES - pixels), F32),
        ),
        limit=ROOM,
        in_specs=[VMEM, SMEM, HBM],
        out_specs=(VMEM,) * 4,
    )(*near(next_pair), crops, own)

    projected, slope, xw_first, tw_first = call(
        functools.partial(context_kernel, patches, peers),
        "context",
        6 * patches * 16 * width * width,
        (
            pltpu.VMEM((width, 2 * patches * 16), BF16),
            pltpu.VMEM((patches * 16, width), F32),
            pltpu.VMEM((width, ROWS), F32),
            pltpu.VMEM((width, ROWS), F32),
        ),
        limit=ROOM,
        in_specs=[SMEM] + [VMEM] * 4 + [HBM] * 2,
        out_specs=(VMEM,) * 4,
        scratch_shapes=[pltpu.VMEM((patches * 16, pixels), F32), pltpu.SemaphoreType.DMA((2,))],
    )(crops, own, other, *near(coarses, projects), *fixed(xw, tw))
    de, last_de, deep, dslot = call(
        middle_kernel,
        "middle",
        6 * count * width * width,
        (
            pltpu.HBM((width, count), F32),
            pltpu.VMEM((width, ROWS), F32),
            pltpu.VMEM((3 * width, values), BF16),
            pltpu.VMEM((patches * 16, width), F32),
        ),
        limit=ROOM,
        in_specs=[VMEM] * 6 + [HBM] * 4,
        out_specs=(HBM,) + (VMEM,) * 3,
        scratch_shapes=[
            pltpu.VMEM((width, count), F32),
            pltpu.VMEM((width, count), F32),
            pltpu.VMEM((2 * patches * 16, ROWS), BF16),
            pltpu.VMEM((2, width, ROWS), F32),
            pltpu.VMEM((2, 3 * width, ROWS), BF16),
            pltpu.VMEM((2 * width, ROWS), BF16),
            pltpu.SemaphoreType.DMA((steps,)),
            pltpu.SemaphoreType.DMA((steps,)),
            pltpu.SemaphoreType.DMA((steps,)),
            pltpu.SemaphoreType.DMA((2,)),
        ],
    )(*near(projected, grams, wanted, xw_first, tw_first, tw_last), *fixed(xw, xw_last, tw, pair))
    back = call(
        closing_kernel,
        "closing",
        6 * patches * 16 * width * width,
        jax.ShapeDtypeStruct((peers * 16, LANES), F32),
        limit=ROOM,
        in_specs=[VMEM] * 6,
        out_specs=VMEM,
    )(*near(dslot, slope, coarses, projects, lay, number))
    returned = lax.all_to_all(back, patch, 0, 0, tiled=True)

    fine_grad = call(
        last_kernel,
        "last",
        6 * count * values * width,
        pltpu.HBM((count, values), F32),
        limit=ROOM,
        in_specs=[HBM, VMEM, VMEM],
        out_specs=HBM,
        scratch_shapes=[
            pltpu.VMEM((width, count), F32),
            pltpu.VMEM((count, values), F32),
            pltpu.VMEM((3 * width, ROWS), BF16),
            pltpu.SemaphoreType.DMA((steps,)),
            pltpu.SemaphoreType.DMA((steps,)),
        ],
    )(*fixed(de), *near(last_de, deep))
    part = (1, half, pixels)
    mine, theirs = call(
        scatter_kernel,
        "scatter",
        10000,
        (jax.ShapeDtypeStruct(part, F32), jax.ShapeDtypeStruct(part, F32)),
        limit=ROOM,
        in_specs=[VMEM, HBM],
        out_specs=(VMEM, VMEM),
        scratch_shapes=[pltpu.VMEM((SIDE * SIDE, pixels), F32)],
    )(returned, *fixed(fine_grad))
    coarse_grad = mine + lax.ppermute(theirs, "lvl", swap)
    return (coarse_grad, fine_grad.reshape(fine_input.shape))


def solution(mesh):
    sides, peers = mesh.shape["lvl"], mesh.shape["patch"]
    fine = jax.sharding.Mesh(mesh.devices.reshape(sides, peers // 4, 2, 2), ("lvl", "far", "y", "core"))
    patch = ("far", "y", "core")
    both = ("lvl",) + patch
    in_specs = (
        P(patch, "lvl", None),
        P(),
        P(both, None, None),
        P(both, None, None),
        P(both, None),
        P(),
        P(),
        P(),
    )
    out_specs = (P(patch, "lvl", None), P(both, None, None))
    return jax.shard_map(body, mesh=fine, in_specs=in_specs, out_specs=out_specs, check_vma=False)
```

```python
import functools
import math

import jax
import jax.numpy as jnp
from jax import lax
from jax.experimental import pallas as pl
from jax.experimental.pallas import tpu as pltpu
from jax.sharding import PartitionSpec as P

F32 = jnp.float32
BF16 = jnp.bfloat16
NN = (((1,), (0,)), ((), ()))
NT = (((1,), (1,)), ((), ()))
TN = (((0,), (0,)), ((), ()))
ROWS = 512
SIDE = 8
LANES = 256
LIMIT = 60 * 1024 * 1024
ROOM = 40 * 1024 * 1024
SMEM = pl.BlockSpec(memory_space=pltpu.SMEM)
VMEM = pl.BlockSpec(memory_space=pltpu.VMEM)
HBM = pl.BlockSpec(memory_space=pltpu.HBM)


def split(value):
    high = value.astype(BF16)
    low = (value - high.astype(F32)).astype(BF16)
    return high, low


def dot(left, right, dims=NN):
    return lax.dot_general(left, right, dims, preferred_element_type=F32)


def dot3(left, right, dims=NN):
    return (
        dot(left[0], right[1], dims) + dot(left[1], right[0], dims) + dot(left[0], right[0], dims)
    )


def side_by_side(value):
    high, low = split(value)
    return jnp.concatenate([high, low, high], axis=1)


def sigmoid(value):
    return 0.5 * jnp.tanh(0.5 * value) + 0.5


def call(kernel, name, flops, out_shape, limit=LIMIT, **kwargs):
    moved = 8 * sum(math.prod(s.shape) for s in jax.tree.leaves(out_shape))
    return pl.pallas_call(
        kernel,
        out_shape=out_shape,
        name=name,
        cost_estimate=pl.CostEstimate(flops=flops, bytes_accessed=moved, transcendentals=0),
        compiler_params=pltpu.CompilerParams(vmem_limit_bytes=limit),
        **kwargs,
    )


def blocks(rows, size):
    return [slice(start, start + size) for start in range(0, rows, size)]


def shift(here, by):
    return slice(here.start + by, here.stop + by)


def pair_product(pair, value, dims):
    rows = pair.shape[0] // 2
    high, low = split(value)
    both = dot(pair[...], high, dims)
    return both[:rows] + (both[rows:] + dot(pair[:rows], low, dims))


def chunk(i):
    return pl.ds(pl.multiple_of(i * ROWS, ROWS), ROWS)


def wide_product(pair, value, high, low, out):
    width = pair.shape[0] // 2
    for here in blocks(high.shape[0], 16):
        high[here], low[here] = split(value[here])
    both = dot(pair[...], high[...], NT)
    rest = dot(pair[:width], low[...], NT)
    for here in blocks(width, 32):
        out[here] = both[here] + (both[shift(here, width)] + rest[here])


def input_kernel(
    x_hbm,
    weight_hbm,
    t_hbm,
    next_weight_hbm,
    crops_hbm,
    out_hbm,
    out_last,
    pair_hbm,
    next_rows,
    next_pair,
    crops,
    x,
    out,
    weight,
    next_weight,
    pair,
    high,
    low,
    in_sems,
    out_sems,
    sems,
):
    width = weight.shape[0]
    chunks = chunk_rows(x.shape[0])
    fetch = pltpu.make_async_copy(weight_hbm, weight, sems.at[0])
    keep = pltpu.make_async_copy(pair, pair_hbm, sems.at[1])
    fetch_next = pltpu.make_async_copy(next_weight_hbm, next_weight, sems.at[2])
    fetch_rows = pltpu.make_async_copy(t_hbm.at[: next_rows.shape[0]], next_rows, sems.at[3])
    fetch_crops = pltpu.make_async_copy(crops_hbm, crops, sems.at[4])
    loads = [
        pltpu.make_async_copy(x_hbm.at[here], x.at[here], in_sems.at[i]) for i, here in enumerate(chunks)
    ]
    stores = [
        pltpu.make_async_copy(out.at[:, here], out_hbm.at[:, here], out_sems.at[i])
        for i, here in enumerate(chunks[:-1])
    ]
    for copy in [fetch] + loads[:2]:
        copy.start()
    for i, here in enumerate(chunks):
        loads[i].wait()
        if i + 2 < len(chunks):
            loads[i + 2].start()
        if i == 0:
            fetch.wait()
            pair[:width], pair[width:] = split(weight[...])
            keep.start()
            fetch_next.start()
        if i == 1:
            fetch_rows.start()
            fetch_crops.start()
        if i == len(chunks) - 1:
            fetch_next.wait()
            next_pair[:width], next_pair[width:] = split(next_weight[...])
        target = out.at[:, here] if i < len(stores) else out_last
        wide_product(pair, x.at[here], high, low, target)
        if i < len(stores):
            stores[i].start()
    for copy in [keep, fetch_rows, fetch_crops] + stores:
        copy.wait()


def target_kernel(
    t_hbm,
    cwgt_hbm,
    xwgt_hbm,
    rows,
    pair,
    before_last,
    out_hbm,
    before_hbm,
    out_last,
    coarses,
    projects,
    t,
    out,
    high,
    low,
    cwgt,
    xwgt,
    in_sems,
    out_sems,
    sems,
):
    chunks = chunk_rows(t.shape[0])
    fetches = [
        pltpu.make_async_copy(cwgt_hbm, cwgt, sems.at[0]),
        pltpu.make_async_copy(xwgt_hbm, xwgt, sems.at[1]),
    ]
    loads = [
        pltpu.make_async_copy(t_hbm.at[here], t.at[here], in_sems.at[i])
        for i, here in enumerate(chunks[1:])
    ]
    stores = [
        pltpu.make_async_copy(out.at[:, here], out_hbm.at[:, here], out_sems.at[i])
        for i, here in enumerate(chunks[:-1])
    ]
    keep = pltpu.make_async_copy(before_last, before_hbm, sems.at[2])
    for copy in loads + fetches:
        copy.start()
    for i, here in enumerate(chunks):
        if i > 0:
            loads[i - 1].wait()
        if i == 2:
            keep.start()
        source = rows if i == 0 else t.at[here]
        if i < len(stores):
            wide_product(pair, source, high, low, out.at[:, here])
            stores[i].start()
        else:
            wide_product(pair, source, high, low, out_last)
    for copy in fetches:
        copy.wait()
    coarses[...] = jnp.concatenate(split(cwgt[...]), axis=0)
    projects[...] = jnp.concatenate(split(xwgt[...]), axis=0)
    for copy in stores + [keep]:
        copy.wait()


def chunk_rows(count):
    return [slice(start, start + ROWS) for start in range(0, count, ROWS)]


def prepare_kernel(patches, pair, crops_ref, before_ref, grams, wanted, lay, number):
    del before_ref
    width = grams.shape[0]
    both = dot(pair[...], pair[:width], NT)
    grams[...] = side_by_side(both[:width] + (both[width:] + both[width:].T))
    wanted[...] = slot_row(crops_ref, patches, wanted.shape[1] // patches)
    frame = row_value(crops_ref, 0, patches, (1, patches * 16), 1, 16)
    slot = lax.broadcasted_iota(jnp.int32, (1, patches * 16), 1) % 16
    line = lax.broadcasted_iota(jnp.int32, lay.shape, 0)
    lay[...] = jnp.where(line == frame * 16 + slot, 1.0, 0.0).astype(BF16)
    slot = lax.broadcasted_iota(jnp.int32, number.shape, 0) % 16
    top = row_value(crops_ref, 1, patches, number.shape, 0, 16)
    left = row_value(crops_ref, 2, patches, number.shape, 0, 16)
    number[...] = ((top + slot // 4) * SIDE + left + slot % 4).astype(F32)


def stack_kernel(*refs):
    *block_refs, _, out_ref = refs
    size = block_refs[0].shape[0]
    for k, ref in enumerate(block_refs):
        out_ref[k * size : (k + 1) * size] = ref[...]


def pack_kernel(*refs):
    *block_refs, _, out_ref = refs
    tokens = block_refs[0].shape[1]
    size = tokens * 3 // 2
    for k, ref in enumerate(block_refs):
        out_ref[k * size : k * size + tokens] = ref[0, :, :128]
        tails = [ref[0, : tokens // 2, 128:], ref[0, tokens // 2 :, 128:]]
        out_ref[k * size + tokens : (k + 1) * size] = jnp.concatenate(tails, axis=1)


def row_value(crops_ref, column, patches, shape, axis, each):
    index = lax.broadcasted_iota(jnp.int32, shape, axis) // each
    found = jnp.zeros(shape, jnp.int32)
    for j in range(patches):
        found = jnp.where(index == j, crops_ref[column, j], found)
    return found


def slot_row(crops_ref, patches, tokens):
    scale = row_value(crops_ref, 3, patches, (1, patches * tokens), 1, tokens)
    token = lax.broadcasted_iota(jnp.int32, (1, patches * tokens), 1)
    row, column = (token % tokens) // 16, token % 16
    return token // tokens * 16 + (row * scale // 8) * 4 + column * scale // 8


def taking(wanted, slots, first):
    slot = lax.broadcasted_iota(jnp.int32, (slots, wanted.shape[1]), 0) + first
    return jnp.where(slot == wanted, 1.0, 0.0).astype(BF16)


def context_kernel(
    patches,
    peers,
    crops_vmem,
    own_ref,
    other_ref,
    coarses,
    projects,
    xw_hbm,
    tw_hbm,
    projected_ref,
    slope_ref,
    xw_first,
    tw_first,
    rows,
    crops_ref,
    sems,
):
    fetches = [
        pltpu.make_async_copy(xw_hbm.at[:, : xw_first.shape[1]], xw_first, sems.at[0]),
        pltpu.make_async_copy(tw_hbm.at[:, : tw_first.shape[1]], tw_first, sems.at[1]),
    ]
    for copy in fetches:
        copy.start()
    take = pltpu.make_async_copy(crops_vmem, crops_ref, sems.at[2])
    take.start()
    take.wait()
    pixels = coarses.shape[0] // 2
    width = projects.shape[1]
    far = peers // 4
    me, side = lax.axis_index(("far", "y", "core")), lax.axis_index("lvl")
    for j in range(patches):
        frame, top, left = crops_ref[0, j], crops_ref[1, j], crops_ref[2, j]
        near_by = lax.bitwise_xor(frame % 4, me % 4)
        k = (me // 4 - frame // 4 + far) % far
        k = jnp.where(k == 1, 2, jnp.where(k == 2, 1, k))
        here = near_by % 2 == 0
        for a in range(4):
            row = jnp.minimum(top + a, SIDE - 1)
            shard = (lax.bitwise_xor(row // 4, side) * 2 + near_by // 2) * far + k
            row = row % 4
            start = shard * (6 * SIDE)
            wide = pl.ds(pl.multiple_of(start + row * SIDE, SIDE), SIDE)
            tail = pl.ds(pl.multiple_of(start + (4 + row % 2) * SIDE, SIDE), SIDE)
            into = slice(j * 16 + a * 4, j * 16 + a * 4 + 4)
            line = jnp.where(here, own_ref[wide, :], other_ref[wide, :])
            rows[into, :128] = pltpu.roll(line, SIDE - left, 0)[:4, :]
            line = pltpu.roll(jnp.where(here, own_ref[tail, :], other_ref[tail, :]), SIDE - left, 0)[:4, :]
            rows[into, 128:] = jnp.where(row >= 2, line[:, 64:], line[:, :64])
    pre = through(rows[...], coarses, NN)
    gate = sigmoid(pre)
    slope_ref[...] = gate * (1.0 + pre * (1.0 - gate))
    projected = through(pre * gate, projects, NN).T
    projected_ref[...] = jnp.concatenate(split(projected), axis=1)
    for copy in fetches:
        copy.wait()


def middle_kernel(
    projected,
    grams,
    wanted,
    xw_first,
    tw_first,
    tw_last,
    xw_hbm,
    xw_last,
    tw_hbm,
    pair_hbm,
    de_hbm,
    de_ref,
    deep_ref,
    dslot_ref,
    xw,
    tw,
    taken,
    factor,
    deep,
    parts,
    xw_sems,
    tw_sems,
    out_sems,
    sems,
):
    width, count = xw.shape
    slots = dslot_ref.shape[0]
    chunks = chunk_rows(count)
    each = slots // len(chunks)
    tw_loads = [
        pltpu.make_async_copy(tw_hbm.at[:, here], tw.at[:, here], tw_sems.at[i])
        for i, here in enumerate(chunks[1:-1])
    ]
    xw_loads = [
        pltpu.make_async_copy(xw_hbm.at[:, here], xw.at[:, here], xw_sems.at[i])
        for i, here in enumerate(chunks[2:-1])
    ]
    xw_loads.append(pltpu.make_async_copy(xw_last, xw.at[:, chunks[-1]], xw_sems.at[len(xw_loads)]))
    stores = [
        pltpu.make_async_copy(xw.at[:, here], de_hbm.at[:, here], out_sems.at[i])
        for i, here in enumerate(chunks[:-1])
    ]
    fetches = [
        pltpu.make_async_copy(pair_hbm, deep_ref.at[: 2 * width], sems.at[0]),
        pltpu.make_async_copy(pair_hbm.at[:width], deep_ref.at[2 * width :], sems.at[1]),
    ]
    for pair in zip(tw_loads, xw_loads):
        for copy in pair:
            copy.start()
    for copy in fetches:
        copy.start()

    def begin(i):
        tokens = chunks[i]
        source = xw_first.at[:, tokens] if i < 2 else xw.at[:, tokens]
        here = taking(wanted[:, tokens], slots, 0)
        taken[:slots], taken[slots:] = here, here
        spread = dot(projected[...], taken[...])
        for here in blocks(width, 32):
            pre = source[here] + spread[here]
            gate = sigmoid(pre)
            hidden = pre * gate
            factor[i % 2, here] = gate + hidden * (1.0 - gate)
            high, low = split(hidden)
            for part, value in enumerate((high, high, low)):
                deep[i % 2, shift(here, part * width)] = value

    begin(0)
    for i, tokens in enumerate(chunks):
        if 0 < i < len(chunks) - 1:
            tw_loads[i - 1].wait()
            xw_loads[i - 1].wait()
        minus = tw_first if i == 0 else tw_last if i == len(chunks) - 1 else tw.at[:, tokens]
        target = de_ref if i == len(chunks) - 1 else xw.at[:, tokens]
        product = dot(grams[...], deep[i % 2])
        if i + 1 < len(chunks):
            begin(i + 1)
        for here in blocks(width, 32):
            de = (product[here] - minus[here]) * factor[i % 2, here]
            target[here] = de
            parts[here], parts[shift(here, width)] = split(de)
        mine = slice(i * each, (i + 1) * each)
        both = dot(taking(wanted[:, tokens], each, i * each), parts[...], NT)
        dslot_ref[mine] = both[:, :width] + both[:, width:]
        if i < len(stores):
            stores[i].start()
    for copy in stores + fetches:
        copy.wait()


def through(value, pair, dims):
    count, rows = value.shape[0], pair.shape[0] // 2
    high, low = split(value)
    both = dot(jnp.concatenate([high, low], axis=0), pair[:rows], dims)
    return both[:count] + (both[count:] + dot(high, pair[rows:], dims))


def closing_kernel(dslot_ref, slope_ref, coarses, projects, lay, number, send_ref):
    grad = through(through(dslot_ref[...], projects, NT) * slope_ref[...], coarses, NT)
    high, low = split(jnp.concatenate([grad, number[...]], axis=1))
    send_ref[...] = dot(lay[...], high) + dot(lay[...], low)


def scatter_kernel(message_ref, done_ref, mine_ref, other_ref, total):
    del done_ref
    pixels = mine_ref.shape[2]
    message = message_ref[...]
    number = lax.broadcasted_iota(jnp.int32, (message.shape[0], SIDE * SIDE), 1).astype(F32)
    pick = jnp.where(message[:, pixels : pixels + 1] == number, 1.0, 0.0).astype(BF16)
    high, low = split(message[:, :pixels])
    total[...] = dot(pick, low, TN) + dot(pick, high, TN)
    half = mine_ref.shape[1]
    side = lax.axis_index("lvl")
    mine_ref[0] = total[pl.ds(pl.multiple_of(side * half, half), half), :]
    other_ref[0] = total[pl.ds(pl.multiple_of((1 - side) * half, half), half), :]


def last_kernel(de_hbm, first, deep, out_hbm, de, out, cat, in_sems, out_sems):
    width = de.shape[0]
    steps = de.shape[1] // ROWS

    def load(i):
        return pltpu.make_async_copy(de_hbm.at[:, chunk(i)], de.at[:, chunk(i)], in_sems.at[i])

    def store(i):
        return pltpu.make_async_copy(out.at[chunk(i)], out_hbm.at[chunk(i)], out_sems.at[i])

    def prepare(source):
        for here in blocks(width, 32):
            high, low = split(source[here])
            cat[here], cat[shift(here, width)], cat[shift(here, 2 * width)] = high, high, low

    for i in range(steps - 1):
        load(i).start()
    prepare(first)

    def step(i, _):
        mine = lax.rem(i + steps - 1, steps)
        out[chunk(mine), :] = dot(cat[...], deep[...], TN)
        store(mine).start()

        @pl.when(i + 1 < steps)
        def _():
            load(i).wait()
            prepare(de.at[:, chunk(i)])

        return 0

    lax.fori_loop(0, steps, step, 0)
    for i in range(steps):
        store(i).wait()


def fixed(*values):
    return [pltpu.with_memory_space_constraint(value, pltpu.HBM) for value in values]


def near(*values):
    return [pltpu.with_memory_space_constraint(value, pltpu.VMEM) for value in values]


def stack(kernel, blocks, before, rows):
    shape = (len(blocks) * rows, 128)
    return call(
        kernel,
        "stack",
        1000,
        jax.ShapeDtypeStruct(shape, F32),
        limit=ROOM,
        in_specs=[VMEM] * len(blocks) + [HBM],
        out_specs=VMEM,
    )(*blocks, *fixed(before))


def body(coarse_input, coarse_weight, fine_input, fine_target, crops, in_weight, context_weight, out_weight):
    patch = ("far", "y", "core")
    peers = lax.axis_size(patch)
    far = peers // 4
    patches, tokens, values = fine_input.shape
    width = in_weight.shape[1]
    pixels = coarse_weight.shape[0]
    half = coarse_input.shape[1]
    count = patches * tokens
    swap = [(0, 1), (1, 0)]

    column = {0: coarse_input}
    for k in range(1, far):
        column[k] = lax.ppermute(coarse_input, "far", [(p, (p + k) % far) for p in range(far)])
    column = [column[k] for k in [0, 2, 1] + list(range(3, far))]

    steps = count // ROWS
    pair_shape = (2 * width, values)
    x, t = fine_input.reshape(count, values), fine_target.reshape(count, values)
    xw, xw_last, pair, rows, next_pair, crops = call(
        input_kernel,
        "input",
        6 * count * values * width,
        (
            pltpu.HBM((width, count - ROWS), F32),
            pltpu.VMEM((width, ROWS), F32),
            pltpu.HBM(pair_shape, BF16),
            pltpu.VMEM((ROWS, values), F32),
            pltpu.VMEM(pair_shape, BF16),
            pltpu.VMEM((4, patches), jnp.int32),
        ),
        in_specs=[HBM] * 5,
        out_specs=(HBM, VMEM, HBM, VMEM, VMEM, VMEM),
        scratch_shapes=[
            pltpu.VMEM((count, values), F32),
            pltpu.VMEM((width, count), F32),
            pltpu.VMEM((width, values), F32),
            pltpu.VMEM((width, values), F32),
            pltpu.VMEM(pair_shape, BF16),
            pltpu.VMEM((ROWS, values), BF16),
            pltpu.VMEM((ROWS, values), BF16),
            pltpu.SemaphoreType.DMA((steps,)),
            pltpu.SemaphoreType.DMA((steps,)),
            pltpu.SemaphoreType.DMA((5,)),
        ],
    )(*fixed(x, in_weight.T, t, out_weight, crops.T))
    column = stack(pack_kernel, column, xw, half * 3 // 2)
    own = [column]
    for flip in range(1, 4):
        own.append(lax.ppermute(column, ("lvl", "y"), [(p, p ^ flip) for p in range(4)]))
    tw, xw_last, tw_last, coarses, projects = call(
        target_kernel,
        "target",
        6 * count * values * width,
        (
            pltpu.HBM((width, count - ROWS), F32),
            pltpu.HBM((width, ROWS), F32),
            pltpu.VMEM((width, ROWS), F32),
            pltpu.VMEM((2 * pixels, width), BF16),
            pltpu.VMEM((2 * width, width), BF16),
        ),
        limit=ROOM,
        in_specs=[HBM] * 3 + [VMEM] * 3,
        out_specs=(HBM, HBM, VMEM, VMEM, VMEM),
        scratch_shapes=[
            pltpu.VMEM((count, values), F32),
            pltpu.VMEM((width, count), F32),
            pltpu.VMEM((ROWS, values), BF16),
            pltpu.VMEM((ROWS, values), BF16),
            pltpu.VMEM((pixels, width), F32),
            pltpu.VMEM((width, width), F32),
            pltpu.SemaphoreType.DMA((steps,)),
            pltpu.SemaphoreType.DMA((steps,)),
            pltpu.SemaphoreType.DMA((3,)),
        ],
    )(*fixed(t, coarse_weight, context_weight), *near(rows, next_pair, xw_last))
    own = stack(stack_kernel, own, tw, column.shape[0])
    other = lax.ppermute(own, "core", swap)
    (crops,) = near(crops)
    grams, wanted, lay, number = call(
        functools.partial(prepare_kernel, patches),
        "prepare",
        8 * values * width * width,
        (
            pltpu.VMEM((width, 3 * width), BF16),
            pltpu.VMEM((1, count), jnp.int32),
            pltpu.VMEM((peers * 16, patches * 16), BF16),
            pltpu.VMEM((patches * 16, LANES - pixels), F32),
        ),
        limit=ROOM,
        in_specs=[VMEM, SMEM, HBM],
        out_specs=(VMEM,) * 4,
    )(*near(next_pair), crops, own)

    projected, slope, xw_first, tw_first = call(
        functools.partial(context_kernel, patches, peers),
        "context",
        6 * patches * 16 * width * width,
        (
            pltpu.VMEM((width, 2 * patches * 16), BF16),
            pltpu.VMEM((patches * 16, width), F32),
            pltpu.VMEM((width, 2 * ROWS), F32),
            pltpu.VMEM((width, ROWS), F32),
        ),
        limit=ROOM,
        in_specs=[VMEM] * 5 + [HBM] * 2,
        out_specs=(VMEM,) * 4,
        scratch_shapes=[
            pltpu.VMEM((patches * 16, pixels), F32),
            pltpu.SMEM((4, patches), jnp.int32),
            pltpu.SemaphoreType.DMA((3,)),
        ],
    )(crops, own, other, *near(coarses, projects), *fixed(xw, tw))
    de, last_de, deep, dslot = call(
        middle_kernel,
        "middle",
        6 * count * width * width,
        (
            pltpu.HBM((width, count), F32),
            pltpu.VMEM((width, ROWS), F32),
            pltpu.VMEM((3 * width, values), BF16),
            pltpu.VMEM((patches * 16, width), F32),
        ),
        limit=ROOM,
        in_specs=[VMEM] * 6 + [HBM] * 4,
        out_specs=(HBM,) + (VMEM,) * 3,
        scratch_shapes=[
            pltpu.VMEM((width, count), F32),
            pltpu.VMEM((width, count), F32),
            pltpu.VMEM((2 * patches * 16, ROWS), BF16),
            pltpu.VMEM((2, width, ROWS), F32),
            pltpu.VMEM((2, 3 * width, ROWS), BF16),
            pltpu.VMEM((2 * width, ROWS), BF16),
            pltpu.SemaphoreType.DMA((steps,)),
            pltpu.SemaphoreType.DMA((steps,)),
            pltpu.SemaphoreType.DMA((steps,)),
            pltpu.SemaphoreType.DMA((2,)),
        ],
    )(*near(projected, grams, wanted, xw_first, tw_first, tw_last), *fixed(xw, xw_last, tw, pair))
    back = call(
        closing_kernel,
        "closing",
        6 * patches * 16 * width * width,
        jax.ShapeDtypeStruct((peers * 16, LANES), F32),
        limit=ROOM,
        in_specs=[VMEM] * 6,
        out_specs=VMEM,
    )(*near(dslot, slope, coarses, projects, lay, number))
    returned = lax.all_to_all(back, patch, 0, 0, tiled=True)

    fine_grad = call(
        last_kernel,
        "last",
        6 * count * values * width,
        pltpu.HBM((count, values), F32),
        limit=ROOM,
        in_specs=[HBM, VMEM, VMEM],
        out_specs=HBM,
        scratch_shapes=[
            pltpu.VMEM((width, count), F32),
            pltpu.VMEM((count, values), F32),
            pltpu.VMEM((3 * width, ROWS), BF16),
            pltpu.SemaphoreType.DMA((steps,)),
            pltpu.SemaphoreType.DMA((steps,)),
        ],
    )(*fixed(de), *near(last_de, deep))
    part = (1, half, pixels)
    mine, theirs = call(
        scatter_kernel,
        "scatter",
        10000,
        (jax.ShapeDtypeStruct(part, F32), jax.ShapeDtypeStruct(part, F32)),
        limit=ROOM,
        in_specs=[VMEM, HBM],
        out_specs=(VMEM, VMEM),
        scratch_shapes=[pltpu.VMEM((SIDE * SIDE, pixels), F32)],
    )(returned, *fixed(fine_grad))
    coarse_grad = mine + lax.ppermute(theirs, "lvl", swap)
    return (coarse_grad, fine_grad.reshape(fine_input.shape))


def solution(mesh):
    sides, peers = mesh.shape["lvl"], mesh.shape["patch"]
    fine = jax.sharding.Mesh(mesh.devices.reshape(sides, peers // 4, 2, 2), ("lvl", "far", "y", "core"))
    patch = ("far", "y", "core")
    both = ("lvl",) + patch
    in_specs = (
        P(patch, "lvl", None),
        P(),
        P(both, None, None),
        P(both, None, None),
        P(both, None),
        P(),
        P(),
        P(),
    )
    out_specs = (P(patch, "lvl", None), P(both, None, None))
    return jax.shard_map(body, mesh=fine, in_specs=in_specs, out_specs=out_specs, check_vma=False)
```

```python
import functools
import math

import jax
import jax.numpy as jnp
from jax import lax
from jax.experimental import pallas as pl
from jax.experimental.pallas import tpu as pltpu
from jax.sharding import PartitionSpec as P

F32 = jnp.float32
BF16 = jnp.bfloat16
NN = (((1,), (0,)), ((), ()))
NT = (((1,), (1,)), ((), ()))
TN = (((0,), (0,)), ((), ()))
ROWS = 512
SIDE = 8
LANES = 256
LIMIT = 60 * 1024 * 1024
ROOM = 40 * 1024 * 1024
SMEM = pl.BlockSpec(memory_space=pltpu.SMEM)
VMEM = pl.BlockSpec(memory_space=pltpu.VMEM)
HBM = pl.BlockSpec(memory_space=pltpu.HBM)


def split(value):
    high = value.astype(BF16)
    low = (value - high.astype(F32)).astype(BF16)
    return high, low


def dot(left, right, dims=NN):
    return lax.dot_general(left, right, dims, preferred_element_type=F32)


def dot3(left, right, dims=NN):
    return (
        dot(left[0], right[1], dims) + dot(left[1], right[0], dims) + dot(left[0], right[0], dims)
    )


def side_by_side(value):
    high, low = split(value)
    return jnp.concatenate([high, low, high], axis=1)


def sigmoid(value):
    return 0.5 * jnp.tanh(0.5 * value) + 0.5


def call(kernel, name, flops, out_shape, limit=LIMIT, **kwargs):
    moved = 8 * sum(math.prod(s.shape) for s in jax.tree.leaves(out_shape))
    return pl.pallas_call(
        kernel,
        out_shape=out_shape,
        name=name,
        cost_estimate=pl.CostEstimate(flops=flops, bytes_accessed=moved, transcendentals=0),
        compiler_params=pltpu.CompilerParams(vmem_limit_bytes=limit),
        **kwargs,
    )


def blocks(rows, size):
    return [slice(start, start + size) for start in range(0, rows, size)]


def shift(here, by):
    return slice(here.start + by, here.stop + by)


def pair_product(pair, value, dims):
    rows = pair.shape[0] // 2
    high, low = split(value)
    both = dot(pair[...], high, dims)
    return both[:rows] + (both[rows:] + dot(pair[:rows], low, dims))


def chunk(i):
    return pl.ds(pl.multiple_of(i * ROWS, ROWS), ROWS)


def wide_product(pair, value, high, low, out):
    width = pair.shape[0] // 2
    for here in blocks(high.shape[0], 16):
        high[here], low[here] = split(value[here])
    both = dot(pair[...], high[...], NT)
    rest = dot(pair[:width], low[...], NT)
    for here in blocks(width, 32):
        out[here] = both[here] + (both[shift(here, width)] + rest[here])


def input_kernel(
    x_hbm,
    weight_hbm,
    t_hbm,
    next_weight_hbm,
    crops_hbm,
    out_hbm,
    out_last,
    pair_hbm,
    next_rows,
    next_pair,
    crops,
    x,
    out,
    weight,
    next_weight,
    pair,
    high,
    low,
    in_sems,
    out_sems,
    sems,
):
    width = weight.shape[0]
    chunks = chunk_rows(x.shape[0])
    fetch = pltpu.make_async_copy(weight_hbm, weight, sems.at[0])
    keep = pltpu.make_async_copy(pair, pair_hbm, sems.at[1])
    fetch_next = pltpu.make_async_copy(next_weight_hbm, next_weight, sems.at[2])
    fetch_rows = pltpu.make_async_copy(t_hbm.at[: next_rows.shape[0]], next_rows, sems.at[3])
    fetch_crops = pltpu.make_async_copy(crops_hbm, crops, sems.at[4])
    loads = [
        pltpu.make_async_copy(x_hbm.at[here], x.at[here], in_sems.at[i]) for i, here in enumerate(chunks)
    ]
    stores = [
        pltpu.make_async_copy(out.at[:, here], out_hbm.at[:, here], out_sems.at[i])
        for i, here in enumerate(chunks[:-1])
    ]
    for copy in [fetch] + loads[:2]:
        copy.start()
    for i, here in enumerate(chunks):
        loads[i].wait()
        if i + 2 < len(chunks):
            loads[i + 2].start()
        if i == 0:
            fetch.wait()
            pair[:width], pair[width:] = split(weight[...])
            keep.start()
            fetch_next.start()
        if i == 1:
            fetch_rows.start()
            fetch_crops.start()
        if i == len(chunks) - 1:
            fetch_next.wait()
            next_pair[:width], next_pair[width:] = split(next_weight[...])
        target = out.at[:, here] if i < len(stores) else out_last
        wide_product(pair, x.at[here], high, low, target)
        if i < len(stores):
            stores[i].start()
    for copy in [keep, fetch_rows, fetch_crops] + stores:
        copy.wait()


def target_kernel(
    t_hbm,
    cwgt_hbm,
    xwgt_hbm,
    rows,
    pair,
    before_last,
    out_hbm,
    before_hbm,
    out_last,
    coarses,
    projects,
    t,
    out,
    high,
    low,
    cwgt,
    xwgt,
    in_sems,
    out_sems,
    sems,
):
    chunks = chunk_rows(t.shape[0])
    fetches = [
        pltpu.make_async_copy(cwgt_hbm, cwgt, sems.at[0]),
        pltpu.make_async_copy(xwgt_hbm, xwgt, sems.at[1]),
    ]
    loads = [
        pltpu.make_async_copy(t_hbm.at[here], t.at[here], in_sems.at[i])
        for i, here in enumerate(chunks[1:])
    ]
    stores = [
        pltpu.make_async_copy(out.at[:, here], out_hbm.at[:, here], out_sems.at[i])
        for i, here in enumerate(chunks[:-1])
    ]
    keep = pltpu.make_async_copy(before_last, before_hbm, sems.at[2])
    for copy in loads + fetches:
        copy.start()
    for i, here in enumerate(chunks):
        if i > 0:
            loads[i - 1].wait()
        if i == 2:
            keep.start()
        source = rows if i == 0 else t.at[here]
        if i < len(stores):
            wide_product(pair, source, high, low, out.at[:, here])
            stores[i].start()
        else:
            wide_product(pair, source, high, low, out_last)
    for copy in fetches:
        copy.wait()
    coarses[...] = jnp.concatenate(split(cwgt[...]), axis=0)
    projects[...] = jnp.concatenate(split(xwgt[...]), axis=0)
    for copy in stores + [keep]:
        copy.wait()


def chunk_rows(count):
    return [slice(start, start + ROWS) for start in range(0, count, ROWS)]


def prepare_kernel(patches, pair, crops_ref, before_ref, grams, wanted, lay, number):
    del before_ref
    width = grams.shape[0]
    both = dot(pair[...], pair[:width], NT)
    grams[...] = side_by_side(both[:width] + (both[width:] + both[width:].T))
    wanted[...] = slot_row(crops_ref, patches, wanted.shape[1] // patches)
    frame = row_value(crops_ref, 0, patches, (1, patches * 16), 1, 16)
    slot = lax.broadcasted_iota(jnp.int32, (1, patches * 16), 1) % 16
    line = lax.broadcasted_iota(jnp.int32, lay.shape, 0)
    lay[...] = jnp.where(line == frame * 16 + slot, 1.0, 0.0).astype(BF16)
    slot = lax.broadcasted_iota(jnp.int32, number.shape, 0) % 16
    top = row_value(crops_ref, 1, patches, number.shape, 0, 16)
    left = row_value(crops_ref, 2, patches, number.shape, 0, 16)
    number[...] = ((top + slot // 4) * SIDE + left + slot % 4).astype(F32)


def stack_kernel(*refs):
    *block_refs, _, out_ref = refs
    size = block_refs[0].shape[0]
    for k, ref in enumerate(block_refs):
        out_ref[k * size : (k + 1) * size] = ref[...]


def pack_kernel(*refs):
    *block_refs, _, out_ref = refs
    tokens = block_refs[0].shape[1]
    size = tokens * 3 // 2
    for k, ref in enumerate(block_refs):
        out_ref[k * size : k * size + tokens] = ref[0, :, :128]
        tails = [ref[0, : tokens // 2, 128:], ref[0, tokens // 2 :, 128:]]
        out_ref[k * size + tokens : (k + 1) * size] = jnp.concatenate(tails, axis=1)


def row_value(crops_ref, column, patches, shape, axis, each):
    index = lax.broadcasted_iota(jnp.int32, shape, axis) // each
    found = jnp.zeros(shape, jnp.int32)
    for j in range(patches):
        found = jnp.where(index == j, crops_ref[column, j], found)
    return found


def slot_row(crops_ref, patches, tokens):
    scale = row_value(crops_ref, 3, patches, (1, patches * tokens), 1, tokens)
    token = lax.broadcasted_iota(jnp.int32, (1, patches * tokens), 1)
    row, column = (token % tokens) // 16, token % 16
    return token // tokens * 16 + (row * scale // 8) * 4 + column * scale // 8


def taking(wanted, slots, first):
    slot = lax.broadcasted_iota(jnp.int32, (slots, wanted.shape[1]), 0) + first
    return jnp.where(slot == wanted, 1.0, 0.0).astype(BF16)


def context_kernel(
    patches,
    peers,
    crops_vmem,
    own_ref,
    other_ref,
    coarses,
    projects,
    xw_hbm,
    tw_hbm,
    projected_ref,
    slope_ref,
    xw_first,
    tw_first,
    rows,
    crops_ref,
    sems,
):
    fetches = [
        pltpu.make_async_copy(xw_hbm.at[:, : xw_first.shape[1]], xw_first, sems.at[0]),
        pltpu.make_async_copy(tw_hbm.at[:, : tw_first.shape[1]], tw_first, sems.at[1]),
    ]
    for copy in fetches:
        copy.start()
    take = pltpu.make_async_copy(crops_vmem, crops_ref, sems.at[2])
    take.start()
    take.wait()
    pixels = coarses.shape[0] // 2
    width = projects.shape[1]
    far = peers // 4
    me, side = lax.axis_index(("far", "y", "core")), lax.axis_index("lvl")
    for j in range(patches):
        frame, top, left = crops_ref[0, j], crops_ref[1, j], crops_ref[2, j]
        near_by = lax.bitwise_xor(frame % 4, me % 4)
        k = lax.bitwise_xor(frame // 4, me // 4)
        k = jnp.where(k == 1, 2, jnp.where(k == 2, 1, k))
        here = near_by % 2 == 0
        for a in range(4):
            row = jnp.minimum(top + a, SIDE - 1)
            shard = (lax.bitwise_xor(row // 4, side) * 2 + near_by // 2) * far + k
            row = row % 4
            start = shard * (6 * SIDE)
            wide = pl.ds(pl.multiple_of(start + row * SIDE, SIDE), SIDE)
            tail = pl.ds(pl.multiple_of(start + (4 + row % 2) * SIDE, SIDE), SIDE)
            into = slice(j * 16 + a * 4, j * 16 + a * 4 + 4)
            line = jnp.where(here, own_ref[wide, :], other_ref[wide, :])
            rows[into, :128] = pltpu.roll(line, SIDE - left, 0)[:4, :]
            line = pltpu.roll(jnp.where(here, own_ref[tail, :], other_ref[tail, :]), SIDE - left, 0)[:4, :]
            rows[into, 128:] = jnp.where(row >= 2, line[:, 64:], line[:, :64])
    pre = through(rows[...], coarses, NN)
    gate = sigmoid(pre)
    slope_ref[...] = gate * (1.0 + pre * (1.0 - gate))
    projected = through(pre * gate, projects, NN).T
    projected_ref[...] = jnp.concatenate(split(projected), axis=1)
    for copy in fetches:
        copy.wait()


def middle_kernel(
    projected,
    grams,
    wanted,
    xw_first,
    tw_first,
    tw_last,
    xw_hbm,
    xw_last,
    tw_hbm,
    pair_hbm,
    de_hbm,
    de_ref,
    deep_ref,
    dslot_ref,
    xw,
    tw,
    taken,
    factor,
    deep,
    parts,
    xw_sems,
    tw_sems,
    out_sems,
    sems,
):
    width, count = xw.shape
    slots = dslot_ref.shape[0]
    chunks = chunk_rows(count)
    each = slots // len(chunks)
    tw_loads = [
        pltpu.make_async_copy(tw_hbm.at[:, here], tw.at[:, here], tw_sems.at[i])
        for i, here in enumerate(chunks[1:-1])
    ]
    xw_loads = [
        pltpu.make_async_copy(xw_hbm.at[:, here], xw.at[:, here], xw_sems.at[i])
        for i, here in enumerate(chunks[2:-1])
    ]
    xw_loads.append(pltpu.make_async_copy(xw_last, xw.at[:, chunks[-1]], xw_sems.at[len(xw_loads)]))
    stores = [
        pltpu.make_async_copy(xw.at[:, here], de_hbm.at[:, here], out_sems.at[i])
        for i, here in enumerate(chunks[:-1])
    ]
    fetches = [
        pltpu.make_async_copy(pair_hbm, deep_ref.at[: 2 * width], sems.at[0]),
        pltpu.make_async_copy(pair_hbm.at[:width], deep_ref.at[2 * width :], sems.at[1]),
    ]
    for pair in zip(tw_loads, xw_loads):
        for copy in pair:
            copy.start()
    for copy in fetches:
        copy.start()

    def begin(i):
        tokens = chunks[i]
        source = xw_first.at[:, tokens] if i < 2 else xw.at[:, tokens]
        here = taking(wanted[:, tokens], slots, 0)
        taken[:slots], taken[slots:] = here, here
        spread = dot(projected[...], taken[...])
        for here in blocks(width, 32):
            pre = source[here] + spread[here]
            gate = sigmoid(pre)
            hidden = pre * gate
            factor[i % 2, here] = gate + hidden * (1.0 - gate)
            high, low = split(hidden)
            for part, value in enumerate((high, high, low)):
                deep[i % 2, shift(here, part * width)] = value

    begin(0)
    for i, tokens in enumerate(chunks):
        if 0 < i < len(chunks) - 1:
            tw_loads[i - 1].wait()
            xw_loads[i - 1].wait()
        minus = tw_first if i == 0 else tw_last if i == len(chunks) - 1 else tw.at[:, tokens]
        target = de_ref if i == len(chunks) - 1 else xw.at[:, tokens]
        product = dot(grams[...], deep[i % 2])
        if i + 1 < len(chunks):
            begin(i + 1)
        for here in blocks(width, 32):
            de = (product[here] - minus[here]) * factor[i % 2, here]
            target[here] = de
            parts[here], parts[shift(here, width)] = split(de)
        mine = slice(i * each, (i + 1) * each)
        both = dot(taking(wanted[:, tokens], each, i * each), parts[...], NT)
        dslot_ref[mine] = both[:, :width] + both[:, width:]
        if i < len(stores):
            stores[i].start()
    for copy in stores + fetches:
        copy.wait()


def through(value, pair, dims):
    count, rows = value.shape[0], pair.shape[0] // 2
    high, low = split(value)
    both = dot(jnp.concatenate([high, low], axis=0), pair[:rows], dims)
    return both[:count] + (both[count:] + dot(high, pair[rows:], dims))


def back_through(value, pair):
    count, rows = value.shape[0], pair.shape[0] // 2
    both = dot(jnp.concatenate(split(value), axis=0), pair[...], NT)
    return both[:count, :rows] + (both[count:, :rows] + both[:count, rows:])


def closing_kernel(dslot_ref, slope_ref, coarses, projects, lay, number, send_ref):
    grad = back_through(back_through(dslot_ref[...], projects) * slope_ref[...], coarses)
    parts = jnp.concatenate(split(jnp.concatenate([grad, number[...]], axis=1)), axis=1)
    both = dot(lay[...], parts)
    send_ref[...] = both[:, :LANES] + both[:, LANES:]


def scatter_kernel(message_ref, done_ref, mine_ref, other_ref, total):
    del done_ref
    pixels = mine_ref.shape[2]
    message = message_ref[...]
    number = lax.broadcasted_iota(jnp.int32, (message.shape[0], SIDE * SIDE), 1).astype(F32)
    pick = jnp.where(message[:, pixels : pixels + 1] == number, 1.0, 0.0).astype(BF16)
    high, low = split(message[:, :pixels])
    total[...] = dot(pick, low, TN) + dot(pick, high, TN)
    half = mine_ref.shape[1]
    side = lax.axis_index("lvl")
    mine_ref[0] = total[pl.ds(pl.multiple_of(side * half, half), half), :]
    other_ref[0] = total[pl.ds(pl.multiple_of((1 - side) * half, half), half), :]


def last_kernel(de_hbm, first, deep, out_hbm, de, out, cat, in_sems, out_sems):
    width = de.shape[0]
    steps = de.shape[1] // ROWS

    def load(i):
        return pltpu.make_async_copy(de_hbm.at[:, chunk(i)], de.at[:, chunk(i)], in_sems.at[i])

    def store(i):
        return pltpu.make_async_copy(out.at[chunk(i)], out_hbm.at[chunk(i)], out_sems.at[i])

    def prepare(source):
        for here in blocks(width, 32):
            high, low = split(source[here])
            cat[here], cat[shift(here, width)], cat[shift(here, 2 * width)] = high, high, low

    for i in range(steps - 1):
        load(i).start()
    prepare(first)

    def step(i, _):
        mine = lax.rem(i + steps - 1, steps)
        out[chunk(mine), :] = dot(cat[...], deep[...], TN)
        store(mine).start()

        @pl.when(i + 1 < steps)
        def _():
            load(i).wait()
            prepare(de.at[:, chunk(i)])

        return 0

    lax.fori_loop(0, steps, step, 0)
    for i in range(steps):
        store(i).wait()


def fixed(*values):
    return [pltpu.with_memory_space_constraint(value, pltpu.HBM) for value in values]


def near(*values):
    return [pltpu.with_memory_space_constraint(value, pltpu.VMEM) for value in values]


def stack(kernel, blocks, before, rows):
    shape = (len(blocks) * rows, 128)
    return call(
        kernel,
        "stack",
        1000,
        jax.ShapeDtypeStruct(shape, F32),
        limit=ROOM,
        in_specs=[VMEM] * len(blocks) + [HBM],
        out_specs=VMEM,
    )(*blocks, *fixed(before))


def body(coarse_input, coarse_weight, fine_input, fine_target, crops, in_weight, context_weight, out_weight):
    patch = ("far", "y", "core")
    peers = lax.axis_size(patch)
    far = peers // 4
    patches, tokens, values = fine_input.shape
    width = in_weight.shape[1]
    pixels = coarse_weight.shape[0]
    half = coarse_input.shape[1]
    count = patches * tokens
    swap = [(0, 1), (1, 0)]

    column = {0: coarse_input}
    for k in range(1, far):
        column[k] = lax.ppermute(coarse_input, "far", [(p, p ^ k) for p in range(far)])
    column = [column[k] for k in [0, 2, 1] + list(range(3, far))]

    steps = count // ROWS
    pair_shape = (2 * width, values)
    x, t = fine_input.reshape(count, values), fine_target.reshape(count, values)
    xw, xw_last, pair, rows, next_pair, crops = call(
        input_kernel,
        "input",
        6 * count * values * width,
        (
            pltpu.HBM((width, count - ROWS), F32),
            pltpu.VMEM((width, ROWS), F32),
            pltpu.HBM(pair_shape, BF16),
            pltpu.VMEM((ROWS, values), F32),
            pltpu.VMEM(pair_shape, BF16),
            pltpu.VMEM((4, patches), jnp.int32),
        ),
        in_specs=[HBM] * 5,
        out_specs=(HBM, VMEM, HBM, VMEM, VMEM, VMEM),
        scratch_shapes=[
            pltpu.VMEM((count, values), F32),
            pltpu.VMEM((width, count), F32),
            pltpu.VMEM((width, values), F32),
            pltpu.VMEM((width, values), F32),
            pltpu.VMEM(pair_shape, BF16),
            pltpu.VMEM((ROWS, values), BF16),
            pltpu.VMEM((ROWS, values), BF16),
            pltpu.SemaphoreType.DMA((steps,)),
            pltpu.SemaphoreType.DMA((steps,)),
            pltpu.SemaphoreType.DMA((5,)),
        ],
    )(*fixed(x, in_weight.T, t, out_weight, crops.T))
    column = stack(pack_kernel, column, xw, half * 3 // 2)
    own = [column]
    for flip in range(1, 4):
        own.append(lax.ppermute(column, ("lvl", "y"), [(p, p ^ flip) for p in range(4)]))
    tw, xw_last, tw_last, coarses, projects = call(
        target_kernel,
        "target",
        6 * count * values * width,
        (
            pltpu.HBM((width, count - ROWS), F32),
            pltpu.HBM((width, ROWS), F32),
            pltpu.VMEM((width, ROWS), F32),
            pltpu.VMEM((2 * pixels, width), BF16),
            pltpu.VMEM((2 * width, width), BF16),
        ),
        limit=ROOM,
        in_specs=[HBM] * 3 + [VMEM] * 3,
        out_specs=(HBM, HBM, VMEM, VMEM, VMEM),
        scratch_shapes=[
            pltpu.VMEM((count, values), F32),
            pltpu.VMEM((width, count), F32),
            pltpu.VMEM((ROWS, values), BF16),
            pltpu.VMEM((ROWS, values), BF16),
            pltpu.VMEM((pixels, width), F32),
            pltpu.VMEM((width, width), F32),
            pltpu.SemaphoreType.DMA((steps,)),
            pltpu.SemaphoreType.DMA((steps,)),
            pltpu.SemaphoreType.DMA((3,)),
        ],
    )(*fixed(t, coarse_weight, context_weight), *near(rows, next_pair, xw_last))
    own = stack(stack_kernel, own, tw, column.shape[0])
    other = lax.ppermute(own, "core", swap)
    (crops,) = near(crops)
    grams, wanted, lay, number = call(
        functools.partial(prepare_kernel, patches),
        "prepare",
        8 * values * width * width,
        (
            pltpu.VMEM((width, 3 * width), BF16),
            pltpu.VMEM((1, count), jnp.int32),
            pltpu.VMEM((peers * 16, patches * 16), BF16),
            pltpu.VMEM((patches * 16, LANES - pixels), F32),
        ),
        limit=ROOM,
        in_specs=[VMEM, SMEM, HBM],
        out_specs=(VMEM,) * 4,
    )(*near(next_pair), crops, own)

    projected, slope, xw_first, tw_first = call(
        functools.partial(context_kernel, patches, peers),
        "context",
        6 * patches * 16 * width * width,
        (
            pltpu.VMEM((width, 2 * patches * 16), BF16),
            pltpu.VMEM((patches * 16, width), F32),
            pltpu.VMEM((width, 2 * ROWS), F32),
            pltpu.VMEM((width, ROWS), F32),
        ),
        limit=ROOM,
        in_specs=[VMEM] * 5 + [HBM] * 2,
        out_specs=(VMEM,) * 4,
        scratch_shapes=[
            pltpu.VMEM((patches * 16, pixels), F32),
            pltpu.SMEM((4, patches), jnp.int32),
            pltpu.SemaphoreType.DMA((3,)),
        ],
    )(crops, own, other, *near(coarses, projects), *fixed(xw, tw))
    de, last_de, deep, dslot = call(
        middle_kernel,
        "middle",
        6 * count * width * width,
        (
            pltpu.HBM((width, count), F32),
            pltpu.VMEM((width, ROWS), F32),
            pltpu.VMEM((3 * width, values), BF16),
            pltpu.VMEM((patches * 16, width), F32),
        ),
        limit=ROOM,
        in_specs=[VMEM] * 6 + [HBM] * 4,
        out_specs=(HBM,) + (VMEM,) * 3,
        scratch_shapes=[
            pltpu.VMEM((width, count), F32),
            pltpu.VMEM((width, count), F32),
            pltpu.VMEM((2 * patches * 16, ROWS), BF16),
            pltpu.VMEM((2, width, ROWS), F32),
            pltpu.VMEM((2, 3 * width, ROWS), BF16),
            pltpu.VMEM((2 * width, ROWS), BF16),
            pltpu.SemaphoreType.DMA((steps,)),
            pltpu.SemaphoreType.DMA((steps,)),
            pltpu.SemaphoreType.DMA((steps,)),
            pltpu.SemaphoreType.DMA((2,)),
        ],
    )(*near(projected, grams, wanted, xw_first, tw_first, tw_last), *fixed(xw, xw_last, tw, pair))
    back = call(
        closing_kernel,
        "closing",
        6 * patches * 16 * width * width,
        jax.ShapeDtypeStruct((peers * 16, LANES), F32),
        limit=ROOM,
        in_specs=[VMEM] * 6,
        out_specs=VMEM,
    )(*near(dslot, slope, coarses, projects, lay, number))
    returned = lax.all_to_all(back, patch, 0, 0, tiled=True)

    fine_grad = call(
        last_kernel,
        "last",
        6 * count * values * width,
        pltpu.HBM((count, values), F32),
        limit=ROOM,
        in_specs=[HBM, VMEM, VMEM],
        out_specs=HBM,
        scratch_shapes=[
            pltpu.VMEM((width, count), F32),
            pltpu.VMEM((count, values), F32),
            pltpu.VMEM((3 * width, ROWS), BF16),
            pltpu.SemaphoreType.DMA((steps,)),
            pltpu.SemaphoreType.DMA((steps,)),
        ],
    )(*fixed(de), *near(last_de, deep))
    part = (1, half, pixels)
    mine, theirs = call(
        scatter_kernel,
        "scatter",
        10000,
        (jax.ShapeDtypeStruct(part, F32), jax.ShapeDtypeStruct(part, F32)),
        limit=ROOM,
        in_specs=[VMEM, HBM],
        out_specs=(VMEM, VMEM),
        scratch_shapes=[pltpu.VMEM((SIDE * SIDE, pixels), F32)],
    )(returned, *fixed(fine_grad))
    coarse_grad = mine + lax.ppermute(theirs, "lvl", swap)
    return (coarse_grad, fine_grad.reshape(fine_input.shape))


def solution(mesh):
    sides, peers = mesh.shape["lvl"], mesh.shape["patch"]
    fine = jax.sharding.Mesh(mesh.devices.reshape(sides, peers // 4, 2, 2), ("lvl", "far", "y", "core"))
    patch = ("far", "y", "core")
    both = ("lvl",) + patch
    in_specs = (
        P(patch, "lvl", None),
        P(),
        P(both, None, None),
        P(both, None, None),
        P(both, None),
        P(),
        P(),
        P(),
    )
    out_specs = (P(patch, "lvl", None), P(both, None, None))
    return jax.shard_map(body, mesh=fine, in_specs=in_specs, out_specs=out_specs, check_vma=False)
```

```python
import functools
import math

import jax
import jax.numpy as jnp
from jax import lax
from jax.experimental import pallas as pl
from jax.experimental.pallas import tpu as pltpu
from jax.sharding import PartitionSpec as P

F32 = jnp.float32
BF16 = jnp.bfloat16
NN = (((1,), (0,)), ((), ()))
NT = (((1,), (1,)), ((), ()))
TN = (((0,), (0,)), ((), ()))
ROWS = 512
SIDE = 8
LANES = 256
LIMIT = 60 * 1024 * 1024
ROOM = 40 * 1024 * 1024
SMEM = pl.BlockSpec(memory_space=pltpu.SMEM)
VMEM = pl.BlockSpec(memory_space=pltpu.VMEM)
HBM = pl.BlockSpec(memory_space=pltpu.HBM)


def split(value):
    high = value.astype(BF16)
    low = (value - high.astype(F32)).astype(BF16)
    return high, low


def dot(left, right, dims=NN):
    return lax.dot_general(left, right, dims, preferred_element_type=F32)


def dot3(left, right, dims=NN):
    return (
        dot(left[0], right[1], dims) + dot(left[1], right[0], dims) + dot(left[0], right[0], dims)
    )


def side_by_side(value):
    high, low = split(value)
    return jnp.concatenate([high, low, high], axis=1)


def sigmoid(value):
    return 0.5 * jnp.tanh(0.5 * value) + 0.5


def call(kernel, name, flops, out_shape, limit=LIMIT, **kwargs):
    moved = 8 * sum(math.prod(s.shape) for s in jax.tree.leaves(out_shape))
    return pl.pallas_call(
        kernel,
        out_shape=out_shape,
        name=name,
        cost_estimate=pl.CostEstimate(flops=flops, bytes_accessed=moved, transcendentals=0),
        compiler_params=pltpu.CompilerParams(vmem_limit_bytes=limit),
        **kwargs,
    )


def blocks(rows, size):
    return [slice(start, start + size) for start in range(0, rows, size)]


def shift(here, by):
    return slice(here.start + by, here.stop + by)


def pair_product(pair, value, dims):
    rows = pair.shape[0] // 2
    high, low = split(value)
    both = dot(pair[...], high, dims)
    return both[:rows] + (both[rows:] + dot(pair[:rows], low, dims))


def chunk(i):
    return pl.ds(pl.multiple_of(i * ROWS, ROWS), ROWS)


def wide_product(pair, value, high, low, out):
    width = pair.shape[0] // 2
    for here in blocks(high.shape[0], 16):
        high[here], low[here] = split(value[here])
    both = dot(pair[...], high[...], NT)
    rest = dot(pair[:width], low[...], NT)
    for here in blocks(width, 32):
        out[here] = both[here] + (both[shift(here, width)] + rest[here])


def input_kernel(
    x_hbm,
    weight_hbm,
    t_hbm,
    next_weight_hbm,
    crops_hbm,
    out_hbm,
    out_last,
    pair_hbm,
    next_rows,
    next_pair,
    crops,
    x,
    out,
    weight,
    next_weight,
    pair,
    high,
    low,
    in_sems,
    out_sems,
    sems,
):
    width = weight.shape[0]
    chunks = chunk_rows(x.shape[0])
    fetch = pltpu.make_async_copy(weight_hbm, weight, sems.at[0])
    keep = pltpu.make_async_copy(pair, pair_hbm, sems.at[1])
    fetch_next = pltpu.make_async_copy(next_weight_hbm, next_weight, sems.at[2])
    fetch_rows = pltpu.make_async_copy(t_hbm.at[: next_rows.shape[0]], next_rows, sems.at[3])
    fetch_crops = pltpu.make_async_copy(crops_hbm, crops, sems.at[4])
    loads = [
        pltpu.make_async_copy(x_hbm.at[here], x.at[here], in_sems.at[i]) for i, here in enumerate(chunks)
    ]
    stores = [
        pltpu.make_async_copy(out.at[:, here], out_hbm.at[:, here], out_sems.at[i])
        for i, here in enumerate(chunks[:-1])
    ]
    for copy in [fetch] + loads[:2]:
        copy.start()
    for i, here in enumerate(chunks):
        loads[i].wait()
        if i + 2 < len(chunks):
            loads[i + 2].start()
        if i == 0:
            fetch.wait()
            pair[:width], pair[width:] = split(weight[...])
            keep.start()
            fetch_next.start()
        if i == 1:
            fetch_rows.start()
            fetch_crops.start()
        if i == len(chunks) - 1:
            fetch_next.wait()
            next_pair[:width], next_pair[width:] = split(next_weight[...])
        target = out.at[:, here] if i < len(stores) else out_last
        wide_product(pair, x.at[here], high, low, target)
        if i < len(stores):
            stores[i].start()
    for copy in [keep, fetch_rows, fetch_crops] + stores:
        copy.wait()


def target_kernel(
    t_hbm,
    cwgt_hbm,
    xwgt_hbm,
    rows,
    pair,
    before_last,
    out_hbm,
    before_hbm,
    out_last,
    coarses,
    projects,
    t,
    out,
    high,
    low,
    cwgt,
    xwgt,
    in_sems,
    out_sems,
    sems,
):
    chunks = chunk_rows(t.shape[0])
    fetches = [
        pltpu.make_async_copy(cwgt_hbm, cwgt, sems.at[0]),
        pltpu.make_async_copy(xwgt_hbm, xwgt, sems.at[1]),
    ]
    loads = [
        pltpu.make_async_copy(t_hbm.at[here], t.at[here], in_sems.at[i])
        for i, here in enumerate(chunks[1:])
    ]
    stores = [
        pltpu.make_async_copy(out.at[:, here], out_hbm.at[:, here], out_sems.at[i])
        for i, here in enumerate(chunks[:-1])
    ]
    keep = pltpu.make_async_copy(before_last, before_hbm, sems.at[2])
    for copy in loads + fetches:
        copy.start()
    for i, here in enumerate(chunks):
        if i > 0:
            loads[i - 1].wait()
        if i == 2:
            keep.start()
        source = rows if i == 0 else t.at[here]
        if i < len(stores):
            wide_product(pair, source, high, low, out.at[:, here])
            stores[i].start()
        else:
            wide_product(pair, source, high, low, out_last)
    for copy in fetches:
        copy.wait()
    coarses[...] = jnp.concatenate(split(cwgt[...]), axis=0)
    projects[...] = jnp.concatenate(split(xwgt[...]), axis=0)
    for copy in stores + [keep]:
        copy.wait()


def chunk_rows(count):
    return [slice(start, start + ROWS) for start in range(0, count, ROWS)]


def prepare_kernel(patches, pair, crops_ref, before_ref, grams, wanted, lay, number):
    del before_ref
    width = grams.shape[0]
    both = dot(pair[...], pair[:width], NT)
    grams[...] = side_by_side(both[:width] + (both[width:] + both[width:].T))
    wanted[...] = slot_row(crops_ref, patches, wanted.shape[1] // patches)
    frame = row_value(crops_ref, 0, patches, (1, patches * 16), 1, 16)
    slot = lax.broadcasted_iota(jnp.int32, (1, patches * 16), 1) % 16
    line = lax.broadcasted_iota(jnp.int32, lay.shape, 0)
    lay[...] = jnp.where(line == frame * 16 + slot, 1.0, 0.0).astype(BF16)
    slot = lax.broadcasted_iota(jnp.int32, number.shape, 0) % 16
    top = row_value(crops_ref, 1, patches, number.shape, 0, 16)
    left = row_value(crops_ref, 2, patches, number.shape, 0, 16)
    number[...] = ((top + slot // 4) * SIDE + left + slot % 4).astype(F32)


def stack_kernel(*refs):
    *block_refs, _, out_ref = refs
    size = block_refs[0].shape[0]
    for k, ref in enumerate(block_refs):
        out_ref[k * size : (k + 1) * size] = ref[...]


def pack_kernel(*refs):
    *block_refs, _, out_ref = refs
    tokens = block_refs[0].shape[1]
    size = tokens * 3 // 2
    for k, ref in enumerate(block_refs):
        out_ref[k * size : k * size + tokens] = ref[0, :, :128]
        tails = [ref[0, : tokens // 2, 128:], ref[0, tokens // 2 :, 128:]]
        out_ref[k * size + tokens : (k + 1) * size] = jnp.concatenate(tails, axis=1)


def row_value(crops_ref, column, patches, shape, axis, each):
    index = lax.broadcasted_iota(jnp.int32, shape, axis) // each
    found = jnp.zeros(shape, jnp.int32)
    for j in range(patches):
        found = jnp.where(index == j, crops_ref[column, j], found)
    return found


def slot_row(crops_ref, patches, tokens):
    scale = row_value(crops_ref, 3, patches, (1, patches * tokens), 1, tokens)
    token = lax.broadcasted_iota(jnp.int32, (1, patches * tokens), 1)
    row, column = (token % tokens) // 16, token % 16
    return token // tokens * 16 + (row * scale // 8) * 4 + column * scale // 8


def taking(wanted, slots, first):
    slot = lax.broadcasted_iota(jnp.int32, (slots, wanted.shape[1]), 0) + first
    return jnp.where(slot == wanted, 1.0, 0.0).astype(BF16)


def context_kernel(
    patches,
    peers,
    crops_vmem,
    own_ref,
    other_ref,
    coarses,
    projects,
    xw_hbm,
    tw_hbm,
    projected_ref,
    slope_ref,
    xw_first,
    tw_first,
    rows,
    crops_ref,
    sems,
):
    fetches = [
        pltpu.make_async_copy(xw_hbm.at[:, : xw_first.shape[1]], xw_first, sems.at[0]),
        pltpu.make_async_copy(tw_hbm.at[:, : tw_first.shape[1]], tw_first, sems.at[1]),
    ]
    for copy in fetches:
        copy.start()
    take = pltpu.make_async_copy(crops_vmem, crops_ref, sems.at[2])
    take.start()
    take.wait()
    pixels = coarses.shape[0] // 2
    width = projects.shape[1]
    far = peers // 4
    me, side = lax.axis_index(("far", "y", "core")), lax.axis_index("lvl")
    for j in range(patches):
        frame, top, left = crops_ref[0, j], crops_ref[1, j], crops_ref[2, j]
        near_by = lax.bitwise_xor(frame % 4, me % 4)
        k = (me // 4 - frame // 4 + far) % far
        k = jnp.where(k == 1, 2, jnp.where(k == 2, 3, jnp.where(k == 3, 1, k)))
        here = near_by % 2 == 0
        for a in range(4):
            row = jnp.minimum(top + a, SIDE - 1)
            shard = (lax.bitwise_xor(row // 4, side) * 2 + near_by // 2) * far + k
            row = row % 4
            start = shard * (6 * SIDE)
            wide = pl.ds(pl.multiple_of(start + row * SIDE, SIDE), SIDE)
            tail = pl.ds(pl.multiple_of(start + (4 + row % 2) * SIDE, SIDE), SIDE)
            into = slice(j * 16 + a * 4, j * 16 + a * 4 + 4)
            line = jnp.where(here, own_ref[wide, :], other_ref[wide, :])
            rows[into, :128] = pltpu.roll(line, SIDE - left, 0)[:4, :]
            line = pltpu.roll(jnp.where(here, own_ref[tail, :], other_ref[tail, :]), SIDE - left, 0)[:4, :]
            rows[into, 128:] = jnp.where(row >= 2, line[:, 64:], line[:, :64])
    pre = through(rows[...], coarses, NN)
    gate = sigmoid(pre)
    slope_ref[...] = gate * (1.0 + pre * (1.0 - gate))
    projected = through(pre * gate, projects, NN).T
    projected_ref[...] = jnp.concatenate(split(projected), axis=1)
    for copy in fetches:
        copy.wait()


def middle_kernel(
    projected,
    grams,
    wanted,
    xw_first,
    tw_first,
    tw_last,
    xw_hbm,
    xw_last,
    tw_hbm,
    pair_hbm,
    de_hbm,
    de_ref,
    deep_ref,
    dslot_ref,
    xw,
    tw,
    taken,
    factor,
    deep,
    parts,
    xw_sems,
    tw_sems,
    out_sems,
    sems,
):
    width, count = xw.shape
    slots = dslot_ref.shape[0]
    chunks = chunk_rows(count)
    each = slots // len(chunks)
    tw_loads = [
        pltpu.make_async_copy(tw_hbm.at[:, here], tw.at[:, here], tw_sems.at[i])
        for i, here in enumerate(chunks[1:-1])
    ]
    xw_loads = [
        pltpu.make_async_copy(xw_hbm.at[:, here], xw.at[:, here], xw_sems.at[i])
        for i, here in enumerate(chunks[2:-1])
    ]
    xw_loads.append(pltpu.make_async_copy(xw_last, xw.at[:, chunks[-1]], xw_sems.at[len(xw_loads)]))
    stores = [
        pltpu.make_async_copy(xw.at[:, here], de_hbm.at[:, here], out_sems.at[i])
        for i, here in enumerate(chunks[:-1])
    ]
    fetches = [
        pltpu.make_async_copy(pair_hbm, deep_ref.at[: 2 * width], sems.at[0]),
        pltpu.make_async_copy(pair_hbm.at[:width], deep_ref.at[2 * width :], sems.at[1]),
    ]
    for pair in zip(tw_loads, xw_loads):
        for copy in pair:
            copy.start()
    for copy in fetches:
        copy.start()

    def begin(i):
        tokens = chunks[i]
        source = xw_first.at[:, tokens] if i < 2 else xw.at[:, tokens]
        here = taking(wanted[:, tokens], slots, 0)
        taken[:slots], taken[slots:] = here, here
        spread = dot(projected[...], taken[...])
        for here in blocks(width, 32):
            pre = source[here] + spread[here]
            gate = sigmoid(pre)
            hidden = pre * gate
            factor[i % 2, here] = gate + hidden * (1.0 - gate)
            high, low = split(hidden)
            for part, value in enumerate((high, high, low)):
                deep[i % 2, shift(here, part * width)] = value

    begin(0)
    for i, tokens in enumerate(chunks):
        if 0 < i < len(chunks) - 1:
            tw_loads[i - 1].wait()
            xw_loads[i - 1].wait()
        minus = tw_first if i == 0 else tw_last if i == len(chunks) - 1 else tw.at[:, tokens]
        target = de_ref if i == len(chunks) - 1 else xw.at[:, tokens]
        product = dot(grams[...], deep[i % 2])
        if i + 1 < len(chunks):
            begin(i + 1)
        for here in blocks(width, 32):
            de = (product[here] - minus[here]) * factor[i % 2, here]
            target[here] = de
            parts[here], parts[shift(here, width)] = split(de)
        mine = slice(i * each, (i + 1) * each)
        both = dot(taking(wanted[:, tokens], each, i * each), parts[...], NT)
        dslot_ref[mine] = both[:, :width] + both[:, width:]
        if i < len(stores):
            stores[i].start()
    for copy in stores + fetches:
        copy.wait()


def through(value, pair, dims):
    count, rows = value.shape[0], pair.shape[0] // 2
    high, low = split(value)
    both = dot(jnp.concatenate([high, low], axis=0), pair[:rows], dims)
    return both[:count] + (both[count:] + dot(high, pair[rows:], dims))


def back_through(value, pair):
    count, rows = value.shape[0], pair.shape[0] // 2
    both = dot(jnp.concatenate(split(value), axis=0), pair[...], NT)
    return both[:count, :rows] + (both[count:, :rows] + both[:count, rows:])


def closing_kernel(dslot_ref, slope_ref, coarses, projects, lay, number, send_ref):
    grad = back_through(back_through(dslot_ref[...], projects) * slope_ref[...], coarses)
    parts = jnp.concatenate(split(jnp.concatenate([grad, number[...]], axis=1)), axis=1)
    both = dot(lay[...], parts)
    send_ref[...] = both[:, :LANES] + both[:, LANES:]


def scatter_kernel(message_ref, done_ref, mine_ref, other_ref, total):
    del done_ref
    pixels = mine_ref.shape[2]
    message = message_ref[...]
    number = lax.broadcasted_iota(jnp.int32, (message.shape[0], SIDE * SIDE), 1).astype(F32)
    pick = jnp.where(message[:, pixels : pixels + 1] == number, 1.0, 0.0).astype(BF16)
    high, low = split(message[:, :pixels])
    total[...] = dot(pick, low, TN) + dot(pick, high, TN)
    half = mine_ref.shape[1]
    side = lax.axis_index("lvl")
    mine_ref[0] = total[pl.ds(pl.multiple_of(side * half, half), half), :]
    other_ref[0] = total[pl.ds(pl.multiple_of((1 - side) * half, half), half), :]


def last_kernel(de_hbm, first, deep, out_hbm, de, out, cat, in_sems, out_sems):
    width = de.shape[0]
    steps = de.shape[1] // ROWS

    def load(i):
        return pltpu.make_async_copy(de_hbm.at[:, chunk(i)], de.at[:, chunk(i)], in_sems.at[i])

    def store(i):
        return pltpu.make_async_copy(out.at[chunk(i)], out_hbm.at[chunk(i)], out_sems.at[i])

    def prepare(source):
        for here in blocks(width, 32):
            high, low = split(source[here])
            cat[here], cat[shift(here, width)], cat[shift(here, 2 * width)] = high, high, low

    for i in range(steps - 1):
        load(i).start()
    prepare(first)

    def step(i, _):
        mine = lax.rem(i + steps - 1, steps)
        out[chunk(mine), :] = dot(cat[...], deep[...], TN)
        store(mine).start()

        @pl.when(i + 1 < steps)
        def _():
            load(i).wait()
            prepare(de.at[:, chunk(i)])

        return 0

    lax.fori_loop(0, steps, step, 0)
    for i in range(steps):
        store(i).wait()


def fixed(*values):
    return [pltpu.with_memory_space_constraint(value, pltpu.HBM) for value in values]


def near(*values):
    return [pltpu.with_memory_space_constraint(value, pltpu.VMEM) for value in values]


def stack(kernel, blocks, before, rows):
    shape = (len(blocks) * rows, 128)
    return call(
        kernel,
        "stack",
        1000,
        jax.ShapeDtypeStruct(shape, F32),
        limit=ROOM,
        in_specs=[VMEM] * len(blocks) + [HBM],
        out_specs=VMEM,
    )(*blocks, *fixed(before))


def body(coarse_input, coarse_weight, fine_input, fine_target, crops, in_weight, context_weight, out_weight):
    patch = ("far", "y", "core")
    peers = lax.axis_size(patch)
    far = peers // 4
    patches, tokens, values = fine_input.shape
    width = in_weight.shape[1]
    pixels = coarse_weight.shape[0]
    half = coarse_input.shape[1]
    count = patches * tokens
    swap = [(0, 1), (1, 0)]

    column = {0: coarse_input}
    for k in range(1, far):
        column[k] = lax.ppermute(coarse_input, "far", [(p, (p + k) % far) for p in range(far)])
    column = [column[k] for k in [0, 3, 1, 2] + list(range(4, far))]

    steps = count // ROWS
    pair_shape = (2 * width, values)
    x, t = fine_input.reshape(count, values), fine_target.reshape(count, values)
    xw, xw_last, pair, rows, next_pair, crops = call(
        input_kernel,
        "input",
        6 * count * values * width,
        (
            pltpu.HBM((width, count - ROWS), F32),
            pltpu.VMEM((width, ROWS), F32),
            pltpu.HBM(pair_shape, BF16),
            pltpu.VMEM((ROWS, values), F32),
            pltpu.VMEM(pair_shape, BF16),
            pltpu.VMEM((4, patches), jnp.int32),
        ),
        in_specs=[HBM] * 5,
        out_specs=(HBM, VMEM, HBM, VMEM, VMEM, VMEM),
        scratch_shapes=[
            pltpu.VMEM((count, values), F32),
            pltpu.VMEM((width, count), F32),
            pltpu.VMEM((width, values), F32),
            pltpu.VMEM((width, values), F32),
            pltpu.VMEM(pair_shape, BF16),
            pltpu.VMEM((ROWS, values), BF16),
            pltpu.VMEM((ROWS, values), BF16),
            pltpu.SemaphoreType.DMA((steps,)),
            pltpu.SemaphoreType.DMA((steps,)),
            pltpu.SemaphoreType.DMA((5,)),
        ],
    )(*fixed(x, in_weight.T, t, out_weight, crops.T))
    column = stack(pack_kernel, column, xw, half * 3 // 2)
    own = [column]
    for flip in range(1, 4):
        own.append(lax.ppermute(column, ("lvl", "y"), [(p, p ^ flip) for p in range(4)]))
    tw, xw_last, tw_last, coarses, projects = call(
        target_kernel,
        "target",
        6 * count * values * width,
        (
            pltpu.HBM((width, count - ROWS), F32),
            pltpu.HBM((width, ROWS), F32),
            pltpu.VMEM((width, ROWS), F32),
            pltpu.VMEM((2 * pixels, width), BF16),
            pltpu.VMEM((2 * width, width), BF16),
        ),
        limit=ROOM,
        in_specs=[HBM] * 3 + [VMEM] * 3,
        out_specs=(HBM, HBM, VMEM, VMEM, VMEM),
        scratch_shapes=[
            pltpu.VMEM((count, values), F32),
            pltpu.VMEM((width, count), F32),
            pltpu.VMEM((ROWS, values), BF16),
            pltpu.VMEM((ROWS, values), BF16),
            pltpu.VMEM((pixels, width), F32),
            pltpu.VMEM((width, width), F32),
            pltpu.SemaphoreType.DMA((steps,)),
            pltpu.SemaphoreType.DMA((steps,)),
            pltpu.SemaphoreType.DMA((3,)),
        ],
    )(*fixed(t, coarse_weight, context_weight), *near(rows, next_pair, xw_last))
    own = stack(stack_kernel, own, tw, column.shape[0])
    other = lax.ppermute(own, "core", swap)
    (crops,) = near(crops)
    grams, wanted, lay, number = call(
        functools.partial(prepare_kernel, patches),
        "prepare",
        8 * values * width * width,
        (
            pltpu.VMEM((width, 3 * width), BF16),
            pltpu.VMEM((1, count), jnp.int32),
            pltpu.VMEM((peers * 16, patches * 16), BF16),
            pltpu.VMEM((patches * 16, LANES - pixels), F32),
        ),
        limit=ROOM,
        in_specs=[VMEM, SMEM, HBM],
        out_specs=(VMEM,) * 4,
    )(*near(next_pair), crops, own)

    projected, slope, xw_first, tw_first = call(
        functools.partial(context_kernel, patches, peers),
        "context",
        6 * patches * 16 * width * width,
        (
            pltpu.VMEM((width, 2 * patches * 16), BF16),
            pltpu.VMEM((patches * 16, width), F32),
            pltpu.VMEM((width, 2 * ROWS), F32),
            pltpu.VMEM((width, ROWS), F32),
        ),
        limit=ROOM,
        in_specs=[VMEM] * 5 + [HBM] * 2,
        out_specs=(VMEM,) * 4,
        scratch_shapes=[
            pltpu.VMEM((patches * 16, pixels), F32),
            pltpu.SMEM((4, patches), jnp.int32),
            pltpu.SemaphoreType.DMA((3,)),
        ],
    )(crops, own, other, *near(coarses, projects), *fixed(xw, tw))
    de, last_de, deep, dslot = call(
        middle_kernel,
        "middle",
        6 * count * width * width,
        (
            pltpu.HBM((width, count), F32),
            pltpu.VMEM((width, ROWS), F32),
            pltpu.VMEM((3 * width, values), BF16),
            pltpu.VMEM((patches * 16, width), F32),
        ),
        limit=ROOM,
        in_specs=[VMEM] * 6 + [HBM] * 4,
        out_specs=(HBM,) + (VMEM,) * 3,
        scratch_shapes=[
            pltpu.VMEM((width, count), F32),
            pltpu.VMEM((width, count), F32),
            pltpu.VMEM((2 * patches * 16, ROWS), BF16),
            pltpu.VMEM((2, width, ROWS), F32),
            pltpu.VMEM((2, 3 * width, ROWS), BF16),
            pltpu.VMEM((2 * width, ROWS), BF16),
            pltpu.SemaphoreType.DMA((steps,)),
            pltpu.SemaphoreType.DMA((steps,)),
            pltpu.SemaphoreType.DMA((steps,)),
            pltpu.SemaphoreType.DMA((2,)),
        ],
    )(*near(projected, grams, wanted, xw_first, tw_first, tw_last), *fixed(xw, xw_last, tw, pair))
    back = call(
        closing_kernel,
        "closing",
        6 * patches * 16 * width * width,
        pltpu.VMEM((peers * 16, LANES), F32),
        limit=ROOM,
        in_specs=[VMEM] * 6,
        out_specs=VMEM,
    )(*near(dslot, slope, coarses, projects, lay, number))
    returned = lax.all_to_all(back, patch, 0, 0, tiled=True)

    fine_grad = call(
        last_kernel,
        "last",
        6 * count * values * width,
        pltpu.HBM((count, values), F32),
        limit=ROOM,
        in_specs=[HBM, VMEM, VMEM],
        out_specs=HBM,
        scratch_shapes=[
            pltpu.VMEM((width, count), F32),
            pltpu.VMEM((count, values), F32),
            pltpu.VMEM((3 * width, ROWS), BF16),
            pltpu.SemaphoreType.DMA((steps,)),
            pltpu.SemaphoreType.DMA((steps,)),
        ],
    )(*fixed(de), *near(last_de, deep))
    part = (1, half, pixels)
    mine, theirs = call(
        scatter_kernel,
        "scatter",
        10000,
        (jax.ShapeDtypeStruct(part, F32), jax.ShapeDtypeStruct(part, F32)),
        limit=ROOM,
        in_specs=[VMEM, HBM],
        out_specs=(VMEM, VMEM),
        scratch_shapes=[pltpu.VMEM((SIDE * SIDE, pixels), F32)],
    )(returned, *fixed(fine_grad))
    coarse_grad = mine + lax.ppermute(theirs, "lvl", swap)
    return (coarse_grad, fine_grad.reshape(fine_input.shape))


def solution(mesh):
    sides, peers = mesh.shape["lvl"], mesh.shape["patch"]
    fine = jax.sharding.Mesh(mesh.devices.reshape(sides, peers // 4, 2, 2), ("lvl", "far", "y", "core"))
    patch = ("far", "y", "core")
    both = ("lvl",) + patch
    in_specs = (
        P(patch, "lvl", None),
        P(),
        P(both, None, None),
        P(both, None, None),
        P(both, None),
        P(),
        P(),
        P(),
    )
    out_specs = (P(patch, "lvl", None), P(both, None, None))
    return jax.shard_map(body, mesh=fine, in_specs=in_specs, out_specs=out_specs, check_vma=False)
```

```python
import functools
import math

import jax
import jax.numpy as jnp
from jax import lax
from jax.experimental import pallas as pl
from jax.experimental.pallas import tpu as pltpu
from jax.sharding import PartitionSpec as P

F32 = jnp.float32
BF16 = jnp.bfloat16
NN = (((1,), (0,)), ((), ()))
NT = (((1,), (1,)), ((), ()))
TN = (((0,), (0,)), ((), ()))
ROWS = 512
SIDE = 8
LANES = 256
LIMIT = 60 * 1024 * 1024
ROOM = 40 * 1024 * 1024
SMEM = pl.BlockSpec(memory_space=pltpu.SMEM)
VMEM = pl.BlockSpec(memory_space=pltpu.VMEM)
HBM = pl.BlockSpec(memory_space=pltpu.HBM)


def split(value):
    high = value.astype(BF16)
    low = (value - high.astype(F32)).astype(BF16)
    return high, low


def dot(left, right, dims=NN):
    return lax.dot_general(left, right, dims, preferred_element_type=F32)


def dot3(left, right, dims=NN):
    return (
        dot(left[0], right[1], dims) + dot(left[1], right[0], dims) + dot(left[0], right[0], dims)
    )


def side_by_side(value):
    high, low = split(value)
    return jnp.concatenate([high, low, high], axis=1)


def sigmoid(value):
    return 0.5 * jnp.tanh(0.5 * value) + 0.5


def call(kernel, name, flops, out_shape, limit=LIMIT, **kwargs):
    moved = 8 * sum(math.prod(s.shape) for s in jax.tree.leaves(out_shape))
    return pl.pallas_call(
        kernel,
        out_shape=out_shape,
        name=name,
        cost_estimate=pl.CostEstimate(flops=flops, bytes_accessed=moved, transcendentals=0),
        compiler_params=pltpu.CompilerParams(vmem_limit_bytes=limit),
        **kwargs,
    )


def blocks(rows, size):
    return [slice(start, start + size) for start in range(0, rows, size)]


def shift(here, by):
    return slice(here.start + by, here.stop + by)


def pair_product(pair, value):
    rows = pair.shape[0] // 2
    high, low = split(value)
    both = dot(pair[...], high)
    return both[:rows] + (both[rows:] + dot(pair[:rows], low))


def chunk(i):
    return pl.ds(pl.multiple_of(i * ROWS, ROWS), ROWS)


def wide_product(pair, value, high, low, out):
    width = pair.shape[0] // 2
    for here in blocks(high.shape[0], 16):
        high[here], low[here] = split(value[here])
    both = dot(pair[...], high[...], NT)
    rest = dot(pair[:width], low[...], NT)
    for here in blocks(width, 32):
        out[here] = both[here] + (both[shift(here, width)] + rest[here])


def input_kernel(
    x_hbm,
    weight_hbm,
    t_hbm,
    next_weight_hbm,
    crops_hbm,
    out_hbm,
    out_last,
    pair_hbm,
    next_rows,
    next_pair,
    crops,
    x,
    out,
    weight,
    next_weight,
    pair,
    high,
    low,
    in_sems,
    out_sems,
    sems,
):
    width = weight.shape[0]
    chunks = chunk_rows(x.shape[0])
    fetch = pltpu.make_async_copy(weight_hbm, weight, sems.at[0])
    keep = pltpu.make_async_copy(pair, pair_hbm, sems.at[1])
    fetch_next = pltpu.make_async_copy(next_weight_hbm, next_weight, sems.at[2])
    fetch_rows = pltpu.make_async_copy(t_hbm.at[: next_rows.shape[0]], next_rows, sems.at[3])
    fetch_crops = pltpu.make_async_copy(crops_hbm, crops, sems.at[4])
    loads = [
        pltpu.make_async_copy(x_hbm.at[here], x.at[here], in_sems.at[i]) for i, here in enumerate(chunks)
    ]
    stores = [
        pltpu.make_async_copy(out.at[:, here], out_hbm.at[:, here], out_sems.at[i])
        for i, here in enumerate(chunks[:-1])
    ]
    for copy in [fetch] + loads[:2]:
        copy.start()
    for i, here in enumerate(chunks):
        loads[i].wait()
        if i + 2 < len(chunks):
            loads[i + 2].start()
        if i == 0:
            fetch.wait()
            pair[:width], pair[width:] = split(weight[...])
            keep.start()
            fetch_next.start()
        if i == 1:
            fetch_rows.start()
            fetch_crops.start()
        if i == len(chunks) - 1:
            fetch_next.wait()
            next_pair[:width], next_pair[width:] = split(next_weight[...])
        target = out.at[:, here] if i < len(stores) else out_last
        wide_product(pair, x.at[here], high, low, target)
        if i < len(stores):
            stores[i].start()
    for copy in [keep, fetch_rows, fetch_crops] + stores:
        copy.wait()


def target_kernel(
    t_hbm,
    cwgt_hbm,
    xwgt_hbm,
    rows,
    pair,
    before_last,
    out_hbm,
    before_hbm,
    out_last,
    coarses,
    projects,
    t,
    out,
    high,
    low,
    cwgt,
    xwgt,
    in_sems,
    out_sems,
    sems,
):
    chunks = chunk_rows(t.shape[0])
    fetches = [
        pltpu.make_async_copy(cwgt_hbm, cwgt, sems.at[0]),
        pltpu.make_async_copy(xwgt_hbm, xwgt, sems.at[1]),
    ]
    loads = [
        pltpu.make_async_copy(t_hbm.at[here], t.at[here], in_sems.at[i])
        for i, here in enumerate(chunks[1:])
    ]
    stores = [
        pltpu.make_async_copy(out.at[:, here], out_hbm.at[:, here], out_sems.at[i])
        for i, here in enumerate(chunks[:-1])
    ]
    keep = pltpu.make_async_copy(before_last, before_hbm, sems.at[2])
    for copy in loads + fetches:
        copy.start()
    for i, here in enumerate(chunks):
        if i > 0:
            loads[i - 1].wait()
        if i == 2:
            keep.start()
        source = rows if i == 0 else t.at[here]
        if i < len(stores):
            wide_product(pair, source, high, low, out.at[:, here])
            stores[i].start()
        else:
            wide_product(pair, source, high, low, out_last)
    for copy in fetches:
        copy.wait()
    coarses[...] = jnp.concatenate(split(cwgt[...]), axis=0)
    projects[...] = jnp.concatenate(split(xwgt[...]), axis=0)
    for copy in stores + [keep]:
        copy.wait()


def chunk_rows(count):
    return [slice(start, start + ROWS) for start in range(0, count, ROWS)]


def prepare_kernel(patches, pair, crops_ref, before_ref, grams, wanted, lay, number):
    del before_ref
    width = grams.shape[0]
    both = dot(pair[...], pair[:width], NT)
    grams[...] = side_by_side(both[:width] + (both[width:] + both[width:].T))
    wanted[...] = slot_row(crops_ref, patches, wanted.shape[1] // patches)
    frame = row_value(crops_ref, 0, patches, (1, patches * 16), 1, 16)
    slot = lax.broadcasted_iota(jnp.int32, (1, patches * 16), 1) % 16
    line = lax.broadcasted_iota(jnp.int32, lay.shape, 0)
    lay[...] = jnp.where(line == frame * 16 + slot, 1.0, 0.0).astype(BF16)
    slot = lax.broadcasted_iota(jnp.int32, number.shape, 1) % 16
    top = row_value(crops_ref, 1, patches, number.shape, 1, 16)
    left = row_value(crops_ref, 2, patches, number.shape, 1, 16)
    number[...] = ((top + slot // 4) * SIDE + left + slot % 4).astype(F32)


def stack_kernel(*refs):
    *block_refs, _, out_ref = refs
    size = block_refs[0].shape[0]
    for k, ref in enumerate(block_refs):
        out_ref[k * size : (k + 1) * size] = ref[...]


def pack_kernel(*refs):
    *block_refs, _, out_ref = refs
    tokens = block_refs[0].shape[1]
    size = tokens * 3 // 2
    for k, ref in enumerate(block_refs):
        out_ref[k * size : k * size + tokens] = ref[0, :, :128]
        tails = [ref[0, : tokens // 2, 128:], ref[0, tokens // 2 :, 128:]]
        out_ref[k * size + tokens : (k + 1) * size] = jnp.concatenate(tails, axis=1)


def row_value(crops_ref, column, patches, shape, axis, each):
    index = lax.broadcasted_iota(jnp.int32, shape, axis) // each
    found = jnp.zeros(shape, jnp.int32)
    for j in range(patches):
        found = jnp.where(index == j, crops_ref[column, j], found)
    return found


def slot_row(crops_ref, patches, tokens):
    scale = row_value(crops_ref, 3, patches, (1, patches * tokens), 1, tokens)
    token = lax.broadcasted_iota(jnp.int32, (1, patches * tokens), 1)
    row, column = (token % tokens) // 16, token % 16
    return token // tokens * 16 + (row * scale // 8) * 4 + column * scale // 8


def taking(wanted, slots, first):
    slot = lax.broadcasted_iota(jnp.int32, (slots, wanted.shape[1]), 0) + first
    return jnp.where(slot == wanted, 1.0, 0.0).astype(BF16)


def context_kernel(
    patches,
    peers,
    crops_vmem,
    own_ref,
    other_ref,
    coarses,
    projects,
    xw_hbm,
    tw_hbm,
    projected_ref,
    slope_ref,
    xw_first,
    tw_first,
    rows,
    crops_ref,
    sems,
):
    fetches = [
        pltpu.make_async_copy(xw_hbm.at[:, : xw_first.shape[1]], xw_first, sems.at[0]),
        pltpu.make_async_copy(tw_hbm.at[:, : tw_first.shape[1]], tw_first, sems.at[1]),
    ]
    for copy in fetches:
        copy.start()
    take = pltpu.make_async_copy(crops_vmem, crops_ref, sems.at[2])
    take.start()
    take.wait()
    pixels = coarses.shape[0] // 2
    width = projects.shape[1]
    far = peers // 4
    me, side = lax.axis_index(("far", "y", "core")), lax.axis_index("lvl")
    for j in range(patches):
        frame, top, left = crops_ref[0, j], crops_ref[1, j], crops_ref[2, j]
        near_by = lax.bitwise_xor(frame % 4, me % 4)
        k = (me // 4 - frame // 4 + far) % far
        k = jnp.where(k == 1, 2, jnp.where(k == 2, 3, jnp.where(k == 3, 1, k)))
        here = near_by % 2 == 0
        for a in range(4):
            row = jnp.minimum(top + a, SIDE - 1)
            shard = (lax.bitwise_xor(row // 4, side) * 2 + near_by // 2) * far + k
            row = row % 4
            start = shard * (6 * SIDE)
            wide = pl.ds(pl.multiple_of(start + row * SIDE, SIDE), SIDE)
            tail = pl.ds(pl.multiple_of(start + (4 + row % 2) * SIDE, SIDE), SIDE)
            into = slice(j * 16 + a * 4, j * 16 + a * 4 + 4)
            line = jnp.where(here, own_ref[wide, :], other_ref[wide, :])
            rows[into, :128] = pltpu.roll(line, SIDE - left, 0)[:4, :]
            line = pltpu.roll(jnp.where(here, own_ref[tail, :], other_ref[tail, :]), SIDE - left, 0)[:4, :]
            rows[into, 128:] = jnp.where(row >= 2, line[:, 64:], line[:, :64])
    pre = through(rows[...], coarses, NN)
    gate = sigmoid(pre)
    slope_ref[...] = (gate * (1.0 + pre * (1.0 - gate))).T
    projected = through(pre * gate, projects, NN).T
    projected_ref[...] = jnp.concatenate(split(projected), axis=1)
    for copy in fetches:
        copy.wait()


def middle_kernel(
    projected,
    grams,
    wanted,
    xw_first,
    tw_first,
    tw_last,
    xw_hbm,
    xw_last,
    tw_hbm,
    pair_hbm,
    de_hbm,
    de_ref,
    deep_ref,
    dslot_ref,
    xw,
    tw,
    taken,
    factor,
    deep,
    parts,
    xw_sems,
    tw_sems,
    out_sems,
    sems,
):
    width, count = xw.shape
    slots = dslot_ref.shape[1]
    chunks = chunk_rows(count)
    each = slots // len(chunks)
    tw_loads = [
        pltpu.make_async_copy(tw_hbm.at[:, here], tw.at[:, here], tw_sems.at[i])
        for i, here in enumerate(chunks[1:-1])
    ]
    xw_loads = [
        pltpu.make_async_copy(xw_hbm.at[:, here], xw.at[:, here], xw_sems.at[i])
        for i, here in enumerate(chunks[2:-1])
    ]
    xw_loads.append(pltpu.make_async_copy(xw_last, xw.at[:, chunks[-1]], xw_sems.at[len(xw_loads)]))
    stores = [
        pltpu.make_async_copy(xw.at[:, here], de_hbm.at[:, here], out_sems.at[i])
        for i, here in enumerate(chunks[:-1])
    ]
    fetches = [
        pltpu.make_async_copy(pair_hbm, deep_ref.at[: 2 * width], sems.at[0]),
        pltpu.make_async_copy(pair_hbm.at[:width], deep_ref.at[2 * width :], sems.at[1]),
    ]
    for pair in zip(tw_loads, xw_loads):
        for copy in pair:
            copy.start()
    for copy in fetches:
        copy.start()

    def begin(i):
        tokens = chunks[i]
        source = xw_first.at[:, tokens] if i < 2 else xw.at[:, tokens]
        here = taking(wanted[:, tokens], slots, 0)
        taken[:slots], taken[slots:] = here, here
        spread = dot(projected[...], taken[...])
        for here in blocks(width, 32):
            pre = source[here] + spread[here]
            gate = sigmoid(pre)
            hidden = pre * gate
            factor[i % 2, here] = gate + hidden * (1.0 - gate)
            high, low = split(hidden)
            for part, value in enumerate((high, high, low)):
                deep[i % 2, shift(here, part * width)] = value

    begin(0)
    for i, tokens in enumerate(chunks):
        if 0 < i < len(chunks) - 1:
            tw_loads[i - 1].wait()
            xw_loads[i - 1].wait()
        minus = tw_first if i == 0 else tw_last if i == len(chunks) - 1 else tw.at[:, tokens]
        target = de_ref if i == len(chunks) - 1 else xw.at[:, tokens]
        product = dot(grams[...], deep[i % 2])
        if i + 1 < len(chunks):
            begin(i + 1)
        for here in blocks(width, 32):
            de = (product[here] - minus[here]) * factor[i % 2, here]
            target[here] = de
            parts[here], parts[shift(here, width)] = split(de)
        mine = slice(i * each, (i + 1) * each)
        both = dot(parts[...], taking(wanted[:, tokens], each, i * each), NT)
        dslot_ref[:, mine] = both[:width] + both[width:]
        if i < len(stores):
            stores[i].start()
    for copy in stores + fetches:
        copy.wait()


def through(value, pair, dims):
    count, rows = value.shape[0], pair.shape[0] // 2
    high, low = split(value)
    both = dot(jnp.concatenate([high, low], axis=0), pair[:rows], dims)
    return both[:count] + (both[count:] + dot(high, pair[rows:], dims))


def closing_kernel(dslot_ref, slope_ref, coarses, projects, lay, number, send_ref):
    grad = pair_product(coarses, pair_product(projects, dslot_ref[...]) * slope_ref[...])
    parts = jnp.concatenate(split(jnp.concatenate([grad, number[...]], axis=0)), axis=0)
    both = dot(lay[...], parts, NT)
    send_ref[...] = both[:, :LANES] + both[:, LANES:]


def scatter_kernel(message_ref, done_ref, mine_ref, other_ref, total):
    del done_ref
    pixels = mine_ref.shape[2]
    message = message_ref[...]
    number = lax.broadcasted_iota(jnp.int32, (message.shape[0], SIDE * SIDE), 1).astype(F32)
    pick = jnp.where(message[:, pixels : pixels + 1] == number, 1.0, 0.0).astype(BF16)
    high, low = split(message[:, :pixels])
    total[...] = dot(pick, low, TN) + dot(pick, high, TN)
    half = mine_ref.shape[1]
    side = lax.axis_index("lvl")
    mine_ref[0] = total[pl.ds(pl.multiple_of(side * half, half), half), :]
    other_ref[0] = total[pl.ds(pl.multiple_of((1 - side) * half, half), half), :]


def last_kernel(de_hbm, first, deep, out_hbm, de, out, cat, in_sems, out_sems):
    width = de.shape[0]
    steps = de.shape[1] // ROWS

    def load(i):
        return pltpu.make_async_copy(de_hbm.at[:, chunk(i)], de.at[:, chunk(i)], in_sems.at[i])

    def store(i):
        return pltpu.make_async_copy(out.at[chunk(i)], out_hbm.at[chunk(i)], out_sems.at[i])

    def prepare(source):
        for here in blocks(width, 32):
            high, low = split(source[here])
            cat[here], cat[shift(here, width)], cat[shift(here, 2 * width)] = high, high, low

    for i in range(steps - 1):
        load(i).start()
    prepare(first)

    def step(i, _):
        mine = lax.rem(i + steps - 1, steps)
        out[chunk(mine), :] = dot(cat[...], deep[...], TN)
        store(mine).start()

        @pl.when(i + 1 < steps)
        def _():
            load(i).wait()
            prepare(de.at[:, chunk(i)])

        return 0

    lax.fori_loop(0, steps, step, 0)
    for i in range(steps):
        store(i).wait()


def fixed(*values):
    return [pltpu.with_memory_space_constraint(value, pltpu.HBM) for value in values]


def near(*values):
    return [pltpu.with_memory_space_constraint(value, pltpu.VMEM) for value in values]


def stack(kernel, blocks, before, rows):
    shape = (len(blocks) * rows, 128)
    return call(
        kernel,
        "stack",
        1000,
        jax.ShapeDtypeStruct(shape, F32),
        limit=ROOM,
        in_specs=[VMEM] * len(blocks) + [HBM],
        out_specs=VMEM,
    )(*blocks, *fixed(before))


def body(coarse_input, coarse_weight, fine_input, fine_target, crops, in_weight, context_weight, out_weight):
    patch = ("far", "y", "core")
    peers = lax.axis_size(patch)
    far = peers // 4
    patches, tokens, values = fine_input.shape
    width = in_weight.shape[1]
    pixels = coarse_weight.shape[0]
    half = coarse_input.shape[1]
    count = patches * tokens
    swap = [(0, 1), (1, 0)]

    column = {0: coarse_input}
    for k in range(1, far):
        column[k] = lax.ppermute(coarse_input, "far", [(p, (p + k) % far) for p in range(far)])
    column = [column[k] for k in [0, 3, 1, 2] + list(range(4, far))]

    steps = count // ROWS
    pair_shape = (2 * width, values)
    x, t = fine_input.reshape(count, values), fine_target.reshape(count, values)
    xw, xw_last, pair, rows, next_pair, crops = call(
        input_kernel,
        "input",
        6 * count * values * width,
        (
            pltpu.HBM((width, count - ROWS), F32),
            pltpu.VMEM((width, ROWS), F32),
            pltpu.HBM(pair_shape, BF16),
            pltpu.VMEM((ROWS, values), F32),
            pltpu.VMEM(pair_shape, BF16),
            pltpu.VMEM((4, patches), jnp.int32),
        ),
        in_specs=[HBM] * 5,
        out_specs=(HBM, VMEM, HBM, VMEM, VMEM, VMEM),
        scratch_shapes=[
            pltpu.VMEM((count, values), F32),
            pltpu.VMEM((width, count), F32),
            pltpu.VMEM((width, values), F32),
            pltpu.VMEM((width, values), F32),
            pltpu.VMEM(pair_shape, BF16),
            pltpu.VMEM((ROWS, values), BF16),
            pltpu.VMEM((ROWS, values), BF16),
            pltpu.SemaphoreType.DMA((steps,)),
            pltpu.SemaphoreType.DMA((steps,)),
            pltpu.SemaphoreType.DMA((5,)),
        ],
    )(*fixed(x, in_weight.T, t, out_weight, crops.T))
    column = stack(pack_kernel, column, xw, half * 3 // 2)
    own = [column]
    for flip in range(1, 4):
        own.append(lax.ppermute(column, ("lvl", "y"), [(p, p ^ flip) for p in range(4)]))
    tw, xw_last, tw_last, coarses, projects = call(
        target_kernel,
        "target",
        6 * count * values * width,
        (
            pltpu.HBM((width, count - ROWS), F32),
            pltpu.HBM((width, ROWS), F32),
            pltpu.VMEM((width, ROWS), F32),
            pltpu.VMEM((2 * pixels, width), BF16),
            pltpu.VMEM((2 * width, width), BF16),
        ),
        limit=ROOM,
        in_specs=[HBM] * 3 + [VMEM] * 3,
        out_specs=(HBM, HBM, VMEM, VMEM, VMEM),
        scratch_shapes=[
            pltpu.VMEM((count, values), F32),
            pltpu.VMEM((width, count), F32),
            pltpu.VMEM((ROWS, values), BF16),
            pltpu.VMEM((ROWS, values), BF16),
            pltpu.VMEM((pixels, width), F32),
            pltpu.VMEM((width, width), F32),
            pltpu.SemaphoreType.DMA((steps,)),
            pltpu.SemaphoreType.DMA((steps,)),
            pltpu.SemaphoreType.DMA((3,)),
        ],
    )(*fixed(t, coarse_weight, context_weight), *near(rows, next_pair, xw_last))
    own = stack(stack_kernel, own, tw, column.shape[0])
    other = lax.ppermute(own, "core", swap)
    (crops,) = near(crops)
    grams, wanted, lay, number = call(
        functools.partial(prepare_kernel, patches),
        "prepare",
        8 * values * width * width,
        (
            pltpu.VMEM((width, 3 * width), BF16),
            pltpu.VMEM((1, count), jnp.int32),
            pltpu.VMEM((peers * 16, patches * 16), BF16),
            pltpu.VMEM((LANES - pixels, patches * 16), F32),
        ),
        limit=ROOM,
        in_specs=[VMEM, SMEM, HBM],
        out_specs=(VMEM,) * 4,
    )(*near(next_pair), crops, own)

    projected, slope, xw_first, tw_first = call(
        functools.partial(context_kernel, patches, peers),
        "context",
        6 * patches * 16 * width * width,
        (
            pltpu.VMEM((width, 2 * patches * 16), BF16),
            pltpu.VMEM((width, patches * 16), F32),
            pltpu.VMEM((width, 2 * ROWS), F32),
            pltpu.VMEM((width, ROWS), F32),
        ),
        limit=ROOM,
        in_specs=[VMEM] * 5 + [HBM] * 2,
        out_specs=(VMEM,) * 4,
        scratch_shapes=[
            pltpu.VMEM((patches * 16, pixels), F32),
            pltpu.SMEM((4, patches), jnp.int32),
            pltpu.SemaphoreType.DMA((3,)),
        ],
    )(crops, own, other, *near(coarses, projects), *fixed(xw, tw))
    de, last_de, deep, dslot = call(
        middle_kernel,
        "middle",
        6 * count * width * width,
        (
            pltpu.HBM((width, count), F32),
            pltpu.VMEM((width, ROWS), F32),
            pltpu.VMEM((3 * width, values), BF16),
            pltpu.VMEM((width, patches * 16), F32),
        ),
        limit=ROOM,
        in_specs=[VMEM] * 6 + [HBM] * 4,
        out_specs=(HBM,) + (VMEM,) * 3,
        scratch_shapes=[
            pltpu.VMEM((width, count), F32),
            pltpu.VMEM((width, count), F32),
            pltpu.VMEM((2 * patches * 16, ROWS), BF16),
            pltpu.VMEM((2, width, ROWS), F32),
            pltpu.VMEM((2, 3 * width, ROWS), BF16),
            pltpu.VMEM((2 * width, ROWS), BF16),
            pltpu.SemaphoreType.DMA((steps,)),
            pltpu.SemaphoreType.DMA((steps,)),
            pltpu.SemaphoreType.DMA((steps,)),
            pltpu.SemaphoreType.DMA((2,)),
        ],
    )(*near(projected, grams, wanted, xw_first, tw_first, tw_last), *fixed(xw, xw_last, tw, pair))
    back = call(
        closing_kernel,
        "closing",
        6 * patches * 16 * width * width,
        pltpu.VMEM((peers * 16, LANES), F32),
        limit=ROOM,
        in_specs=[VMEM] * 6,
        out_specs=VMEM,
    )(*near(dslot, slope, coarses, projects, lay, number))
    returned = lax.all_to_all(back, patch, 0, 0, tiled=True)

    fine_grad = call(
        last_kernel,
        "last",
        6 * count * values * width,
        pltpu.HBM((count, values), F32),
        limit=ROOM,
        in_specs=[HBM, VMEM, VMEM],
        out_specs=HBM,
        scratch_shapes=[
            pltpu.VMEM((width, count), F32),
            pltpu.VMEM((count, values), F32),
            pltpu.VMEM((3 * width, ROWS), BF16),
            pltpu.SemaphoreType.DMA((steps,)),
            pltpu.SemaphoreType.DMA((steps,)),
        ],
    )(*fixed(de), *near(last_de, deep))
    part = (1, half, pixels)
    mine, theirs = call(
        scatter_kernel,
        "scatter",
        10000,
        (jax.ShapeDtypeStruct(part, F32), jax.ShapeDtypeStruct(part, F32)),
        limit=ROOM,
        in_specs=[VMEM, HBM],
        out_specs=(VMEM, VMEM),
        scratch_shapes=[pltpu.VMEM((SIDE * SIDE, pixels), F32)],
    )(returned, *fixed(fine_grad))
    coarse_grad = mine + lax.ppermute(theirs, "lvl", swap)
    return (coarse_grad, fine_grad.reshape(fine_input.shape))


def solution(mesh):
    sides, peers = mesh.shape["lvl"], mesh.shape["patch"]
    fine = jax.sharding.Mesh(mesh.devices.reshape(sides, peers // 4, 2, 2), ("lvl", "far", "y", "core"))
    patch = ("far", "y", "core")
    both = ("lvl",) + patch
    in_specs = (
        P(patch, "lvl", None),
        P(),
        P(both, None, None),
        P(both, None, None),
        P(both, None),
        P(),
        P(),
        P(),
    )
    out_specs = (P(patch, "lvl", None), P(both, None, None))
    return jax.shard_map(body, mesh=fine, in_specs=in_specs, out_specs=out_specs, check_vma=False)
```

```python
import functools
import math

import jax
import jax.numpy as jnp
from jax import lax
from jax.experimental import pallas as pl
from jax.experimental.pallas import tpu as pltpu
from jax.sharding import PartitionSpec as P

F32 = jnp.float32
BF16 = jnp.bfloat16
NN = (((1,), (0,)), ((), ()))
NT = (((1,), (1,)), ((), ()))
TN = (((0,), (0,)), ((), ()))
ROWS = 512
SIDE = 8
LANES = 256
LIMIT = 60 * 1024 * 1024
ROOM = 40 * 1024 * 1024
SMEM = pl.BlockSpec(memory_space=pltpu.SMEM)
VMEM = pl.BlockSpec(memory_space=pltpu.VMEM)
HBM = pl.BlockSpec(memory_space=pltpu.HBM)


def split(value):
    high = value.astype(BF16)
    low = (value - high.astype(F32)).astype(BF16)
    return high, low


def dot(left, right, dims=NN):
    return lax.dot_general(left, right, dims, preferred_element_type=F32)


def dot3(left, right, dims=NN):
    return (
        dot(left[0], right[1], dims) + dot(left[1], right[0], dims) + dot(left[0], right[0], dims)
    )


def side_by_side(value):
    high, low = split(value)
    return jnp.concatenate([high, low, high], axis=1)


def sigmoid(value):
    return 0.5 * jnp.tanh(0.5 * value) + 0.5


def call(kernel, name, flops, out_shape, limit=LIMIT, **kwargs):
    moved = 8 * sum(math.prod(s.shape) for s in jax.tree.leaves(out_shape))
    return pl.pallas_call(
        kernel,
        out_shape=out_shape,
        name=name,
        cost_estimate=pl.CostEstimate(flops=flops, bytes_accessed=moved, transcendentals=0),
        compiler_params=pltpu.CompilerParams(vmem_limit_bytes=limit),
        **kwargs,
    )


def blocks(rows, size):
    return [slice(start, start + size) for start in range(0, rows, size)]


def shift(here, by):
    return slice(here.start + by, here.stop + by)


def pair_product(pair, value, dims):
    rows = pair.shape[0] // 2
    high, low = split(value)
    both = dot(pair[...], high, dims)
    return both[:rows] + (both[rows:] + dot(pair[:rows], low, dims))


def chunk(i):
    return pl.ds(pl.multiple_of(i * ROWS, ROWS), ROWS)


def wide_product(pair, value, high, low, out):
    width = pair.shape[0] // 2
    for here in blocks(high.shape[0], 16):
        high[here], low[here] = split(value[here])
    both = dot(pair[...], high[...], NT)
    rest = dot(pair[:width], low[...], NT)
    for here in blocks(width, 32):
        out[here] = both[here] + (both[shift(here, width)] + rest[here])


def input_kernel(
    x_hbm,
    weight_hbm,
    t_hbm,
    next_weight_hbm,
    crops_hbm,
    out_hbm,
    out_last,
    pair_hbm,
    next_rows,
    next_pair,
    crops,
    x,
    out,
    weight,
    next_weight,
    pair,
    high,
    low,
    in_sems,
    out_sems,
    sems,
):
    width = weight.shape[0]
    chunks = chunk_rows(x.shape[0])
    fetch = pltpu.make_async_copy(weight_hbm, weight, sems.at[0])
    keep = pltpu.make_async_copy(pair, pair_hbm, sems.at[1])
    fetch_next = pltpu.make_async_copy(next_weight_hbm, next_weight, sems.at[2])
    fetch_rows = pltpu.make_async_copy(t_hbm.at[: next_rows.shape[0]], next_rows, sems.at[3])
    fetch_crops = pltpu.make_async_copy(crops_hbm, crops, sems.at[4])
    loads = [
        pltpu.make_async_copy(x_hbm.at[here], x.at[here], in_sems.at[i]) for i, here in enumerate(chunks)
    ]
    stores = [
        pltpu.make_async_copy(out.at[:, here], out_hbm.at[:, here], out_sems.at[i])
        for i, here in enumerate(chunks[:-1])
    ]
    for copy in (fetch, loads[0]):
        copy.start()
    fetch.wait()
    loads[1].start()
    pair[:width], pair[width:] = split(weight[...])
    keep.start()
    for i, here in enumerate(chunks):
        loads[i].wait()
        if i + 2 < len(chunks):
            loads[i + 2].start()
        if i == 0:
            fetch_next.start()
        if i == 1:
            fetch_rows.start()
            fetch_crops.start()
        if i == len(chunks) - 1:
            fetch_next.wait()
            next_pair[:width], next_pair[width:] = split(next_weight[...])
        target = out.at[:, here] if i < len(stores) else out_last
        wide_product(pair, x.at[here], high, low, target)
        if i < len(stores):
            stores[i].start()
    for copy in [keep, fetch_rows, fetch_crops] + stores:
        copy.wait()


def target_kernel(
    t_hbm,
    cwgt_hbm,
    xwgt_hbm,
    rows,
    pair,
    before_last,
    out_hbm,
    before_hbm,
    out_last,
    coarses,
    projects,
    t,
    out,
    high,
    low,
    cwgt,
    xwgt,
    in_sems,
    out_sems,
    sems,
):
    chunks = chunk_rows(t.shape[0])
    fetches = [
        pltpu.make_async_copy(cwgt_hbm, cwgt, sems.at[0]),
        pltpu.make_async_copy(xwgt_hbm, xwgt, sems.at[1]),
    ]
    loads = [
        pltpu.make_async_copy(t_hbm.at[here], t.at[here], in_sems.at[i])
        for i, here in enumerate(chunks[1:])
    ]
    stores = [
        pltpu.make_async_copy(out.at[:, here], out_hbm.at[:, here], out_sems.at[i])
        for i, here in enumerate(chunks[:-1])
    ]
    keep = pltpu.make_async_copy(before_last, before_hbm, sems.at[2])
    for copy in loads + fetches:
        copy.start()
    for i, here in enumerate(chunks):
        if i > 0:
            loads[i - 1].wait()
        if i == 2:
            keep.start()
        source = rows if i == 0 else t.at[here]
        if i < len(stores):
            wide_product(pair, source, high, low, out.at[:, here])
            stores[i].start()
        else:
            wide_product(pair, source, high, low, out_last)
    for copy in fetches:
        copy.wait()
    coarses[...] = jnp.concatenate(split(cwgt[...]), axis=0)
    projects[...] = jnp.concatenate(split(xwgt[...]), axis=0)
    for copy in stores + [keep]:
        copy.wait()


def chunk_rows(count):
    return [slice(start, start + ROWS) for start in range(0, count, ROWS)]


def prepare_kernel(patches, pair, crops_ref, before_ref, grams, wanted, lay, number):
    del before_ref
    width = grams.shape[0]
    both = dot(pair[...], pair[:width], NT)
    grams[...] = side_by_side(both[:width] + (both[width:] + both[width:].T))
    wanted[...] = slot_row(crops_ref, patches, wanted.shape[1] // patches)
    frame = row_value(crops_ref, 0, patches, (1, patches * 16), 1, 16)
    slot = lax.broadcasted_iota(jnp.int32, (1, patches * 16), 1) % 16
    line = lax.broadcasted_iota(jnp.int32, lay.shape, 0)
    lay[...] = jnp.where(line == frame * 16 + slot, 1.0, 0.0).astype(BF16)
    slot = lax.broadcasted_iota(jnp.int32, number.shape, 0) % 16
    top = row_value(crops_ref, 1, patches, number.shape, 0, 16)
    left = row_value(crops_ref, 2, patches, number.shape, 0, 16)
    number[...] = ((top + slot // 4) * SIDE + left + slot % 4).astype(F32)


def stack_kernel(*refs):
    *block_refs, _, out_ref = refs
    size = block_refs[0].shape[0]
    for k, ref in enumerate(block_refs):
        out_ref[k * size : (k + 1) * size] = ref[...]


def pack_kernel(*refs):
    *block_refs, _, out_ref = refs
    tokens = block_refs[0].shape[1]
    size = tokens * 3 // 2
    for k, ref in enumerate(block_refs):
        out_ref[k * size : k * size + tokens] = ref[0, :, :128]
        tails = [ref[0, : tokens // 2, 128:], ref[0, tokens // 2 :, 128:]]
        out_ref[k * size + tokens : (k + 1) * size] = jnp.concatenate(tails, axis=1)


def row_value(crops_ref, column, patches, shape, axis, each):
    index = lax.broadcasted_iota(jnp.int32, shape, axis) // each
    found = jnp.zeros(shape, jnp.int32)
    for j in range(patches):
        found = jnp.where(index == j, crops_ref[column, j], found)
    return found


def slot_row(crops_ref, patches, tokens):
    scale = row_value(crops_ref, 3, patches, (1, patches * tokens), 1, tokens)
    token = lax.broadcasted_iota(jnp.int32, (1, patches * tokens), 1)
    row, column = (token % tokens) // 16, token % 16
    return token // tokens * 16 + (row * scale // 8) * 4 + column * scale // 8


def taking(wanted, slots, first):
    slot = lax.broadcasted_iota(jnp.int32, (slots, wanted.shape[1]), 0) + first
    return jnp.where(slot == wanted, 1.0, 0.0).astype(BF16)


def context_kernel(
    patches,
    peers,
    crops_vmem,
    own_ref,
    other_ref,
    coarses,
    projects,
    xw_hbm,
    tw_hbm,
    projected_ref,
    slope_ref,
    xw_first,
    tw_first,
    rows,
    crops_ref,
    sems,
):
    fetches = [
        pltpu.make_async_copy(xw_hbm.at[:, : xw_first.shape[1]], xw_first, sems.at[0]),
        pltpu.make_async_copy(tw_hbm.at[:, : tw_first.shape[1]], tw_first, sems.at[1]),
    ]
    for copy in fetches:
        copy.start()
    take = pltpu.make_async_copy(crops_vmem, crops_ref, sems.at[2])
    take.start()
    take.wait()
    pixels = coarses.shape[0] // 2
    width = projects.shape[1]
    far = peers // 4
    me, side = lax.axis_index(("far", "y", "core")), lax.axis_index("lvl")
    for j in range(patches):
        frame, top, left = crops_ref[0, j], crops_ref[1, j], crops_ref[2, j]
        near_by = lax.bitwise_xor(frame % 4, me % 4)
        k = (me // 4 - frame // 4 + far) % far
        k = jnp.where(k == 2, 3, jnp.where(k == 3, 2, k))
        here = near_by % 2 == 0
        for a in range(4):
            row = jnp.minimum(top + a, SIDE - 1)
            shard = (lax.bitwise_xor(row // 4, side) * 2 + near_by // 2) * far + k
            row = row % 4
            start = shard * (6 * SIDE)
            wide = pl.ds(pl.multiple_of(start + row * SIDE, SIDE), SIDE)
            tail = pl.ds(pl.multiple_of(start + (4 + row % 2) * SIDE, SIDE), SIDE)
            into = slice(j * 16 + a * 4, j * 16 + a * 4 + 4)
            line = jnp.where(here, own_ref[wide, :], other_ref[wide, :])
            rows[into, :128] = pltpu.roll(line, SIDE - left, 0)[:4, :]
            line = pltpu.roll(jnp.where(here, own_ref[tail, :], other_ref[tail, :]), SIDE - left, 0)[:4, :]
            rows[into, 128:] = jnp.where(row >= 2, line[:, 64:], line[:, :64])
    pre = through(rows[...], coarses, NN)
    gate = sigmoid(pre)
    slope_ref[...] = gate * (1.0 + pre * (1.0 - gate))
    projected = through(pre * gate, projects, NN).T
    projected_ref[...] = jnp.concatenate(split(projected), axis=1)
    for copy in fetches:
        copy.wait()


def middle_kernel(
    projected,
    grams,
    wanted,
    xw_first,
    tw_first,
    tw_last,
    xw_hbm,
    xw_last,
    tw_hbm,
    pair_hbm,
    de_hbm,
    de_ref,
    deep_ref,
    dslot_ref,
    xw,
    tw,
    taken,
    factor,
    deep,
    parts,
    xw_sems,
    tw_sems,
    out_sems,
    sems,
):
    width, count = xw.shape
    slots = dslot_ref.shape[0]
    chunks = chunk_rows(count)
    each = slots // len(chunks)
    tw_loads = [
        pltpu.make_async_copy(tw_hbm.at[:, here], tw.at[:, here], tw_sems.at[i])
        for i, here in enumerate(chunks[1:-1])
    ]
    xw_loads = [
        pltpu.make_async_copy(xw_hbm.at[:, here], xw.at[:, here], xw_sems.at[i])
        for i, here in enumerate(chunks[2:-1])
    ]
    xw_loads.append(pltpu.make_async_copy(xw_last, xw.at[:, chunks[-1]], xw_sems.at[len(xw_loads)]))
    stores = [
        pltpu.make_async_copy(xw.at[:, here], de_hbm.at[:, here], out_sems.at[i])
        for i, here in enumerate(chunks[:-1])
    ]
    fetches = [
        pltpu.make_async_copy(pair_hbm, deep_ref.at[: 2 * width], sems.at[0]),
        pltpu.make_async_copy(pair_hbm.at[:width], deep_ref.at[2 * width :], sems.at[1]),
    ]
    for pair in zip(tw_loads, xw_loads):
        for copy in pair:
            copy.start()
    for copy in fetches:
        copy.start()

    def begin(i):
        tokens = chunks[i]
        source = xw_first.at[:, tokens] if i < 2 else xw.at[:, tokens]
        here = taking(wanted[:, tokens], slots, 0)
        taken[:slots], taken[slots:] = here, here
        spread = dot(projected[...], taken[...])
        for here in blocks(width, 32):
            pre = source[here] + spread[here]
            gate = sigmoid(pre)
            hidden = pre * gate
            factor[i % 2, here] = gate + hidden * (1.0 - gate)
            high, low = split(hidden)
            for part, value in enumerate((high, high, low)):
                deep[i % 2, shift(here, part * width)] = value

    begin(0)
    for i, tokens in enumerate(chunks):
        if 0 < i < len(chunks) - 1:
            tw_loads[i - 1].wait()
            xw_loads[i - 1].wait()
        minus = tw_first if i == 0 else tw_last if i == len(chunks) - 1 else tw.at[:, tokens]
        target = de_ref if i == len(chunks) - 1 else xw.at[:, tokens]
        product = dot(grams[...], deep[i % 2])
        if i + 1 < len(chunks):
            begin(i + 1)
        for here in blocks(width, 32):
            de = (product[here] - minus[here]) * factor[i % 2, here]
            target[here] = de
            parts[here], parts[shift(here, width)] = split(de)
        mine = slice(i * each, (i + 1) * each)
        both = dot(taking(wanted[:, tokens], each, i * each), parts[...], NT)
        dslot_ref[mine] = both[:, :width] + both[:, width:]
        if i < len(stores):
            stores[i].start()
    for copy in stores + fetches:
        copy.wait()


def through(value, pair, dims):
    count, rows = value.shape[0], pair.shape[0] // 2
    high, low = split(value)
    both = dot(jnp.concatenate([high, low], axis=0), pair[:rows], dims)
    return both[:count] + (both[count:] + dot(high, pair[rows:], dims))


def back_through(value, pair):
    count, rows = value.shape[0], pair.shape[0] // 2
    both = dot(jnp.concatenate(split(value), axis=0), pair[...], NT)
    return both[:count, :rows] + (both[count:, :rows] + both[:count, rows:])


def closing_kernel(dslot_ref, slope_ref, coarses, projects, lay, number, send_ref):
    grad = back_through(back_through(dslot_ref[...], projects) * slope_ref[...], coarses)
    parts = jnp.concatenate(split(jnp.concatenate([grad, number[...]], axis=1)), axis=1)
    both = dot(lay[...], parts)
    send_ref[...] = both[:, :LANES] + both[:, LANES:]


def scatter_kernel(message_ref, done_ref, mine_ref, other_ref, total):
    del done_ref
    pixels = mine_ref.shape[2]
    message = message_ref[...]
    number = lax.broadcasted_iota(jnp.int32, (message.shape[0], SIDE * SIDE), 1).astype(F32)
    pick = jnp.where(message[:, pixels : pixels + 1] == number, 1.0, 0.0).astype(BF16)
    high, low = split(message[:, :pixels])
    total[...] = dot(pick, low, TN) + dot(pick, high, TN)
    half = mine_ref.shape[1]
    side = lax.axis_index("lvl")
    mine_ref[0] = total[pl.ds(pl.multiple_of(side * half, half), half), :]
    other_ref[0] = total[pl.ds(pl.multiple_of((1 - side) * half, half), half), :]


def last_kernel(de_hbm, first, deep, out_hbm, de, out, cat, in_sems, out_sems):
    width = de.shape[0]
    steps = de.shape[1] // ROWS

    def load(i):
        return pltpu.make_async_copy(de_hbm.at[:, chunk(i)], de.at[:, chunk(i)], in_sems.at[i])

    def store(i):
        return pltpu.make_async_copy(out.at[chunk(i)], out_hbm.at[chunk(i)], out_sems.at[i])

    def prepare(source):
        for here in blocks(width, 32):
            high, low = split(source[here])
            cat[here], cat[shift(here, width)], cat[shift(here, 2 * width)] = high, high, low

    for i in range(steps - 1):
        load(i).start()
    prepare(first)

    def step(i, _):
        mine = lax.rem(i + steps - 1, steps)
        out[chunk(mine), :] = dot(cat[...], deep[...], TN)
        store(mine).start()

        @pl.when(i + 1 < steps)
        def _():
            load(i).wait()
            prepare(de.at[:, chunk(i)])

        return 0

    lax.fori_loop(0, steps, step, 0)
    for i in range(steps):
        store(i).wait()


def fixed(*values):
    return [pltpu.with_memory_space_constraint(value, pltpu.HBM) for value in values]


def near(*values):
    return [pltpu.with_memory_space_constraint(value, pltpu.VMEM) for value in values]


def stack(kernel, blocks, before, rows):
    shape = (len(blocks) * rows, 128)
    return call(
        kernel,
        "stack",
        1000,
        jax.ShapeDtypeStruct(shape, F32),
        limit=ROOM,
        in_specs=[VMEM] * len(blocks) + [HBM],
        out_specs=VMEM,
    )(*blocks, *fixed(before))


def body(coarse_input, coarse_weight, fine_input, fine_target, crops, in_weight, context_weight, out_weight):
    patch = ("far", "y", "core")
    peers = lax.axis_size(patch)
    far = peers // 4
    patches, tokens, values = fine_input.shape
    width = in_weight.shape[1]
    pixels = coarse_weight.shape[0]
    half = coarse_input.shape[1]
    count = patches * tokens
    swap = [(0, 1), (1, 0)]

    column = {0: coarse_input}
    for k in range(1, far):
        column[k] = lax.ppermute(coarse_input, "far", [(p, (p + k) % far) for p in range(far)])
    column = [column[k] for k in [0, 1, 3, 2] + list(range(4, far))]

    steps = count // ROWS
    pair_shape = (2 * width, values)
    x, t = fine_input.reshape(count, values), fine_target.reshape(count, values)
    xw, xw_last, pair, rows, next_pair, crops = call(
        input_kernel,
        "input",
        6 * count * values * width,
        (
            pltpu.HBM((width, count - ROWS), F32),
            pltpu.VMEM((width, ROWS), F32),
            pltpu.HBM(pair_shape, BF16),
            pltpu.VMEM((ROWS, values), F32),
            pltpu.VMEM(pair_shape, BF16),
            pltpu.VMEM((4, patches), jnp.int32),
        ),
        in_specs=[HBM] * 5,
        out_specs=(HBM, VMEM, HBM, VMEM, VMEM, VMEM),
        scratch_shapes=[
            pltpu.VMEM((count, values), F32),
            pltpu.VMEM((width, count), F32),
            pltpu.VMEM((width, values), F32),
            pltpu.VMEM((width, values), F32),
            pltpu.VMEM(pair_shape, BF16),
            pltpu.VMEM((ROWS, values), BF16),
            pltpu.VMEM((ROWS, values), BF16),
            pltpu.SemaphoreType.DMA((steps,)),
            pltpu.SemaphoreType.DMA((steps,)),
            pltpu.SemaphoreType.DMA((5,)),
        ],
    )(*fixed(x, in_weight.T, t, out_weight, crops.T))
    column = stack(pack_kernel, column, xw, half * 3 // 2)
    own = [column]
    for flip in range(1, 4):
        own.append(lax.ppermute(column, ("lvl", "y"), [(p, p ^ flip) for p in range(4)]))
    tw, xw_last, tw_last, coarses, projects = call(
        target_kernel,
        "target",
        6 * count * values * width,
        (
            pltpu.HBM((width, count - ROWS), F32),
            pltpu.HBM((width, ROWS), F32),
            pltpu.VMEM((width, ROWS), F32),
            pltpu.VMEM((2 * pixels, width), BF16),
            pltpu.VMEM((2 * width, width), BF16),
        ),
        limit=ROOM,
        in_specs=[HBM] * 3 + [VMEM] * 3,
        out_specs=(HBM, HBM, VMEM, VMEM, VMEM),
        scratch_shapes=[
            pltpu.VMEM((count, values), F32),
            pltpu.VMEM((width, count), F32),
            pltpu.VMEM((ROWS, values), BF16),
            pltpu.VMEM((ROWS, values), BF16),
            pltpu.VMEM((pixels, width), F32),
            pltpu.VMEM((width, width), F32),
            pltpu.SemaphoreType.DMA((steps,)),
            pltpu.SemaphoreType.DMA((steps,)),
            pltpu.SemaphoreType.DMA((3,)),
        ],
    )(*fixed(t, coarse_weight, context_weight), *near(rows, next_pair, xw_last))
    own = stack(stack_kernel, own, tw, column.shape[0])
    other = lax.ppermute(own, "core", swap)
    (crops,) = near(crops)
    grams, wanted, lay, number = call(
        functools.partial(prepare_kernel, patches),
        "prepare",
        8 * values * width * width,
        (
            pltpu.VMEM((width, 3 * width), BF16),
            pltpu.VMEM((1, count), jnp.int32),
            pltpu.VMEM((peers * 16, patches * 16), BF16),
            pltpu.VMEM((patches * 16, LANES - pixels), F32),
        ),
        limit=ROOM,
        in_specs=[VMEM, SMEM, HBM],
        out_specs=(VMEM,) * 4,
    )(*near(next_pair), crops, own)

    projected, slope, xw_first, tw_first = call(
        functools.partial(context_kernel, patches, peers),
        "context",
        6 * patches * 16 * width * width,
        (
            pltpu.VMEM((width, 2 * patches * 16), BF16),
            pltpu.VMEM((patches * 16, width), F32),
            pltpu.VMEM((width, 2 * ROWS), F32),
            pltpu.VMEM((width, ROWS), F32),
        ),
        limit=ROOM,
        in_specs=[VMEM] * 5 + [HBM] * 2,
        out_specs=(VMEM,) * 4,
        scratch_shapes=[
            pltpu.VMEM((patches * 16, pixels), F32),
            pltpu.SMEM((4, patches), jnp.int32),
            pltpu.SemaphoreType.DMA((3,)),
        ],
    )(crops, own, other, *near(coarses, projects), *fixed(xw, tw))
    de, last_de, deep, dslot = call(
        middle_kernel,
        "middle",
        6 * count * width * width,
        (
            pltpu.HBM((width, count), F32),
            pltpu.VMEM((width, ROWS), F32),
            pltpu.VMEM((3 * width, values), BF16),
            pltpu.VMEM((patches * 16, width), F32),
        ),
        limit=ROOM,
        in_specs=[VMEM] * 6 + [HBM] * 4,
        out_specs=(HBM,) + (VMEM,) * 3,
        scratch_shapes=[
            pltpu.VMEM((width, count), F32),
            pltpu.VMEM((width, count), F32),
            pltpu.VMEM((2 * patches * 16, ROWS), BF16),
            pltpu.VMEM((2, width, ROWS), F32),
            pltpu.VMEM((2, 3 * width, ROWS), BF16),
            pltpu.VMEM((2 * width, ROWS), BF16),
            pltpu.SemaphoreType.DMA((steps,)),
            pltpu.SemaphoreType.DMA((steps,)),
            pltpu.SemaphoreType.DMA((steps,)),
            pltpu.SemaphoreType.DMA((2,)),
        ],
    )(*near(projected, grams, wanted, xw_first, tw_first, tw_last), *fixed(xw, xw_last, tw, pair))
    back = call(
        closing_kernel,
        "closing",
        6 * patches * 16 * width * width,
        pltpu.VMEM((peers * 16, LANES), F32),
        limit=ROOM,
        in_specs=[VMEM] * 6,
        out_specs=VMEM,
    )(*near(dslot, slope, coarses, projects, lay, number))
    returned = lax.all_to_all(back, patch, 0, 0, tiled=True)

    fine_grad = call(
        last_kernel,
        "last",
        6 * count * values * width,
        pltpu.HBM((count, values), F32),
        limit=ROOM,
        in_specs=[HBM, VMEM, VMEM],
        out_specs=HBM,
        scratch_shapes=[
            pltpu.VMEM((width, count), F32),
            pltpu.VMEM((count, values), F32),
            pltpu.VMEM((3 * width, ROWS), BF16),
            pltpu.SemaphoreType.DMA((steps,)),
            pltpu.SemaphoreType.DMA((steps,)),
        ],
    )(*fixed(de), *near(last_de, deep))
    part = (1, half, pixels)
    mine, theirs = call(
        scatter_kernel,
        "scatter",
        10000,
        (jax.ShapeDtypeStruct(part, F32), jax.ShapeDtypeStruct(part, F32)),
        limit=ROOM,
        in_specs=[VMEM, HBM],
        out_specs=(VMEM, VMEM),
        scratch_shapes=[pltpu.VMEM((SIDE * SIDE, pixels), F32)],
    )(returned, *fixed(fine_grad))
    coarse_grad = mine + lax.ppermute(theirs, "lvl", swap)
    return (coarse_grad, fine_grad.reshape(fine_input.shape))


def solution(mesh):
    sides, peers = mesh.shape["lvl"], mesh.shape["patch"]
    fine = jax.sharding.Mesh(mesh.devices.reshape(sides, peers // 4, 2, 2), ("lvl", "far", "y", "core"))
    patch = ("far", "y", "core")
    both = ("lvl",) + patch
    in_specs = (
        P(patch, "lvl", None),
        P(),
        P(both, None, None),
        P(both, None, None),
        P(both, None),
        P(),
        P(),
        P(),
    )
    out_specs = (P(patch, "lvl", None), P(both, None, None))
    return jax.shard_map(body, mesh=fine, in_specs=in_specs, out_specs=out_specs, check_vma=False)
```

```python
import functools
import math

import jax
import jax.numpy as jnp
from jax import lax
from jax.experimental import pallas as pl
from jax.experimental.pallas import tpu as pltpu
from jax.sharding import PartitionSpec as P

F32 = jnp.float32
BF16 = jnp.bfloat16
NN = (((1,), (0,)), ((), ()))
NT = (((1,), (1,)), ((), ()))
TN = (((0,), (0,)), ((), ()))
ROWS = 512
SIDE = 8
LANES = 256
LIMIT = 60 * 1024 * 1024
ROOM = 40 * 1024 * 1024
SMEM = pl.BlockSpec(memory_space=pltpu.SMEM)
VMEM = pl.BlockSpec(memory_space=pltpu.VMEM)
HBM = pl.BlockSpec(memory_space=pltpu.HBM)


def split(value):
    high = value.astype(BF16)
    low = (value - high.astype(F32)).astype(BF16)
    return high, low


def dot(left, right, dims=NN):
    return lax.dot_general(left, right, dims, preferred_element_type=F32)


def dot3(left, right, dims=NN):
    return (
        dot(left[0], right[1], dims) + dot(left[1], right[0], dims) + dot(left[0], right[0], dims)
    )


def side_by_side(value):
    high, low = split(value)
    return jnp.concatenate([high, low, high], axis=1)


def sigmoid(value):
    return 0.5 * jnp.tanh(0.5 * value) + 0.5


def call(kernel, name, flops, out_shape, limit=LIMIT, **kwargs):
    moved = 8 * sum(math.prod(s.shape) for s in jax.tree.leaves(out_shape))
    return pl.pallas_call(
        kernel,
        out_shape=out_shape,
        name=name,
        cost_estimate=pl.CostEstimate(flops=flops, bytes_accessed=moved, transcendentals=0),
        compiler_params=pltpu.CompilerParams(vmem_limit_bytes=limit),
        **kwargs,
    )


def blocks(rows, size):
    return [slice(start, start + size) for start in range(0, rows, size)]


def shift(here, by):
    return slice(here.start + by, here.stop + by)


def pair_product(pair, value, dims):
    rows = pair.shape[0] // 2
    high, low = split(value)
    both = dot(pair[...], high, dims)
    return both[:rows] + (both[rows:] + dot(pair[:rows], low, dims))


def chunk(i):
    return pl.ds(pl.multiple_of(i * ROWS, ROWS), ROWS)


def wide_product(pair, value, high, low, out):
    width = pair.shape[0] // 2
    for here in blocks(high.shape[0], 16):
        high[here], low[here] = split(value[here])
    both = dot(pair[...], high[...], NT)
    rest = dot(pair[:width], low[...], NT)
    for here in blocks(width, 32):
        out[here] = both[here] + (both[shift(here, width)] + rest[here])


def input_kernel(
    x_hbm,
    weight_hbm,
    t_hbm,
    next_weight_hbm,
    crops_hbm,
    out_hbm,
    out_last,
    pair_hbm,
    next_rows,
    next_pair,
    crops,
    x,
    out,
    weight,
    next_weight,
    pair,
    high,
    low,
    in_sems,
    out_sems,
    sems,
):
    width = weight.shape[0]
    chunks = chunk_rows(x.shape[0])
    fetch = pltpu.make_async_copy(weight_hbm, weight, sems.at[0])
    keep = pltpu.make_async_copy(pair, pair_hbm, sems.at[1])
    fetch_next = pltpu.make_async_copy(next_weight_hbm, next_weight, sems.at[2])
    fetch_rows = pltpu.make_async_copy(t_hbm.at[: next_rows.shape[0]], next_rows, sems.at[3])
    fetch_crops = pltpu.make_async_copy(crops_hbm, crops, sems.at[4])
    loads = [
        pltpu.make_async_copy(x_hbm.at[here], x.at[here], in_sems.at[i]) for i, here in enumerate(chunks)
    ]
    stores = [
        pltpu.make_async_copy(out.at[:, here], out_hbm.at[:, here], out_sems.at[i])
        for i, here in enumerate(chunks[:-1])
    ]
    for copy in [fetch] + loads:
        copy.start()
    for i, here in enumerate(chunks):
        loads[i].wait()
        if i == 0:
            fetch.wait()
            pair[:width], pair[width:] = split(weight[...])
            keep.start()
            fetch_next.start()
        if i == 1:
            fetch_rows.start()
            fetch_crops.start()
        if i == len(chunks) - 1:
            fetch_next.wait()
            next_pair[:width], next_pair[width:] = split(next_weight[...])
        target = out.at[:, here] if i < len(stores) else out_last
        wide_product(pair, x.at[here], high, low, target)
        if i < len(stores):
            stores[i].start()
    for copy in [keep, fetch_rows, fetch_crops] + stores:
        copy.wait()


def target_kernel(
    t_hbm,
    cwgt_hbm,
    xwgt_hbm,
    rows,
    pair,
    before_last,
    out_hbm,
    before_hbm,
    out_last,
    coarses,
    projects,
    t,
    out,
    high,
    low,
    cwgt,
    xwgt,
    in_sems,
    out_sems,
    sems,
):
    chunks = chunk_rows(t.shape[0])
    fetches = [
        pltpu.make_async_copy(cwgt_hbm, cwgt, sems.at[0]),
        pltpu.make_async_copy(xwgt_hbm, xwgt, sems.at[1]),
    ]
    loads = [
        pltpu.make_async_copy(t_hbm.at[here], t.at[here], in_sems.at[i])
        for i, here in enumerate(chunks[1:])
    ]
    stores = [
        pltpu.make_async_copy(out.at[:, here], out_hbm.at[:, here], out_sems.at[i])
        for i, here in enumerate(chunks[:-1])
    ]
    keep = pltpu.make_async_copy(before_last, before_hbm, sems.at[2])
    for copy in loads + fetches:
        copy.start()
    for i, here in enumerate(chunks):
        if i > 0:
            loads[i - 1].wait()
        if i == 2:
            keep.start()
        source = rows if i == 0 else t.at[here]
        if i < len(stores):
            wide_product(pair, source, high, low, out.at[:, here])
            stores[i].start()
        else:
            wide_product(pair, source, high, low, out_last)
    for copy in fetches:
        copy.wait()
    coarses[...] = jnp.concatenate(split(cwgt[...]), axis=0)
    projects[...] = jnp.concatenate(split(xwgt[...]), axis=0)
    for copy in stores + [keep]:
        copy.wait()


def chunk_rows(count):
    return [slice(start, start + ROWS) for start in range(0, count, ROWS)]


def prepare_kernel(patches, pair, crops_ref, before_ref, grams, wanted, lay, number):
    del before_ref
    width = grams.shape[0]
    both = dot(pair[...], pair[:width], NT)
    grams[...] = side_by_side(both[:width] + (both[width:] + both[width:].T))
    wanted[...] = slot_row(crops_ref, patches, wanted.shape[1] // patches)
    frame = row_value(crops_ref, 0, patches, (1, patches * 16), 1, 16)
    slot = lax.broadcasted_iota(jnp.int32, (1, patches * 16), 1) % 16
    line = lax.broadcasted_iota(jnp.int32, lay.shape, 0)
    lay[...] = jnp.where(line == frame * 16 + slot, 1.0, 0.0).astype(BF16)
    slot = lax.broadcasted_iota(jnp.int32, number.shape, 0) % 16
    top = row_value(crops_ref, 1, patches, number.shape, 0, 16)
    left = row_value(crops_ref, 2, patches, number.shape, 0, 16)
    number[...] = ((top + slot // 4) * SIDE + left + slot % 4).astype(F32)


def stack_kernel(*refs):
    *block_refs, _, out_ref = refs
    size = block_refs[0].shape[0]
    for k, ref in enumerate(block_refs):
        out_ref[k * size : (k + 1) * size] = ref[...]


def pack_kernel(*refs):
    *block_refs, _, out_ref = refs
    tokens = block_refs[0].shape[1]
    size = tokens * 3 // 2
    for k, ref in enumerate(block_refs):
        out_ref[k * size : k * size + tokens] = ref[0, :, :128]
        tails = [ref[0, : tokens // 2, 128:], ref[0, tokens // 2 :, 128:]]
        out_ref[k * size + tokens : (k + 1) * size] = jnp.concatenate(tails, axis=1)


def row_value(crops_ref, column, patches, shape, axis, each):
    index = lax.broadcasted_iota(jnp.int32, shape, axis) // each
    found = jnp.zeros(shape, jnp.int32)
    for j in range(patches):
        found = jnp.where(index == j, crops_ref[column, j], found)
    return found


def slot_row(crops_ref, patches, tokens):
    scale = row_value(crops_ref, 3, patches, (1, patches * tokens), 1, tokens)
    token = lax.broadcasted_iota(jnp.int32, (1, patches * tokens), 1)
    row, column = (token % tokens) // 16, token % 16
    return token // tokens * 16 + (row * scale // 8) * 4 + column * scale // 8


def taking(wanted, slots, first):
    slot = lax.broadcasted_iota(jnp.int32, (slots, wanted.shape[1]), 0) + first
    return jnp.where(slot == wanted, 1.0, 0.0).astype(BF16)


def context_kernel(
    patches,
    peers,
    crops_vmem,
    own_ref,
    other_ref,
    coarses,
    projects,
    xw_hbm,
    tw_hbm,
    projected_ref,
    slope_ref,
    xw_first,
    tw_first,
    rows,
    crops_ref,
    sems,
):
    fetches = [
        pltpu.make_async_copy(xw_hbm.at[:, : xw_first.shape[1]], xw_first, sems.at[0]),
        pltpu.make_async_copy(tw_hbm.at[:, : tw_first.shape[1]], tw_first, sems.at[1]),
    ]
    for copy in fetches:
        copy.start()
    take = pltpu.make_async_copy(crops_vmem, crops_ref, sems.at[2])
    take.start()
    take.wait()
    pixels = coarses.shape[0] // 2
    width = projects.shape[1]
    far = peers // 4
    me, side = lax.axis_index(("far", "y", "core")), lax.axis_index("lvl")
    for j in range(patches):
        frame, top, left = crops_ref[0, j], crops_ref[1, j], crops_ref[2, j]
        near_by = lax.bitwise_xor(frame % 4, me % 4)
        k = (me // 4 - frame // 4 + far) % far
        k = jnp.where(k == 1, 2, jnp.where(k == 2, 3, jnp.where(k == 3, 1, k)))
        here = near_by % 2 == 0
        for a in range(4):
            row = jnp.minimum(top + a, SIDE - 1)
            shard = (lax.bitwise_xor(row // 4, side) * 2 + near_by // 2) * far + k
            row = row % 4
            start = shard * (6 * SIDE)
            wide = pl.ds(pl.multiple_of(start + row * SIDE, SIDE), SIDE)
            tail = pl.ds(pl.multiple_of(start + (4 + row % 2) * SIDE, SIDE), SIDE)
            into = slice(j * 16 + a * 4, j * 16 + a * 4 + 4)
            line = jnp.where(here, own_ref[wide, :], other_ref[wide, :])
            rows[into, :128] = pltpu.roll(line, SIDE - left, 0)[:4, :]
            line = pltpu.roll(jnp.where(here, own_ref[tail, :], other_ref[tail, :]), SIDE - left, 0)[:4, :]
            rows[into, 128:] = jnp.where(row >= 2, line[:, 64:], line[:, :64])
    pre = through(rows[...], coarses, NN)
    gate = sigmoid(pre)
    slope_ref[...] = gate * (1.0 + pre * (1.0 - gate))
    projected = through(pre * gate, projects, NN).T
    projected_ref[...] = jnp.concatenate(split(projected), axis=1)
    for copy in fetches:
        copy.wait()


def middle_kernel(
    projected,
    grams,
    wanted,
    xw_first,
    tw_first,
    tw_last,
    xw_hbm,
    xw_last,
    tw_hbm,
    pair_hbm,
    de_hbm,
    de_ref,
    deep_ref,
    dslot_ref,
    xw,
    tw,
    taken,
    factor,
    deep,
    parts,
    xw_sems,
    tw_sems,
    out_sems,
    sems,
):
    width, count = xw.shape
    slots = dslot_ref.shape[0]
    chunks = chunk_rows(count)
    each = slots // len(chunks)
    tw_loads = [
        pltpu.make_async_copy(tw_hbm.at[:, here], tw.at[:, here], tw_sems.at[i])
        for i, here in enumerate(chunks[1:-1])
    ]
    xw_loads = [
        pltpu.make_async_copy(xw_hbm.at[:, here], xw.at[:, here], xw_sems.at[i])
        for i, here in enumerate(chunks[2:-1])
    ]
    xw_loads.append(pltpu.make_async_copy(xw_last, xw.at[:, chunks[-1]], xw_sems.at[len(xw_loads)]))
    stores = [
        pltpu.make_async_copy(xw.at[:, here], de_hbm.at[:, here], out_sems.at[i])
        for i, here in enumerate(chunks[:-1])
    ]
    fetches = [
        pltpu.make_async_copy(pair_hbm, deep_ref.at[: 2 * width], sems.at[0]),
        pltpu.make_async_copy(pair_hbm.at[:width], deep_ref.at[2 * width :], sems.at[1]),
    ]
    for pair in zip(tw_loads, xw_loads):
        for copy in pair:
            copy.start()
    for copy in fetches:
        copy.start()

    def begin(i):
        tokens = chunks[i]
        source = xw_first.at[:, tokens] if i < 2 else xw.at[:, tokens]
        here = taking(wanted[:, tokens], slots, 0)
        taken[:slots], taken[slots:] = here, here
        spread = dot(projected[...], taken[...])
        for here in blocks(width, 32):
            pre = source[here] + spread[here]
            gate = sigmoid(pre)
            hidden = pre * gate
            factor[i % 2, here] = gate + hidden * (1.0 - gate)
            high, low = split(hidden)
            for part, value in enumerate((high, high, low)):
                deep[i % 2, shift(here, part * width)] = value

    begin(0)
    for i, tokens in enumerate(chunks):
        if 0 < i < len(chunks) - 1:
            tw_loads[i - 1].wait()
            xw_loads[i - 1].wait()
        minus = tw_first if i == 0 else tw_last if i == len(chunks) - 1 else tw.at[:, tokens]
        target = de_ref if i == len(chunks) - 1 else xw.at[:, tokens]
        product = dot(grams[...], deep[i % 2])
        if i + 1 < len(chunks):
            begin(i + 1)
        for here in blocks(width, 32):
            de = (product[here] - minus[here]) * factor[i % 2, here]
            target[here] = de
            parts[here], parts[shift(here, width)] = split(de)
        mine = slice(i * each, (i + 1) * each)
        both = dot(taking(wanted[:, tokens], each, i * each), parts[...], NT)
        dslot_ref[mine] = both[:, :width] + both[:, width:]
        if i < len(stores):
            stores[i].start()
    for copy in stores + fetches:
        copy.wait()


def through(value, pair, dims):
    count, rows = value.shape[0], pair.shape[0] // 2
    high, low = split(value)
    both = dot(jnp.concatenate([high, low], axis=0), pair[:rows], dims)
    return both[:count] + (both[count:] + dot(high, pair[rows:], dims))


def back_through(value, pair):
    count, rows = value.shape[0], pair.shape[0] // 2
    both = dot(jnp.concatenate(split(value), axis=0), pair[...], NT)
    return both[:count, :rows] + (both[count:, :rows] + both[:count, rows:])


def closing_kernel(dslot_ref, slope_ref, coarses, projects, lay, number, send_ref):
    grad = back_through(back_through(dslot_ref[...], projects) * slope_ref[...], coarses)
    parts = jnp.concatenate(split(jnp.concatenate([grad, number[...]], axis=1)), axis=1)
    both = dot(lay[...], parts)
    send_ref[...] = both[:, :LANES] + both[:, LANES:]


def scatter_kernel(message_ref, done_ref, mine_ref, other_ref, total):
    del done_ref
    pixels = mine_ref.shape[2]
    message = message_ref[...]
    number = lax.broadcasted_iota(jnp.int32, (message.shape[0], SIDE * SIDE), 1).astype(F32)
    pick = jnp.where(message[:, pixels : pixels + 1] == number, 1.0, 0.0).astype(BF16)
    high, low = split(message[:, :pixels])
    total[...] = dot(pick, low, TN) + dot(pick, high, TN)
    half = mine_ref.shape[1]
    side = lax.axis_index("lvl")
    mine_ref[0] = total[pl.ds(pl.multiple_of(side * half, half), half), :]
    other_ref[0] = total[pl.ds(pl.multiple_of((1 - side) * half, half), half), :]


def last_kernel(de_hbm, first, deep, out_hbm, de, out, cat, in_sems, out_sems):
    width = de.shape[0]
    steps = de.shape[1] // ROWS

    def load(i):
        return pltpu.make_async_copy(de_hbm.at[:, chunk(i)], de.at[:, chunk(i)], in_sems.at[i])

    def store(i):
        return pltpu.make_async_copy(out.at[chunk(i)], out_hbm.at[chunk(i)], out_sems.at[i])

    def prepare(source):
        for here in blocks(width, 32):
            high, low = split(source[here])
            cat[here], cat[shift(here, width)], cat[shift(here, 2 * width)] = high, high, low

    for i in range(steps - 1):
        load(i).start()
    prepare(first)

    def step(i, _):
        mine = lax.rem(i + steps - 1, steps)
        out[chunk(mine), :] = dot(cat[...], deep[...], TN)
        store(mine).start()

        @pl.when(i + 1 < steps)
        def _():
            load(i).wait()
            prepare(de.at[:, chunk(i)])

        return 0

    lax.fori_loop(0, steps, step, 0)
    for i in range(steps):
        store(i).wait()


def fixed(*values):
    return [pltpu.with_memory_space_constraint(value, pltpu.HBM) for value in values]


def near(*values):
    return [pltpu.with_memory_space_constraint(value, pltpu.VMEM) for value in values]


def stack(kernel, blocks, before, rows):
    shape = (len(blocks) * rows, 128)
    return call(
        kernel,
        "stack",
        1000,
        jax.ShapeDtypeStruct(shape, F32),
        limit=ROOM,
        in_specs=[VMEM] * len(blocks) + [HBM],
        out_specs=VMEM,
    )(*blocks, *fixed(before))


def body(coarse_input, coarse_weight, fine_input, fine_target, crops, in_weight, context_weight, out_weight):
    patch = ("far", "y", "core")
    peers = lax.axis_size(patch)
    far = peers // 4
    patches, tokens, values = fine_input.shape
    width = in_weight.shape[1]
    pixels = coarse_weight.shape[0]
    half = coarse_input.shape[1]
    count = patches * tokens
    swap = [(0, 1), (1, 0)]

    column = {0: coarse_input}
    for k in range(1, far):
        column[k] = lax.ppermute(coarse_input, "far", [(p, (p + k) % far) for p in range(far)])
    column = [column[k] for k in [0, 3, 1, 2] + list(range(4, far))]

    steps = count // ROWS
    pair_shape = (2 * width, values)
    x, t = fine_input.reshape(count, values), fine_target.reshape(count, values)
    xw, xw_last, pair, rows, next_pair, crops = call(
        input_kernel,
        "input",
        6 * count * values * width,
        (
            pltpu.HBM((width, count - ROWS), F32),
            pltpu.VMEM((width, ROWS), F32),
            pltpu.HBM(pair_shape, BF16),
            pltpu.VMEM((ROWS, values), F32),
            pltpu.VMEM(pair_shape, BF16),
            pltpu.VMEM((4, patches), jnp.int32),
        ),
        in_specs=[HBM] * 5,
        out_specs=(HBM, VMEM, HBM, VMEM, VMEM, VMEM),
        scratch_shapes=[
            pltpu.VMEM((count, values), F32),
            pltpu.VMEM((width, count), F32),
            pltpu.VMEM((width, values), F32),
            pltpu.VMEM((width, values), F32),
            pltpu.VMEM(pair_shape, BF16),
            pltpu.VMEM((ROWS, values), BF16),
            pltpu.VMEM((ROWS, values), BF16),
            pltpu.SemaphoreType.DMA((steps,)),
            pltpu.SemaphoreType.DMA((steps,)),
            pltpu.SemaphoreType.DMA((5,)),
        ],
    )(*fixed(x, in_weight.T, t, out_weight, crops.T))
    column = stack(pack_kernel, column, xw, half * 3 // 2)
    own = [column]
    for flip in range(1, 4):
        own.append(lax.ppermute(column, ("lvl", "y"), [(p, p ^ flip) for p in range(4)]))
    tw, xw_last, tw_last, coarses, projects = call(
        target_kernel,
        "target",
        6 * count * values * width,
        (
            pltpu.HBM((width, count - ROWS), F32),
            pltpu.HBM((width, ROWS), F32),
            pltpu.VMEM((width, ROWS), F32),
            pltpu.VMEM((2 * pixels, width), BF16),
            pltpu.VMEM((2 * width, width), BF16),
        ),
        limit=ROOM,
        in_specs=[HBM] * 3 + [VMEM] * 3,
        out_specs=(HBM, HBM, VMEM, VMEM, VMEM),
        scratch_shapes=[
            pltpu.VMEM((count, values), F32),
            pltpu.VMEM((width, count), F32),
            pltpu.VMEM((ROWS, values), BF16),
            pltpu.VMEM((ROWS, values), BF16),
            pltpu.VMEM((pixels, width), F32),
            pltpu.VMEM((width, width), F32),
            pltpu.SemaphoreType.DMA((steps,)),
            pltpu.SemaphoreType.DMA((steps,)),
            pltpu.SemaphoreType.DMA((3,)),
        ],
    )(*fixed(t, coarse_weight, context_weight), *near(rows, next_pair, xw_last))
    own = stack(stack_kernel, own, tw, column.shape[0])
    other = lax.ppermute(own, "core", swap)
    (crops,) = near(crops)
    grams, wanted, lay, number = call(
        functools.partial(prepare_kernel, patches),
        "prepare",
        8 * values * width * width,
        (
            pltpu.VMEM((width, 3 * width), BF16),
            pltpu.VMEM((1, count), jnp.int32),
            pltpu.VMEM((peers * 16, patches * 16), BF16),
            pltpu.VMEM((patches * 16, LANES - pixels), F32),
        ),
        limit=ROOM,
        in_specs=[VMEM, SMEM, HBM],
        out_specs=(VMEM,) * 4,
    )(*near(next_pair), crops, own)

    projected, slope, xw_first, tw_first = call(
        functools.partial(context_kernel, patches, peers),
        "context",
        6 * patches * 16 * width * width,
        (
            pltpu.VMEM((width, 2 * patches * 16), BF16),
            pltpu.VMEM((patches * 16, width), F32),
            pltpu.VMEM((width, 2 * ROWS), F32),
            pltpu.VMEM((width, ROWS), F32),
        ),
        limit=ROOM,
        in_specs=[VMEM] * 5 + [HBM] * 2,
        out_specs=(VMEM,) * 4,
        scratch_shapes=[
            pltpu.VMEM((patches * 16, pixels), F32),
            pltpu.SMEM((4, patches), jnp.int32),
            pltpu.SemaphoreType.DMA((3,)),
        ],
    )(crops, own, other, *near(coarses, projects), *fixed(xw, tw))
    de, last_de, deep, dslot = call(
        middle_kernel,
        "middle",
        6 * count * width * width,
        (
            pltpu.HBM((width, count), F32),
            pltpu.VMEM((width, ROWS), F32),
            pltpu.VMEM((3 * width, values), BF16),
            pltpu.VMEM((patches * 16, width), F32),
        ),
        limit=ROOM,
        in_specs=[VMEM] * 6 + [HBM] * 4,
        out_specs=(HBM,) + (VMEM,) * 3,
        scratch_shapes=[
            pltpu.VMEM((width, count), F32),
            pltpu.VMEM((width, count), F32),
            pltpu.VMEM((2 * patches * 16, ROWS), BF16),
            pltpu.VMEM((2, width, ROWS), F32),
            pltpu.VMEM((2, 3 * width, ROWS), BF16),
            pltpu.VMEM((2 * width, ROWS), BF16),
            pltpu.SemaphoreType.DMA((steps,)),
            pltpu.SemaphoreType.DMA((steps,)),
            pltpu.SemaphoreType.DMA((steps,)),
            pltpu.SemaphoreType.DMA((2,)),
        ],
    )(*near(projected, grams, wanted, xw_first, tw_first, tw_last), *fixed(xw, xw_last, tw, pair))
    back = call(
        closing_kernel,
        "closing",
        6 * patches * 16 * width * width,
        pltpu.VMEM((peers * 16, LANES), F32),
        limit=ROOM,
        in_specs=[VMEM] * 6,
        out_specs=VMEM,
    )(*near(dslot, slope, coarses, projects, lay, number))
    returned = lax.all_to_all(back, patch, 0, 0, tiled=True)

    fine_grad = call(
        last_kernel,
        "last",
        6 * count * values * width,
        pltpu.HBM((count, values), F32),
        limit=ROOM,
        in_specs=[HBM, VMEM, VMEM],
        out_specs=HBM,
        scratch_shapes=[
            pltpu.VMEM((width, count), F32),
            pltpu.VMEM((count, values), F32),
            pltpu.VMEM((3 * width, ROWS), BF16),
            pltpu.SemaphoreType.DMA((steps,)),
            pltpu.SemaphoreType.DMA((steps,)),
        ],
    )(*fixed(de), *near(last_de, deep))
    part = (1, half, pixels)
    mine, theirs = call(
        scatter_kernel,
        "scatter",
        10000,
        (jax.ShapeDtypeStruct(part, F32), jax.ShapeDtypeStruct(part, F32)),
        limit=ROOM,
        in_specs=[VMEM, HBM],
        out_specs=(VMEM, VMEM),
        scratch_shapes=[pltpu.VMEM((SIDE * SIDE, pixels), F32)],
    )(returned, *fixed(fine_grad))
    coarse_grad = mine + lax.ppermute(theirs, "lvl", swap)
    return (coarse_grad, fine_grad.reshape(fine_input.shape))


def solution(mesh):
    sides, peers = mesh.shape["lvl"], mesh.shape["patch"]
    fine = jax.sharding.Mesh(mesh.devices.reshape(sides, peers // 4, 2, 2), ("lvl", "far", "y", "core"))
    patch = ("far", "y", "core")
    both = ("lvl",) + patch
    in_specs = (
        P(patch, "lvl", None),
        P(),
        P(both, None, None),
        P(both, None, None),
        P(both, None),
        P(),
        P(),
        P(),
    )
    out_specs = (P(patch, "lvl", None), P(both, None, None))
    return jax.shard_map(body, mesh=fine, in_specs=in_specs, out_specs=out_specs, check_vma=False)
```

```python
import functools
import math

import jax
import jax.numpy as jnp
from jax import lax
from jax.experimental import pallas as pl
from jax.experimental.pallas import tpu as pltpu
from jax.sharding import PartitionSpec as P

F32 = jnp.float32
BF16 = jnp.bfloat16
NN = (((1,), (0,)), ((), ()))
NT = (((1,), (1,)), ((), ()))
TN = (((0,), (0,)), ((), ()))
ROWS = 512
SIDE = 8
LANES = 256
LIMIT = 60 * 1024 * 1024
ROOM = 40 * 1024 * 1024
SMEM = pl.BlockSpec(memory_space=pltpu.SMEM)
VMEM = pl.BlockSpec(memory_space=pltpu.VMEM)
HBM = pl.BlockSpec(memory_space=pltpu.HBM)


def split(value):
    high = value.astype(BF16)
    low = (value - high.astype(F32)).astype(BF16)
    return high, low


def dot(left, right, dims=NN):
    return lax.dot_general(left, right, dims, preferred_element_type=F32)


def dot3(left, right, dims=NN):
    return (
        dot(left[0], right[1], dims) + dot(left[1], right[0], dims) + dot(left[0], right[0], dims)
    )


def side_by_side(value):
    high, low = split(value)
    return jnp.concatenate([high, low, high], axis=1)


def sigmoid(value):
    return 0.5 * jnp.tanh(0.5 * value) + 0.5


def call(kernel, name, flops, out_shape, limit=LIMIT, **kwargs):
    moved = 8 * sum(math.prod(s.shape) for s in jax.tree.leaves(out_shape))
    return pl.pallas_call(
        kernel,
        out_shape=out_shape,
        name=name,
        cost_estimate=pl.CostEstimate(flops=flops, bytes_accessed=moved, transcendentals=0),
        compiler_params=pltpu.CompilerParams(vmem_limit_bytes=limit),
        **kwargs,
    )


def blocks(rows, size):
    return [slice(start, start + size) for start in range(0, rows, size)]


def shift(here, by):
    return slice(here.start + by, here.stop + by)


def pair_product(pair, value, dims):
    rows = pair.shape[0] // 2
    high, low = split(value)
    both = dot(pair[...], high, dims)
    return both[:rows] + (both[rows:] + dot(pair[:rows], low, dims))


def chunk(i):
    return pl.ds(pl.multiple_of(i * ROWS, ROWS), ROWS)


def wide_product(pair, value, high, low, out):
    width = pair.shape[0] // 2
    for here in blocks(high.shape[0], 16):
        high[here], low[here] = split(value[here])
    both = dot(pair[...], high[...], NT)
    rest = dot(pair[:width], low[...], NT)
    for here in blocks(width, 32):
        out[here] = both[here] + (both[shift(here, width)] + rest[here])


def input_kernel(
    x_hbm,
    weight_hbm,
    t_hbm,
    next_weight_hbm,
    crops_hbm,
    out_hbm,
    out_last,
    pair_hbm,
    next_rows,
    next_pair,
    crops,
    x,
    out,
    weight,
    next_weight,
    pair,
    high,
    low,
    in_sems,
    out_sems,
    sems,
):
    width = weight.shape[0]
    chunks = chunk_rows(x.shape[0])
    fetch = pltpu.make_async_copy(weight_hbm, weight, sems.at[0])
    keep = pltpu.make_async_copy(pair, pair_hbm, sems.at[1])
    fetch_next = pltpu.make_async_copy(next_weight_hbm, next_weight, sems.at[2])
    fetch_rows = pltpu.make_async_copy(t_hbm.at[: next_rows.shape[0]], next_rows, sems.at[3])
    fetch_crops = pltpu.make_async_copy(crops_hbm, crops, sems.at[4])
    loads = [
        pltpu.make_async_copy(x_hbm.at[here], x.at[here], in_sems.at[i]) for i, here in enumerate(chunks)
    ]
    stores = [
        pltpu.make_async_copy(out.at[:, here], out_hbm.at[:, here], out_sems.at[i])
        for i, here in enumerate(chunks[:-1])
    ]
    for copy in [fetch] + loads[:2]:
        copy.start()
    for i, here in enumerate(chunks):
        loads[i].wait()
        if i + 2 < len(chunks):
            loads[i + 2].start()
        if i == 0:
            fetch.wait()
            pair[:width], pair[width:] = split(weight[...])
            keep.start()
            fetch_next.start()
        if i == 1:
            fetch_rows.start()
            fetch_crops.start()
        if i == len(chunks) - 1:
            fetch_next.wait()
            next_pair[:width], next_pair[width:] = split(next_weight[...])
        target = out.at[:, here] if i < len(stores) else out_last
        wide_product(pair, x.at[here], high, low, target)
        if i < len(stores):
            stores[i].start()
    for copy in [keep, fetch_rows, fetch_crops] + stores:
        copy.wait()


def target_kernel(
    t_hbm,
    cwgt_hbm,
    xwgt_hbm,
    rows,
    pair,
    before_last,
    out_hbm,
    before_hbm,
    out_last,
    coarses,
    projects,
    t,
    out,
    high,
    low,
    cwgt,
    xwgt,
    in_sems,
    out_sems,
    sems,
):
    chunks = chunk_rows(t.shape[0])
    fetches = [
        pltpu.make_async_copy(cwgt_hbm, cwgt, sems.at[0]),
        pltpu.make_async_copy(xwgt_hbm, xwgt, sems.at[1]),
    ]
    loads = [
        pltpu.make_async_copy(t_hbm.at[here], t.at[here], in_sems.at[i])
        for i, here in enumerate(chunks[1:])
    ]
    stores = [
        pltpu.make_async_copy(out.at[:, here], out_hbm.at[:, here], out_sems.at[i])
        for i, here in enumerate(chunks[:-1])
    ]
    keep = pltpu.make_async_copy(before_last, before_hbm, sems.at[2])
    for copy in loads[:2]:
        copy.start()
    for i, here in enumerate(chunks):
        if i > 0:
            loads[i - 1].wait()
        if i == 1:
            for copy in loads[2:] + fetches:
                copy.start()
        if i == 2:
            keep.start()
        source = rows if i == 0 else t.at[here]
        if i < len(stores):
            wide_product(pair, source, high, low, out.at[:, here])
            stores[i].start()
        else:
            wide_product(pair, source, high, low, out_last)
    for copy in fetches:
        copy.wait()
    coarses[...] = jnp.concatenate(split(cwgt[...]), axis=0)
    projects[...] = jnp.concatenate(split(xwgt[...]), axis=0)
    for copy in stores + [keep]:
        copy.wait()


def chunk_rows(count):
    return [slice(start, start + ROWS) for start in range(0, count, ROWS)]


def prepare_kernel(patches, pair, crops_ref, before_ref, grams, wanted, lay, number):
    del before_ref
    width = grams.shape[0]
    both = dot(pair[...], pair[:width], NT)
    grams[...] = side_by_side(both[:width] + (both[width:] + both[width:].T))
    wanted[...] = slot_row(crops_ref, patches, wanted.shape[1] // patches)
    frame = row_value(crops_ref, 0, patches, (1, patches * 16), 1, 16)
    slot = lax.broadcasted_iota(jnp.int32, (1, patches * 16), 1) % 16
    line = lax.broadcasted_iota(jnp.int32, lay.shape, 0)
    lay[...] = jnp.where(line == frame * 16 + slot, 1.0, 0.0).astype(BF16)
    slot = lax.broadcasted_iota(jnp.int32, number.shape, 0) % 16
    top = row_value(crops_ref, 1, patches, number.shape, 0, 16)
    left = row_value(crops_ref, 2, patches, number.shape, 0, 16)
    number[...] = ((top + slot // 4) * SIDE + left + slot % 4).astype(F32)


def stack_kernel(*refs):
    *block_refs, _, out_ref = refs
    size = block_refs[0].shape[0]
    for k, ref in enumerate(block_refs):
        out_ref[k * size : (k + 1) * size] = ref[...]


def pack_kernel(*refs):
    *block_refs, _, out_ref = refs
    tokens = block_refs[0].shape[1]
    size = tokens * 3 // 2
    for k, ref in enumerate(block_refs):
        out_ref[k * size : k * size + tokens] = ref[0, :, :128]
        tails = [ref[0, : tokens // 2, 128:], ref[0, tokens // 2 :, 128:]]
        out_ref[k * size + tokens : (k + 1) * size] = jnp.concatenate(tails, axis=1)


def row_value(crops_ref, column, patches, shape, axis, each):
    index = lax.broadcasted_iota(jnp.int32, shape, axis) // each
    found = jnp.zeros(shape, jnp.int32)
    for j in range(patches):
        found = jnp.where(index == j, crops_ref[column, j], found)
    return found


def slot_row(crops_ref, patches, tokens):
    scale = row_value(crops_ref, 3, patches, (1, patches * tokens), 1, tokens)
    token = lax.broadcasted_iota(jnp.int32, (1, patches * tokens), 1)
    row, column = (token % tokens) // 16, token % 16
    return token // tokens * 16 + (row * scale // 8) * 4 + column * scale // 8


def taking(wanted, slots, first):
    slot = lax.broadcasted_iota(jnp.int32, (slots, wanted.shape[1]), 0) + first
    return jnp.where(slot == wanted, 1.0, 0.0).astype(BF16)


def context_kernel(
    patches,
    peers,
    crops_vmem,
    own_ref,
    other_ref,
    coarses,
    projects,
    xw_hbm,
    tw_hbm,
    projected_ref,
    slope_ref,
    xw_first,
    tw_first,
    rows,
    crops_ref,
    sems,
):
    fetches = [
        pltpu.make_async_copy(xw_hbm.at[:, : xw_first.shape[1]], xw_first, sems.at[0]),
        pltpu.make_async_copy(tw_hbm.at[:, : tw_first.shape[1]], tw_first, sems.at[1]),
    ]
    for copy in fetches:
        copy.start()
    take = pltpu.make_async_copy(crops_vmem, crops_ref, sems.at[2])
    take.start()
    take.wait()
    pixels = coarses.shape[0] // 2
    width = projects.shape[1]
    far = peers // 4
    me, side = lax.axis_index(("far", "y", "core")), lax.axis_index("lvl")
    for j in range(patches):
        frame, top, left = crops_ref[0, j], crops_ref[1, j], crops_ref[2, j]
        near_by = lax.bitwise_xor(frame % 4, me % 4)
        k = (me // 4 - frame // 4 + far) % far
        k = jnp.where(k == 1, 2, jnp.where(k == 2, 3, jnp.where(k == 3, 1, k)))
        here = near_by % 2 == 0
        for a in range(4):
            row = jnp.minimum(top + a, SIDE - 1)
            code = lax.bitwise_xor(row // 4, side) * 2 + near_by // 2
            shard = jnp.where(code == 0, 0, 4 - code) * far + k
            row = row % 4
            start = shard * (6 * SIDE)
            wide = pl.ds(pl.multiple_of(start + row * SIDE, SIDE), SIDE)
            tail = pl.ds(pl.multiple_of(start + (4 + row % 2) * SIDE, SIDE), SIDE)
            into = slice(j * 16 + a * 4, j * 16 + a * 4 + 4)
            line = jnp.where(here, own_ref[wide, :], other_ref[wide, :])
            rows[into, :128] = pltpu.roll(line, SIDE - left, 0)[:4, :]
            line = pltpu.roll(jnp.where(here, own_ref[tail, :], other_ref[tail, :]), SIDE - left, 0)[:4, :]
            rows[into, 128:] = jnp.where(row >= 2, line[:, 64:], line[:, :64])
    pre = through(rows[...], coarses, NN)
    gate = sigmoid(pre)
    slope_ref[...] = gate * (1.0 + pre * (1.0 - gate))
    projected = through(pre * gate, projects, NN).T
    projected_ref[...] = jnp.concatenate(split(projected), axis=1)
    for copy in fetches:
        copy.wait()


def middle_kernel(
    projected,
    grams,
    wanted,
    xw_first,
    tw_first,
    tw_last,
    xw_hbm,
    xw_last,
    tw_hbm,
    pair_hbm,
    de_hbm,
    de_ref,
    deep_ref,
    dslot_ref,
    xw,
    tw,
    taken,
    factor,
    deep,
    parts,
    xw_sems,
    tw_sems,
    out_sems,
    sems,
):
    width, count = xw.shape
    slots = dslot_ref.shape[0]
    chunks = chunk_rows(count)
    each = slots // len(chunks)
    tw_loads = [
        pltpu.make_async_copy(tw_hbm.at[:, here], tw.at[:, here], tw_sems.at[i])
        for i, here in enumerate(chunks[1:-1])
    ]
    xw_loads = [
        pltpu.make_async_copy(xw_hbm.at[:, here], xw.at[:, here], xw_sems.at[i])
        for i, here in enumerate(chunks[2:-1])
    ]
    xw_loads.append(pltpu.make_async_copy(xw_last, xw.at[:, chunks[-1]], xw_sems.at[len(xw_loads)]))
    stores = [
        pltpu.make_async_copy(xw.at[:, here], de_hbm.at[:, here], out_sems.at[i])
        for i, here in enumerate(chunks[:-1])
    ]
    fetches = [
        pltpu.make_async_copy(pair_hbm, deep_ref.at[: 2 * width], sems.at[0]),
        pltpu.make_async_copy(pair_hbm.at[:width], deep_ref.at[2 * width :], sems.at[1]),
    ]
    for pair in zip(tw_loads, xw_loads):
        for copy in pair:
            copy.start()
    for copy in fetches:
        copy.start()

    def begin(i):
        tokens = chunks[i]
        source = xw_first.at[:, tokens] if i < 2 else xw.at[:, tokens]
        here = taking(wanted[:, tokens], slots, 0)
        taken[:slots], taken[slots:] = here, here
        spread = dot(projected[...], taken[...])
        for here in blocks(width, 32):
            pre = source[here] + spread[here]
            gate = sigmoid(pre)
            hidden = pre * gate
            factor[i % 2, here] = gate + hidden * (1.0 - gate)
            high, low = split(hidden)
            for part, value in enumerate((high, high, low)):
                deep[i % 2, shift(here, part * width)] = value

    begin(0)
    for i, tokens in enumerate(chunks):
        if 0 < i < len(chunks) - 1:
            tw_loads[i - 1].wait()
            xw_loads[i - 1].wait()
        minus = tw_first if i == 0 else tw_last if i == len(chunks) - 1 else tw.at[:, tokens]
        target = de_ref if i == len(chunks) - 1 else xw.at[:, tokens]
        product = dot(grams[...], deep[i % 2])
        if i + 1 < len(chunks):
            begin(i + 1)
        for here in blocks(width, 32):
            de = (product[here] - minus[here]) * factor[i % 2, here]
            target[here] = de
            parts[here], parts[shift(here, width)] = split(de)
        mine = slice(i * each, (i + 1) * each)
        both = dot(taking(wanted[:, tokens], each, i * each), parts[...], NT)
        dslot_ref[mine] = both[:, :width] + both[:, width:]
        if i < len(stores):
            stores[i].start()
    for copy in stores + fetches:
        copy.wait()


def through(value, pair, dims):
    count, rows = value.shape[0], pair.shape[0] // 2
    high, low = split(value)
    both = dot(jnp.concatenate([high, low], axis=0), pair[:rows], dims)
    return both[:count] + (both[count:] + dot(high, pair[rows:], dims))


def back_through(value, pair):
    count, rows = value.shape[0], pair.shape[0] // 2
    both = dot(jnp.concatenate(split(value), axis=0), pair[...], NT)
    return both[:count, :rows] + (both[count:, :rows] + both[:count, rows:])


def closing_kernel(dslot_ref, slope_ref, coarses, projects, lay, number, send_ref):
    grad = back_through(back_through(dslot_ref[...], projects) * slope_ref[...], coarses)
    parts = jnp.concatenate(split(jnp.concatenate([grad, number[...]], axis=1)), axis=1)
    both = dot(lay[...], parts)
    send_ref[...] = both[:, :LANES] + both[:, LANES:]


def scatter_kernel(message_ref, done_ref, mine_ref, other_ref, total):
    del done_ref
    pixels = mine_ref.shape[2]
    message = message_ref[...]
    number = lax.broadcasted_iota(jnp.int32, (message.shape[0], SIDE * SIDE), 1).astype(F32)
    pick = jnp.where(message[:, pixels : pixels + 1] == number, 1.0, 0.0).astype(BF16)
    high, low = split(message[:, :pixels])
    total[...] = dot(pick, low, TN) + dot(pick, high, TN)
    half = mine_ref.shape[1]
    side = lax.axis_index("lvl")
    mine_ref[0] = total[pl.ds(pl.multiple_of(side * half, half), half), :]
    other_ref[0] = total[pl.ds(pl.multiple_of((1 - side) * half, half), half), :]


def last_kernel(de_hbm, first, deep, out_hbm, de, out, cat, in_sems, out_sems):
    width = de.shape[0]
    steps = de.shape[1] // ROWS

    def load(i):
        return pltpu.make_async_copy(de_hbm.at[:, chunk(i)], de.at[:, chunk(i)], in_sems.at[i])

    def store(i):
        return pltpu.make_async_copy(out.at[chunk(i)], out_hbm.at[chunk(i)], out_sems.at[i])

    def prepare(source):
        for here in blocks(width, 32):
            high, low = split(source[here])
            cat[here], cat[shift(here, width)], cat[shift(here, 2 * width)] = high, high, low

    for i in range(steps - 1):
        load(i).start()
    prepare(first)

    def step(i, _):
        mine = lax.rem(i + steps - 1, steps)
        out[chunk(mine), :] = dot(cat[...], deep[...], TN)
        store(mine).start()

        @pl.when(i + 1 < steps)
        def _():
            load(i).wait()
            prepare(de.at[:, chunk(i)])

        return 0

    lax.fori_loop(0, steps, step, 0)
    for i in range(steps):
        store(i).wait()


def fixed(*values):
    return [pltpu.with_memory_space_constraint(value, pltpu.HBM) for value in values]


def near(*values):
    return [pltpu.with_memory_space_constraint(value, pltpu.VMEM) for value in values]


def stack(kernel, blocks, before, rows):
    shape = (len(blocks) * rows, 128)
    return call(
        kernel,
        "stack",
        1000,
        jax.ShapeDtypeStruct(shape, F32),
        limit=ROOM,
        in_specs=[VMEM] * len(blocks) + [HBM],
        out_specs=VMEM,
    )(*blocks, *fixed(before))


def body(coarse_input, coarse_weight, fine_input, fine_target, crops, in_weight, context_weight, out_weight):
    patch = ("far", "y", "core")
    peers = lax.axis_size(patch)
    far = peers // 4
    patches, tokens, values = fine_input.shape
    width = in_weight.shape[1]
    pixels = coarse_weight.shape[0]
    half = coarse_input.shape[1]
    count = patches * tokens
    swap = [(0, 1), (1, 0)]

    column = {0: coarse_input}
    for k in range(1, far):
        column[k] = lax.ppermute(coarse_input, "far", [(p, (p + k) % far) for p in range(far)])
    column = [column[k] for k in [0, 3, 1, 2] + list(range(4, far))]

    steps = count // ROWS
    pair_shape = (2 * width, values)
    x, t = fine_input.reshape(count, values), fine_target.reshape(count, values)
    xw, xw_last, pair, rows, next_pair, crops = call(
        input_kernel,
        "input",
        6 * count * values * width,
        (
            pltpu.HBM((width, count - ROWS), F32),
            pltpu.VMEM((width, ROWS), F32),
            pltpu.HBM(pair_shape, BF16),
            pltpu.VMEM((ROWS, values), F32),
            pltpu.VMEM(pair_shape, BF16),
            pltpu.VMEM((4, patches), jnp.int32),
        ),
        in_specs=[HBM] * 5,
        out_specs=(HBM, VMEM, HBM, VMEM, VMEM, VMEM),
        scratch_shapes=[
            pltpu.VMEM((count, values), F32),
            pltpu.VMEM((width, count), F32),
            pltpu.VMEM((width, values), F32),
            pltpu.VMEM((width, values), F32),
            pltpu.VMEM(pair_shape, BF16),
            pltpu.VMEM((ROWS, values), BF16),
            pltpu.VMEM((ROWS, values), BF16),
            pltpu.SemaphoreType.DMA((steps,)),
            pltpu.SemaphoreType.DMA((steps,)),
            pltpu.SemaphoreType.DMA((5,)),
        ],
    )(*fixed(x, in_weight.T, t, out_weight, crops.T))
    column = stack(pack_kernel, column, xw, half * 3 // 2)
    own = [column]
    for flip in (3, 2, 1):
        own.append(lax.ppermute(column, ("lvl", "y"), [(p, p ^ flip) for p in range(4)]))
    tw, xw_last, tw_last, coarses, projects = call(
        target_kernel,
        "target",
        6 * count * values * width,
        (
            pltpu.HBM((width, count - ROWS), F32),
            pltpu.HBM((width, ROWS), F32),
            pltpu.VMEM((width, ROWS), F32),
            pltpu.VMEM((2 * pixels, width), BF16),
            pltpu.VMEM((2 * width, width), BF16),
        ),
        limit=ROOM,
        in_specs=[HBM] * 3 + [VMEM] * 3,
        out_specs=(HBM, HBM, VMEM, VMEM, VMEM),
        scratch_shapes=[
            pltpu.VMEM((count, values), F32),
            pltpu.VMEM((width, count), F32),
            pltpu.VMEM((ROWS, values), BF16),
            pltpu.VMEM((ROWS, values), BF16),
            pltpu.VMEM((pixels, width), F32),
            pltpu.VMEM((width, width), F32),
            pltpu.SemaphoreType.DMA((steps,)),
            pltpu.SemaphoreType.DMA((steps,)),
            pltpu.SemaphoreType.DMA((3,)),
        ],
    )(*fixed(t, coarse_weight, context_weight), *near(rows, next_pair, xw_last))
    own = stack(stack_kernel, own, tw, column.shape[0])
    other = lax.ppermute(own, "core", swap)
    (crops,) = near(crops)
    grams, wanted, lay, number = call(
        functools.partial(prepare_kernel, patches),
        "prepare",
        8 * values * width * width,
        (
            pltpu.VMEM((width, 3 * width), BF16),
            pltpu.VMEM((1, count), jnp.int32),
            pltpu.VMEM((peers * 16, patches * 16), BF16),
            pltpu.VMEM((patches * 16, LANES - pixels), F32),
        ),
        limit=ROOM,
        in_specs=[VMEM, SMEM, HBM],
        out_specs=(VMEM,) * 4,
    )(*near(next_pair), crops, own)

    projected, slope, xw_first, tw_first = call(
        functools.partial(context_kernel, patches, peers),
        "context",
        6 * patches * 16 * width * width,
        (
            pltpu.VMEM((width, 2 * patches * 16), BF16),
            pltpu.VMEM((patches * 16, width), F32),
            pltpu.VMEM((width, 2 * ROWS), F32),
            pltpu.VMEM((width, ROWS), F32),
        ),
        limit=ROOM,
        in_specs=[VMEM] * 5 + [HBM] * 2,
        out_specs=(VMEM,) * 4,
        scratch_shapes=[
            pltpu.VMEM((patches * 16, pixels), F32),
            pltpu.SMEM((4, patches), jnp.int32),
            pltpu.SemaphoreType.DMA((3,)),
        ],
    )(crops, own, other, *near(coarses, projects), *fixed(xw, tw))
    de, last_de, deep, dslot = call(
        middle_kernel,
        "middle",
        6 * count * width * width,
        (
            pltpu.HBM((width, count), F32),
            pltpu.VMEM((width, ROWS), F32),
            pltpu.VMEM((3 * width, values), BF16),
            pltpu.VMEM((patches * 16, width), F32),
        ),
        limit=ROOM,
        in_specs=[VMEM] * 6 + [HBM] * 4,
        out_specs=(HBM,) + (VMEM,) * 3,
        scratch_shapes=[
            pltpu.VMEM((width, count), F32),
            pltpu.VMEM((width, count), F32),
            pltpu.VMEM((2 * patches * 16, ROWS), BF16),
            pltpu.VMEM((2, width, ROWS), F32),
            pltpu.VMEM((2, 3 * width, ROWS), BF16),
            pltpu.VMEM((2 * width, ROWS), BF16),
            pltpu.SemaphoreType.DMA((steps,)),
            pltpu.SemaphoreType.DMA((steps,)),
            pltpu.SemaphoreType.DMA((steps,)),
            pltpu.SemaphoreType.DMA((2,)),
        ],
    )(*near(projected, grams, wanted, xw_first, tw_first, tw_last), *fixed(xw, xw_last, tw, pair))
    back = call(
        closing_kernel,
        "closing",
        6 * patches * 16 * width * width,
        pltpu.VMEM((peers * 16, LANES), F32),
        limit=ROOM,
        in_specs=[VMEM] * 6,
        out_specs=VMEM,
    )(*near(dslot, slope, coarses, projects, lay, number))
    returned = lax.all_to_all(back, patch, 0, 0, tiled=True)

    fine_grad = call(
        last_kernel,
        "last",
        6 * count * values * width,
        pltpu.HBM((count, values), F32),
        limit=ROOM,
        in_specs=[HBM, VMEM, VMEM],
        out_specs=HBM,
        scratch_shapes=[
            pltpu.VMEM((width, count), F32),
            pltpu.VMEM((count, values), F32),
            pltpu.VMEM((3 * width, ROWS), BF16),
            pltpu.SemaphoreType.DMA((steps,)),
            pltpu.SemaphoreType.DMA((steps,)),
        ],
    )(*fixed(de), *near(last_de, deep))
    part = (1, half, pixels)
    mine, theirs = call(
        scatter_kernel,
        "scatter",
        10000,
        (jax.ShapeDtypeStruct(part, F32), jax.ShapeDtypeStruct(part, F32)),
        limit=ROOM,
        in_specs=[VMEM, HBM],
        out_specs=(VMEM, VMEM),
        scratch_shapes=[pltpu.VMEM((SIDE * SIDE, pixels), F32)],
    )(returned, *fixed(fine_grad))
    coarse_grad = mine + lax.ppermute(theirs, "lvl", swap)
    return (coarse_grad, fine_grad.reshape(fine_input.shape))


def solution(mesh):
    sides, peers = mesh.shape["lvl"], mesh.shape["patch"]
    fine = jax.sharding.Mesh(mesh.devices.reshape(sides, peers // 4, 2, 2), ("lvl", "far", "y", "core"))
    patch = ("far", "y", "core")
    both = ("lvl",) + patch
    in_specs = (
        P(patch, "lvl", None),
        P(),
        P(both, None, None),
        P(both, None, None),
        P(both, None),
        P(),
        P(),
        P(),
    )
    out_specs = (P(patch, "lvl", None), P(both, None, None))
    return jax.shard_map(body, mesh=fine, in_specs=in_specs, out_specs=out_specs, check_vma=False)
```
